32 devices in a mesh: section: 2 (over x), tensor: 2 (over core), dp: 8 (over z, y).
Axes of the slice: x: 2, y: 2, z: 4, core: 2. Of those that a mesh axis runs over, the one named last changes fastest.
Arguments:
- tokens: bfloat16 [2048, 2048], P('dp'), may hold values from -6 to 6
- cotangent: bfloat16 [2048, 2048], P('dp'), may hold values from -6 to 6
- seq_lengths: int32 [48], replicated, may hold values from 0 to 128, as said below
- seq_group: int32 [48], replicated, may hold values from 0 to 7
- seq_micro: int32 [48], replicated, may hold values from 0 to 1
- attn_gain: bfloat16 [2, 2048], P('section', 'dp'), may hold values from 0.099609375 to 1.8984375
- w_query: bfloat16 [2, 2048, 2048], P('section', 'dp', 'tensor'), may hold values from -0.1875 to 0.1875
- key_matrix: bfloat16 [2, 2048, 256], P('section', 'dp', 'tensor'), may hold values from -0.1875 to 0.1875
- value_matrix: bfloat16 [2, 2048, 256], P('section', 'dp', 'tensor'), may hold values from -0.125 to 0.125
- w_out: bfloat16 [2, 2048, 2048], P('section', ('tensor', 'dp')), may hold values from -0.5 to 0.5
- mlp_gain: bfloat16 [2, 2048], P('section', 'dp'), may hold values from 0.099609375 to 1.8984375
- w_gate: bfloat16 [2, 2048, 5632], P('section', 'dp', 'tensor'), may hold values from -0.125 to 0.125
- w_up: bfloat16 [2, 2048, 5632], P('section', 'dp', 'tensor'), may hold values from -0.125 to 0.125
- w_down: bfloat16 [2, 5632, 2048], P('section', ('tensor', 'dp')), may hold values from -0.109375 to 0.109375
Outputs:
- section_out: bfloat16 [2, 2048, 2048], P('section', 'dp')
- input_grad: float32 [2, 2048, 2048], P('section', 'dp')
- grad_attn_gain: float32 [2, 2048], P('section', 'dp')
- grad_w_query: float32 [2, 2048, 2048], P('section', 'dp', 'tensor')
- grad_w_key: float32 [2, 2048, 256], P('section', 'dp', 'tensor')
- grad_w_value: float32 [2, 2048, 256], P('section', 'dp', 'tensor')
- grad_w_out: float32 [2, 2048, 2048], P('section', ('tensor', 'dp'))
- grad_mlp_gain: float32 [2, 2048], P('section', 'dp')
- grad_w_gate: float32 [2, 2048, 5632], P('section', 'dp', 'tensor')
- grad_w_up: float32 [2, 2048, 5632], P('section', 'dp', 'tensor')
- grad_w_down: float32 [2, 5632, 2048], P('section', ('tensor', 'dp'))
The draws below stay inside these ranges and needn't reach their ends.
Inputs may be any that keep to these rules, and one draw needn't show every extreme that they name: `seq_lengths`: every slot (data group, micro-batch) is named by exactly three sequences; the lengths of one slot's sequences sum to between 64 and 128; in one slot a single sequence fills all 128 rows and the slot's other two have length 0.
All inputs are finite; a program needn't handle non-finite values.
Results may differ from the reference program's by a relative error of at most 0.03.
Values may be sent and summed in bfloat16 or wider, within the bound.
A program may use at most 384 MiB of HBM per device.

```python
import jax
import jax.numpy as jnp
from jax import lax

MODEL_DIM = 2048
QUERY_HEADS = 32
KEY_VALUE_HEADS = 4
HEAD_DIM = 64
FF = 5632
CAP = 128
MICRO = 2
TOKENS = 2048
N_SECTION = 2
N_DP = 8


def layout_draw(key):
    slot_count = N_DP * MICRO
    key_list = jax.random.split(key, 7)
    slot_order = jnp.concatenate([jax.random.permutation(key_list[0], slot_count), jax.random.permutation(key_list[1], slot_count), jax.random.permutation(key_list[2], slot_count)]).astype(jnp.int32)
    seq_share = jnp.concatenate([jax.random.randint(key_list[3], (slot_count,), 1, 4), jax.random.randint(key_list[4], (2 * slot_count,), 0, 4)]).astype(jnp.int32)
    slot_totals = jax.random.randint(key_list[5], (slot_count,), CAP // 2, CAP + 1)
    fullest = jax.random.randint(key_list[6], (), 0, slot_count)
    slot_totals = jnp.where(jnp.arange(slot_count) == fullest, CAP, slot_totals).astype(jnp.int32)
    seq_index = jnp.arange(3 * slot_count)
    seq_share = jnp.where((slot_order == fullest) & (seq_index >= slot_count), 0, seq_share).astype(jnp.int32)
    same_slot = (slot_order[:, None] == slot_order[None, :]).astype(jnp.int32)
    earlier = (seq_index[None, :] <= seq_index[:, None]).astype(jnp.int32)
    reached = jnp.sum(same_slot * earlier * seq_share[None, :], axis=1)
    summed = jnp.sum(same_slot * seq_share[None, :], axis=1)
    slot_span = slot_totals[slot_order]
    lengths = slot_span * reached // summed - slot_span * (reached - seq_share) // summed
    return (lengths.astype(jnp.int32), (slot_order // MICRO).astype(jnp.int32), (slot_order % MICRO).astype(jnp.int32))


def draw_seq_lengths(key, part):
    return layout_draw(key)[0]


def draw_seq_group(key, part):
    return layout_draw(key)[1]


def draw_seq_micro(key, part):
    return layout_draw(key)[2]


def level_of(key, shape, shards, least, largest):
    factor_of, own = 1.0, jax.random.fold_in(key, 6)
    for axis_at, parts in shards:
        steps = jnp.exp(jax.random.uniform(jax.random.fold_in(own, axis_at), (parts,), jnp.float32, least / len(shards), largest / len(shards)))
        factor_of = factor_of * jnp.repeat(steps, shape[axis_at] // parts).reshape([-1 if axis == axis_at else 1 for axis in range(len(shape))])
    return factor_of


def bell_draw(own_key, dims, scale, most, cuts=(), kind=jnp.bfloat16):
    values = jax.random.normal(own_key, dims, jnp.float32) * scale
    if len(cuts) > 0:
        values = level_of(own_key, dims, cuts, -0.22, 0.18) * values
    return jnp.clip(values, min=-most, max=most).astype(kind)


def setup_inputs(seed: int = 0) -> dict:
    streams_of = jax.random.split(jax.random.key(seed), 15)
    return {
        "tokens": bell_draw(streams_of[0], (TOKENS, MODEL_DIM), 1.0, 6.0, ((0, 8),)),
        "cotangent": bell_draw(streams_of[1], (TOKENS, MODEL_DIM), 1.0, 6.0, ((0, 8),)),
        "seq_lengths": draw_seq_lengths(jax.random.fold_in(streams_of[14], 71), 0),
        "seq_group": draw_seq_group(jax.random.fold_in(streams_of[14], 71), 0),
        "seq_micro": draw_seq_micro(jax.random.fold_in(streams_of[14], 71), 0),
        "attn_gain": jnp.clip(1.0 + 0.18 * jax.random.normal(streams_of[5], (N_SECTION, MODEL_DIM), jnp.float32), 0.099609375, 1.8984375).astype(jnp.bfloat16),
        "w_query": bell_draw(streams_of[6], (N_SECTION, MODEL_DIM, QUERY_HEADS * HEAD_DIM), (MODEL_DIM // 2) ** -0.5, 0.1875, ((0, 2), (1, 8), (2, 2))),
        "key_matrix": bell_draw(streams_of[7], (N_SECTION, MODEL_DIM, KEY_VALUE_HEADS * HEAD_DIM), (MODEL_DIM // 2) ** -0.5, 0.1875, ((0, 2), (1, 8), (2, 2))),
        "value_matrix": bell_draw(streams_of[8], (N_SECTION, MODEL_DIM, KEY_VALUE_HEADS * HEAD_DIM), MODEL_DIM ** -0.5, 0.125, ((0, 2), (1, 8), (2, 2))),
        "w_out": bell_draw(streams_of[9], (N_SECTION, QUERY_HEADS * HEAD_DIM, MODEL_DIM), (QUERY_HEADS * HEAD_DIM // 16) ** -0.5, 0.5, ((0, 2), (1, 16))),
        "mlp_gain": jnp.clip(1.0 + 0.18 * jax.random.normal(streams_of[10], (N_SECTION, MODEL_DIM), jnp.float32), 0.099609375, 1.8984375).astype(jnp.bfloat16),
        "w_gate": bell_draw(streams_of[11], (N_SECTION, MODEL_DIM, FF), MODEL_DIM ** -0.5, 0.125, ((0, 2), (1, 8), (2, 2))),
        "w_up": bell_draw(streams_of[12], (N_SECTION, MODEL_DIM, FF), MODEL_DIM ** -0.5, 0.125, ((0, 2), (1, 8), (2, 2))),
        "w_down": bell_draw(streams_of[13], (N_SECTION, FF, MODEL_DIM), (FF // 2) ** -0.5, 0.109375, ((0, 2), (1, 16))),
    }


HIGH_PRECISION = lax.Precision.HIGHEST
eps_norm = 1e-05
rope_base = 10000.0

@jax.custom_vjp
def low_precision(v):
    return lax.optimization_barrier(v.astype(jnp.bfloat16)).astype(jnp.float32)

@jax.custom_vjp
def low_precision_backward(v):
    return v

def low_keep(v):
    return (low_precision(v), None)

def low_pass(kept, grad):
    return (grad,)

def back_keep(v):
    return (v, None)

def back_low(kept, grad):
    return (low_precision(grad),)
low_precision.defvjp(low_keep, low_pass)
low_precision_backward.defvjp(back_keep, back_low)

def slot_layout(seq_lengths, seq_group, seq_micro):
    row_ids = jnp.arange(CAP, dtype=jnp.int32)
    numbers = jnp.arange(seq_lengths.shape[0], dtype=jnp.int32) + 1
    slot_of = seq_group * MICRO + seq_micro

    def one_slot(slot_id):
        inside = (slot_of == slot_id).astype(jnp.int32)
        taken_len = seq_lengths * inside
        starts = jnp.cumsum(taken_len) - taken_len
        member = ((row_ids[:, None] >= starts[None, :]) & (row_ids[:, None] < (starts + taken_len)[None, :])).astype(jnp.int32)
        labels = lax.optimization_barrier(jnp.sum(member * numbers[None, :], axis=1))
        token_positions = lax.optimization_barrier(jnp.sum(member * (row_ids[:, None] - starts[None, :]), axis=1))
        return (labels, token_positions)
    return jax.vmap(one_slot)(jnp.arange(N_DP * MICRO, dtype=jnp.int32))

def apply_rotary(value_rows, token_positions, direction):
    half_size = value_rows.shape[-1] // 2
    frequency = rope_base ** (-2.0 * jnp.arange(half_size, dtype=jnp.float32) / value_rows.shape[-1])
    angles = token_positions.astype(jnp.float32)[:, None] * frequency[None, :]
    cosines = jnp.cos(angles)[:, None, :]
    sines_part = direction * jnp.sin(angles)[:, None, :]
    first_half = value_rows[..., :half_size]
    second_half = value_rows[..., half_size:]
    return jnp.concatenate([first_half * cosines - second_half * sines_part, second_half * cosines + first_half * sines_part], axis=-1)

def rms_scale(value_rows):
    return value_rows * lax.rsqrt(lax.optimization_barrier(jnp.mean(value_rows * value_rows, axis=-1, keepdims=True)) + eps_norm)

def block_forward(inputs, params, labels, token_positions):
    attn_gain, w_query, key_matrix, value_matrix, w_out, mlp_gain, w_gate, w_up, w_down = params
    total_row_count = inputs.shape[0]
    query_group_width = QUERY_HEADS // KEY_VALUE_HEADS
    normalized_input = low_precision(rms_scale(inputs) * attn_gain)
    query_rows = low_precision_backward(jnp.dot(normalized_input, w_query, precision=HIGH_PRECISION))
    unrotated_keys = low_precision_backward(jnp.dot(normalized_input, key_matrix, precision=HIGH_PRECISION))
    value_rows = low_precision(low_precision_backward(jnp.dot(normalized_input, value_matrix, precision=HIGH_PRECISION))).reshape(total_row_count, KEY_VALUE_HEADS, HEAD_DIM)
    query_rows = low_precision(apply_rotary(query_rows.reshape(total_row_count, QUERY_HEADS, HEAD_DIM), token_positions, 1.0)).reshape(total_row_count, KEY_VALUE_HEADS, query_group_width, HEAD_DIM)
    rotated_keys = low_precision(apply_rotary(unrotated_keys.reshape(total_row_count, KEY_VALUE_HEADS, HEAD_DIM), token_positions, 1.0))
    row_ids = jnp.arange(total_row_count, dtype=jnp.int32)
    allowed = (labels[:, None] == labels[None, :]) & (row_ids[None, :] <= row_ids[:, None])
    scores = low_precision_backward(jnp.einsum('qgjd,kgd->gjqk', query_rows, rotated_keys, precision=HIGH_PRECISION)) * HEAD_DIM ** (-0.5)
    scores = jnp.where(allowed, scores, -1e+30)
    attn_probs = low_precision(jax.nn.softmax(scores, axis=-1))
    mixed_heads = jnp.einsum('gjqk,kgd->qgjd', attn_probs, value_rows, precision=HIGH_PRECISION).reshape(total_row_count, QUERY_HEADS * HEAD_DIM)
    mixed_heads = low_precision(low_precision_backward(mixed_heads))
    residual = inputs + low_precision_backward(jnp.dot(mixed_heads, w_out, precision=HIGH_PRECISION))
    normed_mlp = low_precision(rms_scale(residual) * mlp_gain)
    gate_proj = low_precision_backward(jnp.dot(normed_mlp, w_gate, precision=HIGH_PRECISION))
    up_proj = low_precision_backward(jnp.dot(normed_mlp, w_up, precision=HIGH_PRECISION))
    hidden = low_precision(jax.nn.silu(gate_proj) * up_proj)
    return residual + low_precision_backward(jnp.dot(hidden, w_down, precision=HIGH_PRECISION))

def reference(tokens, cotangent, seq_lengths, seq_group, seq_micro, attn_gain, w_query, key_matrix, value_matrix, w_out, mlp_gain, w_gate, w_up, w_down):
    labels, token_positions = slot_layout(seq_lengths, seq_group, seq_micro)
    weights = tuple((weight_part.astype(jnp.float32) for weight_part in (attn_gain, w_query, key_matrix, value_matrix, w_out, mlp_gain, w_gate, w_up, w_down)))
    first_layer = tuple((weight_part[0] for weight_part in weights))
    second_layer = tuple((weight_part[1] for weight_part in weights))
    slot_count = labels.shape[0]
    entry_all = tokens.astype(jnp.float32).reshape(slot_count, CAP, MODEL_DIM)
    target_all = cotangent.astype(jnp.float32).reshape(slot_count, CAP, MODEL_DIM)

    def one_slot(totals, slot_data):
        entry_rows, target, slot_labels, slot_places = slot_data
        live_rows = (slot_labels > 0).astype(jnp.float32)[:, None]

        def loss_of(entry_in, first_params, second_params, extra_in):
            middle = block_forward(entry_in, first_params, slot_labels, slot_places)
            handed = low_precision(low_precision_backward(middle)) + extra_in
            final_out = block_forward(handed, second_params, slot_labels, slot_places)
            return (jnp.sum(final_out * target * live_rows), (handed, final_out))
        loss_value, backward, (handed, final_out) = jax.vjp(loss_of, entry_rows, first_layer, second_layer, jnp.zeros_like(entry_rows), has_aux=True)
        grad_entry, grad_first, grad_second, grad_extra = backward(jnp.ones_like(loss_value))
        totals = jax.tree.map(lambda whole_sum, addend: whole_sum + addend, totals, (grad_first, grad_second))
        return (totals, (handed, final_out, grad_entry, grad_extra))
    zero_grads = jax.tree.map(jnp.zeros_like, (first_layer, second_layer))
    totals, (handed, final_out, grad_entry, grad_extra) = lax.scan(one_slot, zero_grads, (entry_all, target_all, labels, token_positions))
    token_count = slot_count * CAP
    section_out = jnp.stack([handed.reshape(token_count, MODEL_DIM), final_out.reshape(token_count, MODEL_DIM)]).astype(jnp.bfloat16)
    input_grad = jnp.stack([grad_entry.reshape(token_count, MODEL_DIM), grad_extra.reshape(token_count, MODEL_DIM)])
    stacked = [jnp.stack([first_g, second_g]) for first_g, second_g in zip(totals[0], totals[1])]
    return (section_out, input_grad, stacked[0], stacked[1], stacked[2], stacked[3], stacked[4], stacked[5], stacked[6], stacked[7], stacked[8])
```

```python
import functools
import types

import jax
import jax.numpy as jnp
from jax import lax
from jax.experimental import pallas as pl
from jax.experimental.pallas import tpu as pltpu
from jax.sharding import PartitionSpec as P

HEAD_DIM = 64
CAP = 128
MICRO = 2


eps_norm = 1e-05
rope_base = 10000.0


def passed_along(shard, axis, by):
    count = lax.axis_size(axis)
    pairs = [(i, i + by) for i in range(count) if 0 <= i + by < count]
    return lax.ppermute(shard, axis, pairs)


def slot_layout(seq_lengths, seq_group, seq_micro, group_id, micro_total, slot_rows):
    row_ids = jnp.arange(slot_rows, dtype=jnp.int32)
    numbers = jnp.arange(seq_lengths.shape[0], dtype=jnp.int32) + 1
    label_list = []
    place_list = []
    for micro_id in range(micro_total):
        inside = ((seq_group == group_id) & (seq_micro == micro_id)).astype(jnp.int32)
        taken_len = seq_lengths * inside
        starts = jnp.cumsum(taken_len) - taken_len
        member = (
            (row_ids[:, None] >= starts[None, :])
            & (row_ids[:, None] < (starts + taken_len)[None, :])
        ).astype(jnp.int32)
        label_list.append(jnp.sum(member * numbers[None, :], axis=1))
        place_list.append(jnp.sum(member * (row_ids[:, None] - starts[None, :]), axis=1))
    return (jnp.stack(label_list), jnp.stack(place_list))


def apply_rotary(value_rows, token_positions, direction):
    half_size = value_rows.shape[-1] // 2
    frequency = rope_base ** (
        -2.0 * jnp.arange(half_size, dtype=jnp.float32) / value_rows.shape[-1]
    )
    angles = token_positions.astype(jnp.float32)[:, None] * frequency[None, :]
    cosines = jnp.cos(angles)[:, None, :]
    sines_part = direction * jnp.sin(angles)[:, None, :]
    first_half = value_rows[..., :half_size]
    second_half = value_rows[..., half_size:]
    return jnp.concatenate(
        [
            first_half * cosines - second_half * sines_part,
            second_half * cosines + first_half * sines_part,
        ],
        axis=-1,
    )


def rms_parts(value_rows):
    inverse = lax.rsqrt(jnp.mean(value_rows * value_rows, axis=-1, keepdims=True) + eps_norm)
    return (value_rows * inverse, inverse)


def dot_trans(left, right):
    return lax.dot_general(
        left, right, (((1,), (1,)), ((), ())), preferred_element_type=jnp.float32
    )


def dot_rows(left, right):
    return lax.dot_general(
        left, right, (((0,), (0,)), ((), ())), preferred_element_type=jnp.float32
    )


def tensor_total(partial_sum):
    return lax.psum(partial_sum, "tensor")


def input_total(partial_sum):
    return lax.psum(partial_sum.astype(jnp.bfloat16), "tensor").astype(jnp.float32)


def mask_of(labels):
    row_ids = jnp.arange(labels.shape[0], dtype=jnp.int32)
    return (labels[:, None] == labels[None, :]) & (row_ids[None, :] <= row_ids[:, None])


def forward_slot(inputs, labels, token_positions, attn_w, mlp_w):
    attn_gain, w_query, key_matrix, value_matrix, w_out = attn_w
    mlp_gain, w_gate, w_up, w_down = mlp_w
    total_row_count = inputs.shape[0]
    head_count = w_query.shape[1] // HEAD_DIM
    kv_count = key_matrix.shape[1] // HEAD_DIM
    query_group_width = head_count // kv_count
    scaled, inverse_attn = rms_parts(inputs)
    normalized_input = (scaled * attn_gain.astype(jnp.float32)).astype(jnp.bfloat16)
    query_rows = jnp.dot(normalized_input, w_query, preferred_element_type=jnp.float32)
    unrotated_keys = jnp.dot(normalized_input, key_matrix, preferred_element_type=jnp.float32)
    value_rows = (
        jnp.dot(normalized_input, value_matrix, preferred_element_type=jnp.float32)
        .astype(jnp.bfloat16)
        .reshape(total_row_count, kv_count, HEAD_DIM)
    )
    query_rows = (
        apply_rotary(
            query_rows.reshape(total_row_count, head_count, HEAD_DIM), token_positions, 1.0
        )
        .astype(jnp.bfloat16)
        .reshape(total_row_count, kv_count, query_group_width, HEAD_DIM)
    )
    rotated_keys = apply_rotary(
        unrotated_keys.reshape(total_row_count, kv_count, HEAD_DIM), token_positions, 1.0
    ).astype(jnp.bfloat16)
    scores = jnp.einsum(
        "qgjd,kgd->gjqk", query_rows, rotated_keys, preferred_element_type=jnp.float32
    ) * HEAD_DIM ** (-0.5)
    scores = jnp.where(mask_of(labels), scores, -1e30)
    top_score = jnp.max(scores, axis=-1, keepdims=True)
    exp_scores = jnp.exp(scores - top_score)
    total_mass = jnp.sum(exp_scores, axis=-1, keepdims=True)
    attn_probs = (exp_scores / total_mass).astype(jnp.bfloat16)
    log_mass = top_score + jnp.log(total_mass)
    mixed_heads = jnp.einsum(
        "gjqk,kgd->qgjd", attn_probs, value_rows, preferred_element_type=jnp.float32
    )
    mixed_heads = mixed_heads.reshape(total_row_count, head_count * HEAD_DIM).astype(jnp.bfloat16)
    residual = inputs + tensor_total(
        jnp.dot(mixed_heads, w_out, preferred_element_type=jnp.float32)
    )
    scaled_mlp, inverse_mlp = rms_parts(residual)
    normed_mlp = (scaled_mlp * mlp_gain.astype(jnp.float32)).astype(jnp.bfloat16)
    gate_proj = jnp.dot(normed_mlp, w_gate, preferred_element_type=jnp.float32)
    up_proj = jnp.dot(normed_mlp, w_up, preferred_element_type=jnp.float32)
    hidden = (jax.nn.silu(gate_proj) * up_proj).astype(jnp.bfloat16)
    result = residual + tensor_total(jnp.dot(hidden, w_down, preferred_element_type=jnp.float32))
    kept_state = (
        inputs,
        inverse_attn,
        normalized_input,
        query_rows,
        rotated_keys,
        value_rows,
        log_mass,
        mixed_heads,
        residual,
        inverse_mlp,
        normed_mlp,
        gate_proj,
        up_proj,
        hidden,
    )
    return (result, kept_state)


def backward_slot(grad_out, kept_state, labels, token_positions, attn_w, mlp_w):
    attn_gain, w_query, key_matrix, value_matrix, w_out = attn_w
    mlp_gain, w_gate, w_up, w_down = mlp_w
    (
        inputs,
        inverse_attn,
        normalized_input,
        query_rows,
        rotated_keys,
        value_rows,
        log_mass,
        mixed_heads,
        residual,
        inverse_mlp,
        normed_mlp,
        gate_proj,
        up_proj,
        hidden,
    ) = kept_state
    total_row_count = inputs.shape[0]
    head_count = w_query.shape[1] // HEAD_DIM
    kv_count = key_matrix.shape[1] // HEAD_DIM
    query_group_width = head_count // kv_count
    down_in = grad_out.astype(jnp.bfloat16)
    grad_hidden = dot_trans(down_in, w_down)
    grad_w_down = dot_rows(hidden, down_in)
    sigmoid_gate = jax.nn.sigmoid(gate_proj)
    grad_gate = (
        grad_hidden * up_proj * sigmoid_gate * (1.0 + gate_proj * (1.0 - sigmoid_gate))
    ).astype(jnp.bfloat16)
    grad_up = (grad_hidden * gate_proj * sigmoid_gate).astype(jnp.bfloat16)
    grad_w_gate = dot_rows(normed_mlp, grad_gate)
    grad_w_up = dot_rows(normed_mlp, grad_up)
    grad_normed_mlp = input_total(dot_trans(grad_gate, w_gate) + dot_trans(grad_up, w_up))
    scaled_mlp = residual * inverse_mlp
    grad_mlp_gain = jnp.sum(grad_normed_mlp * scaled_mlp, axis=0)
    inner_mlp = grad_normed_mlp * mlp_gain.astype(jnp.float32)
    grad_residual = grad_out + inverse_mlp * (
        inner_mlp - scaled_mlp * jnp.mean(inner_mlp * scaled_mlp, axis=-1, keepdims=True)
    )
    out_in = grad_residual.astype(jnp.bfloat16)
    grad_w_out = dot_rows(mixed_heads, out_in)
    grad_mixed = (
        dot_trans(out_in, w_out)
        .astype(jnp.bfloat16)
        .reshape(total_row_count, kv_count, query_group_width, HEAD_DIM)
    )
    scores = jnp.einsum(
        "qgjd,kgd->gjqk", query_rows, rotated_keys, preferred_element_type=jnp.float32
    ) * HEAD_DIM ** (-0.5)
    scores = jnp.where(mask_of(labels), scores, -1e30)
    probs_full = jnp.exp(scores - log_mass)
    attn_probs = probs_full.astype(jnp.bfloat16)
    grad_probs = jnp.einsum(
        "qgjd,kgd->gjqk", grad_mixed, value_rows, preferred_element_type=jnp.float32
    )
    grad_values = jnp.einsum(
        "gjqk,qgjd->kgd", attn_probs, grad_mixed, preferred_element_type=jnp.float32
    )
    spread_term = jnp.sum(grad_probs * probs_full, axis=-1, keepdims=True)
    grad_scores = (probs_full * (grad_probs - spread_term) * HEAD_DIM ** (-0.5)).astype(
        jnp.bfloat16
    )
    grad_queries = jnp.einsum(
        "gjqk,kgd->qgjd", grad_scores, rotated_keys, preferred_element_type=jnp.float32
    )
    grad_keys = jnp.einsum(
        "gjqk,qgjd->kgd", grad_scores, query_rows, preferred_element_type=jnp.float32
    )
    grad_queries = (
        apply_rotary(
            grad_queries.reshape(total_row_count, head_count, HEAD_DIM), token_positions, -1.0
        )
        .reshape(total_row_count, head_count * HEAD_DIM)
        .astype(jnp.bfloat16)
    )
    grad_keys = (
        apply_rotary(grad_keys, token_positions, -1.0)
        .reshape(total_row_count, kv_count * HEAD_DIM)
        .astype(jnp.bfloat16)
    )
    grad_values = grad_values.reshape(total_row_count, kv_count * HEAD_DIM).astype(jnp.bfloat16)
    grad_w_query = dot_rows(normalized_input, grad_queries)
    grad_w_key = dot_rows(normalized_input, grad_keys)
    grad_w_value = dot_rows(normalized_input, grad_values)
    grad_normed = input_total(
        dot_trans(grad_queries, w_query)
        + dot_trans(grad_keys, key_matrix)
        + dot_trans(grad_values, value_matrix)
    )
    scaled = inputs * inverse_attn
    grad_attn_gain = jnp.sum(grad_normed * scaled, axis=0)
    inner_attn = grad_normed * attn_gain.astype(jnp.float32)
    grad_inputs = grad_residual + inverse_attn * (
        inner_attn - scaled * jnp.mean(inner_attn * scaled, axis=-1, keepdims=True)
    )
    attn_grads = (grad_attn_gain, grad_w_query, grad_w_key, grad_w_value, grad_w_out)
    mlp_grads = (grad_mlp_gain, grad_w_gate, grad_w_up, grad_w_down)
    return (grad_inputs, attn_grads, mlp_grads)


def general_device(
    tokens,
    cotangent,
    seq_lengths,
    seq_group,
    seq_micro,
    attn_gain,
    w_query,
    key_matrix,
    value_matrix,
    w_out,
    mlp_gain,
    w_gate,
    w_up,
    w_down,
):
    section_count = lax.axis_size("section")
    section_id = lax.axis_index("section")
    group_id = lax.axis_index("dp")
    slot_rows = CAP
    micro_total = MICRO
    tick_count = micro_total + section_count - 1
    model_width = tokens.shape[1]
    labels, token_positions = slot_layout(
        seq_lengths, seq_group, seq_micro, group_id, micro_total, slot_rows
    )
    live_rows = (labels > 0).astype(jnp.float32)
    attn_w = (
        lax.all_gather(attn_gain[0], "dp", axis=0, tiled=True),
        lax.all_gather(w_query[0], "dp", axis=0, tiled=True),
        lax.all_gather(key_matrix[0], "dp", axis=0, tiled=True),
        lax.all_gather(value_matrix[0], "dp", axis=0, tiled=True),
        lax.all_gather(w_out[0], "dp", axis=0, tiled=True),
    )
    mlp_w = (
        lax.all_gather(mlp_gain[0], "dp", axis=0, tiled=True),
        lax.all_gather(w_gate[0], "dp", axis=0, tiled=True),
        lax.all_gather(w_up[0], "dp", axis=0, tiled=True),
        lax.all_gather(w_down[0], "dp", axis=0, tiled=True),
    )
    is_first = section_id == 0
    received = jnp.zeros((slot_rows, model_width), jnp.bfloat16)
    sent_list = []
    kept_list = []
    for tick_id in range(tick_count):
        micro_id = jnp.clip(tick_id - section_id, 0, micro_total - 1)
        fresh_slot = min(tick_id, micro_total - 1)
        fresh_rows = tokens[fresh_slot * slot_rows : (fresh_slot + 1) * slot_rows]
        section_input = jnp.where(is_first, fresh_rows, received).astype(jnp.float32)
        result, kept_state = forward_slot(
            section_input, labels[micro_id], token_positions[micro_id], attn_w, mlp_w
        )
        handed = result.astype(jnp.bfloat16)
        sent_list.append(handed)
        kept_list.append(kept_state)
        if tick_id + 1 < tick_count:
            received = passed_along(handed, "section", 1)
    sent_all = jnp.stack(sent_list)
    section_out = lax.dynamic_slice_in_dim(sent_all, section_id, micro_total, 0).reshape(
        micro_total * slot_rows, model_width
    )[None]
    kept_all = jax.tree.map(lambda *pieces: jnp.stack(pieces), *kept_list)
    attn_w = (
        lax.all_gather(attn_gain[0], "dp", axis=0, tiled=True),
        lax.all_gather(w_query[0], "dp", axis=0, tiled=True),
        lax.all_gather(key_matrix[0], "dp", axis=0, tiled=True),
        lax.all_gather(value_matrix[0], "dp", axis=0, tiled=True),
        lax.all_gather(w_out[0], "dp", axis=0, tiled=True),
    )
    mlp_w = (
        lax.all_gather(mlp_gain[0], "dp", axis=0, tiled=True),
        lax.all_gather(w_gate[0], "dp", axis=0, tiled=True),
        lax.all_gather(w_up[0], "dp", axis=0, tiled=True),
        lax.all_gather(w_down[0], "dp", axis=0, tiled=True),
    )
    is_last = section_id == section_count - 1
    back_received = jnp.zeros((slot_rows, model_width), jnp.bfloat16)
    grad_list = []
    attn_sum = None
    mlp_sum = None
    for tick_id in range(tick_count):
        micro_raw = tick_id - (section_count - 1 - section_id)
        active = ((micro_raw >= 0) & (micro_raw < micro_total)).astype(jnp.float32)
        micro_id = jnp.clip(micro_raw, 0, micro_total - 1)
        target = lax.dynamic_slice_in_dim(cotangent, micro_id * slot_rows, slot_rows, 0).astype(
            jnp.float32
        )
        grad_out = (
            jnp.where(
                is_last, target * live_rows[micro_id][:, None], back_received.astype(jnp.float32)
            )
            * active
        )
        kept_state = jax.tree.map(lambda stacked: stacked[micro_id + section_id], kept_all)
        grad_inputs, attn_grads, mlp_grads = backward_slot(
            grad_out, kept_state, labels[micro_id], token_positions[micro_id], attn_w, mlp_w
        )
        grad_list.append(grad_inputs)
        gain_a, query_g, key_g, value_g, out_g = attn_grads
        attn_grads = (
            lax.psum_scatter(
                gain_a.astype(jnp.bfloat16), "dp", scatter_dimension=0, tiled=True
            ).astype(jnp.float32),
            lax.psum_scatter(
                query_g.astype(jnp.bfloat16), "dp", scatter_dimension=0, tiled=True
            ).astype(jnp.float32),
            lax.psum_scatter(
                key_g.astype(jnp.bfloat16), "dp", scatter_dimension=0, tiled=True
            ).astype(jnp.float32),
            lax.psum_scatter(
                value_g.astype(jnp.bfloat16), "dp", scatter_dimension=0, tiled=True
            ).astype(jnp.float32),
            lax.psum_scatter(
                out_g.astype(jnp.bfloat16), "dp", scatter_dimension=0, tiled=True
            ).astype(jnp.float32),
        )
        gain_m, gate_g, up_g, down_g = mlp_grads
        mlp_grads = (
            lax.psum_scatter(
                gain_m.astype(jnp.bfloat16), "dp", scatter_dimension=0, tiled=True
            ).astype(jnp.float32),
            lax.psum_scatter(
                gate_g.astype(jnp.bfloat16), "dp", scatter_dimension=0, tiled=True
            ).astype(jnp.float32),
            lax.psum_scatter(
                up_g.astype(jnp.bfloat16), "dp", scatter_dimension=0, tiled=True
            ).astype(jnp.float32),
            lax.psum_scatter(
                down_g.astype(jnp.bfloat16), "dp", scatter_dimension=0, tiled=True
            ).astype(jnp.float32),
        )
        attn_sum = attn_grads if attn_sum is None else jax.tree.map(jnp.add, attn_sum, attn_grads)
        mlp_sum = mlp_grads if mlp_sum is None else jax.tree.map(jnp.add, mlp_sum, mlp_grads)
        if tick_id + 1 < tick_count:
            back_received = passed_along(grad_inputs.astype(jnp.bfloat16), "section", -1)
    grad_all = jnp.stack(grad_list)
    input_grad = lax.dynamic_slice_in_dim(
        grad_all, section_count - 1 - section_id, micro_total, 0
    ).reshape(micro_total * slot_rows, model_width)[None]
    return (
        section_out,
        input_grad,
        attn_sum[0][None],
        attn_sum[1][None],
        attn_sum[2][None],
        attn_sum[3][None],
        attn_sum[4][None],
        mlp_sum[0][None],
        mlp_sum[1][None],
        mlp_sum[2][None],
        mlp_sum[3][None],
    )


RING = 8
LANES = 128
MESH_ID = pl.DeviceIdType.MESH
VMEM_BYTES = 60 * 2**20


def ring_fits(mesh):
    shape = dict(mesh.shape)
    return shape["section"] == 2 and shape["tensor"] == 2 and shape["dp"] == RING and MICRO == 2


def ring_place(group_id):
    z, y = group_id // 2, group_id % 2
    return jnp.where(y == 0, z, RING - 1 - z)


def ring_group(place):
    place = lax.rem(place + 2 * RING, RING)
    return jnp.where(place < RING // 2, 2 * place, 2 * (RING - 1 - place) + 1)


def copy_to(device, src, dst, send_sem, recv_sem):
    return pltpu.make_async_remote_copy(
        src_ref=src,
        dst_ref=dst,
        send_sem=send_sem,
        recv_sem=recv_sem,
        device_id=device,
        device_id_type=MESH_ID,
    )


class Ring:
    def __init__(self, names, lazy, refs):
        self.ref = types.SimpleNamespace(**dict(zip(names, refs)))
        self.lazy = lazy
        self.loads = {}
        self.stores = []
        self.sent = []
        self.section = lax.axis_index("section")
        self.core = lax.axis_index("tensor")
        self.group = lax.axis_index("dp")
        self.first = self.section == 0
        self.place = ring_place(self.group)
        self.right = (self.section, self.core, ring_group(self.place + 1))
        self.left = (self.section, self.core, ring_group(self.place - 1))
        self.sibling = (self.section, 1 - self.core, self.group)
        self.across = (1 - self.section, self.core, self.group)
        self.far = [(f, g) for f in (0, 1) for g in range(RING) if (f, g) != (0, 0)]

    def load_all(self):
        for n, name in enumerate(self.lazy):
            source, here = getattr(self.ref, name + "_"), getattr(self.ref, name)
            self.loads[name] = pltpu.make_async_copy(source, here, self.ref.load_sem.at[n])
            self.loads[name].start()

    def need(self, *names):
        for name in names:
            if name in self.loads:
                self.loads.pop(name).wait()

    def store(self, here, there, n):
        copy = pltpu.make_async_copy(here, there, self.ref.store_sem.at[n])
        copy.start()
        self.stores.append(copy)

    def start(self, copy):
        copy.start()
        self.sent.append(copy)
        return copy

    def finish(self):
        self.need(*list(self.loads))
        for copy in self.sent:
            copy.wait_send()
        for copy in self.stores:
            copy.wait()

    def greet(self, devices):
        barrier = pltpu.get_barrier_semaphore()
        for device in devices:
            pl.semaphore_signal(barrier, inc=1, device_id=device, device_id_type=MESH_ID)
        pl.semaphore_wait(barrier, len(devices))

    def greet_ring(self):
        self.greet([self.right, self.left, self.sibling])

    def greet_all(self):
        self.greet([self.sibling] + [self.far_device(f, g) for f, g in self.far])

    def far_step(self, f, g):
        return lax.rem(self.section + f, 2), lax.rem(self.group + g, RING)

    def far_device(self, f, g):
        section, group = self.far_step(f, g)
        return (section, self.core, group)

    def far_from(self, f, g):
        section = lax.rem(self.section + 2 - f, 2)
        return section * RING + lax.rem(self.group + RING - g, RING)

    def row_of(self, offset, c=0):
        return pl.multiple_of(ring_group(self.place + offset) * CAP + c * (CAP // 2), CAP // 2)

    def columns(self, width, own=True):
        half = width // 2
        core = self.core if own else 1 - self.core
        return pl.ds(pl.multiple_of(core * half, half), half)

    def gather_work_sum(self, work, shadow):
        ref = self.ref
        whole, part, mate, total = ref.whole, ref.part, ref.mate, ref.total
        width, half_r = whole.shape[1], CAP // 2
        own_cols, other_cols = self.columns(width), self.columns(width, False)
        ways = ((0, self.right), (1, self.left))
        stream = ((0, 0), (0, 1), (1, 0), (1, 1), (2, 0), (2, 1), (3, 0))

        def landing(way, k, c, columns):
            offset, chunk = (-k, c) if way == 0 else (k, 1 - c)
            return whole.at[pl.ds(self.row_of(offset, chunk), half_r), columns]

        def move(device, where, sems, way, i):
            return copy_to(device, where, where, sems.at[0, way, i], sems.at[1, way, i])

        def forward(i, way, device):
            k, c = stream[i]
            self.start(move(device, landing(way, k, c, own_cols), ref.gather_sem, way, i))

        def arrived(i, way, device):
            k, c = stream[i]
            where = landing(way, k + 1, c, own_cols)
            move(device, where, ref.gather_sem, way, i).wait_recv()
            self.start(move(self.sibling, where, ref.pass_sem, way, i))

        def passed(i, way):
            k, c = stream[i]
            where = landing(way, k + 1, c, other_cols)
            move(self.sibling, where, ref.pass_sem, way, i).wait_recv()

        mate_in = {}

        def work_on(offset):
            if offset == RING // 2:
                for way in (0, 1):
                    passed(6, way)
            elif offset != 0:
                way, k = (0, -offset) if offset < 0 else (1, offset)
                for i in (2 * k - 2, 2 * k - 1):
                    passed(i, way)
            work(self.row_of(offset))
            q = offset % RING
            mate_in[q] = self.start(
                copy_to(
                    self.sibling,
                    part.at[pl.ds(self.row_of(offset), CAP), other_cols],
                    mate.at[q],
                    ref.mate_sem.at[0, q],
                    ref.mate_sem.at[1, q],
                )
            )

        for i in (0, 1):
            for way, device in ways:
                forward(i, way, device)
        work_on(0)
        for i in range(7):
            for way, device in ways:
                arrived(i, way, device)
                if i < 5:
                    forward(i + 2, way, device)
            for offset in ((), (-1,), (1,), (-2,), (2,), (-3, 3), (4,))[i]:
                work_on(offset)

        ready = set()

        def mine(offset, c):
            q = offset % RING
            if q not in ready:
                mate_in[q].wait_recv()
                ready.add(q)
            return part[pl.ds(self.row_of(q, c), half_r), own_cols].astype(jnp.float32) + mate[
                q, pl.ds(c * half_r, half_r)
            ].astype(jnp.float32)

        stream_sum = ((4, 0), (3, 1), (3, 0), (2, 1), (2, 0), (1, 1), (1, 0))
        moves = []
        for i, (q, c) in enumerate(stream_sum):
            for way, device in ways:
                offset, chunk = (q, c) if way == 0 else (-q, 1 - c)
                value = mine(offset, chunk)
                if i >= 2:
                    moves[2 * (i - 2) + way].wait_recv()
                    value = value + ref.sum_recv[way, i - 2].astype(jnp.float32)
                ref.sum_send[way, i] = value.astype(jnp.bfloat16)
                moves.append(
                    self.start(
                        copy_to(
                            device,
                            ref.sum_send.at[way, i],
                            ref.sum_recv.at[way, i],
                            ref.sum_sem.at[0, way, i],
                            ref.sum_sem.at[1, way, i],
                        )
                    )
                )
            shadow(i)
        halves = []
        for c in (1, 0):
            value = mine(0, c)
            at = (5, 6) if c == 1 else (6, 5)
            for way in (0, 1):
                moves[2 * at[way] + way].wait_recv()
                value = value + ref.sum_recv[way, at[way]].astype(jnp.float32)
            here = (pl.ds(c * half_r, half_r), own_cols)
            total[here] = value
            halves.append(
                self.start(
                    copy_to(
                        self.sibling,
                        total.at[here],
                        total.at[here],
                        ref.half_sem.at[0, c],
                        ref.half_sem.at[1, c],
                    )
                )
            )
        for copy in halves:
            copy.wait_recv()


def by_rows(body, step=16):
    @pl.loop(0, CAP, step=step)
    def _(at):
        body(pl.ds(pl.multiple_of(at, step), step), at)


def inverse_rms(value):
    return lax.rsqrt(jnp.mean(value * value, axis=-1, keepdims=True) + eps_norm)


def norm_rows(ring, source, gain):
    own = ring.row_of(0)

    def body(here, at):
        value = source[here, :].astype(jnp.float32)
        low = (value * inverse_rms(value) * gain).astype(jnp.bfloat16)
        ring.ref.whole[pl.ds(pl.multiple_of(own + at, 16), 16), :] = low

    by_rows(body)


def back_rows(ring, base, source, also=None):
    ref = ring.ref
    gain = ref.gain[...]
    ref.gain_grad[...] = jnp.zeros_like(ref.gain_grad)

    def body(here, at):
        x = source[here, :].astype(jnp.float32)
        inverse = inverse_rms(x)
        scaled = x * inverse
        grad = ref.total[here, :]
        moved = grad * scaled
        ref.gain_grad[...] += moved[:8] + moved[8:]
        inner = grad * gain
        value = base[here, :].astype(jnp.float32) + inverse * (
            inner - scaled * jnp.mean(inner * scaled, axis=-1, keepdims=True)
        )
        ref.out[here, :] = value
        if also is not None:
            also[here, :] = value.astype(jnp.bfloat16)

    by_rows(body)


def lane_low(shape, span):
    return lax.rem(lax.broadcasted_iota(jnp.int32, shape, 1), span) < span // 2


def rot_rows(value, cosines, sines):
    low = lane_low(value.shape, HEAD_DIM)
    partner = jnp.where(
        low, pltpu.roll(value, LANES - HEAD_DIM // 2, 1), pltpu.roll(value, HEAD_DIM // 2, 1)
    )
    return value * cosines + partner * sines


def pick(first, a, b):
    return jnp.where(first, a, b), jnp.where(first, b, a)


def heads_apart(value):
    low = lane_low(value.shape, LANES)
    return jnp.concatenate([jnp.where(low, value, 0.0), jnp.where(low, 0.0, value)], axis=0)


def heads_together(value):
    rows = value.shape[0] // 2
    return jnp.where(lane_low((rows, LANES), LANES), value[:rows], value[rows:])


def twice(kv):
    low = lane_low(kv.shape, LANES)
    other = pltpu.roll(kv, HEAD_DIM, 1)
    return (
        jnp.where(low, kv, other).astype(jnp.bfloat16),
        jnp.where(low, other, kv).astype(jnp.bfloat16),
    )


def dot_wide(left, right):
    return jnp.dot(left, right, preferred_element_type=jnp.float32)


def attend_kernel(has_gains, names, lazy, *refs):
    ring = Ring(names, lazy, refs)
    ref = ring.ref
    width = ref.whole.shape[1]
    ring.load_all()
    if has_gains:
        ring.greet_all()
        mine_at = ring.section * RING + ring.group
        ref.gains[mine_at] = ref.own_gain[...]
        for n, (f, g) in enumerate(ring.far):
            ring.start(
                copy_to(
                    ring.far_device(f, g),
                    ref.own_gain,
                    ref.gains.at[mine_at],
                    ref.far_sem.at[0, n],
                    ref.far_sem.at[1, n],
                )
            )
        for n, (f, g) in enumerate(ring.far):
            copy_to(
                ring.sibling,
                ref.own_gain,
                ref.gains.at[ring.far_from(f, g)],
                ref.far_sem.at[0, n],
                ref.far_sem.at[1, n],
            ).wait_recv()
        gain = jnp.concatenate([ref.gains[g, 0:1, :] for g in range(RING)], axis=-1)
    else:
        ring.greet_ring()
        gain = ref.gain[...]
    norm_rows(ring, ref.x, gain)

    def work(row):
        here = pl.ds(row, CAP)
        normed = ref.whole[here, :]
        ring.need("mine", "other", "cosines", "sines", "mask", "w_out")
        queries, kv = pick(
            ring.first, dot_wide(normed, ref.mine[...]), dot_wide(normed, ref.other[...])
        )
        cosines, sines = ref.cosines[here, :], ref.sines[here, :]
        queries = rot_rows(queries, cosines, sines)
        kv = jnp.where(lane_low(kv.shape, LANES), rot_rows(kv, cosines, sines), kv)
        ref.queries[here, :] = queries.astype(jnp.bfloat16)
        ref.kv[here, :] = kv.astype(jnp.bfloat16)
        keys, values = twice(kv)
        apart = heads_apart(queries).astype(jnp.bfloat16)
        allowed = ref.mask[here, :] > 0.5
        allowed = jnp.concatenate([allowed, allowed], axis=0)
        scores = jnp.where(allowed, dot_trans(apart, keys) * HEAD_DIM ** (-0.5), -1e30)
        weights = jnp.exp(scores - jnp.max(scores, axis=-1, keepdims=True))
        probs = weights / jnp.sum(weights, axis=-1, keepdims=True)
        ref.probs[pl.ds(pl.multiple_of(2 * row, 2 * CAP), 2 * CAP), :] = probs
        mixed = heads_together(dot_wide(probs.astype(jnp.bfloat16), values)).astype(jnp.bfloat16)
        ref.mixed[here, :] = mixed
        ref.part[here, :] = dot_wide(mixed, ref.w_out[...]).astype(jnp.bfloat16)

    def shadow(i):
        if i == 0:
            ring.store(ref.whole, ref.normed, 0)

    ring.gather_work_sum(work, shadow)

    def body(here, at):
        ref.out[here, :] = ref.x[here, :].astype(jnp.float32) + ref.total[here, :]

    by_rows(body)
    ring.finish()


def feed_kernel(names, lazy, *refs):
    ring = Ring(names, lazy, refs)
    ref = ring.ref
    ring.load_all()
    ring.greet_ring()
    norm_rows(ring, ref.x, ref.gain[...])

    def work(row):
        here = pl.ds(row, CAP)
        normed = ref.whole[here, :]
        ring.need("mine", "other", "w_down")
        gate, up = pick(
            ring.first, dot_wide(normed, ref.mine[...]), dot_wide(normed, ref.other[...])
        )
        ref.gate[here, :] = gate
        ref.up[here, :] = up
        hidden = (gate * jax.nn.sigmoid(gate) * up).astype(jnp.bfloat16)
        ref.hidden[here, :] = hidden
        ref.part[here, :] = dot_wide(hidden, ref.w_down[...]).astype(jnp.bfloat16)

    def shadow(i):
        if i == 0:
            ring.store(ref.whole, ref.normed, 0)

    ring.gather_work_sum(work, shadow)

    def body(here, at):
        ref.out[here, :] = (ref.x[here, :] + ref.total[here, :]).astype(jnp.bfloat16)

    by_rows(body)
    ring.finish()


def weight_grads(ring, i, steps, columns=256):
    ref = ring.ref
    width = ref.whole.shape[1]
    pieces = width // columns
    span = ref.g_mine.shape[1]
    for j in range(i * pieces // steps, (i + 1) * pieces // steps):
        at = slice(j * columns, (j + 1) * columns)
        piece = ref.normed[:, at]
        ref.grad_mine[at, :] = dot_rows(piece, ref.g_mine[...]).astype(jnp.bfloat16)
        ref.grad_other[at, :] = dot_rows(piece, ref.g_other[...]).astype(jnp.bfloat16)


def feed_back_kernel(names, lazy, *refs):
    ring = Ring(names, lazy, refs)
    ref = ring.ref
    ring.load_all()
    ring.greet_ring()
    ref.whole[pl.ds(ring.row_of(0), CAP), :] = ref.base[...]

    def work(row):
        here = pl.ds(row, CAP)
        ring.need("mine", "other", "w_down", "gate", "up")
        grad_hidden = dot_trans(ref.whole[here, :], ref.w_down[...])
        gate, up = ref.gate[here, :], ref.up[here, :]
        sigmoid = jax.nn.sigmoid(gate)
        grad_gate = grad_hidden * up * sigmoid * (1.0 + gate * (1.0 - sigmoid))
        grad_up = grad_hidden * gate * sigmoid
        g_mine, g_other = pick(ring.first, grad_gate, grad_up)
        g_mine, g_other = g_mine.astype(jnp.bfloat16), g_other.astype(jnp.bfloat16)
        ref.g_mine[here, :] = g_mine
        ref.g_other[here, :] = g_other
        ref.part[here, :] = (
            dot_trans(g_mine, ref.mine[...]) + dot_trans(g_other, ref.other[...])
        ).astype(jnp.bfloat16)

    def shadow(i):
        ring.need("normed", "hidden")
        if i < 5:
            weight_grads(ring, i, 5)
        else:
            half = ref.whole.shape[1] // 2
            at = slice((i - 5) * half, (i - 4) * half)
            ref.grad_down[:, at] = dot_rows(ref.hidden[...], ref.whole[:, at]).astype(jnp.bfloat16)

    ring.gather_work_sum(work, shadow)
    back_rows(ring, ref.base, ref.x)
    ring.finish()


def attend_back_kernel(last, names, lazy, *refs):
    ring = Ring(names, lazy, refs)
    ref = ring.ref
    ring.load_all()
    if last:
        ring.greet_all()
    else:
        ring.greet_ring()
    own = ring.row_of(0)

    def body(here, at):
        low = ref.base[here, :].astype(jnp.bfloat16)
        ref.whole[pl.ds(pl.multiple_of(own + at, 16), 16), :] = low

    by_rows(body)

    def work(row):
        here = pl.ds(row, CAP)
        ring.need("mine", "other", "w_out", "queries", "kv", "probs", "cosines", "sines")
        grad_mixed = dot_trans(ref.whole[here, :], ref.w_out[...])
        grad_apart = heads_apart(grad_mixed).astype(jnp.bfloat16)
        keys, values = twice(ref.kv[here, :].astype(jnp.float32))
        apart = heads_apart(ref.queries[here, :].astype(jnp.float32)).astype(jnp.bfloat16)
        probs = ref.probs[pl.ds(pl.multiple_of(2 * row, 2 * CAP), 2 * CAP), :]
        grad_probs = dot_trans(grad_apart, values)
        grad_values = dot_rows(probs.astype(jnp.bfloat16), grad_apart)
        spread = jnp.sum(grad_probs * probs, axis=-1, keepdims=True)
        grad_scores = (probs * (grad_probs - spread) * HEAD_DIM ** (-0.5)).astype(jnp.bfloat16)
        grad_queries = heads_together(dot_wide(grad_scores, keys))
        grad_keys = dot_rows(grad_scores, apart)
        cosines, sines = ref.cosines[here, :], -ref.sines[here, :]
        grad_queries = rot_rows(grad_queries, cosines, sines)
        grad_keys = rot_rows(grad_keys + pltpu.roll(grad_keys, HEAD_DIM, 1), cosines, sines)
        grad_values = grad_values + pltpu.roll(grad_values, HEAD_DIM, 1)
        grad_kv = jnp.where(lane_low(grad_keys.shape, LANES), grad_keys, grad_values)
        g_mine, g_other = pick(ring.first, grad_queries, grad_kv)
        g_mine, g_other = g_mine.astype(jnp.bfloat16), g_other.astype(jnp.bfloat16)
        ref.g_mine[here, :] = g_mine
        ref.g_other[here, :] = g_other
        ref.part[here, :] = (
            dot_trans(g_mine, ref.mine[...]) + dot_trans(g_other, ref.other[...])
        ).astype(jnp.bfloat16)

    def shadow(i):
        ring.need("normed", "mixed")
        if i < 5:
            weight_grads(ring, i, 5)
        elif i == 5:
            ref.grad_out[...] = dot_rows(ref.mixed[...], ref.whole[...]).astype(jnp.bfloat16)

    ring.gather_work_sum(work, shadow)
    back_rows(ring, ref.base, ref.x, ref.low if last else None)
    if last:
        last_exchange(ring)
    ring.finish()


def last_exchange(ring):
    ref = ring.ref
    width = ref.whole.shape[1]
    shard, half_r = width // RING, CAP // 2
    own_cols, other_cols = ring.columns(width), ring.columns(width, False)
    halves = []
    for c in (0, 1):
        here = (pl.ds(c * half_r, half_r), own_cols)
        halves.append(
            ring.start(
                copy_to(
                    ring.across,
                    ref.low.at[here],
                    ref.far_low.at[here],
                    ref.half_sem.at[0, 2 + c],
                    ref.half_sem.at[1, 2 + c],
                )
            )
        )
    mine_at = ring.section * RING + ring.group
    grads = ((ref.gain_grad, ref.gg0m), (ref.gg1a, ref.gg1m))
    for layer in (0, 1):
        for g in range(RING):
            for kind in (0, 1):
                ref.gains_out[layer * RING + g, kind] = grads[layer][kind][
                    :, g * shard : (g + 1) * shard
                ]
    ref.gains_in[mine_at] = ref.gains_out[mine_at]
    for n, (f, g) in enumerate(ring.far):
        to_s, to_g = ring.far_step(f, g)
        ring.start(
            copy_to(
                ring.far_device(f, g),
                ref.gains_out.at[to_s * RING + to_g],
                ref.gains_in.at[mine_at],
                ref.far_sem.at[0, n],
                ref.far_sem.at[1, n],
            )
        )
    for c in (0, 1):
        halves[c].wait_recv()
        where = ref.far_low.at[pl.ds(c * half_r, half_r), own_cols]
        ring.start(
            copy_to(
                ring.sibling, where, where, ref.half_sem.at[0, 4 + c], ref.half_sem.at[1, 4 + c]
            )
        )
    for n, (f, g) in enumerate(ring.far):
        copy_to(
            ring.sibling,
            ref.gains_out.at[0],
            ref.gains_in.at[ring.far_from(f, g)],
            ref.far_sem.at[0, n],
            ref.far_sem.at[1, n],
        ).wait_recv()
    for kind in (0, 1):
        ref.gain_sum[kind : kind + 1, :] = jnp.sum(
            jnp.sum(ref.gains_in[:, kind], axis=0), axis=0, keepdims=True
        )
    for c in (0, 1):
        where = ref.far_low.at[pl.ds(c * half_r, half_r), other_cols]
        copy_to(
            ring.sibling, where, where, ref.half_sem.at[0, 4 + c], ref.half_sem.at[1, 4 + c]
        ).wait_recv()


F32, LOW = jnp.float32, jnp.bfloat16


def ring_call(kernel, collective_id, width, now, later, outs, far=False, hbm_outs=(), **scratch):
    rows = CAP
    arrays = dict(
        whole=((RING * rows, width), LOW),
        part=((RING * rows, width), LOW),
        mate=((RING, rows, width // 2), LOW),
        sum_send=((2, 7, rows // 2, width // 2), LOW),
        sum_recv=((2, 7, rows // 2, width // 2), LOW),
        total=((rows, width), F32),
        **scratch,
    )
    sems = dict(
        gather_sem=(2, 2, 7),
        pass_sem=(2, 2, 7),
        mate_sem=(2, RING),
        sum_sem=(2, 2, 7),
        half_sem=(2, 6),
        load_sem=(max(len(later), 1),),
        store_sem=(1,),
    )
    if far:
        sems.update(far_sem=(2, 2 * RING - 1))
    vmem, anywhere = pl.BlockSpec(memory_space=pltpu.VMEM), pl.BlockSpec(memory_space=pl.ANY)
    names = list(now) + [name + "_" for name in later] + list(outs) + list(later)
    names += list(arrays) + list(sems)
    results = pl.pallas_call(
        functools.partial(kernel, names, tuple(later)),
        out_shape=tuple(jax.ShapeDtypeStruct(*outs[name]) for name in outs),
        in_specs=[vmem] * len(now) + [anywhere] * len(later),
        out_specs=tuple(anywhere if name in hbm_outs else vmem for name in outs),
        scratch_shapes=[pltpu.VMEM(a.shape, a.dtype) for a in later.values()]
        + [pltpu.VMEM(*a) for a in arrays.values()]
        + [pltpu.SemaphoreType.DMA(a) for a in sems.values()],
        compiler_params=pltpu.CompilerParams(
            collective_id=collective_id, has_side_effects=True, vmem_limit_bytes=VMEM_BYTES
        ),
        cost_estimate=pl.CostEstimate(
            flops=40 * 10**9, bytes_accessed=180 * 10**6, transcendentals=0
        ),
    )(*now.values(), *later.values())
    return types.SimpleNamespace(**dict(zip(outs, results)))


def blocks_out(matrix, count, span=None):
    rows, columns = matrix.shape
    blocks = matrix.reshape(rows, count, columns // count).transpose(1, 0, 2)
    if span is not None:
        blocks = jnp.pad(blocks, ((0, 0), (0, 0), (0, span - columns // count)))
    return blocks


def blocks_in(blocks, columns):
    count, rows, _ = blocks.shape
    return blocks[:, :, :columns].transpose(1, 0, 2).reshape(rows, count * columns)


def across(value, *pairs):
    return lax.ppermute(value, "section", pairs)


def swapped(value):
    return across(value, (0, 1), (1, 0))


def exchanged(blocks):
    return lax.all_to_all(blocks, "dp", 0, 0, tiled=True)


def ring_device(
    tokens,
    cotangent,
    seq_lengths,
    seq_group,
    seq_micro,
    attn_gain,
    w_query,
    key_matrix,
    value_matrix,
    w_out,
    mlp_gain,
    w_gate,
    w_up,
    w_down,
):
    section_id = lax.axis_index("section")
    group_id = lax.axis_index("dp")
    first = section_id == 0
    width = tokens.shape[1]
    rows = CAP
    whole_rows = RING * rows
    shard = w_query.shape[1]
    groups = jnp.arange(RING, dtype=jnp.int32)

    kv_heads = key_matrix.shape[2] // HEAD_DIM
    units = w_down.shape[1]
    span = -(-units // LANES) * LANES
    down = jnp.pad(w_down[0], ((0, span - units), (0, 0)))

    def kv_blocks(matrix):
        return jnp.repeat(blocks_out(matrix, kv_heads), RING // kv_heads, axis=0)

    def halves(one, two):
        kept = jnp.where(first, one, two)
        got = swapped(jnp.where(first, two, one))
        return pick(first, kept, got)

    attn_pair = halves(
        blocks_out(w_query[0], RING),
        jnp.concatenate([kv_blocks(key_matrix[0]), kv_blocks(value_matrix[0])], axis=-1),
    )
    mlp_pair = halves(blocks_out(w_gate[0], RING, span), blocks_out(w_up[0], RING, span))
    layers = []
    for layer in (0, 1):
        w_a = exchanged(attn_pair[layer]).reshape(RING * shard, -1)
        w_m = exchanged(mlp_pair[layer]).reshape(RING * shard, -1)
        pair = (layer, 1 - layer)
        own = section_id == layer
        w_o = jnp.where(own, w_out[0], across(w_out[0], pair))
        w_d = jnp.where(own, down, across(down, pair))
        layers.append(
            (
                dict(mine=w_a, other=swapped(w_a), w_out=w_o),
                dict(mine=w_m, other=swapped(w_m), w_down=w_d),
            )
        )

    labels, places = jax.vmap(
        lambda g: jax.tree.map(
            lambda a: a[0],
            slot_layout(
                seq_lengths,
                jnp.where(seq_micro == section_id, seq_group, -1),
                seq_micro * 0,
                g,
                1,
                rows,
            ),
        )
    )(groups)
    row_ids = jnp.arange(rows, dtype=jnp.int32)
    mask = (labels[:, :, None] == labels[:, None, :]) & (row_ids[None, :] <= row_ids[:, None])
    half = HEAD_DIM // 2
    frequency = rope_base ** (-2.0 * jnp.arange(half, dtype=jnp.float32) / HEAD_DIM)
    angles = places.astype(jnp.float32).reshape(whole_rows, 1) * frequency
    cosines, sines = jnp.cos(angles), jnp.sin(angles)
    tables = dict(
        cosines=jnp.concatenate([cosines] * (LANES // half), axis=1),
        sines=jnp.concatenate([-sines, sines] * (LANES // HEAD_DIM), axis=1),
    )
    mask = mask.astype(F32).reshape(whole_rows, rows)

    own_tokens = lax.dynamic_slice_in_dim(tokens, section_id * rows, rows, 0)
    own_live = lax.dynamic_index_in_dim(labels, group_id, 0, keepdims=False) > 0
    own_target = jnp.where(
        own_live[:, None], lax.dynamic_slice_in_dim(cotangent, section_id * rows, rows, 0), 0
    )
    own_gains = jnp.concatenate([attn_gain, mlp_gain]).astype(F32)
    own_gains = jnp.pad(own_gains, ((0, 6), (0, 0)))

    heads = w_out.shape[1]
    row_out = ((rows, width), F32)
    attend_outs = dict(
        out=row_out,
        normed=((whole_rows, width), LOW),
        queries=((whole_rows, heads), LOW),
        kv=((whole_rows, heads), LOW),
        probs=((2 * whole_rows, rows), F32),
        mixed=((whole_rows, heads), LOW),
    )
    feed_outs = dict(
        out=((rows, width), LOW),
        normed=((whole_rows, width), LOW),
        gate=((whole_rows, span), F32),
        up=((whole_rows, span), F32),
        hidden=((whole_rows, span), LOW),
    )
    kept = []
    x = own_tokens
    for layer in (0, 1):
        w_attn, w_mlp = layers[layer]
        later = dict(**w_attn, **tables, mask=mask)
        if layer == 0:
            attn = ring_call(
                functools.partial(attend_kernel, True),
                1,
                width,
                dict(x=x, own_gain=own_gains),
                later,
                dict(**attend_outs, gains=((2 * RING, 8, shard), F32)),
                far=True,
                hbm_outs=("normed",),
            )
            gains = attn.gains.reshape(2, RING, 8, shard)[:, :, :2].transpose(0, 2, 1, 3)
            gains = gains.reshape(2, 2, 1, width)
        else:
            attn = ring_call(
                functools.partial(attend_kernel, False),
                2,
                width,
                dict(x=x, gain=gains[1, 0]),
                later,
                attend_outs,
                hbm_outs=("normed",),
            )
        mlp = ring_call(
            feed_kernel,
            3 + layer,
            width,
            dict(x=attn.out, gain=gains[layer, 1]),
            w_mlp,
            feed_outs,
            hbm_outs=("normed",),
        )
        kept.append((x, attn, mlp))
        x = mlp.out

    def pair_sum(mine, far):
        both = mine.astype(F32) + swapped(far).astype(F32)
        return exchanged(both.astype(LOW).reshape(RING, shard, -1))

    def row_sum(layer, grad):
        return grad.astype(F32) + across(grad, (1 - layer, layer)).astype(F32)

    low = own_target
    grads = [None, None]
    input_grads = [None, None]
    gain_outs = dict(out=row_out, gain_grad=((8, width), F32))
    for layer in (1, 0):
        w_attn, w_mlp = layers[layer]
        x, attn, mlp = kept[layer]
        back = ring_call(
            feed_back_kernel,
            5 + layer,
            width,
            dict(base=low, x=attn.out, gain=gains[layer, 1]),
            dict(**w_mlp, gate=mlp.gate, up=mlp.up, hidden=mlp.hidden, normed=mlp.normed),
            dict(
                **gain_outs,
                grad_mine=((width, span), LOW),
                grad_other=((width, span), LOW),
                grad_down=((span, width), LOW),
            ),
            g_mine=((whole_rows, span), LOW),
            g_other=((whole_rows, span), LOW),
        )
        mlp_half = pair_sum(back.grad_mine, back.grad_other)
        mlp_far = across(mlp_half, (1 - layer, layer))
        grad_down = row_sum(layer, back.grad_down)
        mlp_gain_grad = back.gain_grad
        now = dict(base=back.out, x=x, gain=gains[layer, 0])
        outs = dict(
            **gain_outs,
            grad_mine=((width, heads), LOW),
            grad_other=((width, heads), LOW),
            grad_out=((heads, width), LOW),
        )
        more = dict(g_mine=((whole_rows, heads), LOW), g_other=((whole_rows, heads), LOW))
        if layer == 0:
            now.update(gg0m=mlp_gain_grad, gg1a=gain_grad_1[0], gg1m=gain_grad_1[1])
            outs.update(far_low=((rows, width), LOW), gain_sum=((2, shard), F32))
            more.update(
                low=((rows, width), LOW),
                gains_out=((2 * RING, 2, 8, shard), F32),
                gains_in=((2 * RING, 2, 8, shard), F32),
            )
        back = ring_call(
            functools.partial(attend_back_kernel, layer == 0),
            7 + layer,
            width,
            now,
            dict(
                **w_attn,
                **tables,
                queries=attn.queries,
                kv=attn.kv,
                probs=attn.probs,
                mixed=attn.mixed,
                normed=attn.normed,
            ),
            outs,
            far=layer == 0,
            **more,
        )
        attn_half = pair_sum(back.grad_mine, back.grad_other)
        attn_far = across(attn_half, (1 - layer, layer))
        grad_out = row_sum(layer, back.grad_out)
        grads[layer] = (mlp_half, mlp_far, grad_down, attn_half, attn_far, grad_out)
        input_grads[layer] = back.out
        if layer == 1:
            low = back.out.astype(LOW)
            gain_grad_1 = (back.gain_grad, mlp_gain_grad)

    mlp_half, mlp_far, grad_down, attn_half, attn_far, grad_out = (
        jnp.where(first, a, b) for a, b in zip(*grads)
    )
    gate, up = pick(first, mlp_half, mlp_far)
    query, kv = pick(first, attn_half, attn_far)
    kv = kv.astype(F32).reshape(kv_heads, RING // kv_heads, shard, 2, HEAD_DIM)
    kv = jnp.sum(kv, axis=1)

    def micros(low_first, low_second, high_first, high_second):
        return jnp.where(
            first,
            jnp.concatenate([low_first, low_second]),
            jnp.concatenate([high_first, high_second]),
        )[None]

    out_0, out_1 = kept[0][2].out, kept[1][2].out
    grad_0, grad_1 = input_grads
    return (
        micros(out_0, across(out_0, (1, 0)), across(out_1, (0, 1)), out_1),
        micros(grad_0, back.far_low.astype(F32), across(grad_1, (0, 1)), grad_1),
        back.gain_sum[:1],
        blocks_in(query, heads).astype(F32)[None],
        blocks_in(kv[:, :, 0], HEAD_DIM)[None],
        blocks_in(kv[:, :, 1], HEAD_DIM)[None],
        grad_out[None],
        back.gain_sum[1:],
        blocks_in(gate, units).astype(F32)[None],
        blocks_in(up, units).astype(F32)[None],
        grad_down[:units][None],
    )


def solution(mesh):
    in_specs = (
        P("dp", None),
        P("dp", None),
        P(),
        P(),
        P(),
        P("section", "dp"),
        P("section", "dp", "tensor"),
        P("section", "dp", "tensor"),
        P("section", "dp", "tensor"),
        P("section", ("tensor", "dp"), None),
        P("section", "dp"),
        P("section", "dp", "tensor"),
        P("section", "dp", "tensor"),
        P("section", ("tensor", "dp"), None),
    )
    out_specs = (
        P("section", "dp", None),
        P("section", "dp", None),
        P("section", "dp"),
        P("section", "dp", "tensor"),
        P("section", "dp", "tensor"),
        P("section", "dp", "tensor"),
        P("section", ("tensor", "dp"), None),
        P("section", "dp"),
        P("section", "dp", "tensor"),
        P("section", "dp", "tensor"),
        P("section", ("tensor", "dp"), None),
    )
    per_device = ring_device if ring_fits(mesh) else general_device
    return jax.shard_map(
        per_device, mesh=mesh, in_specs=in_specs, out_specs=out_specs, check_vma=False
    )
```

```python
import functools
import types

import jax
import jax.numpy as jnp
from jax import lax
from jax.experimental import pallas as pl
from jax.experimental.pallas import tpu as pltpu
from jax.sharding import PartitionSpec as P

HEAD_DIM = 64
CAP = 128
MICRO = 2


eps_norm = 1e-05
rope_base = 10000.0


def passed_along(shard, axis, by):
    count = lax.axis_size(axis)
    pairs = [(i, i + by) for i in range(count) if 0 <= i + by < count]
    return lax.ppermute(shard, axis, pairs)


def slot_layout(seq_lengths, seq_group, seq_micro, group_id, micro_total, slot_rows):
    row_ids = jnp.arange(slot_rows, dtype=jnp.int32)
    numbers = jnp.arange(seq_lengths.shape[0], dtype=jnp.int32) + 1
    label_list = []
    place_list = []
    for micro_id in range(micro_total):
        inside = ((seq_group == group_id) & (seq_micro == micro_id)).astype(jnp.int32)
        taken_len = seq_lengths * inside
        starts = jnp.cumsum(taken_len) - taken_len
        member = (
            (row_ids[:, None] >= starts[None, :])
            & (row_ids[:, None] < (starts + taken_len)[None, :])
        ).astype(jnp.int32)
        label_list.append(jnp.sum(member * numbers[None, :], axis=1))
        place_list.append(jnp.sum(member * (row_ids[:, None] - starts[None, :]), axis=1))
    return (jnp.stack(label_list), jnp.stack(place_list))


def apply_rotary(value_rows, token_positions, direction):
    half_size = value_rows.shape[-1] // 2
    frequency = rope_base ** (
        -2.0 * jnp.arange(half_size, dtype=jnp.float32) / value_rows.shape[-1]
    )
    angles = token_positions.astype(jnp.float32)[:, None] * frequency[None, :]
    cosines = jnp.cos(angles)[:, None, :]
    sines_part = direction * jnp.sin(angles)[:, None, :]
    first_half = value_rows[..., :half_size]
    second_half = value_rows[..., half_size:]
    return jnp.concatenate(
        [
            first_half * cosines - second_half * sines_part,
            second_half * cosines + first_half * sines_part,
        ],
        axis=-1,
    )


def rms_parts(value_rows):
    inverse = lax.rsqrt(jnp.mean(value_rows * value_rows, axis=-1, keepdims=True) + eps_norm)
    return (value_rows * inverse, inverse)


def dot_trans(left, right):
    return lax.dot_general(
        left, right, (((1,), (1,)), ((), ())), preferred_element_type=jnp.float32
    )


def dot_rows(left, right):
    return lax.dot_general(
        left, right, (((0,), (0,)), ((), ())), preferred_element_type=jnp.float32
    )


def tensor_total(partial_sum):
    return lax.psum(partial_sum, "tensor")


def input_total(partial_sum):
    return lax.psum(partial_sum.astype(jnp.bfloat16), "tensor").astype(jnp.float32)


def mask_of(labels):
    row_ids = jnp.arange(labels.shape[0], dtype=jnp.int32)
    return (labels[:, None] == labels[None, :]) & (row_ids[None, :] <= row_ids[:, None])


def forward_slot(inputs, labels, token_positions, attn_w, mlp_w):
    attn_gain, w_query, key_matrix, value_matrix, w_out = attn_w
    mlp_gain, w_gate, w_up, w_down = mlp_w
    total_row_count = inputs.shape[0]
    head_count = w_query.shape[1] // HEAD_DIM
    kv_count = key_matrix.shape[1] // HEAD_DIM
    query_group_width = head_count // kv_count
    scaled, inverse_attn = rms_parts(inputs)
    normalized_input = (scaled * attn_gain.astype(jnp.float32)).astype(jnp.bfloat16)
    query_rows = jnp.dot(normalized_input, w_query, preferred_element_type=jnp.float32)
    unrotated_keys = jnp.dot(normalized_input, key_matrix, preferred_element_type=jnp.float32)
    value_rows = (
        jnp.dot(normalized_input, value_matrix, preferred_element_type=jnp.float32)
        .astype(jnp.bfloat16)
        .reshape(total_row_count, kv_count, HEAD_DIM)
    )
    query_rows = (
        apply_rotary(
            query_rows.reshape(total_row_count, head_count, HEAD_DIM), token_positions, 1.0
        )
        .astype(jnp.bfloat16)
        .reshape(total_row_count, kv_count, query_group_width, HEAD_DIM)
    )
    rotated_keys = apply_rotary(
        unrotated_keys.reshape(total_row_count, kv_count, HEAD_DIM), token_positions, 1.0
    ).astype(jnp.bfloat16)
    scores = jnp.einsum(
        "qgjd,kgd->gjqk", query_rows, rotated_keys, preferred_element_type=jnp.float32
    ) * HEAD_DIM ** (-0.5)
    scores = jnp.where(mask_of(labels), scores, -1e30)
    top_score = jnp.max(scores, axis=-1, keepdims=True)
    exp_scores = jnp.exp(scores - top_score)
    total_mass = jnp.sum(exp_scores, axis=-1, keepdims=True)
    attn_probs = (exp_scores / total_mass).astype(jnp.bfloat16)
    log_mass = top_score + jnp.log(total_mass)
    mixed_heads = jnp.einsum(
        "gjqk,kgd->qgjd", attn_probs, value_rows, preferred_element_type=jnp.float32
    )
    mixed_heads = mixed_heads.reshape(total_row_count, head_count * HEAD_DIM).astype(jnp.bfloat16)
    residual = inputs + tensor_total(
        jnp.dot(mixed_heads, w_out, preferred_element_type=jnp.float32)
    )
    scaled_mlp, inverse_mlp = rms_parts(residual)
    normed_mlp = (scaled_mlp * mlp_gain.astype(jnp.float32)).astype(jnp.bfloat16)
    gate_proj = jnp.dot(normed_mlp, w_gate, preferred_element_type=jnp.float32)
    up_proj = jnp.dot(normed_mlp, w_up, preferred_element_type=jnp.float32)
    hidden = (jax.nn.silu(gate_proj) * up_proj).astype(jnp.bfloat16)
    result = residual + tensor_total(jnp.dot(hidden, w_down, preferred_element_type=jnp.float32))
    kept_state = (
        inputs,
        inverse_attn,
        normalized_input,
        query_rows,
        rotated_keys,
        value_rows,
        log_mass,
        mixed_heads,
        residual,
        inverse_mlp,
        normed_mlp,
        gate_proj,
        up_proj,
        hidden,
    )
    return (result, kept_state)


def backward_slot(grad_out, kept_state, labels, token_positions, attn_w, mlp_w):
    attn_gain, w_query, key_matrix, value_matrix, w_out = attn_w
    mlp_gain, w_gate, w_up, w_down = mlp_w
    (
        inputs,
        inverse_attn,
        normalized_input,
        query_rows,
        rotated_keys,
        value_rows,
        log_mass,
        mixed_heads,
        residual,
        inverse_mlp,
        normed_mlp,
        gate_proj,
        up_proj,
        hidden,
    ) = kept_state
    total_row_count = inputs.shape[0]
    head_count = w_query.shape[1] // HEAD_DIM
    kv_count = key_matrix.shape[1] // HEAD_DIM
    query_group_width = head_count // kv_count
    down_in = grad_out.astype(jnp.bfloat16)
    grad_hidden = dot_trans(down_in, w_down)
    grad_w_down = dot_rows(hidden, down_in)
    sigmoid_gate = jax.nn.sigmoid(gate_proj)
    grad_gate = (
        grad_hidden * up_proj * sigmoid_gate * (1.0 + gate_proj * (1.0 - sigmoid_gate))
    ).astype(jnp.bfloat16)
    grad_up = (grad_hidden * gate_proj * sigmoid_gate).astype(jnp.bfloat16)
    grad_w_gate = dot_rows(normed_mlp, grad_gate)
    grad_w_up = dot_rows(normed_mlp, grad_up)
    grad_normed_mlp = input_total(dot_trans(grad_gate, w_gate) + dot_trans(grad_up, w_up))
    scaled_mlp = residual * inverse_mlp
    grad_mlp_gain = jnp.sum(grad_normed_mlp * scaled_mlp, axis=0)
    inner_mlp = grad_normed_mlp * mlp_gain.astype(jnp.float32)
    grad_residual = grad_out + inverse_mlp * (
        inner_mlp - scaled_mlp * jnp.mean(inner_mlp * scaled_mlp, axis=-1, keepdims=True)
    )
    out_in = grad_residual.astype(jnp.bfloat16)
    grad_w_out = dot_rows(mixed_heads, out_in)
    grad_mixed = (
        dot_trans(out_in, w_out)
        .astype(jnp.bfloat16)
        .reshape(total_row_count, kv_count, query_group_width, HEAD_DIM)
    )
    scores = jnp.einsum(
        "qgjd,kgd->gjqk", query_rows, rotated_keys, preferred_element_type=jnp.float32
    ) * HEAD_DIM ** (-0.5)
    scores = jnp.where(mask_of(labels), scores, -1e30)
    probs_full = jnp.exp(scores - log_mass)
    attn_probs = probs_full.astype(jnp.bfloat16)
    grad_probs = jnp.einsum(
        "qgjd,kgd->gjqk", grad_mixed, value_rows, preferred_element_type=jnp.float32
    )
    grad_values = jnp.einsum(
        "gjqk,qgjd->kgd", attn_probs, grad_mixed, preferred_element_type=jnp.float32
    )
    spread_term = jnp.sum(grad_probs * probs_full, axis=-1, keepdims=True)
    grad_scores = (probs_full * (grad_probs - spread_term) * HEAD_DIM ** (-0.5)).astype(
        jnp.bfloat16
    )
    grad_queries = jnp.einsum(
        "gjqk,kgd->qgjd", grad_scores, rotated_keys, preferred_element_type=jnp.float32
    )
    grad_keys = jnp.einsum(
        "gjqk,qgjd->kgd", grad_scores, query_rows, preferred_element_type=jnp.float32
    )
    grad_queries = (
        apply_rotary(
            grad_queries.reshape(total_row_count, head_count, HEAD_DIM), token_positions, -1.0
        )
        .reshape(total_row_count, head_count * HEAD_DIM)
        .astype(jnp.bfloat16)
    )
    grad_keys = (
        apply_rotary(grad_keys, token_positions, -1.0)
        .reshape(total_row_count, kv_count * HEAD_DIM)
        .astype(jnp.bfloat16)
    )
    grad_values = grad_values.reshape(total_row_count, kv_count * HEAD_DIM).astype(jnp.bfloat16)
    grad_w_query = dot_rows(normalized_input, grad_queries)
    grad_w_key = dot_rows(normalized_input, grad_keys)
    grad_w_value = dot_rows(normalized_input, grad_values)
    grad_normed = input_total(
        dot_trans(grad_queries, w_query)
        + dot_trans(grad_keys, key_matrix)
        + dot_trans(grad_values, value_matrix)
    )
    scaled = inputs * inverse_attn
    grad_attn_gain = jnp.sum(grad_normed * scaled, axis=0)
    inner_attn = grad_normed * attn_gain.astype(jnp.float32)
    grad_inputs = grad_residual + inverse_attn * (
        inner_attn - scaled * jnp.mean(inner_attn * scaled, axis=-1, keepdims=True)
    )
    attn_grads = (grad_attn_gain, grad_w_query, grad_w_key, grad_w_value, grad_w_out)
    mlp_grads = (grad_mlp_gain, grad_w_gate, grad_w_up, grad_w_down)
    return (grad_inputs, attn_grads, mlp_grads)


def general_device(
    tokens,
    cotangent,
    seq_lengths,
    seq_group,
    seq_micro,
    attn_gain,
    w_query,
    key_matrix,
    value_matrix,
    w_out,
    mlp_gain,
    w_gate,
    w_up,
    w_down,
):
    section_count = lax.axis_size("section")
    section_id = lax.axis_index("section")
    group_id = lax.axis_index("dp")
    slot_rows = CAP
    micro_total = MICRO
    tick_count = micro_total + section_count - 1
    model_width = tokens.shape[1]
    labels, token_positions = slot_layout(
        seq_lengths, seq_group, seq_micro, group_id, micro_total, slot_rows
    )
    live_rows = (labels > 0).astype(jnp.float32)
    attn_w = (
        lax.all_gather(attn_gain[0], "dp", axis=0, tiled=True),
        lax.all_gather(w_query[0], "dp", axis=0, tiled=True),
        lax.all_gather(key_matrix[0], "dp", axis=0, tiled=True),
        lax.all_gather(value_matrix[0], "dp", axis=0, tiled=True),
        lax.all_gather(w_out[0], "dp", axis=0, tiled=True),
    )
    mlp_w = (
        lax.all_gather(mlp_gain[0], "dp", axis=0, tiled=True),
        lax.all_gather(w_gate[0], "dp", axis=0, tiled=True),
        lax.all_gather(w_up[0], "dp", axis=0, tiled=True),
        lax.all_gather(w_down[0], "dp", axis=0, tiled=True),
    )
    is_first = section_id == 0
    received = jnp.zeros((slot_rows, model_width), jnp.bfloat16)
    sent_list = []
    kept_list = []
    for tick_id in range(tick_count):
        micro_id = jnp.clip(tick_id - section_id, 0, micro_total - 1)
        fresh_slot = min(tick_id, micro_total - 1)
        fresh_rows = tokens[fresh_slot * slot_rows : (fresh_slot + 1) * slot_rows]
        section_input = jnp.where(is_first, fresh_rows, received).astype(jnp.float32)
        result, kept_state = forward_slot(
            section_input, labels[micro_id], token_positions[micro_id], attn_w, mlp_w
        )
        handed = result.astype(jnp.bfloat16)
        sent_list.append(handed)
        kept_list.append(kept_state)
        if tick_id + 1 < tick_count:
            received = passed_along(handed, "section", 1)
    sent_all = jnp.stack(sent_list)
    section_out = lax.dynamic_slice_in_dim(sent_all, section_id, micro_total, 0).reshape(
        micro_total * slot_rows, model_width
    )[None]
    kept_all = jax.tree.map(lambda *pieces: jnp.stack(pieces), *kept_list)
    attn_w = (
        lax.all_gather(attn_gain[0], "dp", axis=0, tiled=True),
        lax.all_gather(w_query[0], "dp", axis=0, tiled=True),
        lax.all_gather(key_matrix[0], "dp", axis=0, tiled=True),
        lax.all_gather(value_matrix[0], "dp", axis=0, tiled=True),
        lax.all_gather(w_out[0], "dp", axis=0, tiled=True),
    )
    mlp_w = (
        lax.all_gather(mlp_gain[0], "dp", axis=0, tiled=True),
        lax.all_gather(w_gate[0], "dp", axis=0, tiled=True),
        lax.all_gather(w_up[0], "dp", axis=0, tiled=True),
        lax.all_gather(w_down[0], "dp", axis=0, tiled=True),
    )
    is_last = section_id == section_count - 1
    back_received = jnp.zeros((slot_rows, model_width), jnp.bfloat16)
    grad_list = []
    attn_sum = None
    mlp_sum = None
    for tick_id in range(tick_count):
        micro_raw = tick_id - (section_count - 1 - section_id)
        active = ((micro_raw >= 0) & (micro_raw < micro_total)).astype(jnp.float32)
        micro_id = jnp.clip(micro_raw, 0, micro_total - 1)
        target = lax.dynamic_slice_in_dim(cotangent, micro_id * slot_rows, slot_rows, 0).astype(
            jnp.float32
        )
        grad_out = (
            jnp.where(
                is_last, target * live_rows[micro_id][:, None], back_received.astype(jnp.float32)
            )
            * active
        )
        kept_state = jax.tree.map(lambda stacked: stacked[micro_id + section_id], kept_all)
        grad_inputs, attn_grads, mlp_grads = backward_slot(
            grad_out, kept_state, labels[micro_id], token_positions[micro_id], attn_w, mlp_w
        )
        grad_list.append(grad_inputs)
        gain_a, query_g, key_g, value_g, out_g = attn_grads
        attn_grads = (
            lax.psum_scatter(
                gain_a.astype(jnp.bfloat16), "dp", scatter_dimension=0, tiled=True
            ).astype(jnp.float32),
            lax.psum_scatter(
                query_g.astype(jnp.bfloat16), "dp", scatter_dimension=0, tiled=True
            ).astype(jnp.float32),
            lax.psum_scatter(
                key_g.astype(jnp.bfloat16), "dp", scatter_dimension=0, tiled=True
            ).astype(jnp.float32),
            lax.psum_scatter(
                value_g.astype(jnp.bfloat16), "dp", scatter_dimension=0, tiled=True
            ).astype(jnp.float32),
            lax.psum_scatter(
                out_g.astype(jnp.bfloat16), "dp", scatter_dimension=0, tiled=True
            ).astype(jnp.float32),
        )
        gain_m, gate_g, up_g, down_g = mlp_grads
        mlp_grads = (
            lax.psum_scatter(
                gain_m.astype(jnp.bfloat16), "dp", scatter_dimension=0, tiled=True
            ).astype(jnp.float32),
            lax.psum_scatter(
                gate_g.astype(jnp.bfloat16), "dp", scatter_dimension=0, tiled=True
            ).astype(jnp.float32),
            lax.psum_scatter(
                up_g.astype(jnp.bfloat16), "dp", scatter_dimension=0, tiled=True
            ).astype(jnp.float32),
            lax.psum_scatter(
                down_g.astype(jnp.bfloat16), "dp", scatter_dimension=0, tiled=True
            ).astype(jnp.float32),
        )
        attn_sum = attn_grads if attn_sum is None else jax.tree.map(jnp.add, attn_sum, attn_grads)
        mlp_sum = mlp_grads if mlp_sum is None else jax.tree.map(jnp.add, mlp_sum, mlp_grads)
        if tick_id + 1 < tick_count:
            back_received = passed_along(grad_inputs.astype(jnp.bfloat16), "section", -1)
    grad_all = jnp.stack(grad_list)
    input_grad = lax.dynamic_slice_in_dim(
        grad_all, section_count - 1 - section_id, micro_total, 0
    ).reshape(micro_total * slot_rows, model_width)[None]
    return (
        section_out,
        input_grad,
        attn_sum[0][None],
        attn_sum[1][None],
        attn_sum[2][None],
        attn_sum[3][None],
        attn_sum[4][None],
        mlp_sum[0][None],
        mlp_sum[1][None],
        mlp_sum[2][None],
        mlp_sum[3][None],
    )


RING = 8
LANES = 128
MESH_ID = pl.DeviceIdType.MESH
VMEM_BYTES = 60 * 2**20


def ring_fits(mesh):
    shape = dict(mesh.shape)
    return shape["section"] == 2 and shape["tensor"] == 2 and shape["dp"] == RING and MICRO == 2


def ring_place(group_id):
    z, y = group_id // 2, group_id % 2
    return jnp.where(y == 0, z, RING - 1 - z)


def ring_group(place):
    place = lax.rem(place + 2 * RING, RING)
    return jnp.where(place < RING // 2, 2 * place, 2 * (RING - 1 - place) + 1)


def copy_to(device, src, dst, send_sem, recv_sem):
    return pltpu.make_async_remote_copy(
        src_ref=src,
        dst_ref=dst,
        send_sem=send_sem,
        recv_sem=recv_sem,
        device_id=device,
        device_id_type=MESH_ID,
    )


class Ring:
    def __init__(self, names, lazy, refs):
        self.ref = types.SimpleNamespace(**dict(zip(names, refs)))
        self.lazy = lazy
        self.loads = {}
        self.stores = []
        self.sent = []
        self.side = []
        self.section = lax.axis_index("section")
        self.core = lax.axis_index("tensor")
        self.group = lax.axis_index("dp")
        self.place = ring_place(self.group)
        self.right = (self.section, self.core, ring_group(self.place + 1))
        self.left = (self.section, self.core, ring_group(self.place - 1))
        self.sibling = (self.section, 1 - self.core, self.group)
        self.across = (1 - self.section, self.core, self.group)
        self.far = [(f, g) for f in (0, 1) for g in range(RING) if (f, g) != (0, 0)]

    def load_all(self):
        for n, (name, at) in enumerate(self.lazy):
            source, here = getattr(self.ref, name + "_"), getattr(self.ref, name)
            if at is not None:
                source = source.at[at]
            self.loads[name] = pltpu.make_async_copy(source, here, self.ref.load_sem.at[n])
            self.loads[name].start()

    def need(self, *names):
        for name in names:
            if name in self.loads:
                self.loads.pop(name).wait()

    def local(self, here, there):
        copy = pltpu.make_async_copy(here, there, self.ref.store_sem.at[len(self.stores)])
        copy.start()
        self.stores.append(copy)
        return copy

    def store(self, *names):
        for name in names:
            self.local(getattr(self.ref, name), getattr(self.ref, name + "_out"))

    def start(self, copy):
        copy.start()
        self.sent.append(copy)
        return copy

    def start_side(self, copy):
        copy.start()
        self.side.append(copy)
        return copy

    def drain(self):
        for copy in self.sent:
            copy.wait_send()
        self.sent = []

    def finish(self):
        self.need(*list(self.loads))
        self.drain()
        for copy in self.side:
            copy.wait_send()
        for copy in self.stores:
            if copy is not None:
                copy.wait()

    def stored(self, copy):
        copy.wait()
        self.stores = [None if other is copy else other for other in self.stores]

    def greet(self, devices):
        barrier = pltpu.get_barrier_semaphore()
        for device in devices:
            pl.semaphore_signal(barrier, inc=1, device_id=device, device_id_type=MESH_ID)
        pl.semaphore_wait(barrier, len(devices))

    def greet_ring(self):
        self.greet([self.right, self.left, self.sibling])

    def greet_all(self):
        self.greet([self.sibling] + [self.far_device(f, g) for f, g in self.far])

    def far_step(self, f, g):
        return lax.rem(self.section + f, 2), lax.rem(self.group + g, RING)

    def far_device(self, f, g):
        section, group = self.far_step(f, g)
        return (section, self.core, group)

    def group_from(self, g):
        return lax.rem(self.group + RING - g, RING)

    def far_from(self, f, g):
        return lax.rem(self.section + 2 - f, 2) * RING + self.group_from(g)

    def row_of(self, offset, c=0):
        return pl.multiple_of(ring_group(self.place + offset) * CAP + c * (CAP // 2), CAP // 2)

    def columns(self, width, own=True):
        half = width // 2
        core = self.core if own else 1 - self.core
        return pl.ds(pl.multiple_of(core * half, half), half)

    def gather_work_sum(self, work, early=(), gathered=None, summed=None, ready=None):
        ref = self.ref
        whole, part, mate, total = ref.whole, ref.part, ref.mate, ref.total
        width, half_r = whole.shape[1], CAP // 2
        own_cols, other_cols = self.columns(width), self.columns(width, False)
        ways = ((0, self.right), (1, self.left))
        stream = ((0, 0), (0, 1), (1, 0), (1, 1), (2, 0), (2, 1), (3, 0))

        def landing(way, k, c, columns):
            offset, chunk = (-k, c) if way == 0 else (k, 1 - c)
            return whole.at[pl.ds(self.row_of(offset, chunk), half_r), columns]

        def move(device, where, sems, way, i):
            return copy_to(device, where, where, sems.at[0, way, i], sems.at[1, way, i])

        def forward(i, way, device):
            k, c = stream[i]
            self.start(move(device, landing(way, k, c, own_cols), ref.gather_sem, way, i))

        def arrived(i, way, device):
            k, c = stream[i]
            where = landing(way, k + 1, c, own_cols)
            move(device, where, ref.gather_sem, way, i).wait_recv()
            self.start(move(self.sibling, where, ref.pass_sem, way, i))

        whole_in = set()

        def passed(i, way):
            if (i, way) in whole_in:
                return
            whole_in.add((i, way))
            k, c = stream[i]
            where = landing(way, k + 1, c, other_cols)
            move(self.sibling, where, ref.pass_sem, way, i).wait_recv()

        mate_in = {}

        def work_on(offset):
            q = offset % RING
            if q in mate_in:
                return
            if offset == RING // 2:
                for way in (0, 1):
                    passed(6, way)
            elif offset != 0:
                way, k = (0, -offset) if offset < 0 else (1, offset)
                for i in (2 * k - 2, 2 * k - 1):
                    passed(i, way)
            work(self.row_of(offset))
            mate_in[q] = self.start(
                copy_to(
                    self.sibling,
                    part.at[pl.ds(self.row_of(offset), CAP), other_cols],
                    mate.at[q],
                    ref.mate_sem.at[0, q],
                    ref.mate_sem.at[1, q],
                )
            )

        for i in (0, 1):
            for way, device in ways:
                forward(i, way, device)
        if 0 in early:
            work_on(0)
        for i in range(7):
            for way, device in ways:
                arrived(i, way, device)
                if i < 5:
                    forward(i + 2, way, device)
            if gathered is not None:
                gathered(i)
            for offset in ((), (-1,), (1,), (-2,), (2,), (), ())[i]:
                if offset in early:
                    work_on(offset)
        gather_sent, self.sent = self.sent, []
        if ready is not None:
            ready()
        work_on(4)

        seen = set()

        def mine(offset, c):
            q = offset % RING
            if q not in seen:
                mate_in[q].wait_recv()
                seen.add(q)
            return part[pl.ds(self.row_of(q, c), half_r), own_cols].astype(jnp.float32) + mate[
                q, pl.ds(c * half_r, half_r)
            ].astype(jnp.float32)

        stream_sum = ((4, 0), (3, 1), (3, 0), (2, 1), (2, 0), (1, 1), (1, 0))
        ahead = ((3, -3), (2, -2), (), (1, -1), (0,), (), ())
        moves = []
        for i, (q, c) in enumerate(stream_sum):
            if i == 5:
                for copy in gather_sent:
                    copy.wait_send()
            for way, device in ways:
                offset, chunk = (q, c) if way == 0 else (-q, 1 - c)
                value = mine(offset, chunk)
                if i >= 2:
                    moves[2 * (i - 2) + way].wait_recv()
                    value = value + ref.sum_recv[way, i - 2].astype(jnp.float32)
                ref.sum_send[way, i] = value.astype(jnp.bfloat16)
                moves.append(
                    self.start(
                        copy_to(
                            device,
                            ref.sum_send.at[way, i],
                            ref.sum_recv.at[way, i],
                            ref.sum_sem.at[0, way, i],
                            ref.sum_sem.at[1, way, i],
                        )
                    )
                )
            for offset in ahead[i]:
                work_on(offset)
            if i == 0:
                for j in range(7):
                    for way in (0, 1):
                        passed(j, way)
            if summed is not None:
                summed(i)
        halves = []
        for c in (1, 0):
            value = mine(0, c)
            at = (5, 6) if c == 1 else (6, 5)
            for way in (0, 1):
                moves[2 * at[way] + way].wait_recv()
                value = value + ref.sum_recv[way, at[way]].astype(jnp.float32)
            here = (pl.ds(c * half_r, half_r), own_cols)
            total[here] = value
            halves.append(
                self.start(
                    copy_to(
                        self.sibling,
                        total.at[here],
                        total.at[here],
                        ref.half_sem.at[0, c],
                        ref.half_sem.at[1, c],
                    )
                )
            )
        for copy in halves:
            copy.wait_recv()
        self.drain()


def by_rows(body, step=16):
    @pl.loop(0, CAP, step=step)
    def _(at):
        body(pl.ds(pl.multiple_of(at, step), step), at)


def inverse_rms(value):
    return lax.rsqrt(jnp.mean(value * value, axis=-1, keepdims=True) + eps_norm)


def norm_rows(ring, source, gain):
    own = ring.row_of(0)

    def body(here, at):
        value = source[here, :].astype(jnp.float32)
        low = (value * inverse_rms(value) * gain).astype(jnp.bfloat16)
        ring.ref.whole[pl.ds(pl.multiple_of(own + at, 16), 16), :] = low

    by_rows(body)


def back_rows(ring, base, source, gain, out, gain_grad, also=None):
    gain_grad[...] = jnp.zeros_like(gain_grad)

    def body(here, at):
        x = source[here, :].astype(jnp.float32)
        inverse = inverse_rms(x)
        scaled = x * inverse
        grad = ring.ref.total[here, :]
        moved = grad * scaled
        gain_grad[...] += moved[:8] + moved[8:]
        inner = grad * gain
        value = base[here, :].astype(jnp.float32) + inverse * (
            inner - scaled * jnp.mean(inner * scaled, axis=-1, keepdims=True)
        )
        out[here, :] = value
        if also is not None:
            also[here, :] = value.astype(jnp.bfloat16)

    by_rows(body)


def lane_low(shape, span):
    return lax.rem(lax.broadcasted_iota(jnp.int32, shape, 1), span) < span // 2


def rot_rows(value, cosines, sines):
    low = lane_low(value.shape, HEAD_DIM)
    partner = jnp.where(
        low, pltpu.roll(value, LANES - HEAD_DIM // 2, 1), pltpu.roll(value, HEAD_DIM // 2, 1)
    )
    return value * cosines + partner * sines


def heads_apart(value):
    low = lane_low(value.shape, LANES)
    return jnp.concatenate([jnp.where(low, value, 0.0), jnp.where(low, 0.0, value)], axis=0)


def heads_together(value):
    rows = value.shape[0] // 2
    return jnp.where(lane_low((rows, LANES), LANES), value[:rows], value[rows:])


def twice(kv):
    low = lane_low(kv.shape, LANES)
    other = pltpu.roll(kv, HEAD_DIM, 1)
    return (
        jnp.where(low, kv, other).astype(jnp.bfloat16),
        jnp.where(low, other, kv).astype(jnp.bfloat16),
    )


def dot_wide(left, right):
    return jnp.dot(left, right, preferred_element_type=jnp.float32)


def side_moves(ring, source, place, sems, shard):
    to = [lax.rem(ring.group + g, RING) for g in range(RING)]

    def rows_of(group):
        return place.at[ring.section, pl.ds(pl.multiple_of(group * shard, shard), shard)]

    def send(g):
        if g == 0:
            return ring.local(source.at[ring.group], rows_of(ring.group))
        return ring.start_side(
            copy_to(
                ring.far_device(0, g),
                source.at[to[g]],
                rows_of(ring.group),
                sems.at[0, 0, g],
                sems.at[0, 1, g],
            )
        )

    def pass_on(g):
        block = rows_of(ring.group_from(g))
        if g == 0:
            where = source.at[ring.group]
        else:
            where = block
            copy_to(ring.sibling, where, where, sems.at[0, 0, g], sems.at[0, 1, g]).wait_recv()
        ring.start_side(
            copy_to(ring.across, where, block, sems.at[1, 0, g], sems.at[1, 1, g])
        )

    def wait_passed(g):
        group = ring.group_from(g)
        block = place.at[
            1 - ring.section, pl.ds(pl.multiple_of(group * shard, shard), shard)
        ]
        copy_to(ring.across, block, block, sems.at[1, 0, g], sems.at[1, 1, g]).wait_recv()

    return send, pass_on, wait_passed


def layer_kernel(moving, names, lazy, *refs):
    ring = Ring(names, lazy, refs)
    ref = ring.ref
    width = ref.whole.shape[1]
    shard = width // RING
    ring.load_all()
    if moving:
        ring.greet_all()
        mine_at = ring.section * RING + ring.group
        ref.gains[mine_at] = ref.own_gain[...]
        for n, (f, g) in enumerate(ring.far):
            ring.start_side(
                copy_to(
                    ring.far_device(f, g),
                    ref.own_gain,
                    ref.gains.at[mine_at],
                    ref.far_sem.at[0, n],
                    ref.far_sem.at[1, n],
                )
            )
        send_attn, pass_attn, attn_passed = side_moves(
            ring, ref.attn_blocks, ref.w_attn, ref.attn_sem, shard
        )
        send_mlp, pass_mlp, mlp_passed = side_moves(
            ring, ref.mlp_blocks, ref.w_mlp, ref.mlp_sem, shard
        )
        at_home = [send_attn(g) for g in range(RING)][:1]
        pass_attn(0)

        def across_big(own, place, n):
            where = place.at[ring.section]
            at_home.append(ring.local(own, where))
            ring.start_side(
                copy_to(ring.across, own, where, ref.big_sem.at[0, n], ref.big_sem.at[1, n])
            )

        def big_passed(place, n):
            where = place.at[1 - ring.section]
            copy_to(
                ring.across, where, where, ref.big_sem.at[0, n], ref.big_sem.at[1, n]
            ).wait_recv()

        across_big(ref.own_out, ref.w_out, 0)
        for n, (f, g) in enumerate(ring.far):
            copy_to(
                ring.sibling,
                ref.own_gain,
                ref.gains.at[ring.far_from(f, g)],
                ref.far_sem.at[0, n],
                ref.far_sem.at[1, n],
            ).wait_recv()

        def gain_of(kind):
            return jnp.concatenate(
                [ref.gains[g, kind : kind + 1, :] for g in range(RING)], axis=-1
            )

        w_attn, w_out = ref.w_attn.at[0], ref.w_out.at[0]
        w_mlp, w_down = ref.w_mlp.at[0], ref.w_down.at[0]
    else:
        ring.greet_ring()

        def gain_of(kind):
            return ref.gains[kind]

        w_attn, w_out, w_mlp, w_down = ref.w_attn, ref.w_out, ref.w_mlp, ref.w_down
    norm_rows(ring, ref.x, gain_of(0))
    heads = w_out.shape[0]
    span = w_down.shape[0]

    def attend(row):
        here = pl.ds(row, CAP)
        both = dot_wide(ref.whole[here, :], w_attn[...])
        queries, kv = both[:, :heads], both[:, heads:]
        cosines, sines = ref.cosines[here, :], ref.sines[here, :]
        queries = rot_rows(queries, cosines, sines)
        kv = jnp.where(lane_low(kv.shape, LANES), rot_rows(kv, cosines, sines), kv)
        ref.queries[here, :] = queries.astype(jnp.bfloat16)
        ref.kv[here, :] = kv.astype(jnp.bfloat16)
        keys, values = twice(kv)
        apart = heads_apart(queries).astype(jnp.bfloat16)
        allowed = ref.mask[here, :] > 0.5
        allowed = jnp.concatenate([allowed, allowed], axis=0)
        scores = jnp.where(allowed, dot_trans(apart, keys) * HEAD_DIM ** (-0.5), -1e30)
        weights = jnp.exp(scores - jnp.max(scores, axis=-1, keepdims=True))
        probs = weights / jnp.sum(weights, axis=-1, keepdims=True)
        ref.probs[pl.ds(pl.multiple_of(2 * row, 2 * CAP), 2 * CAP), :] = probs
        mixed = heads_together(dot_wide(probs.astype(jnp.bfloat16), values)).astype(jnp.bfloat16)
        ref.mixed[here, :] = mixed
        ref.part[here, :] = dot_wide(mixed, w_out[...]).astype(jnp.bfloat16)

    keeping = []

    def attn_gathered(i):
        if moving:
            pass_attn(i + 1)
            if i == 2:
                at_home.append([send_mlp(g) for g in range(RING)][0])
                pass_mlp(0)
                across_big(ref.own_down, ref.w_down, 1)

    def attn_ready():
        ring.need("cosines", "sines", "mask")
        if moving:
            for copy in at_home[:2]:
                ring.stored(copy)

            @pl.when(ring.section == 1)
            def _():
                for g in range(RING):
                    attn_passed(g)
                big_passed(ref.w_out, 0)

        else:
            ring.need("w_attn", "w_out")

    def keep(there):
        def summed(i):
            if i == 0:
                keeping.append(ring.local(ref.whole, there))
            if i == 4:
                ring.stored(keeping.pop())

        return summed

    ring.gather_work_sum(attend, gathered=attn_gathered, ready=attn_ready, summed=keep(ref.normed_out))
    ring.store("queries", "kv", "probs", "mixed")

    def add_rows(here, at):
        ref.residual[here, :] = ref.x[here, :].astype(jnp.float32) + ref.total[here, :]

    by_rows(add_rows)
    norm_rows(ring, ref.residual, gain_of(1))

    def feed(row):
        here = pl.ds(row, CAP)
        both = dot_wide(ref.whole[here, :], w_mlp[...])
        gate, up = both[:, :span], both[:, span:]
        ref.gate[here, :] = gate
        ref.up[here, :] = up
        hidden = (gate * jax.nn.sigmoid(gate) * up).astype(jnp.bfloat16)
        ref.hidden[here, :] = hidden
        ref.part[here, :] = dot_wide(hidden, w_down[...]).astype(jnp.bfloat16)

    def mlp_gathered(i):
        if moving:
            pass_mlp(i + 1)

    def mlp_ready():
        if moving:
            for copy in at_home[2:]:
                ring.stored(copy)

            @pl.when(ring.section == 1)
            def _():
                for g in range(RING):
                    mlp_passed(g)
                big_passed(ref.w_down, 1)

        else:
            ring.need("w_mlp", "w_down")

    ring.gather_work_sum(feed, gathered=mlp_gathered, ready=mlp_ready, summed=keep(ref.normed_mlp_out))
    ring.store("gate", "up", "hidden")

    def round_rows(here, at):
        ref.out[here, :] = (ref.residual[here, :] + ref.total[here, :]).astype(jnp.bfloat16)

    by_rows(round_rows)
    if moving:

        @pl.when(ring.section == 0)
        def _():
            for g in range(RING):
                attn_passed(g)
                mlp_passed(g)
            big_passed(ref.w_out, 0)
            big_passed(ref.w_down, 1)

    ring.finish()


def back_kernel(last, names, lazy, *refs):
    ring = Ring(names, lazy, refs)
    ref = ring.ref
    width = ref.whole.shape[1]
    shard = width // RING
    span, heads = ref.w_down.shape[0], ref.w_out.shape[0]
    ring.load_all()
    if last:
        ring.greet_all()
    else:
        ring.greet_ring()
    ref.whole[pl.ds(ring.row_of(0), CAP), :] = ref.base[...]

    def block(matrix, g):
        at = lax.rem(ring.group + g, RING) * shard
        return matrix.at[pl.ds(pl.multiple_of(at, shard), shard)]

    order = (1, 2, 3, 4, 5, 6, 7, 0)
    if last:

        def cross(source, place, sems):
            return copy_to(ring.across, source, place, sems.at[0], sems.at[1])

        def cross_mlp(g, source):
            return cross(block(source, g), block(ref.stage_mlp, g), ref.cross_sem.at[0, g])

        def cross_attn(g, source):
            return cross(block(source, g), block(ref.stage_attn, g), ref.cross_sem.at[1, g])

        def cross_big(n, source):
            return cross(source, (ref.stage_down, ref.stage_out)[n], ref.big_sem.at[n])

        def deal(g, own, fin, n):
            if g == 0:
                return pltpu.make_async_copy(
                    block(own, 0), fin.at[ring.group], ref.deal_sem.at[n, 0, 0]
                )
            return copy_to(
                ring.far_device(0, g),
                block(own, g),
                fin.at[ring.group],
                ref.deal_sem.at[n, 0, g],
                ref.deal_sem.at[n, 1, g],
            )

        def add_and_deal(g, own, n):
            crossed = (cross_mlp, cross_attn)[n](g, own)
            crossed.wait_recv()
            stage, fin = ((ref.stage_mlp, ref.fin_mlp), (ref.stage_attn, ref.fin_attn))[n]
            rows, other = block(own, g), block(stage, g)
            rows[...] = (rows[...].astype(F32) + other[...].astype(F32)).astype(LOW)
            deal(g, own, fin, n).start()

        def dealt(own, n):
            fin = (ref.fin_mlp, ref.fin_attn)[n]
            for g in range(RING):
                copy = deal(g, own, fin, n)
                if g == 0:
                    copy.wait()
                else:
                    copy.wait_send()
                    where = fin.at[ring.group_from(g)]
                    copy_to(
                        ring.sibling,
                        where,
                        where,
                        ref.deal_sem.at[n, 0, g],
                        ref.deal_sem.at[n, 1, g],
                    ).wait_recv()

        @pl.when(ring.section == 0)
        def _():
            for g in order:
                cross_mlp(g, ref.late_mlp_).start()
            for g in order:
                cross_attn(g, ref.late_attn_).start()
            cross_big(1, ref.late_out).start()
            cross_big(0, ref.late_down).start()
            cross(ref.late_rows, ref.far_rows, ref.big_sem.at[2]).start()

    def when(section, body):
        if last:
            pl.when(ring.section == section)(body)

    def layer_1(n, *steps):
        if not steps:
            return

        def body():
            for g in steps:
                add_and_deal(g, (ref.late_mlp, ref.late_attn)[n], n)

        when(1, body)

    def layer_0(n, *steps):
        if not steps:
            return

        def body():
            for g in steps:
                add_and_deal(g, (ref.grad_mlp, ref.grad_attn)[n], n)

        when(0, body)

    def feed_back(row):
        here = pl.ds(row, CAP)
        ring.need("w_mlp", "w_down", "gate", "up")
        grad_hidden = dot_trans(ref.whole[here, :], ref.w_down[...])
        gate, up = ref.gate[here, :], ref.up[here, :]
        sigmoid = jax.nn.sigmoid(gate)
        grad_gate = grad_hidden * up * sigmoid * (1.0 + gate * (1.0 - sigmoid))
        grad_up = grad_hidden * gate * sigmoid
        both = jnp.concatenate([grad_gate, grad_up], axis=1).astype(jnp.bfloat16)
        ref.g_mlp[here, :] = both
        ref.part[here, :] = dot_trans(both, ref.w_mlp[...]).astype(jnp.bfloat16)

    def weight_rows(g, grads, place):
        at = pl.multiple_of(lax.rem(ring.group + g, RING) * shard, shard)
        piece = ref.normed[:, pl.ds(at, shard)]
        place[pl.ds(at, shard), :] = dot_rows(piece, grads[...]).astype(jnp.bfloat16)

    def mlp_summed(i):
        ring.need("normed", "hidden")
        for g in ((), (1, 2, 3), (4, 5, 6), (7, 0), (), (), ())[i]:
            weight_rows(g, ref.g_mlp, ref.grad_mlp)
            when(1, lambda: cross_mlp(g, ref.grad_mlp).start())
        piece = width // 4
        for j in ((), (), (), (0,), (1, 2), (3,), ())[i]:
            at = slice(j * piece, (j + 1) * piece)
            ref.grad_down[:, at] = dot_rows(ref.hidden[...], ref.whole[:, at]).astype(LOW)
        if last:
            if i == 2:
                ring.need("late_mlp", "late_attn")
            layer_1(0, *((), (), (1, 2), (), (3,), (), (4,))[i])

    early = (0, 1, -1, 2, -2)
    ring.gather_work_sum(feed_back, early=early, summed=mlp_summed)
    again = pltpu.make_async_copy(ref.normed_attn_, ref.normed, ref.again_sem.at[0])
    again.start()
    if not last:
        ring.store("grad_mlp", "grad_down")
    back_rows(ring, ref.base, ref.residual, ref.gains[1], ref.middle, ref.gain_grad_mlp)
    own = ring.row_of(0)

    def low_rows(here, at):
        low = ref.middle[here, :].astype(jnp.bfloat16)
        ref.whole[pl.ds(pl.multiple_of(own + at, 16), 16), :] = low

    by_rows(low_rows)

    def attend_back(row):
        here = pl.ds(row, CAP)
        ring.need("w_attn", "w_out", "queries", "kv", "probs", "cosines", "sines")
        grad_mixed = dot_trans(ref.whole[here, :], ref.w_out[...])
        grad_apart = heads_apart(grad_mixed).astype(jnp.bfloat16)
        keys, values = twice(ref.kv[here, :].astype(jnp.float32))
        apart = heads_apart(ref.queries[here, :].astype(jnp.float32)).astype(jnp.bfloat16)
        probs = ref.probs[pl.ds(pl.multiple_of(2 * row, 2 * CAP), 2 * CAP), :]
        grad_probs = dot_trans(grad_apart, values)
        grad_values = dot_rows(probs.astype(jnp.bfloat16), grad_apart)
        spread = jnp.sum(grad_probs * probs, axis=-1, keepdims=True)
        grad_scores = (probs * (grad_probs - spread) * HEAD_DIM ** (-0.5)).astype(jnp.bfloat16)
        grad_queries = heads_together(dot_wide(grad_scores, keys))
        grad_keys = dot_rows(grad_scores, apart)
        cosines, sines = ref.cosines[here, :], -ref.sines[here, :]
        grad_queries = rot_rows(grad_queries, cosines, sines)
        grad_keys = rot_rows(grad_keys + pltpu.roll(grad_keys, HEAD_DIM, 1), cosines, sines)
        grad_values = grad_values + pltpu.roll(grad_values, HEAD_DIM, 1)
        grad_kv = jnp.where(lane_low(grad_keys.shape, LANES), grad_keys, grad_values)
        both = jnp.concatenate([grad_queries, grad_kv], axis=1).astype(jnp.bfloat16)
        ref.g_attn[here, :] = both
        ref.part[here, :] = dot_trans(both, ref.w_attn[...]).astype(jnp.bfloat16)

    def attn_gathered(i):
        layer_1(0, *((), (5,), (), (6,), (), (7,), (0,))[i])
        layer_0(0, *((1,), (2,), (), (3,), (), (), (4,))[i])

    def attn_summed(i):
        if i == 1:
            again.wait()
        for g in ((), (1, 2, 3, 4), (5, 6, 7, 0), (), (), (), ())[i]:
            weight_rows(g, ref.g_attn, ref.grad_attn)
            when(1, lambda: cross_attn(g, ref.grad_attn).start())
        if i == 3:
            ring.need("mixed")
            ref.grad_out[...] = dot_rows(ref.mixed[...], ref.whole[...]).astype(LOW)

            def rest():
                cross_big(1, ref.grad_out).start()
                cross_big(0, ref.grad_down).start()

            when(1, rest)
        layer_1(1, *((), (), (1,), (2,), (3,), (4,), (5,))[i])
        layer_0(0, *((), (), (5,), (), (), (6,), ())[i])

    ring.gather_work_sum(attend_back, early=early, gathered=attn_gathered, summed=attn_summed)
    back_rows(
        ring,
        ref.middle,
        ref.x,
        ref.gains[0],
        ref.out,
        ref.gain_grad_attn,
        ref.low if last else None,
    )
    if last:
        end_exchange = last_exchange(ring)
        ring.store("grad_down", "grad_out")

        @pl.when(ring.section == 1)
        def _():
            for g in (6, 7, 0):
                add_and_deal(g, ref.late_attn, 1)
            dealt(ref.late_mlp, 0)
            dealt(ref.late_attn, 1)
            for n, place in enumerate((ref.stage_down, ref.stage_out, ref.far_rows)):
                copy_to(
                    ring.across, place, place, ref.big_sem.at[n, 0], ref.big_sem.at[n, 1]
                ).wait_recv()
            for g in range(RING):
                cross_mlp(g, ref.grad_mlp).wait_send()
                cross_attn(g, ref.grad_attn).wait_send()
            cross_big(0, ref.grad_down).wait_send()
            cross_big(1, ref.grad_out).wait_send()

        @pl.when(ring.section == 0)
        def _():
            for g in (7, 0):
                add_and_deal(g, ref.grad_mlp, 0)
            for g in order:
                add_and_deal(g, ref.grad_attn, 1)
            dealt(ref.grad_mlp, 0)
            dealt(ref.grad_attn, 1)
            for n, place in enumerate((ref.stage_down, ref.stage_out)):
                copy_to(
                    ring.across, place, place, ref.big_sem.at[n, 0], ref.big_sem.at[n, 1]
                ).wait_recv()
            for g in range(RING):
                cross_mlp(g, ref.late_mlp_).wait_send()
                cross_attn(g, ref.late_attn_).wait_send()
            cross_big(0, ref.late_down).wait_send()
            cross_big(1, ref.late_out).wait_send()
            cross(ref.late_rows, ref.far_rows, ref.big_sem.at[2]).wait_send()

        end_exchange()
    else:
        ring.store("grad_attn", "grad_out")
    ring.finish()


def last_exchange(ring):
    ref = ring.ref
    width = ref.whole.shape[1]
    shard, half_r = width // RING, CAP // 2
    own_cols = ring.columns(width)
    halves = []
    for c in (0, 1):
        here = (pl.ds(c * half_r, half_r), own_cols)
        halves.append(
            ring.start(
                copy_to(
                    ring.across,
                    ref.low.at[here],
                    ref.far_low.at[here],
                    ref.half_sem.at[0, 2 + c],
                    ref.half_sem.at[1, 2 + c],
                )
            )
        )
    mine_at = ring.section * RING + ring.group
    grads = ((ref.gain_grad_attn, ref.gain_grad_mlp), (ref.gg1a, ref.gg1m))
    for layer in (0, 1):
        for g in range(RING):
            for kind in (0, 1):
                ref.gains_out[layer * RING + g, kind] = grads[layer][kind][
                    :, g * shard : (g + 1) * shard
                ]
    ref.gains_in[mine_at] = ref.gains_out[mine_at]
    for n, (f, g) in enumerate(ring.far):
        to_s, to_g = ring.far_step(f, g)
        ring.start(
            copy_to(
                ring.far_device(f, g),
                ref.gains_out.at[to_s * RING + to_g],
                ref.gains_in.at[mine_at],
                ref.far_sem.at[0, n],
                ref.far_sem.at[1, n],
            )
        )
    return lambda: last_waits(ring, halves)


def last_waits(ring, halves):
    ref = ring.ref
    width = ref.whole.shape[1]
    half_r = CAP // 2
    own_cols, other_cols = ring.columns(width), ring.columns(width, False)
    for c in (0, 1):
        halves[c].wait_recv()
        where = ref.far_low.at[pl.ds(c * half_r, half_r), own_cols]
        ring.start(
            copy_to(
                ring.sibling, where, where, ref.half_sem.at[0, 4 + c], ref.half_sem.at[1, 4 + c]
            )
        )
    for n, (f, g) in enumerate(ring.far):
        copy_to(
            ring.sibling,
            ref.gains_out.at[0],
            ref.gains_in.at[ring.far_from(f, g)],
            ref.far_sem.at[0, n],
            ref.far_sem.at[1, n],
        ).wait_recv()
    for kind in (0, 1):
        ref.gain_sum[kind : kind + 1, :] = jnp.sum(
            jnp.sum(ref.gains_in[:, kind], axis=0), axis=0, keepdims=True
        )
    for c in (0, 1):
        where = ref.far_low.at[pl.ds(c * half_r, half_r), other_cols]
        copy_to(
            ring.sibling, where, where, ref.half_sem.at[0, 4 + c], ref.half_sem.at[1, 4 + c]
        ).wait_recv()


F32, LOW = jnp.float32, jnp.bfloat16
MLP, ATTN, DOWN, OUT = "grad_mlp", "grad_attn", "grad_down", "grad_out"
SAVED = ("gate", "up", "hidden", "queries", "kv", "probs", "mixed")


def ring_call(
    kernel, collective_id, width, now, later, beside, outs, kept, direct, scratch, sems
):
    rows = CAP
    later = {name: a if isinstance(a, tuple) else (a, None) for name, a in later.items()}
    arrays = dict(
        whole=((RING * rows, width), LOW),
        part=((RING * rows, width), LOW),
        mate=((RING, rows, width // 2), LOW),
        sum_send=((2, 7, rows // 2, width // 2), LOW),
        sum_recv=((2, 7, rows // 2, width // 2), LOW),
        total=((rows, width), F32),
        **kept,
        **scratch,
    )
    sems = dict(
        gather_sem=(2, 2, 7),
        pass_sem=(2, 2, 7),
        mate_sem=(2, RING),
        sum_sem=(2, 2, 7),
        half_sem=(2, 6),
        load_sem=(len(later),),
        store_sem=(16,),
        **sems,
    )
    vmem, anywhere = pl.BlockSpec(memory_space=pltpu.VMEM), pl.BlockSpec(memory_space=pl.ANY)
    names = list(now) + [name + "_" for name in later] + list(beside) + list(outs)
    names += [name + "_out" for name in kept] + list(direct) + list(later)
    names += list(arrays) + list(sems)
    results = pl.pallas_call(
        functools.partial(kernel, names, [(name, at) for name, (_, at) in later.items()]),
        out_shape=tuple(
            jax.ShapeDtypeStruct(*a) for a in (*outs.values(), *kept.values(), *direct.values())
        ),
        in_specs=[vmem] * len(now) + [anywhere] * (len(later) + len(beside)),
        out_specs=tuple([vmem] * len(outs) + [anywhere] * (len(kept) + len(direct))),
        scratch_shapes=[
            pltpu.VMEM(a.shape if at is None else a.shape[1:], a.dtype) for a, at in later.values()
        ]
        + [pltpu.VMEM(*a) for a in arrays.values()]
        + [pltpu.SemaphoreType.DMA(a) for a in sems.values()],
        compiler_params=pltpu.CompilerParams(
            collective_id=collective_id, has_side_effects=True, vmem_limit_bytes=VMEM_BYTES
        ),
        cost_estimate=pl.CostEstimate(
            flops=80 * 10**9, bytes_accessed=360 * 10**6, transcendentals=0
        ),
    )(*now.values(), *[a for a, _ in later.values()], *beside.values())
    return types.SimpleNamespace(**dict(zip([*outs, *kept, *direct], results)))


def blocks_out(matrix, count, span=None):
    rows, columns = matrix.shape
    blocks = matrix.reshape(rows, count, columns // count).transpose(1, 0, 2)
    if span is not None:
        blocks = jnp.pad(blocks, ((0, 0), (0, 0), (0, span - columns // count)))
    return blocks


def blocks_in(blocks):
    count, rows, columns = blocks.shape
    return blocks.transpose(1, 0, 2).reshape(rows, count * columns)


def across(value, *pairs):
    return lax.ppermute(value, "section", pairs)


def after(value, *others):
    return lax.optimization_barrier((value, *others))[0]


def ring_device(
    tokens,
    cotangent,
    seq_lengths,
    seq_group,
    seq_micro,
    attn_gain,
    w_query,
    key_matrix,
    value_matrix,
    w_out,
    mlp_gain,
    w_gate,
    w_up,
    w_down,
):
    section_id = lax.axis_index("section")
    group_id = lax.axis_index("dp")
    first = section_id == 0
    width = tokens.shape[1]
    rows = CAP
    whole_rows = RING * rows
    shard = w_query.shape[1]
    groups = jnp.arange(RING, dtype=jnp.int32)

    kv_heads = key_matrix.shape[2] // HEAD_DIM
    units = w_down.shape[1]
    span = -(-units // LANES) * LANES
    heads = w_out.shape[1]

    def kv_blocks(matrix):
        return jnp.repeat(blocks_out(matrix, kv_heads), RING // kv_heads, axis=0)

    attn_blocks = jnp.concatenate(
        [blocks_out(w_query[0], RING), kv_blocks(key_matrix[0]), kv_blocks(value_matrix[0])],
        axis=-1,
    )
    mlp_blocks = jnp.concatenate(
        [blocks_out(w_gate[0], RING, span), blocks_out(w_up[0], RING, span)], axis=-1
    )
    own_down = jnp.pad(w_down[0], ((0, span - units), (0, 0)))

    labels, places = jax.vmap(
        lambda g: jax.tree.map(
            lambda a: a[0],
            slot_layout(
                seq_lengths,
                jnp.where(seq_micro == section_id, seq_group, -1),
                seq_micro * 0,
                g,
                1,
                rows,
            ),
        )
    )(groups)
    row_ids = jnp.arange(rows, dtype=jnp.int32)
    mask = (labels[:, :, None] == labels[:, None, :]) & (row_ids[None, :] <= row_ids[:, None])
    half = HEAD_DIM // 2
    frequency = rope_base ** (-2.0 * jnp.arange(half, dtype=jnp.float32) / HEAD_DIM)
    angles = places.astype(jnp.float32).reshape(whole_rows, 1) * frequency
    cosines, sines = jnp.cos(angles), jnp.sin(angles)
    tables = dict(
        cosines=jnp.concatenate([cosines] * (LANES // half), axis=1),
        sines=jnp.concatenate([-sines, sines] * (LANES // HEAD_DIM), axis=1),
    )
    mask = mask.astype(F32).reshape(whole_rows, rows)

    own_tokens = lax.dynamic_slice_in_dim(tokens, section_id * rows, rows, 0)
    own_live = lax.dynamic_index_in_dim(labels, group_id, 0, keepdims=False) > 0
    own_target = jnp.where(
        own_live[:, None], lax.dynamic_slice_in_dim(cotangent, section_id * rows, rows, 0), 0
    )
    own_gains = jnp.concatenate([attn_gain, mlp_gain]).astype(F32)
    own_gains = jnp.pad(own_gains, ((0, 6), (0, 0)))

    row_f32, row_low = ((rows, width), F32), ((rows, width), LOW)
    weights = dict(
        w_attn=((2, width, 2 * heads), LOW),
        w_out=((2, heads, width), LOW),
        w_mlp=((2, width, 2 * span), LOW),
        w_down=((2, span, width), LOW),
    )
    kept = dict(
        queries=((whole_rows, heads), LOW),
        kv=((whole_rows, heads), LOW),
        probs=((2 * whole_rows, rows), F32),
        mixed=((whole_rows, heads), LOW),
        gate=((whole_rows, span), F32),
        up=((whole_rows, span), F32),
        hidden=((whole_rows, span), LOW),
    )
    direct = dict(normed_out=((whole_rows, width), LOW), normed_mlp_out=((whole_rows, width), LOW))
    outs = dict(out=row_low, residual=row_f32)
    layer_0 = ring_call(
        functools.partial(layer_kernel, True),
        1,
        width,
        dict(x=own_tokens, own_gain=own_gains),
        dict(**tables, mask=mask),
        dict(
            attn_blocks=attn_blocks, mlp_blocks=mlp_blocks, own_out=w_out[0], own_down=own_down
        ),
        dict(**outs, **weights, gains=((2 * RING, 8, shard), F32)),
        kept,
        direct,
        {},
        dict(
            far_sem=(2, 2 * RING - 1),
            attn_sem=(2, 2, RING),
            mlp_sem=(2, 2, RING),
            big_sem=(2, 2),
        ),
    )
    gains = layer_0.gains.reshape(2, RING, 8, shard)[:, :, :2].transpose(0, 2, 1, 3)
    gains = gains.reshape(2, 2, 1, width)

    def weights_of(layer):
        return {name: (getattr(layer_0, name), layer) for name in weights}

    layer_1 = ring_call(
        functools.partial(layer_kernel, False),
        2,
        width,
        dict(x=layer_0.out, gains=gains[1]),
        dict(**weights_of(1), **tables, mask=mask),
        {},
        outs,
        kept,
        direct,
        {},
        {},
    )

    def back(layer, forward, x, base, now, later, beside, outs, kept, direct, scratch, sems):
        return ring_call(
            functools.partial(back_kernel, layer == 0),
            3 + layer,
            width,
            dict(base=base, x=x, residual=forward.residual, gains=gains[layer], **now),
            dict(
                **weights_of(layer),
                **tables,
                **{name: getattr(forward, name) for name in SAVED},
                normed=forward.normed_mlp_out,
                **later,
            ),
            dict(normed_attn_=forward.normed_out, **beside),
            dict(
                out=row_f32,
                gain_grad_mlp=((8, width), F32),
                gain_grad_attn=((8, width), F32),
                **outs,
            ),
            kept,
            direct,
            dict(
                g_mlp=((whole_rows, 2 * span), LOW),
                g_attn=((whole_rows, 2 * heads), LOW),
                middle=row_f32,
                **scratch,
            ),
            dict(again_sem=(1,), **sems),
        )

    pairs = dict(grad_mlp=((width, 2 * span), LOW), grad_attn=((width, 2 * heads), LOW))
    grad_rows = dict(grad_down=((span, width), LOW), grad_out=((heads, width), LOW))
    back_1 = back(
        1,
        layer_1,
        layer_0.out,
        own_target,
        {},
        {},
        {},
        {},
        dict(**pairs, **grad_rows),
        {},
        {},
        {},
    )
    out_0 = across(layer_0.out, (1, 0))
    out_1 = across(layer_1.out, (0, 1))
    back_0 = back(
        0,
        layer_0,
        own_tokens,
        after(back_1.out.astype(LOW), out_0, out_1),
        dict(gg1a=back_1.gain_grad_attn, gg1m=back_1.gain_grad_mlp),
        dict(late_mlp=back_1.grad_mlp, late_attn=back_1.grad_attn),
        dict(late_down=back_1.grad_down, late_out=back_1.grad_out, late_rows=back_1.out),
        dict(far_low=row_low, gain_sum=((2, shard), F32)),
        grad_rows,
        dict(
            fin_mlp=((RING, shard, 2 * span), LOW),
            fin_attn=((RING, shard, 2 * heads), LOW),
            stage_down=grad_rows[DOWN],
            stage_out=grad_rows[OUT],
            far_rows=row_f32,
        ),
        dict(
            **pairs,
            low=row_low,
            gains_out=((2 * RING, 2, 8, shard), F32),
            gains_in=((2 * RING, 2, 8, shard), F32),
            stage_mlp=pairs[MLP],
            stage_attn=pairs[ATTN],
        ),
        dict(
            far_sem=(2, 2 * RING - 1),
            cross_sem=(2, RING, 2),
            big_sem=(3, 2),
            deal_sem=(2, 2, RING),
        ),
    )
    down = jnp.where(first, back_0.grad_down, back_1.grad_down).astype(F32)
    down = (down + back_0.stage_down.astype(F32))[:units]
    out = jnp.where(first, back_0.grad_out, back_1.grad_out).astype(F32)
    out = out + back_0.stage_out.astype(F32)
    gate, up = back_0.fin_mlp[:, :, :units], back_0.fin_mlp[:, :, span : span + units]
    query, kv = back_0.fin_attn[:, :, :heads], back_0.fin_attn[:, :, heads:]
    kv = kv.astype(F32).reshape(kv_heads, RING // kv_heads, shard, 2, HEAD_DIM)
    kv = jnp.sum(kv, axis=1)

    def micros(low_first, low_second, high_first, high_second):
        return jnp.where(
            first,
            jnp.concatenate([low_first, low_second]),
            jnp.concatenate([high_first, high_second]),
        )[None]

    return (
        micros(layer_0.out, out_0, out_1, layer_1.out),
        micros(back_0.out, back_0.far_low.astype(F32), back_0.far_rows, back_1.out),
        back_0.gain_sum[:1],
        blocks_in(query).astype(F32)[None],
        blocks_in(kv[:, :, 0])[None],
        blocks_in(kv[:, :, 1])[None],
        out[None],
        back_0.gain_sum[1:],
        blocks_in(gate).astype(F32)[None],
        blocks_in(up).astype(F32)[None],
        down[None],
    )


def solution(mesh):
    in_specs = (
        P("dp", None),
        P("dp", None),
        P(),
        P(),
        P(),
        P("section", "dp"),
        P("section", "dp", "tensor"),
        P("section", "dp", "tensor"),
        P("section", "dp", "tensor"),
        P("section", ("tensor", "dp"), None),
        P("section", "dp"),
        P("section", "dp", "tensor"),
        P("section", "dp", "tensor"),
        P("section", ("tensor", "dp"), None),
    )
    out_specs = (
        P("section", "dp", None),
        P("section", "dp", None),
        P("section", "dp"),
        P("section", "dp", "tensor"),
        P("section", "dp", "tensor"),
        P("section", "dp", "tensor"),
        P("section", ("tensor", "dp"), None),
        P("section", "dp"),
        P("section", "dp", "tensor"),
        P("section", "dp", "tensor"),
        P("section", ("tensor", "dp"), None),
    )
    per_device = ring_device if ring_fits(mesh) else general_device
    return jax.shard_map(
        per_device, mesh=mesh, in_specs=in_specs, out_specs=out_specs, check_vma=False
    )
```

```python
import functools
import types

import jax
import jax.numpy as jnp
from jax import lax
from jax.experimental import pallas as pl
from jax.experimental.pallas import tpu as pltpu
from jax.sharding import PartitionSpec as P

HEAD_DIM = 64
CAP = 128
MICRO = 2


eps_norm = 1e-05
rope_base = 10000.0


def passed_along(shard, axis, by):
    count = lax.axis_size(axis)
    pairs = [(i, i + by) for i in range(count) if 0 <= i + by < count]
    return lax.ppermute(shard, axis, pairs)


def slot_layout(seq_lengths, seq_group, seq_micro, group_id, micro_total, slot_rows):
    row_ids = jnp.arange(slot_rows, dtype=jnp.int32)
    numbers = jnp.arange(seq_lengths.shape[0], dtype=jnp.int32) + 1
    label_list = []
    place_list = []
    for micro_id in range(micro_total):
        inside = ((seq_group == group_id) & (seq_micro == micro_id)).astype(jnp.int32)
        taken_len = seq_lengths * inside
        starts = jnp.cumsum(taken_len) - taken_len
        member = (
            (row_ids[:, None] >= starts[None, :])
            & (row_ids[:, None] < (starts + taken_len)[None, :])
        ).astype(jnp.int32)
        label_list.append(jnp.sum(member * numbers[None, :], axis=1))
        place_list.append(jnp.sum(member * (row_ids[:, None] - starts[None, :]), axis=1))
    return (jnp.stack(label_list), jnp.stack(place_list))


def apply_rotary(value_rows, token_positions, direction):
    half_size = value_rows.shape[-1] // 2
    frequency = rope_base ** (
        -2.0 * jnp.arange(half_size, dtype=jnp.float32) / value_rows.shape[-1]
    )
    angles = token_positions.astype(jnp.float32)[:, None] * frequency[None, :]
    cosines = jnp.cos(angles)[:, None, :]
    sines_part = direction * jnp.sin(angles)[:, None, :]
    first_half = value_rows[..., :half_size]
    second_half = value_rows[..., half_size:]
    return jnp.concatenate(
        [
            first_half * cosines - second_half * sines_part,
            second_half * cosines + first_half * sines_part,
        ],
        axis=-1,
    )


def rms_parts(value_rows):
    inverse = lax.rsqrt(jnp.mean(value_rows * value_rows, axis=-1, keepdims=True) + eps_norm)
    return (value_rows * inverse, inverse)


def dot_trans(left, right):
    return lax.dot_general(
        left, right, (((1,), (1,)), ((), ())), preferred_element_type=jnp.float32
    )


def dot_rows(left, right):
    return lax.dot_general(
        left, right, (((0,), (0,)), ((), ())), preferred_element_type=jnp.float32
    )


def tensor_total(partial_sum):
    return lax.psum(partial_sum, "tensor")


def input_total(partial_sum):
    return lax.psum(partial_sum.astype(jnp.bfloat16), "tensor").astype(jnp.float32)


def mask_of(labels):
    row_ids = jnp.arange(labels.shape[0], dtype=jnp.int32)
    return (labels[:, None] == labels[None, :]) & (row_ids[None, :] <= row_ids[:, None])


def forward_slot(inputs, labels, token_positions, attn_w, mlp_w):
    attn_gain, w_query, key_matrix, value_matrix, w_out = attn_w
    mlp_gain, w_gate, w_up, w_down = mlp_w
    total_row_count = inputs.shape[0]
    head_count = w_query.shape[1] // HEAD_DIM
    kv_count = key_matrix.shape[1] // HEAD_DIM
    query_group_width = head_count // kv_count
    scaled, inverse_attn = rms_parts(inputs)
    normalized_input = (scaled * attn_gain.astype(jnp.float32)).astype(jnp.bfloat16)
    query_rows = jnp.dot(normalized_input, w_query, preferred_element_type=jnp.float32)
    unrotated_keys = jnp.dot(normalized_input, key_matrix, preferred_element_type=jnp.float32)
    value_rows = (
        jnp.dot(normalized_input, value_matrix, preferred_element_type=jnp.float32)
        .astype(jnp.bfloat16)
        .reshape(total_row_count, kv_count, HEAD_DIM)
    )
    query_rows = (
        apply_rotary(
            query_rows.reshape(total_row_count, head_count, HEAD_DIM), token_positions, 1.0
        )
        .astype(jnp.bfloat16)
        .reshape(total_row_count, kv_count, query_group_width, HEAD_DIM)
    )
    rotated_keys = apply_rotary(
        unrotated_keys.reshape(total_row_count, kv_count, HEAD_DIM), token_positions, 1.0
    ).astype(jnp.bfloat16)
    scores = jnp.einsum(
        "qgjd,kgd->gjqk", query_rows, rotated_keys, preferred_element_type=jnp.float32
    ) * HEAD_DIM ** (-0.5)
    scores = jnp.where(mask_of(labels), scores, -1e30)
    top_score = jnp.max(scores, axis=-1, keepdims=True)
    exp_scores = jnp.exp(scores - top_score)
    total_mass = jnp.sum(exp_scores, axis=-1, keepdims=True)
    attn_probs = (exp_scores / total_mass).astype(jnp.bfloat16)
    log_mass = top_score + jnp.log(total_mass)
    mixed_heads = jnp.einsum(
        "gjqk,kgd->qgjd", attn_probs, value_rows, preferred_element_type=jnp.float32
    )
    mixed_heads = mixed_heads.reshape(total_row_count, head_count * HEAD_DIM).astype(jnp.bfloat16)
    residual = inputs + tensor_total(
        jnp.dot(mixed_heads, w_out, preferred_element_type=jnp.float32)
    )
    scaled_mlp, inverse_mlp = rms_parts(residual)
    normed_mlp = (scaled_mlp * mlp_gain.astype(jnp.float32)).astype(jnp.bfloat16)
    gate_proj = jnp.dot(normed_mlp, w_gate, preferred_element_type=jnp.float32)
    up_proj = jnp.dot(normed_mlp, w_up, preferred_element_type=jnp.float32)
    hidden = (jax.nn.silu(gate_proj) * up_proj).astype(jnp.bfloat16)
    result = residual + tensor_total(jnp.dot(hidden, w_down, preferred_element_type=jnp.float32))
    kept_state = (
        inputs,
        inverse_attn,
        normalized_input,
        query_rows,
        rotated_keys,
        value_rows,
        log_mass,
        mixed_heads,
        residual,
        inverse_mlp,
        normed_mlp,
        gate_proj,
        up_proj,
        hidden,
    )
    return (result, kept_state)


def backward_slot(grad_out, kept_state, labels, token_positions, attn_w, mlp_w):
    attn_gain, w_query, key_matrix, value_matrix, w_out = attn_w
    mlp_gain, w_gate, w_up, w_down = mlp_w
    (
        inputs,
        inverse_attn,
        normalized_input,
        query_rows,
        rotated_keys,
        value_rows,
        log_mass,
        mixed_heads,
        residual,
        inverse_mlp,
        normed_mlp,
        gate_proj,
        up_proj,
        hidden,
    ) = kept_state
    total_row_count = inputs.shape[0]
    head_count = w_query.shape[1] // HEAD_DIM
    kv_count = key_matrix.shape[1] // HEAD_DIM
    query_group_width = head_count // kv_count
    down_in = grad_out.astype(jnp.bfloat16)
    grad_hidden = dot_trans(down_in, w_down)
    grad_w_down = dot_rows(hidden, down_in)
    sigmoid_gate = jax.nn.sigmoid(gate_proj)
    grad_gate = (
        grad_hidden * up_proj * sigmoid_gate * (1.0 + gate_proj * (1.0 - sigmoid_gate))
    ).astype(jnp.bfloat16)
    grad_up = (grad_hidden * gate_proj * sigmoid_gate).astype(jnp.bfloat16)
    grad_w_gate = dot_rows(normed_mlp, grad_gate)
    grad_w_up = dot_rows(normed_mlp, grad_up)
    grad_normed_mlp = input_total(dot_trans(grad_gate, w_gate) + dot_trans(grad_up, w_up))
    scaled_mlp = residual * inverse_mlp
    grad_mlp_gain = jnp.sum(grad_normed_mlp * scaled_mlp, axis=0)
    inner_mlp = grad_normed_mlp * mlp_gain.astype(jnp.float32)
    grad_residual = grad_out + inverse_mlp * (
        inner_mlp - scaled_mlp * jnp.mean(inner_mlp * scaled_mlp, axis=-1, keepdims=True)
    )
    out_in = grad_residual.astype(jnp.bfloat16)
    grad_w_out = dot_rows(mixed_heads, out_in)
    grad_mixed = (
        dot_trans(out_in, w_out)
        .astype(jnp.bfloat16)
        .reshape(total_row_count, kv_count, query_group_width, HEAD_DIM)
    )
    scores = jnp.einsum(
        "qgjd,kgd->gjqk", query_rows, rotated_keys, preferred_element_type=jnp.float32
    ) * HEAD_DIM ** (-0.5)
    scores = jnp.where(mask_of(labels), scores, -1e30)
    probs_full = jnp.exp(scores - log_mass)
    attn_probs = probs_full.astype(jnp.bfloat16)
    grad_probs = jnp.einsum(
        "qgjd,kgd->gjqk", grad_mixed, value_rows, preferred_element_type=jnp.float32
    )
    grad_values = jnp.einsum(
        "gjqk,qgjd->kgd", attn_probs, grad_mixed, preferred_element_type=jnp.float32
    )
    spread_term = jnp.sum(grad_probs * probs_full, axis=-1, keepdims=True)
    grad_scores = (probs_full * (grad_probs - spread_term) * HEAD_DIM ** (-0.5)).astype(
        jnp.bfloat16
    )
    grad_queries = jnp.einsum(
        "gjqk,kgd->qgjd", grad_scores, rotated_keys, preferred_element_type=jnp.float32
    )
    grad_keys = jnp.einsum(
        "gjqk,qgjd->kgd", grad_scores, query_rows, preferred_element_type=jnp.float32
    )
    grad_queries = (
        apply_rotary(
            grad_queries.reshape(total_row_count, head_count, HEAD_DIM), token_positions, -1.0
        )
        .reshape(total_row_count, head_count * HEAD_DIM)
        .astype(jnp.bfloat16)
    )
    grad_keys = (
        apply_rotary(grad_keys, token_positions, -1.0)
        .reshape(total_row_count, kv_count * HEAD_DIM)
        .astype(jnp.bfloat16)
    )
    grad_values = grad_values.reshape(total_row_count, kv_count * HEAD_DIM).astype(jnp.bfloat16)
    grad_w_query = dot_rows(normalized_input, grad_queries)
    grad_w_key = dot_rows(normalized_input, grad_keys)
    grad_w_value = dot_rows(normalized_input, grad_values)
    grad_normed = input_total(
        dot_trans(grad_queries, w_query)
        + dot_trans(grad_keys, key_matrix)
        + dot_trans(grad_values, value_matrix)
    )
    scaled = inputs * inverse_attn
    grad_attn_gain = jnp.sum(grad_normed * scaled, axis=0)
    inner_attn = grad_normed * attn_gain.astype(jnp.float32)
    grad_inputs = grad_residual + inverse_attn * (
        inner_attn - scaled * jnp.mean(inner_attn * scaled, axis=-1, keepdims=True)
    )
    attn_grads = (grad_attn_gain, grad_w_query, grad_w_key, grad_w_value, grad_w_out)
    mlp_grads = (grad_mlp_gain, grad_w_gate, grad_w_up, grad_w_down)
    return (grad_inputs, attn_grads, mlp_grads)


def general_device(
    tokens,
    cotangent,
    seq_lengths,
    seq_group,
    seq_micro,
    attn_gain,
    w_query,
    key_matrix,
    value_matrix,
    w_out,
    mlp_gain,
    w_gate,
    w_up,
    w_down,
):
    section_count = lax.axis_size("section")
    section_id = lax.axis_index("section")
    group_id = lax.axis_index("dp")
    slot_rows = CAP
    micro_total = MICRO
    tick_count = micro_total + section_count - 1
    model_width = tokens.shape[1]
    labels, token_positions = slot_layout(
        seq_lengths, seq_group, seq_micro, group_id, micro_total, slot_rows
    )
    live_rows = (labels > 0).astype(jnp.float32)
    attn_w = (
        lax.all_gather(attn_gain[0], "dp", axis=0, tiled=True),
        lax.all_gather(w_query[0], "dp", axis=0, tiled=True),
        lax.all_gather(key_matrix[0], "dp", axis=0, tiled=True),
        lax.all_gather(value_matrix[0], "dp", axis=0, tiled=True),
        lax.all_gather(w_out[0], "dp", axis=0, tiled=True),
    )
    mlp_w = (
        lax.all_gather(mlp_gain[0], "dp", axis=0, tiled=True),
        lax.all_gather(w_gate[0], "dp", axis=0, tiled=True),
        lax.all_gather(w_up[0], "dp", axis=0, tiled=True),
        lax.all_gather(w_down[0], "dp", axis=0, tiled=True),
    )
    is_first = section_id == 0
    received = jnp.zeros((slot_rows, model_width), jnp.bfloat16)
    sent_list = []
    kept_list = []
    for tick_id in range(tick_count):
        micro_id = jnp.clip(tick_id - section_id, 0, micro_total - 1)
        fresh_slot = min(tick_id, micro_total - 1)
        fresh_rows = tokens[fresh_slot * slot_rows : (fresh_slot + 1) * slot_rows]
        section_input = jnp.where(is_first, fresh_rows, received).astype(jnp.float32)
        result, kept_state = forward_slot(
            section_input, labels[micro_id], token_positions[micro_id], attn_w, mlp_w
        )
        handed = result.astype(jnp.bfloat16)
        sent_list.append(handed)
        kept_list.append(kept_state)
        if tick_id + 1 < tick_count:
            received = passed_along(handed, "section", 1)
    sent_all = jnp.stack(sent_list)
    section_out = lax.dynamic_slice_in_dim(sent_all, section_id, micro_total, 0).reshape(
        micro_total * slot_rows, model_width
    )[None]
    kept_all = jax.tree.map(lambda *pieces: jnp.stack(pieces), *kept_list)
    attn_w = (
        lax.all_gather(attn_gain[0], "dp", axis=0, tiled=True),
        lax.all_gather(w_query[0], "dp", axis=0, tiled=True),
        lax.all_gather(key_matrix[0], "dp", axis=0, tiled=True),
        lax.all_gather(value_matrix[0], "dp", axis=0, tiled=True),
        lax.all_gather(w_out[0], "dp", axis=0, tiled=True),
    )
    mlp_w = (
        lax.all_gather(mlp_gain[0], "dp", axis=0, tiled=True),
        lax.all_gather(w_gate[0], "dp", axis=0, tiled=True),
        lax.all_gather(w_up[0], "dp", axis=0, tiled=True),
        lax.all_gather(w_down[0], "dp", axis=0, tiled=True),
    )
    is_last = section_id == section_count - 1
    back_received = jnp.zeros((slot_rows, model_width), jnp.bfloat16)
    grad_list = []
    attn_sum = None
    mlp_sum = None
    for tick_id in range(tick_count):
        micro_raw = tick_id - (section_count - 1 - section_id)
        active = ((micro_raw >= 0) & (micro_raw < micro_total)).astype(jnp.float32)
        micro_id = jnp.clip(micro_raw, 0, micro_total - 1)
        target = lax.dynamic_slice_in_dim(cotangent, micro_id * slot_rows, slot_rows, 0).astype(
            jnp.float32
        )
        grad_out = (
            jnp.where(
                is_last, target * live_rows[micro_id][:, None], back_received.astype(jnp.float32)
            )
            * active
        )
        kept_state = jax.tree.map(lambda stacked: stacked[micro_id + section_id], kept_all)
        grad_inputs, attn_grads, mlp_grads = backward_slot(
            grad_out, kept_state, labels[micro_id], token_positions[micro_id], attn_w, mlp_w
        )
        grad_list.append(grad_inputs)
        gain_a, query_g, key_g, value_g, out_g = attn_grads
        attn_grads = (
            lax.psum_scatter(
                gain_a.astype(jnp.bfloat16), "dp", scatter_dimension=0, tiled=True
            ).astype(jnp.float32),
            lax.psum_scatter(
                query_g.astype(jnp.bfloat16), "dp", scatter_dimension=0, tiled=True
            ).astype(jnp.float32),
            lax.psum_scatter(
                key_g.astype(jnp.bfloat16), "dp", scatter_dimension=0, tiled=True
            ).astype(jnp.float32),
            lax.psum_scatter(
                value_g.astype(jnp.bfloat16), "dp", scatter_dimension=0, tiled=True
            ).astype(jnp.float32),
            lax.psum_scatter(
                out_g.astype(jnp.bfloat16), "dp", scatter_dimension=0, tiled=True
            ).astype(jnp.float32),
        )
        gain_m, gate_g, up_g, down_g = mlp_grads
        mlp_grads = (
            lax.psum_scatter(
                gain_m.astype(jnp.bfloat16), "dp", scatter_dimension=0, tiled=True
            ).astype(jnp.float32),
            lax.psum_scatter(
                gate_g.astype(jnp.bfloat16), "dp", scatter_dimension=0, tiled=True
            ).astype(jnp.float32),
            lax.psum_scatter(
                up_g.astype(jnp.bfloat16), "dp", scatter_dimension=0, tiled=True
            ).astype(jnp.float32),
            lax.psum_scatter(
                down_g.astype(jnp.bfloat16), "dp", scatter_dimension=0, tiled=True
            ).astype(jnp.float32),
        )
        attn_sum = attn_grads if attn_sum is None else jax.tree.map(jnp.add, attn_sum, attn_grads)
        mlp_sum = mlp_grads if mlp_sum is None else jax.tree.map(jnp.add, mlp_sum, mlp_grads)
        if tick_id + 1 < tick_count:
            back_received = passed_along(grad_inputs.astype(jnp.bfloat16), "section", -1)
    grad_all = jnp.stack(grad_list)
    input_grad = lax.dynamic_slice_in_dim(
        grad_all, section_count - 1 - section_id, micro_total, 0
    ).reshape(micro_total * slot_rows, model_width)[None]
    return (
        section_out,
        input_grad,
        attn_sum[0][None],
        attn_sum[1][None],
        attn_sum[2][None],
        attn_sum[3][None],
        attn_sum[4][None],
        mlp_sum[0][None],
        mlp_sum[1][None],
        mlp_sum[2][None],
        mlp_sum[3][None],
    )


RING = 8
LANES = 128
MESH_ID = pl.DeviceIdType.MESH
VMEM_BYTES = 60 * 2**20


def ring_fits(mesh):
    shape = dict(mesh.shape)
    return shape["section"] == 2 and shape["tensor"] == 2 and shape["dp"] == RING and MICRO == 2


def ring_place(group_id):
    z, y = group_id // 2, group_id % 2
    return jnp.where(y == 0, z, RING - 1 - z)


def ring_group(place):
    place = lax.rem(place + 2 * RING, RING)
    return jnp.where(place < RING // 2, 2 * place, 2 * (RING - 1 - place) + 1)


def copy_to(device, src, dst, send_sem, recv_sem):
    return pltpu.make_async_remote_copy(
        src_ref=src,
        dst_ref=dst,
        send_sem=send_sem,
        recv_sem=recv_sem,
        device_id=device,
        device_id_type=MESH_ID,
    )


class Ring:
    def __init__(self, names, lazy, refs):
        self.ref = types.SimpleNamespace(**dict(zip(names, refs)))
        self.lazy = lazy
        self.loads = {}
        self.stores = []
        self.sent = []
        self.side = []
        self.section = lax.axis_index("section")
        self.core = lax.axis_index("tensor")
        self.group = lax.axis_index("dp")
        self.place = ring_place(self.group)
        self.right = (self.section, self.core, ring_group(self.place + 1))
        self.left = (self.section, self.core, ring_group(self.place - 1))
        self.sibling = (self.section, 1 - self.core, self.group)
        self.across = (1 - self.section, self.core, self.group)
        self.far = [(f, g) for f in (0, 1) for g in range(RING) if (f, g) != (0, 0)]

    def load_all(self):
        for n, (name, at) in enumerate(self.lazy):
            source, here = getattr(self.ref, name + "_"), getattr(self.ref, name)
            if at is not None:
                source = source.at[at]
            self.loads[name] = pltpu.make_async_copy(source, here, self.ref.load_sem.at[n])
            self.loads[name].start()

    def need(self, *names):
        for name in names:
            if name in self.loads:
                self.loads.pop(name).wait()

    def local(self, here, there):
        copy = pltpu.make_async_copy(here, there, self.ref.store_sem.at[len(self.stores)])
        copy.start()
        self.stores.append(copy)
        return copy

    def store(self, *names):
        for name in names:
            self.local(getattr(self.ref, name), getattr(self.ref, name + "_out"))

    def start(self, copy):
        copy.start()
        self.sent.append(copy)
        return copy

    def start_side(self, copy):
        copy.start()
        self.side.append(copy)
        return copy

    def drain(self):
        for copy in self.sent:
            copy.wait_send()
        self.sent = []

    def finish(self):
        self.need(*list(self.loads))
        self.drain()
        for copy in self.side:
            copy.wait_send()
        for copy in self.stores:
            if copy is not None:
                copy.wait()

    def stored(self, copy):
        copy.wait()
        self.stores = [None if other is copy else other for other in self.stores]

    def greet(self, devices):
        barrier = pltpu.get_barrier_semaphore()
        for device in devices:
            pl.semaphore_signal(barrier, inc=1, device_id=device, device_id_type=MESH_ID)
        pl.semaphore_wait(barrier, len(devices))

    def greet_ring(self):
        self.greet([self.right, self.left, self.sibling])

    def greet_all(self):
        self.greet([self.sibling] + [self.far_device(f, g) for f, g in self.far])

    def far_step(self, f, g):
        return lax.rem(self.section + f, 2), lax.rem(self.group + g, RING)

    def far_device(self, f, g):
        section, group = self.far_step(f, g)
        return (section, self.core, group)

    def group_from(self, g):
        return lax.rem(self.group + RING - g, RING)

    def far_from(self, f, g):
        return lax.rem(self.section + 2 - f, 2) * RING + self.group_from(g)

    def row_of(self, offset, c=0):
        return pl.multiple_of(ring_group(self.place + offset) * CAP + c * (CAP // 2), CAP // 2)

    def columns(self, width, own=True):
        half = width // 2
        core = self.core if own else 1 - self.core
        return pl.ds(pl.multiple_of(core * half, half), half)

    def gather_work_sum(self, work, early=(), gathered=None, summed=None, ready=None):
        ref = self.ref
        whole, part, mate, total = ref.whole, ref.part, ref.mate, ref.total
        width, half_r = whole.shape[1], CAP // 2
        own_cols, other_cols = self.columns(width), self.columns(width, False)
        ways = ((0, self.right), (1, self.left))
        stream = ((0, 0), (0, 1), (1, 0), (1, 1), (2, 0), (2, 1), (3, 0))

        def landing(way, k, c, columns):
            offset, chunk = (-k, c) if way == 0 else (k, 1 - c)
            return whole.at[pl.ds(self.row_of(offset, chunk), half_r), columns]

        def move(device, where, sems, way, i):
            return copy_to(device, where, where, sems.at[0, way, i], sems.at[1, way, i])

        def forward(i, way, device):
            k, c = stream[i]
            self.start(move(device, landing(way, k, c, own_cols), ref.gather_sem, way, i))

        def arrived(i, way, device):
            k, c = stream[i]
            where = landing(way, k + 1, c, own_cols)
            move(device, where, ref.gather_sem, way, i).wait_recv()
            self.start(move(self.sibling, where, ref.pass_sem, way, i))

        whole_in = set()

        def passed(i, way):
            if (i, way) in whole_in:
                return
            whole_in.add((i, way))
            k, c = stream[i]
            where = landing(way, k + 1, c, other_cols)
            move(self.sibling, where, ref.pass_sem, way, i).wait_recv()

        mate_in = {}

        def work_on(offset):
            q = offset % RING
            if q in mate_in:
                return
            if offset == RING // 2:
                for way in (0, 1):
                    passed(6, way)
            elif offset != 0:
                way, k = (0, -offset) if offset < 0 else (1, offset)
                for i in (2 * k - 2, 2 * k - 1):
                    passed(i, way)
            work(self.row_of(offset))
            mate_in[q] = self.start(
                copy_to(
                    self.sibling,
                    part.at[pl.ds(self.row_of(offset), CAP), other_cols],
                    mate.at[q],
                    ref.mate_sem.at[0, q],
                    ref.mate_sem.at[1, q],
                )
            )

        for i in (0, 1):
            for way, device in ways:
                forward(i, way, device)
        if 0 in early:
            work_on(0)
        for i in range(7):
            for way, device in ways:
                arrived(i, way, device)
                if i < 5:
                    forward(i + 2, way, device)
            if gathered is not None:
                gathered(i)
            for offset in ((), (-1,), (1,), (-2,), (2,), (), ())[i]:
                if offset in early:
                    work_on(offset)
        gather_sent, self.sent = self.sent, []
        if ready is not None:
            ready()
        work_on(4)

        seen = set()

        def mine(offset, c):
            q = offset % RING
            if q not in seen:
                mate_in[q].wait_recv()
                seen.add(q)
            return part[pl.ds(self.row_of(q, c), half_r), own_cols].astype(jnp.float32) + mate[
                q, pl.ds(c * half_r, half_r)
            ].astype(jnp.float32)

        stream_sum = ((4, 0), (3, 1), (3, 0), (2, 1), (2, 0), (1, 1), (1, 0))
        ahead = ((3, -3), (2, -2), (), (1, -1), (0,), (), ())
        moves = []
        for i, (q, c) in enumerate(stream_sum):
            if i == 5:
                for copy in gather_sent:
                    copy.wait_send()
            for way, device in ways:
                offset, chunk = (q, c) if way == 0 else (-q, 1 - c)
                value = mine(offset, chunk)
                if i >= 2:
                    moves[2 * (i - 2) + way].wait_recv()
                    value = value + ref.sum_recv[way, i - 2].astype(jnp.float32)
                ref.sum_send[way, i] = value.astype(jnp.bfloat16)
                moves.append(
                    self.start(
                        copy_to(
                            device,
                            ref.sum_send.at[way, i],
                            ref.sum_recv.at[way, i],
                            ref.sum_sem.at[0, way, i],
                            ref.sum_sem.at[1, way, i],
                        )
                    )
                )
            for offset in ahead[i]:
                work_on(offset)
            if i == 0:
                for j in range(7):
                    for way in (0, 1):
                        passed(j, way)
            if summed is not None:
                summed(i)
        halves = []
        for c in (1, 0):
            value = mine(0, c)
            at = (5, 6) if c == 1 else (6, 5)
            for way in (0, 1):
                moves[2 * at[way] + way].wait_recv()
                value = value + ref.sum_recv[way, at[way]].astype(jnp.float32)
            here = (pl.ds(c * half_r, half_r), own_cols)
            total[here] = value
            halves.append(
                self.start(
                    copy_to(
                        self.sibling,
                        total.at[here],
                        total.at[here],
                        ref.half_sem.at[0, c],
                        ref.half_sem.at[1, c],
                    )
                )
            )
        for copy in halves:
            copy.wait_recv()
        self.drain()


def by_rows(body, step=16):
    @pl.loop(0, CAP, step=step)
    def _(at):
        body(pl.ds(pl.multiple_of(at, step), step), at)


def inverse_rms(value):
    return lax.rsqrt(jnp.mean(value * value, axis=-1, keepdims=True) + eps_norm)


def norm_rows(ring, source, gain):
    own = ring.row_of(0)

    def body(here, at):
        value = source[here, :].astype(jnp.float32)
        low = (value * inverse_rms(value) * gain).astype(jnp.bfloat16)
        ring.ref.whole[pl.ds(pl.multiple_of(own + at, 16), 16), :] = low

    by_rows(body)


def back_rows(ring, base, source, gain, out, gain_grad, also=None):
    gain_grad[...] = jnp.zeros_like(gain_grad)

    def body(here, at):
        x = source[here, :].astype(jnp.float32)
        inverse = inverse_rms(x)
        scaled = x * inverse
        grad = ring.ref.total[here, :]
        moved = grad * scaled
        gain_grad[...] += moved[:8] + moved[8:]
        inner = grad * gain
        value = base[here, :].astype(jnp.float32) + inverse * (
            inner - scaled * jnp.mean(inner * scaled, axis=-1, keepdims=True)
        )
        out[here, :] = value
        if also is not None:
            also[here, :] = value.astype(jnp.bfloat16)

    by_rows(body)


def lane_low(shape, span):
    return lax.rem(lax.broadcasted_iota(jnp.int32, shape, 1), span) < span // 2


def rot_rows(value, cosines, sines):
    low = lane_low(value.shape, HEAD_DIM)
    partner = jnp.where(
        low, pltpu.roll(value, LANES - HEAD_DIM // 2, 1), pltpu.roll(value, HEAD_DIM // 2, 1)
    )
    return value * cosines + partner * sines


def heads_apart(value):
    low = lane_low(value.shape, LANES)
    return jnp.concatenate([jnp.where(low, value, 0.0), jnp.where(low, 0.0, value)], axis=0)


def heads_together(value):
    rows = value.shape[0] // 2
    return jnp.where(lane_low((rows, LANES), LANES), value[:rows], value[rows:])


def twice(kv):
    low = lane_low(kv.shape, LANES)
    other = pltpu.roll(kv, HEAD_DIM, 1)
    return (
        jnp.where(low, kv, other).astype(jnp.bfloat16),
        jnp.where(low, other, kv).astype(jnp.bfloat16),
    )


def dot_wide(left, right):
    return jnp.dot(left, right, preferred_element_type=jnp.float32)


def side_moves(ring, sources, place, sems, shard):
    def rows_of(section, group, columns=slice(None)):
        at = pl.ds(pl.multiple_of(group * shard, shard), shard)
        return place.at[section, at, columns]

    def send(g):
        copies = []
        for n, (block, columns) in enumerate(sources):
            there = rows_of(ring.section, ring.group, columns)
            if g == 0:
                copies.append(ring.local(block(ring.group), there))
            else:
                copies.append(
                    ring.start_side(
                        copy_to(
                            ring.far_device(0, g),
                            block(lax.rem(ring.group + g, RING)),
                            there,
                            sems.at[0, n, g],
                            sems.at[1, n, g],
                        )
                    )
                )
        return copies

    def pass_on(g):
        group = ring.group_from(g)
        if g > 0:
            for n, (_, columns) in enumerate(sources):
                where = rows_of(ring.section, group, columns)
                copy_to(
                    ring.sibling, where, where, sems.at[0, n, g], sems.at[1, n, g]
                ).wait_recv()
        where = rows_of(ring.section, group)
        ring.start_side(copy_to(ring.across, where, where, sems.at[0, 2, g], sems.at[1, 2, g]))

    def wait_passed(g):
        where = rows_of(1 - ring.section, ring.group_from(g))
        copy_to(ring.across, where, where, sems.at[0, 2, g], sems.at[1, 2, g]).wait_recv()

    return send, pass_on, wait_passed


def unit_blocks(source, span, units, b):
    at = b * units
    base, turn = at // LANES * LANES, at % LANES
    wide = -(-(turn + units) // LANES) * LANES
    value = source[:, base : base + wide].astype(F32)
    if turn:
        value = pltpu.roll(value, wide - turn, 1)
    value = value[:, :span]
    lanes = lax.broadcasted_iota(jnp.int32, value.shape, 1)
    return jnp.where(lanes < units, value, 0.0).astype(LOW)


def layer_kernel(moving, names, lazy, *refs):
    ring = Ring(names, lazy, refs)
    ref = ring.ref
    width = ref.whole.shape[1]
    shard = width // RING
    ring.load_all()
    if moving:
        ring.greet_all()
        mine_at = ring.section * RING + ring.group
        ref.gains[mine_at] = ref.own_gain[...]
        for n, (f, g) in enumerate(ring.far):
            ring.start_side(
                copy_to(
                    ring.far_device(f, g),
                    ref.own_gain,
                    ref.gains.at[mine_at],
                    ref.far_sem.at[0, n],
                    ref.far_sem.at[1, n],
                )
            )
        key, value = ref.key[...].astype(F32), ref.value[...].astype(F32)
        low = lane_low(key.shape, LANES)
        ref.kv_blocks[0] = jnp.where(low, key, pltpu.roll(value, HEAD_DIM, 1)).astype(LOW)
        ref.kv_blocks[1] = jnp.where(low, pltpu.roll(key, HEAD_DIM, 1), value).astype(LOW)
        q_width = ref.w_out.shape[1]

        def query_block(group):
            at = pl.multiple_of(group * q_width, q_width)
            return ref.w_query.at[0, :, pl.ds(at, q_width)]

        def kv_block(group):
            return ref.kv_blocks.at[group // (RING // 2)]

        send_attn, pass_attn, attn_passed = side_moves(
            ring,
            ((query_block, slice(0, q_width)), (kv_block, slice(q_width, 2 * q_width))),
            ref.w_attn,
            ref.attn_sem,
            shard,
        )
        send_mlp, pass_mlp, mlp_passed = side_moves(
            ring,
            ((lambda group: ref.mlp_blocks.at[group], slice(None)),),
            ref.w_mlp,
            ref.mlp_sem,
            shard,
        )
        at_home = [send_attn(g) for g in range(RING)][0]
        units = ref.own_down.shape[1]
        span = ref.w_down.shape[1]
        if span > units:
            ref.w_down[:, units:, :] = jnp.zeros((2, span - units, width), LOW)

        def across_big(own, place, n):
            where = place.at[ring.section, pl.ds(0, own.shape[1])]
            at_home.append(ring.local(own.at[0], where))
            ring.start_side(
                copy_to(
                    ring.across, own.at[0], where, ref.big_sem.at[0, n], ref.big_sem.at[1, n]
                )
            )

        def big_passed(own, place, n):
            where = place.at[1 - ring.section, pl.ds(0, own.shape[1])]
            copy_to(
                ring.across, where, where, ref.big_sem.at[0, n], ref.big_sem.at[1, n]
            ).wait_recv()

        across_big(ref.own_out, ref.w_out, 0)
        for n, (f, g) in enumerate(ring.far):
            copy_to(
                ring.sibling,
                ref.own_gain,
                ref.gains.at[ring.far_from(f, g)],
                ref.far_sem.at[0, n],
                ref.far_sem.at[1, n],
            ).wait_recv()

        def gain_of(kind):
            return jnp.concatenate(
                [ref.gains[g, kind : kind + 1, :] for g in range(RING)], axis=-1
            )

        w_attn, w_out = ref.w_attn.at[0], ref.w_out.at[0]
        w_mlp, w_down = ref.w_mlp.at[0], ref.w_down.at[0]
    else:
        ring.greet_ring()

        def gain_of(kind):
            return ref.gains[kind]

        w_attn, w_out, w_mlp, w_down = ref.w_attn, ref.w_out, ref.w_mlp, ref.w_down
    norm_rows(ring, ref.x, gain_of(0))
    heads = w_out.shape[0]
    span = w_down.shape[0]

    def attend(row):
        here = pl.ds(row, CAP)
        both = dot_wide(ref.whole[here, :], w_attn[...])
        queries, kv = both[:, :heads], both[:, heads:]
        cosines, sines = ref.cosines[here, :], ref.sines[here, :]
        queries = rot_rows(queries, cosines, sines)
        kv = jnp.where(lane_low(kv.shape, LANES), rot_rows(kv, cosines, sines), kv)
        ref.queries[here, :] = queries.astype(jnp.bfloat16)
        ref.kv[here, :] = kv.astype(jnp.bfloat16)
        keys, values = twice(kv)
        apart = heads_apart(queries).astype(jnp.bfloat16)
        allowed = ref.mask[here, :] > 0.5
        allowed = jnp.concatenate([allowed, allowed], axis=0)
        scores = jnp.where(allowed, dot_trans(apart, keys) * HEAD_DIM ** (-0.5), -1e30)
        weights = jnp.exp(scores - jnp.max(scores, axis=-1, keepdims=True))
        probs = weights / jnp.sum(weights, axis=-1, keepdims=True)
        ref.probs[pl.ds(pl.multiple_of(2 * row, 2 * CAP), 2 * CAP), :] = probs
        mixed = heads_together(dot_wide(probs.astype(jnp.bfloat16), values)).astype(jnp.bfloat16)
        ref.mixed[here, :] = mixed
        ref.part[here, :] = dot_wide(mixed, w_out[...]).astype(jnp.bfloat16)

    keeping = []

    def attn_gathered(i):
        if moving:
            if i == 0:
                for copy in at_home[:2]:
                    ring.stored(copy)
                pass_attn(0)
                ring.need("w_gate", "w_up")
            pass_attn(i + 1)
            for b in (i,) if i < 6 else (6, 7):
                ref.mlp_blocks[b, :, :span] = unit_blocks(ref.w_gate, span, units, b)
                ref.mlp_blocks[b, :, span:] = unit_blocks(ref.w_up, span, units, b)
            if i == 6:
                for g in range(1, RING):
                    send_mlp(g)
                at_home.extend(send_mlp(0))
                across_big(ref.own_down, ref.w_down, 1)

    def attn_ready():
        ring.need("cosines", "sines", "mask")
        if moving:
            ring.stored(at_home[2])

            @pl.when(ring.section == 1)
            def _():
                for g in range(RING):
                    attn_passed(g)
                big_passed(ref.own_out, ref.w_out, 0)

        else:
            ring.need("w_attn", "w_out")

    def attn_summed(i):
        if moving:
            if i == 0:
                ring.stored(at_home[3])
            for g in ((0,), (), (1,), (2,), (3,), (4,), ())[i]:
                pass_mlp(g)

    def keep(there, also=None):
        def summed(i):
            if also is not None:
                also(i)
            if i == 0:
                keeping.append(ring.local(ref.whole, there))
            if i == 4:
                ring.stored(keeping.pop())

        return summed

    ring.gather_work_sum(attend, gathered=attn_gathered, ready=attn_ready, summed=keep(ref.normed_out, attn_summed))
    ring.store("queries", "kv", "probs", "mixed")

    def add_rows(here, at):
        ref.residual[here, :] = ref.x[here, :].astype(jnp.float32) + ref.total[here, :]

    by_rows(add_rows)
    norm_rows(ring, ref.residual, gain_of(1))

    def feed(row):
        here = pl.ds(row, CAP)
        both = dot_wide(ref.whole[here, :], w_mlp[...])
        gate, up = both[:, :span], both[:, span:]
        ref.gate[here, :] = gate
        ref.up[here, :] = up
        hidden = (gate * jax.nn.sigmoid(gate) * up).astype(jnp.bfloat16)
        ref.hidden[here, :] = hidden
        ref.part[here, :] = dot_wide(hidden, w_down[...]).astype(jnp.bfloat16)

    def mlp_gathered(i):
        if moving:
            for g in ((5,), (), (6,), (), (7,), (), ())[i]:
                pass_mlp(g)

    def mlp_ready():
        if moving:
            ring.stored(at_home[4])

            @pl.when(ring.section == 1)
            def _():
                for g in range(RING):
                    mlp_passed(g)
                big_passed(ref.own_down, ref.w_down, 1)

        else:
            ring.need("w_mlp", "w_down")

    ring.gather_work_sum(feed, gathered=mlp_gathered, ready=mlp_ready, summed=keep(ref.normed_mlp_out))
    ring.store("gate", "up", "hidden")

    def round_rows(here, at):
        ref.out[here, :] = (ref.residual[here, :] + ref.total[here, :]).astype(jnp.bfloat16)

    by_rows(round_rows)
    if moving:

        @pl.when(ring.section == 0)
        def _():
            for g in range(RING):
                attn_passed(g)
                mlp_passed(g)
            big_passed(ref.own_out, ref.w_out, 0)
            big_passed(ref.own_down, ref.w_down, 1)

    ring.finish()


def back_kernel(last, names, lazy, *refs):
    ring = Ring(names, lazy, refs)
    ref = ring.ref
    width = ref.whole.shape[1]
    shard = width // RING
    span, heads = ref.w_down.shape[0], ref.w_out.shape[0]
    ring.load_all()
    if last:
        ring.greet_all()
    else:
        ring.greet_ring()
    ref.whole[pl.ds(ring.row_of(0), CAP), :] = ref.base[...]

    def block(matrix, g):
        at = lax.rem(ring.group + g, RING) * shard
        return matrix.at[pl.ds(pl.multiple_of(at, shard), shard)]

    order = (1, 2, 3, 4, 5, 6, 7, 0)
    if last:

        def cross(source, place, sems):
            return copy_to(ring.across, source, place, sems.at[0], sems.at[1])

        def cross_mlp(g, source):
            return cross(block(source, g), block(ref.stage_mlp, g), ref.cross_sem.at[0, g])

        def cross_attn(g, source):
            return cross(block(source, g), block(ref.stage_attn, g), ref.cross_sem.at[1, g])

        def cross_big(n, source):
            return cross(source, (ref.stage_down, ref.stage_out)[n], ref.big_sem.at[n])

        def deal(g, own, fin, n):
            if g == 0:
                return pltpu.make_async_copy(
                    block(own, 0), fin.at[ring.group], ref.deal_sem.at[n, 0, 0]
                )
            return copy_to(
                ring.far_device(0, g),
                block(own, g),
                fin.at[ring.group],
                ref.deal_sem.at[n, 0, g],
                ref.deal_sem.at[n, 1, g],
            )

        def add_and_deal(g, own, n):
            crossed = (cross_mlp, cross_attn)[n](g, own)
            crossed.wait_recv()
            stage, fin = ((ref.stage_mlp, ref.fin_mlp), (ref.stage_attn, ref.fin_attn))[n]
            rows, other = block(own, g), block(stage, g)
            rows[...] = (rows[...].astype(F32) + other[...].astype(F32)).astype(LOW)
            deal(g, own, fin, n).start()

        def dealt(own, n):
            fin = (ref.fin_mlp, ref.fin_attn)[n]
            for g in range(RING):
                copy = deal(g, own, fin, n)
                if g == 0:
                    copy.wait()
                else:
                    copy.wait_send()
                    where = fin.at[ring.group_from(g)]
                    copy_to(
                        ring.sibling,
                        where,
                        where,
                        ref.deal_sem.at[n, 0, g],
                        ref.deal_sem.at[n, 1, g],
                    ).wait_recv()

        @pl.when(ring.section == 0)
        def _():
            for g in order:
                cross_mlp(g, ref.late_mlp_).start()
            for g in order:
                cross_attn(g, ref.late_attn_).start()
            cross_big(1, ref.late_out).start()
            cross_big(0, ref.late_down).start()
            cross(ref.late_rows, ref.far_rows, ref.big_sem.at[2]).start()
            cross(ref.out_1, ref.far_out, ref.big_sem.at[3]).start()

        @pl.when(ring.section == 1)
        def _():
            cross(ref.out_0, ref.far_out, ref.big_sem.at[3]).start()

    def when(section, body):
        if last:
            pl.when(ring.section == section)(body)

    def layer_1(n, *steps):
        if not steps:
            return

        def body():
            for g in steps:
                add_and_deal(g, (ref.late_mlp, ref.late_attn)[n], n)

        when(1, body)

    def layer_0(n, *steps):
        if not steps:
            return

        def body():
            for g in steps:
                add_and_deal(g, (ref.grad_mlp, ref.grad_attn)[n], n)

        when(0, body)

    def feed_back(row):
        here = pl.ds(row, CAP)
        ring.need("w_mlp", "w_down", "gate", "up")
        grad_hidden = dot_trans(ref.whole[here, :], ref.w_down[...])
        gate, up = ref.gate[here, :], ref.up[here, :]
        sigmoid = jax.nn.sigmoid(gate)
        grad_gate = grad_hidden * up * sigmoid * (1.0 + gate * (1.0 - sigmoid))
        grad_up = grad_hidden * gate * sigmoid
        both = jnp.concatenate([grad_gate, grad_up], axis=1).astype(jnp.bfloat16)
        ref.g_mlp[here, :] = both
        ref.part[here, :] = dot_trans(both, ref.w_mlp[...]).astype(jnp.bfloat16)

    def weight_rows(g, grads, place):
        at = pl.multiple_of(lax.rem(ring.group + g, RING) * shard, shard)
        piece = ref.normed[:, pl.ds(at, shard)]
        place[pl.ds(at, shard), :] = dot_rows(piece, grads[...]).astype(jnp.bfloat16)

    def mlp_summed(i):
        ring.need("normed", "hidden")
        for g in ((), (1, 2, 3), (4, 5, 6), (7, 0), (), (), ())[i]:
            weight_rows(g, ref.g_mlp, ref.grad_mlp)
            when(1, lambda: cross_mlp(g, ref.grad_mlp).start())
        piece = width // 4
        for j in ((), (), (), (0,), (1, 2), (3,), ())[i]:
            at = slice(j * piece, (j + 1) * piece)
            ref.grad_down[:, at] = dot_rows(ref.hidden[...], ref.whole[:, at]).astype(LOW)
        if last:
            if i == 2:
                ring.need("late_mlp", "late_attn")
            layer_1(0, *((), (), (1,), (), (), (2,), ())[i])
            layer_0(0, *((), (), (), (), (), (1,), (2,))[i])

    early = (0, 1, -1, 2, -2)
    ring.gather_work_sum(feed_back, early=early, summed=mlp_summed)
    again = pltpu.make_async_copy(ref.normed_attn_, ref.normed, ref.again_sem.at[0])
    again.start()
    if not last:
        ring.store("grad_mlp", "grad_down")
    back_rows(ring, ref.base, ref.residual, ref.gains[1], ref.middle, ref.gain_grad_mlp)
    own = ring.row_of(0)

    def low_rows(here, at):
        low = ref.middle[here, :].astype(jnp.bfloat16)
        ref.whole[pl.ds(pl.multiple_of(own + at, 16), 16), :] = low

    by_rows(low_rows)

    def attend_back(row):
        here = pl.ds(row, CAP)
        ring.need("w_attn", "w_out", "queries", "kv", "probs", "cosines", "sines")
        grad_mixed = dot_trans(ref.whole[here, :], ref.w_out[...])
        grad_apart = heads_apart(grad_mixed).astype(jnp.bfloat16)
        keys, values = twice(ref.kv[here, :].astype(jnp.float32))
        apart = heads_apart(ref.queries[here, :].astype(jnp.float32)).astype(jnp.bfloat16)
        probs = ref.probs[pl.ds(pl.multiple_of(2 * row, 2 * CAP), 2 * CAP), :]
        grad_probs = dot_trans(grad_apart, values)
        grad_values = dot_rows(probs.astype(jnp.bfloat16), grad_apart)
        spread = jnp.sum(grad_probs * probs, axis=-1, keepdims=True)
        grad_scores = (probs * (grad_probs - spread) * HEAD_DIM ** (-0.5)).astype(jnp.bfloat16)
        grad_queries = heads_together(dot_wide(grad_scores, keys))
        grad_keys = dot_rows(grad_scores, apart)
        cosines, sines = ref.cosines[here, :], -ref.sines[here, :]
        grad_queries = rot_rows(grad_queries, cosines, sines)
        grad_keys = rot_rows(grad_keys + pltpu.roll(grad_keys, HEAD_DIM, 1), cosines, sines)
        grad_values = grad_values + pltpu.roll(grad_values, HEAD_DIM, 1)
        grad_kv = jnp.where(lane_low(grad_keys.shape, LANES), grad_keys, grad_values)
        both = jnp.concatenate([grad_queries, grad_kv], axis=1).astype(jnp.bfloat16)
        ref.g_attn[here, :] = both
        ref.part[here, :] = dot_trans(both, ref.w_attn[...]).astype(jnp.bfloat16)

    def attn_gathered(i):
        layer_1(0, *((), (), (3,), (), (), (), ())[i])
        layer_0(0, *((3,), (), (), (4,), (), (), (5,))[i])

    def attn_summed(i):
        if i == 1:
            again.wait()
        for g in ((), (1, 2, 3, 4), (5, 6, 7, 0), (), (), (), ())[i]:
            weight_rows(g, ref.g_attn, ref.grad_attn)
            when(1, lambda: cross_attn(g, ref.grad_attn).start())
        if i == 3:
            ring.need("mixed")
            ref.grad_out[...] = dot_rows(ref.mixed[...], ref.whole[...]).astype(LOW)

            def rest():
                cross_big(1, ref.grad_out).start()
                cross_big(0, ref.grad_down).start()

            when(1, rest)
        layer_1(0, *((), (4,), (), (), (), (), ())[i])
        layer_0(0, *((), (6,), (), (), (7,), (), (0,))[i])

    ring.gather_work_sum(attend_back, early=early, gathered=attn_gathered, summed=attn_summed)
    back_rows(
        ring,
        ref.middle,
        ref.x,
        ref.gains[0],
        ref.out,
        ref.gain_grad_attn,
        ref.low if last else None,
    )
    if last:
        end_exchange = last_exchange(ring)
        ring.store("grad_down", "grad_out")

        @pl.when(ring.section == 1)
        def _():
            for g in (5, 6, 7, 0):
                add_and_deal(g, ref.late_mlp, 0)
            for g in order:
                add_and_deal(g, ref.late_attn, 1)
            dealt(ref.late_mlp, 0)
            dealt(ref.late_attn, 1)
            places = (ref.stage_down, ref.stage_out, ref.far_rows, ref.far_out)
            for n, place in enumerate(places):
                copy_to(
                    ring.across, place, place, ref.big_sem.at[n, 0], ref.big_sem.at[n, 1]
                ).wait_recv()
            for g in range(RING):
                cross_mlp(g, ref.grad_mlp).wait_send()
                cross_attn(g, ref.grad_attn).wait_send()
            cross_big(0, ref.grad_down).wait_send()
            cross_big(1, ref.grad_out).wait_send()
            cross(ref.out_0, ref.far_out, ref.big_sem.at[3]).wait_send()

        @pl.when(ring.section == 0)
        def _():
            for g in order:
                add_and_deal(g, ref.grad_attn, 1)
            dealt(ref.grad_mlp, 0)
            dealt(ref.grad_attn, 1)
            for n, place in ((0, ref.stage_down), (1, ref.stage_out), (3, ref.far_out)):
                copy_to(
                    ring.across, place, place, ref.big_sem.at[n, 0], ref.big_sem.at[n, 1]
                ).wait_recv()
            for g in range(RING):
                cross_mlp(g, ref.late_mlp_).wait_send()
                cross_attn(g, ref.late_attn_).wait_send()
            cross_big(0, ref.late_down).wait_send()
            cross_big(1, ref.late_out).wait_send()
            cross(ref.late_rows, ref.far_rows, ref.big_sem.at[2]).wait_send()
            cross(ref.out_1, ref.far_out, ref.big_sem.at[3]).wait_send()

        end_exchange()
    else:
        ring.store("grad_attn", "grad_out")
    ring.finish()


def last_exchange(ring):
    ref = ring.ref
    width = ref.whole.shape[1]
    shard, half_r = width // RING, CAP // 2
    own_cols = ring.columns(width)
    halves = []
    for c in (0, 1):
        here = (pl.ds(c * half_r, half_r), own_cols)
        halves.append(
            ring.start(
                copy_to(
                    ring.across,
                    ref.low.at[here],
                    ref.far_low.at[here],
                    ref.half_sem.at[0, 2 + c],
                    ref.half_sem.at[1, 2 + c],
                )
            )
        )
    mine_at = ring.section * RING + ring.group
    grads = ((ref.gain_grad_attn, ref.gain_grad_mlp), (ref.gg1a, ref.gg1m))
    for layer in (0, 1):
        for g in range(RING):
            for kind in (0, 1):
                ref.gains_out[layer * RING + g, kind] = grads[layer][kind][
                    :, g * shard : (g + 1) * shard
                ]
    ref.gains_in[mine_at] = ref.gains_out[mine_at]
    for n, (f, g) in enumerate(ring.far):
        to_s, to_g = ring.far_step(f, g)
        ring.start(
            copy_to(
                ring.far_device(f, g),
                ref.gains_out.at[to_s * RING + to_g],
                ref.gains_in.at[mine_at],
                ref.far_sem.at[0, n],
                ref.far_sem.at[1, n],
            )
        )
    return lambda: last_waits(ring, halves)


def last_waits(ring, halves):
    ref = ring.ref
    width = ref.whole.shape[1]
    half_r = CAP // 2
    own_cols, other_cols = ring.columns(width), ring.columns(width, False)
    for c in (0, 1):
        halves[c].wait_recv()
        where = ref.far_low.at[pl.ds(c * half_r, half_r), own_cols]
        ring.start(
            copy_to(
                ring.sibling, where, where, ref.half_sem.at[0, 4 + c], ref.half_sem.at[1, 4 + c]
            )
        )
    for n, (f, g) in enumerate(ring.far):
        copy_to(
            ring.sibling,
            ref.gains_out.at[0],
            ref.gains_in.at[ring.far_from(f, g)],
            ref.far_sem.at[0, n],
            ref.far_sem.at[1, n],
        ).wait_recv()
    for kind in (0, 1):
        ref.gain_sum[kind : kind + 1, :] = jnp.sum(
            jnp.sum(ref.gains_in[:, kind], axis=0), axis=0, keepdims=True
        )
    for c in (0, 1):
        where = ref.far_low.at[pl.ds(c * half_r, half_r), other_cols]
        copy_to(
            ring.sibling, where, where, ref.half_sem.at[0, 4 + c], ref.half_sem.at[1, 4 + c]
        ).wait_recv()


F32, LOW = jnp.float32, jnp.bfloat16
MLP, ATTN, DOWN, OUT = "grad_mlp", "grad_attn", "grad_down", "grad_out"
SAVED = ("gate", "up", "hidden", "queries", "kv", "probs", "mixed")


def ring_call(
    kernel, collective_id, width, now, later, beside, outs, kept, direct, scratch, sems
):
    rows = CAP
    later = {name: a if isinstance(a, tuple) else (a, None) for name, a in later.items()}
    arrays = dict(
        whole=((RING * rows, width), LOW),
        part=((RING * rows, width), LOW),
        mate=((RING, rows, width // 2), LOW),
        sum_send=((2, 7, rows // 2, width // 2), LOW),
        sum_recv=((2, 7, rows // 2, width // 2), LOW),
        total=((rows, width), F32),
        **kept,
        **scratch,
    )
    sems = dict(
        gather_sem=(2, 2, 7),
        pass_sem=(2, 2, 7),
        mate_sem=(2, RING),
        sum_sem=(2, 2, 7),
        half_sem=(2, 6),
        load_sem=(len(later),),
        store_sem=(16,),
        **sems,
    )
    vmem, anywhere = pl.BlockSpec(memory_space=pltpu.VMEM), pl.BlockSpec(memory_space=pl.ANY)
    names = list(now) + [name + "_" for name in later] + list(beside) + list(outs)
    names += [name + "_out" for name in kept] + list(direct) + list(later)
    names += list(arrays) + list(sems)
    results = pl.pallas_call(
        functools.partial(kernel, names, [(name, at) for name, (_, at) in later.items()]),
        out_shape=tuple(
            jax.ShapeDtypeStruct(*a) for a in (*outs.values(), *kept.values(), *direct.values())
        ),
        in_specs=[vmem] * len(now) + [anywhere] * (len(later) + len(beside)),
        out_specs=tuple([vmem] * len(outs) + [anywhere] * (len(kept) + len(direct))),
        scratch_shapes=[
            pltpu.VMEM(a.shape if at is None else a.shape[1:], a.dtype) for a, at in later.values()
        ]
        + [pltpu.VMEM(*a) for a in arrays.values()]
        + [pltpu.SemaphoreType.DMA(a) for a in sems.values()],
        compiler_params=pltpu.CompilerParams(
            collective_id=collective_id, has_side_effects=True, vmem_limit_bytes=VMEM_BYTES
        ),
        cost_estimate=pl.CostEstimate(
            flops=80 * 10**9, bytes_accessed=360 * 10**6, transcendentals=0
        ),
    )(*now.values(), *[a for a, _ in later.values()], *beside.values())
    return types.SimpleNamespace(**dict(zip([*outs, *kept, *direct], results)))


def side_by_side_kernel(units, mlp, attn, gate, up, query, key, value):
    rows, span = mlp.shape[1], mlp.shape[2] // 2
    for start, place in ((0, gate), (span, up)):
        place[...] = jnp.zeros_like(place)
        for b in range(RING):
            at = b * units
            base, turn = at // LANES * LANES, at % LANES
            wide = -(-(turn + units) // LANES) * LANES
            block = mlp[b, :, start : start + span].astype(F32)
            if wide > span:
                block = jnp.concatenate([block, jnp.zeros((rows, wide - span), F32)], axis=1)
            if turn:
                block = pltpu.roll(block, turn, 1)
            place[0, :, base : base + wide] += block[:, :wide]
    q_width = attn.shape[2] // 2
    for b in range(RING):
        query[0, :, b * q_width : (b + 1) * q_width] = attn[b, :, :q_width].astype(F32)
    sums = []
    for head in (0, 1):
        blocks = range(head * RING // 2, (head + 1) * RING // 2)
        sums.append(sum(attn[b, :, q_width:].astype(F32) for b in blocks))
    low = lane_low(sums[0].shape, LANES)
    key[0] = jnp.where(low, sums[0], pltpu.roll(sums[1], HEAD_DIM, 1))
    value[0] = jnp.where(low, pltpu.roll(sums[0], HEAD_DIM, 1), sums[1])


def side_by_side(mlp, attn, units):
    _, rows, mlp_width = mlp.shape
    attn_width = attn.shape[2]
    widths = [RING * units] * 2 + [RING * attn_width // 2] + [attn_width // 2] * 2
    step = 32
    return pl.pallas_call(
        functools.partial(side_by_side_kernel, units),
        grid=(rows // step,),
        in_specs=[
            pl.BlockSpec((RING, step, mlp_width), lambda i: (0, i, 0)),
            pl.BlockSpec((RING, step, attn_width), lambda i: (0, i, 0)),
        ],
        out_shape=[jax.ShapeDtypeStruct((1, rows, width), F32) for width in widths],
        out_specs=[pl.BlockSpec((1, step, width), lambda i: (0, i, 0)) for width in widths],
        compiler_params=pltpu.CompilerParams(vmem_limit_bytes=VMEM_BYTES),
    )(mlp, attn)


def ring_device(
    tokens,
    cotangent,
    seq_lengths,
    seq_group,
    seq_micro,
    attn_gain,
    w_query,
    key_matrix,
    value_matrix,
    w_out,
    mlp_gain,
    w_gate,
    w_up,
    w_down,
):
    section_id = lax.axis_index("section")
    group_id = lax.axis_index("dp")
    first = section_id == 0
    width = tokens.shape[1]
    rows = CAP
    whole_rows = RING * rows
    shard = w_query.shape[1]
    groups = jnp.arange(RING, dtype=jnp.int32)

    kv_heads = key_matrix.shape[2] // HEAD_DIM
    units = w_down.shape[1]
    span = -(-units // LANES) * LANES
    heads = w_out.shape[1]

    labels, places = jax.vmap(
        lambda g: jax.tree.map(
            lambda a: a[0],
            slot_layout(
                seq_lengths,
                jnp.where(seq_micro == section_id, seq_group, -1),
                seq_micro * 0,
                g,
                1,
                rows,
            ),
        )
    )(groups)
    row_ids = jnp.arange(rows, dtype=jnp.int32)
    mask = (labels[:, :, None] == labels[:, None, :]) & (row_ids[None, :] <= row_ids[:, None])
    half = HEAD_DIM // 2
    frequency = rope_base ** (-2.0 * jnp.arange(half, dtype=jnp.float32) / HEAD_DIM)
    angles = places.astype(jnp.float32).reshape(whole_rows, 1) * frequency
    cosines, sines = jnp.cos(angles), jnp.sin(angles)
    tables = dict(
        cosines=jnp.concatenate([cosines] * (LANES // half), axis=1),
        sines=jnp.concatenate([-sines, sines] * (LANES // HEAD_DIM), axis=1),
    )
    mask = mask.astype(F32).reshape(whole_rows, rows)

    own_tokens = lax.dynamic_slice_in_dim(tokens, section_id * rows, rows, 0)
    own_live = lax.dynamic_index_in_dim(labels, group_id, 0, keepdims=False) > 0
    own_target = jnp.where(
        own_live[:, None], lax.dynamic_slice_in_dim(cotangent, section_id * rows, rows, 0), 0
    )
    own_gains = jnp.concatenate([attn_gain, mlp_gain]).astype(F32)
    own_gains = jnp.pad(own_gains, ((0, 6), (0, 0)))

    row_f32, row_low = ((rows, width), F32), ((rows, width), LOW)
    weights = dict(
        w_attn=((2, width, 2 * heads), LOW),
        w_out=((2, heads, width), LOW),
        w_mlp=((2, width, 2 * span), LOW),
        w_down=((2, span, width), LOW),
    )
    kept = dict(
        queries=((whole_rows, heads), LOW),
        kv=((whole_rows, heads), LOW),
        probs=((2 * whole_rows, rows), F32),
        mixed=((whole_rows, heads), LOW),
        gate=((whole_rows, span), F32),
        up=((whole_rows, span), F32),
        hidden=((whole_rows, span), LOW),
    )
    direct = dict(normed_out=((whole_rows, width), LOW), normed_mlp_out=((whole_rows, width), LOW))
    outs = dict(out=row_low, residual=row_f32)
    layer_0 = ring_call(
        functools.partial(layer_kernel, True),
        1,
        width,
        dict(x=own_tokens, own_gain=own_gains, key=key_matrix[0], value=value_matrix[0]),
        dict(w_gate=(w_gate, 0), w_up=(w_up, 0), **tables, mask=mask),
        dict(w_query=w_query, own_out=w_out, own_down=w_down),
        dict(**outs, **weights, gains=((2 * RING, 8, shard), F32)),
        kept,
        direct,
        dict(
            kv_blocks=((kv_heads, shard, heads), LOW),
            mlp_blocks=((RING, shard, 2 * span), LOW),
        ),
        dict(
            far_sem=(2, 2 * RING - 1),
            attn_sem=(2, 3, RING),
            mlp_sem=(2, 3, RING),
            big_sem=(2, 2),
        ),
    )
    gains = layer_0.gains.reshape(2, RING, 8, shard)[:, :, :2].transpose(0, 2, 1, 3)
    gains = gains.reshape(2, 2, 1, width)

    def weights_of(layer):
        return {name: (getattr(layer_0, name), layer) for name in weights}

    layer_1 = ring_call(
        functools.partial(layer_kernel, False),
        2,
        width,
        dict(x=layer_0.out, gains=gains[1]),
        dict(**weights_of(1), **tables, mask=mask),
        {},
        outs,
        kept,
        direct,
        {},
        {},
    )

    def back(layer, forward, x, base, now, later, beside, outs, kept, direct, scratch, sems):
        return ring_call(
            functools.partial(back_kernel, layer == 0),
            3 + layer,
            width,
            dict(base=base, x=x, residual=forward.residual, gains=gains[layer], **now),
            dict(
                **weights_of(layer),
                **tables,
                **{name: getattr(forward, name) for name in SAVED},
                normed=forward.normed_mlp_out,
                **later,
            ),
            dict(normed_attn_=forward.normed_out, **beside),
            dict(
                out=row_f32,
                gain_grad_mlp=((8, width), F32),
                gain_grad_attn=((8, width), F32),
                **outs,
            ),
            kept,
            direct,
            dict(
                g_mlp=((whole_rows, 2 * span), LOW),
                g_attn=((whole_rows, 2 * heads), LOW),
                middle=row_f32,
                **scratch,
            ),
            dict(again_sem=(1,), **sems),
        )

    pairs = dict(grad_mlp=((width, 2 * span), LOW), grad_attn=((width, 2 * heads), LOW))
    grad_rows = dict(grad_down=((span, width), LOW), grad_out=((heads, width), LOW))
    back_1 = back(
        1,
        layer_1,
        layer_0.out,
        own_target,
        {},
        {},
        {},
        {},
        dict(**pairs, **grad_rows),
        {},
        {},
        {},
    )
    back_0 = back(
        0,
        layer_0,
        own_tokens,
        back_1.out.astype(LOW),
        dict(gg1a=back_1.gain_grad_attn, gg1m=back_1.gain_grad_mlp),
        dict(late_mlp=back_1.grad_mlp, late_attn=back_1.grad_attn),
        dict(
            late_down=back_1.grad_down,
            late_out=back_1.grad_out,
            late_rows=back_1.out,
            out_0=layer_0.out,
            out_1=layer_1.out,
        ),
        dict(far_low=row_low, gain_sum=((2, shard), F32)),
        grad_rows,
        dict(
            fin_mlp=((RING, shard, 2 * span), LOW),
            fin_attn=((RING, shard, 2 * heads), LOW),
            stage_down=grad_rows[DOWN],
            stage_out=grad_rows[OUT],
            far_rows=row_f32,
            far_out=row_low,
        ),
        dict(
            **pairs,
            low=row_low,
            gains_out=((2 * RING, 2, 8, shard), F32),
            gains_in=((2 * RING, 2, 8, shard), F32),
            stage_mlp=pairs[MLP],
            stage_attn=pairs[ATTN],
        ),
        dict(
            far_sem=(2, 2 * RING - 1),
            cross_sem=(2, RING, 2),
            big_sem=(4, 2),
            deal_sem=(2, 2, RING),
        ),
    )
    down = jnp.where(first, back_0.grad_down, back_1.grad_down).astype(F32)
    down = (down + back_0.stage_down.astype(F32))[:units]
    out = jnp.where(first, back_0.grad_out, back_1.grad_out).astype(F32)
    out = out + back_0.stage_out.astype(F32)
    gate, up, query, key, value = side_by_side(back_0.fin_mlp, back_0.fin_attn, units)

    def micros(low_first, low_second, high_first, high_second):
        return jnp.where(
            first,
            jnp.concatenate([low_first, low_second]),
            jnp.concatenate([high_first, high_second]),
        )[None]

    return (
        micros(layer_0.out, back_0.far_out, back_0.far_out, layer_1.out),
        micros(back_0.out, back_0.far_low.astype(F32), back_0.far_rows, back_1.out),
        back_0.gain_sum[:1],
        query,
        key,
        value,
        out[None],
        back_0.gain_sum[1:],
        gate,
        up,
        down[None],
    )


def solution(mesh):
    in_specs = (
        P("dp", None),
        P("dp", None),
        P(),
        P(),
        P(),
        P("section", "dp"),
        P("section", "dp", "tensor"),
        P("section", "dp", "tensor"),
        P("section", "dp", "tensor"),
        P("section", ("tensor", "dp"), None),
        P("section", "dp"),
        P("section", "dp", "tensor"),
        P("section", "dp", "tensor"),
        P("section", ("tensor", "dp"), None),
    )
    out_specs = (
        P("section", "dp", None),
        P("section", "dp", None),
        P("section", "dp"),
        P("section", "dp", "tensor"),
        P("section", "dp", "tensor"),
        P("section", "dp", "tensor"),
        P("section", ("tensor", "dp"), None),
        P("section", "dp"),
        P("section", "dp", "tensor"),
        P("section", "dp", "tensor"),
        P("section", ("tensor", "dp"), None),
    )
    per_device = ring_device if ring_fits(mesh) else general_device
    return jax.shard_map(
        per_device, mesh=mesh, in_specs=in_specs, out_specs=out_specs, check_vma=False
    )
```

```python
import functools
import types

import jax
import jax.numpy as jnp
from jax import lax
from jax.experimental import pallas as pl
from jax.experimental.pallas import tpu as pltpu
from jax.sharding import PartitionSpec as P

HEAD_DIM = 64
CAP = 128
MICRO = 2


eps_norm = 1e-05
rope_base = 10000.0


def passed_along(shard, axis, by):
    count = lax.axis_size(axis)
    pairs = [(i, i + by) for i in range(count) if 0 <= i + by < count]
    return lax.ppermute(shard, axis, pairs)


def slot_layout(seq_lengths, seq_group, seq_micro, group_id, micro_total, slot_rows):
    row_ids = jnp.arange(slot_rows, dtype=jnp.int32)
    numbers = jnp.arange(seq_lengths.shape[0], dtype=jnp.int32) + 1
    label_list = []
    place_list = []
    for micro_id in range(micro_total):
        inside = ((seq_group == group_id) & (seq_micro == micro_id)).astype(jnp.int32)
        taken_len = seq_lengths * inside
        starts = jnp.cumsum(taken_len) - taken_len
        member = (
            (row_ids[:, None] >= starts[None, :])
            & (row_ids[:, None] < (starts + taken_len)[None, :])
        ).astype(jnp.int32)
        label_list.append(jnp.sum(member * numbers[None, :], axis=1))
        place_list.append(jnp.sum(member * (row_ids[:, None] - starts[None, :]), axis=1))
    return (jnp.stack(label_list), jnp.stack(place_list))


def apply_rotary(value_rows, token_positions, direction):
    half_size = value_rows.shape[-1] // 2
    frequency = rope_base ** (
        -2.0 * jnp.arange(half_size, dtype=jnp.float32) / value_rows.shape[-1]
    )
    angles = token_positions.astype(jnp.float32)[:, None] * frequency[None, :]
    cosines = jnp.cos(angles)[:, None, :]
    sines_part = direction * jnp.sin(angles)[:, None, :]
    first_half = value_rows[..., :half_size]
    second_half = value_rows[..., half_size:]
    return jnp.concatenate(
        [
            first_half * cosines - second_half * sines_part,
            second_half * cosines + first_half * sines_part,
        ],
        axis=-1,
    )


def rms_parts(value_rows):
    inverse = lax.rsqrt(jnp.mean(value_rows * value_rows, axis=-1, keepdims=True) + eps_norm)
    return (value_rows * inverse, inverse)


def dot_trans(left, right):
    return lax.dot_general(
        left, right, (((1,), (1,)), ((), ())), preferred_element_type=jnp.float32
    )


def dot_rows(left, right):
    return lax.dot_general(
        left, right, (((0,), (0,)), ((), ())), preferred_element_type=jnp.float32
    )


def tensor_total(partial_sum):
    return lax.psum(partial_sum, "tensor")


def input_total(partial_sum):
    return lax.psum(partial_sum.astype(jnp.bfloat16), "tensor").astype(jnp.float32)


def mask_of(labels):
    row_ids = jnp.arange(labels.shape[0], dtype=jnp.int32)
    return (labels[:, None] == labels[None, :]) & (row_ids[None, :] <= row_ids[:, None])


def forward_slot(inputs, labels, token_positions, attn_w, mlp_w):
    attn_gain, w_query, key_matrix, value_matrix, w_out = attn_w
    mlp_gain, w_gate, w_up, w_down = mlp_w
    total_row_count = inputs.shape[0]
    head_count = w_query.shape[1] // HEAD_DIM
    kv_count = key_matrix.shape[1] // HEAD_DIM
    query_group_width = head_count // kv_count
    scaled, inverse_attn = rms_parts(inputs)
    normalized_input = (scaled * attn_gain.astype(jnp.float32)).astype(jnp.bfloat16)
    query_rows = jnp.dot(normalized_input, w_query, preferred_element_type=jnp.float32)
    unrotated_keys = jnp.dot(normalized_input, key_matrix, preferred_element_type=jnp.float32)
    value_rows = (
        jnp.dot(normalized_input, value_matrix, preferred_element_type=jnp.float32)
        .astype(jnp.bfloat16)
        .reshape(total_row_count, kv_count, HEAD_DIM)
    )
    query_rows = (
        apply_rotary(
            query_rows.reshape(total_row_count, head_count, HEAD_DIM), token_positions, 1.0
        )
        .astype(jnp.bfloat16)
        .reshape(total_row_count, kv_count, query_group_width, HEAD_DIM)
    )
    rotated_keys = apply_rotary(
        unrotated_keys.reshape(total_row_count, kv_count, HEAD_DIM), token_positions, 1.0
    ).astype(jnp.bfloat16)
    scores = jnp.einsum(
        "qgjd,kgd->gjqk", query_rows, rotated_keys, preferred_element_type=jnp.float32
    ) * HEAD_DIM ** (-0.5)
    scores = jnp.where(mask_of(labels), scores, -1e30)
    top_score = jnp.max(scores, axis=-1, keepdims=True)
    exp_scores = jnp.exp(scores - top_score)
    total_mass = jnp.sum(exp_scores, axis=-1, keepdims=True)
    attn_probs = (exp_scores / total_mass).astype(jnp.bfloat16)
    log_mass = top_score + jnp.log(total_mass)
    mixed_heads = jnp.einsum(
        "gjqk,kgd->qgjd", attn_probs, value_rows, preferred_element_type=jnp.float32
    )
    mixed_heads = mixed_heads.reshape(total_row_count, head_count * HEAD_DIM).astype(jnp.bfloat16)
    residual = inputs + tensor_total(
        jnp.dot(mixed_heads, w_out, preferred_element_type=jnp.float32)
    )
    scaled_mlp, inverse_mlp = rms_parts(residual)
    normed_mlp = (scaled_mlp * mlp_gain.astype(jnp.float32)).astype(jnp.bfloat16)
    gate_proj = jnp.dot(normed_mlp, w_gate, preferred_element_type=jnp.float32)
    up_proj = jnp.dot(normed_mlp, w_up, preferred_element_type=jnp.float32)
    hidden = (jax.nn.silu(gate_proj) * up_proj).astype(jnp.bfloat16)
    result = residual + tensor_total(jnp.dot(hidden, w_down, preferred_element_type=jnp.float32))
    kept_state = (
        inputs,
        inverse_attn,
        normalized_input,
        query_rows,
        rotated_keys,
        value_rows,
        log_mass,
        mixed_heads,
        residual,
        inverse_mlp,
        normed_mlp,
        gate_proj,
        up_proj,
        hidden,
    )
    return (result, kept_state)


def backward_slot(grad_out, kept_state, labels, token_positions, attn_w, mlp_w):
    attn_gain, w_query, key_matrix, value_matrix, w_out = attn_w
    mlp_gain, w_gate, w_up, w_down = mlp_w
    (
        inputs,
        inverse_attn,
        normalized_input,
        query_rows,
        rotated_keys,
        value_rows,
        log_mass,
        mixed_heads,
        residual,
        inverse_mlp,
        normed_mlp,
        gate_proj,
        up_proj,
        hidden,
    ) = kept_state
    total_row_count = inputs.shape[0]
    head_count = w_query.shape[1] // HEAD_DIM
    kv_count = key_matrix.shape[1] // HEAD_DIM
    query_group_width = head_count // kv_count
    down_in = grad_out.astype(jnp.bfloat16)
    grad_hidden = dot_trans(down_in, w_down)
    grad_w_down = dot_rows(hidden, down_in)
    sigmoid_gate = jax.nn.sigmoid(gate_proj)
    grad_gate = (
        grad_hidden * up_proj * sigmoid_gate * (1.0 + gate_proj * (1.0 - sigmoid_gate))
    ).astype(jnp.bfloat16)
    grad_up = (grad_hidden * gate_proj * sigmoid_gate).astype(jnp.bfloat16)
    grad_w_gate = dot_rows(normed_mlp, grad_gate)
    grad_w_up = dot_rows(normed_mlp, grad_up)
    grad_normed_mlp = input_total(dot_trans(grad_gate, w_gate) + dot_trans(grad_up, w_up))
    scaled_mlp = residual * inverse_mlp
    grad_mlp_gain = jnp.sum(grad_normed_mlp * scaled_mlp, axis=0)
    inner_mlp = grad_normed_mlp * mlp_gain.astype(jnp.float32)
    grad_residual = grad_out + inverse_mlp * (
        inner_mlp - scaled_mlp * jnp.mean(inner_mlp * scaled_mlp, axis=-1, keepdims=True)
    )
    out_in = grad_residual.astype(jnp.bfloat16)
    grad_w_out = dot_rows(mixed_heads, out_in)
    grad_mixed = (
        dot_trans(out_in, w_out)
        .astype(jnp.bfloat16)
        .reshape(total_row_count, kv_count, query_group_width, HEAD_DIM)
    )
    scores = jnp.einsum(
        "qgjd,kgd->gjqk", query_rows, rotated_keys, preferred_element_type=jnp.float32
    ) * HEAD_DIM ** (-0.5)
    scores = jnp.where(mask_of(labels), scores, -1e30)
    probs_full = jnp.exp(scores - log_mass)
    attn_probs = probs_full.astype(jnp.bfloat16)
    grad_probs = jnp.einsum(
        "qgjd,kgd->gjqk", grad_mixed, value_rows, preferred_element_type=jnp.float32
    )
    grad_values = jnp.einsum(
        "gjqk,qgjd->kgd", attn_probs, grad_mixed, preferred_element_type=jnp.float32
    )
    spread_term = jnp.sum(grad_probs * probs_full, axis=-1, keepdims=True)
    grad_scores = (probs_full * (grad_probs - spread_term) * HEAD_DIM ** (-0.5)).astype(
        jnp.bfloat16
    )
    grad_queries = jnp.einsum(
        "gjqk,kgd->qgjd", grad_scores, rotated_keys, preferred_element_type=jnp.float32
    )
    grad_keys = jnp.einsum(
        "gjqk,qgjd->kgd", grad_scores, query_rows, preferred_element_type=jnp.float32
    )
    grad_queries = (
        apply_rotary(
            grad_queries.reshape(total_row_count, head_count, HEAD_DIM), token_positions, -1.0
        )
        .reshape(total_row_count, head_count * HEAD_DIM)
        .astype(jnp.bfloat16)
    )
    grad_keys = (
        apply_rotary(grad_keys, token_positions, -1.0)
        .reshape(total_row_count, kv_count * HEAD_DIM)
        .astype(jnp.bfloat16)
    )
    grad_values = grad_values.reshape(total_row_count, kv_count * HEAD_DIM).astype(jnp.bfloat16)
    grad_w_query = dot_rows(normalized_input, grad_queries)
    grad_w_key = dot_rows(normalized_input, grad_keys)
    grad_w_value = dot_rows(normalized_input, grad_values)
    grad_normed = input_total(
        dot_trans(grad_queries, w_query)
        + dot_trans(grad_keys, key_matrix)
        + dot_trans(grad_values, value_matrix)
    )
    scaled = inputs * inverse_attn
    grad_attn_gain = jnp.sum(grad_normed * scaled, axis=0)
    inner_attn = grad_normed * attn_gain.astype(jnp.float32)
    grad_inputs = grad_residual + inverse_attn * (
        inner_attn - scaled * jnp.mean(inner_attn * scaled, axis=-1, keepdims=True)
    )
    attn_grads = (grad_attn_gain, grad_w_query, grad_w_key, grad_w_value, grad_w_out)
    mlp_grads = (grad_mlp_gain, grad_w_gate, grad_w_up, grad_w_down)
    return (grad_inputs, attn_grads, mlp_grads)


def general_device(
    tokens,
    cotangent,
    seq_lengths,
    seq_group,
    seq_micro,
    attn_gain,
    w_query,
    key_matrix,
    value_matrix,
    w_out,
    mlp_gain,
    w_gate,
    w_up,
    w_down,
):
    section_count = lax.axis_size("section")
    section_id = lax.axis_index("section")
    group_id = lax.axis_index("dp")
    slot_rows = CAP
    micro_total = MICRO
    tick_count = micro_total + section_count - 1
    model_width = tokens.shape[1]
    labels, token_positions = slot_layout(
        seq_lengths, seq_group, seq_micro, group_id, micro_total, slot_rows
    )
    live_rows = (labels > 0).astype(jnp.float32)
    attn_w = (
        lax.all_gather(attn_gain[0], "dp", axis=0, tiled=True),
        lax.all_gather(w_query[0], "dp", axis=0, tiled=True),
        lax.all_gather(key_matrix[0], "dp", axis=0, tiled=True),
        lax.all_gather(value_matrix[0], "dp", axis=0, tiled=True),
        lax.all_gather(w_out[0], "dp", axis=0, tiled=True),
    )
    mlp_w = (
        lax.all_gather(mlp_gain[0], "dp", axis=0, tiled=True),
        lax.all_gather(w_gate[0], "dp", axis=0, tiled=True),
        lax.all_gather(w_up[0], "dp", axis=0, tiled=True),
        lax.all_gather(w_down[0], "dp", axis=0, tiled=True),
    )
    is_first = section_id == 0
    received = jnp.zeros((slot_rows, model_width), jnp.bfloat16)
    sent_list = []
    kept_list = []
    for tick_id in range(tick_count):
        micro_id = jnp.clip(tick_id - section_id, 0, micro_total - 1)
        fresh_slot = min(tick_id, micro_total - 1)
        fresh_rows = tokens[fresh_slot * slot_rows : (fresh_slot + 1) * slot_rows]
        section_input = jnp.where(is_first, fresh_rows, received).astype(jnp.float32)
        result, kept_state = forward_slot(
            section_input, labels[micro_id], token_positions[micro_id], attn_w, mlp_w
        )
        handed = result.astype(jnp.bfloat16)
        sent_list.append(handed)
        kept_list.append(kept_state)
        if tick_id + 1 < tick_count:
            received = passed_along(handed, "section", 1)
    sent_all = jnp.stack(sent_list)
    section_out = lax.dynamic_slice_in_dim(sent_all, section_id, micro_total, 0).reshape(
        micro_total * slot_rows, model_width
    )[None]
    kept_all = jax.tree.map(lambda *pieces: jnp.stack(pieces), *kept_list)
    attn_w = (
        lax.all_gather(attn_gain[0], "dp", axis=0, tiled=True),
        lax.all_gather(w_query[0], "dp", axis=0, tiled=True),
        lax.all_gather(key_matrix[0], "dp", axis=0, tiled=True),
        lax.all_gather(value_matrix[0], "dp", axis=0, tiled=True),
        lax.all_gather(w_out[0], "dp", axis=0, tiled=True),
    )
    mlp_w = (
        lax.all_gather(mlp_gain[0], "dp", axis=0, tiled=True),
        lax.all_gather(w_gate[0], "dp", axis=0, tiled=True),
        lax.all_gather(w_up[0], "dp", axis=0, tiled=True),
        lax.all_gather(w_down[0], "dp", axis=0, tiled=True),
    )
    is_last = section_id == section_count - 1
    back_received = jnp.zeros((slot_rows, model_width), jnp.bfloat16)
    grad_list = []
    attn_sum = None
    mlp_sum = None
    for tick_id in range(tick_count):
        micro_raw = tick_id - (section_count - 1 - section_id)
        active = ((micro_raw >= 0) & (micro_raw < micro_total)).astype(jnp.float32)
        micro_id = jnp.clip(micro_raw, 0, micro_total - 1)
        target = lax.dynamic_slice_in_dim(cotangent, micro_id * slot_rows, slot_rows, 0).astype(
            jnp.float32
        )
        grad_out = (
            jnp.where(
                is_last, target * live_rows[micro_id][:, None], back_received.astype(jnp.float32)
            )
            * active
        )
        kept_state = jax.tree.map(lambda stacked: stacked[micro_id + section_id], kept_all)
        grad_inputs, attn_grads, mlp_grads = backward_slot(
            grad_out, kept_state, labels[micro_id], token_positions[micro_id], attn_w, mlp_w
        )
        grad_list.append(grad_inputs)
        gain_a, query_g, key_g, value_g, out_g = attn_grads
        attn_grads = (
            lax.psum_scatter(
                gain_a.astype(jnp.bfloat16), "dp", scatter_dimension=0, tiled=True
            ).astype(jnp.float32),
            lax.psum_scatter(
                query_g.astype(jnp.bfloat16), "dp", scatter_dimension=0, tiled=True
            ).astype(jnp.float32),
            lax.psum_scatter(
                key_g.astype(jnp.bfloat16), "dp", scatter_dimension=0, tiled=True
            ).astype(jnp.float32),
            lax.psum_scatter(
                value_g.astype(jnp.bfloat16), "dp", scatter_dimension=0, tiled=True
            ).astype(jnp.float32),
            lax.psum_scatter(
                out_g.astype(jnp.bfloat16), "dp", scatter_dimension=0, tiled=True
            ).astype(jnp.float32),
        )
        gain_m, gate_g, up_g, down_g = mlp_grads
        mlp_grads = (
            lax.psum_scatter(
                gain_m.astype(jnp.bfloat16), "dp", scatter_dimension=0, tiled=True
            ).astype(jnp.float32),
            lax.psum_scatter(
                gate_g.astype(jnp.bfloat16), "dp", scatter_dimension=0, tiled=True
            ).astype(jnp.float32),
            lax.psum_scatter(
                up_g.astype(jnp.bfloat16), "dp", scatter_dimension=0, tiled=True
            ).astype(jnp.float32),
            lax.psum_scatter(
                down_g.astype(jnp.bfloat16), "dp", scatter_dimension=0, tiled=True
            ).astype(jnp.float32),
        )
        attn_sum = attn_grads if attn_sum is None else jax.tree.map(jnp.add, attn_sum, attn_grads)
        mlp_sum = mlp_grads if mlp_sum is None else jax.tree.map(jnp.add, mlp_sum, mlp_grads)
        if tick_id + 1 < tick_count:
            back_received = passed_along(grad_inputs.astype(jnp.bfloat16), "section", -1)
    grad_all = jnp.stack(grad_list)
    input_grad = lax.dynamic_slice_in_dim(
        grad_all, section_count - 1 - section_id, micro_total, 0
    ).reshape(micro_total * slot_rows, model_width)[None]
    return (
        section_out,
        input_grad,
        attn_sum[0][None],
        attn_sum[1][None],
        attn_sum[2][None],
        attn_sum[3][None],
        attn_sum[4][None],
        mlp_sum[0][None],
        mlp_sum[1][None],
        mlp_sum[2][None],
        mlp_sum[3][None],
    )


RING = 8
LANES = 128
MESH_ID = pl.DeviceIdType.MESH
VMEM_BYTES = 60 * 2**20


def ring_fits(mesh):
    shape = dict(mesh.shape)
    return shape["section"] == 2 and shape["tensor"] == 2 and shape["dp"] == RING and MICRO == 2


def ring_place(group_id):
    z, y = group_id // 2, group_id % 2
    return jnp.where(y == 0, z, RING - 1 - z)


def ring_group(place):
    place = lax.rem(place + 2 * RING, RING)
    return jnp.where(place < RING // 2, 2 * place, 2 * (RING - 1 - place) + 1)


def copy_to(device, src, dst, send_sem, recv_sem):
    return pltpu.make_async_remote_copy(
        src_ref=src,
        dst_ref=dst,
        send_sem=send_sem,
        recv_sem=recv_sem,
        device_id=device,
        device_id_type=MESH_ID,
    )


class Ring:
    def __init__(self, names, lazy, refs):
        self.ref = types.SimpleNamespace(**dict(zip(names, refs)))
        self.lazy = lazy
        self.loads = {}
        self.loaded = set()
        self.stores = []
        self.sent = []
        self.side = []
        self.section = lax.axis_index("section")
        self.core = lax.axis_index("tensor")
        self.group = lax.axis_index("dp")
        self.place = ring_place(self.group)
        self.right = (self.section, self.core, ring_group(self.place + 1))
        self.left = (self.section, self.core, ring_group(self.place - 1))
        self.sibling = (self.section, 1 - self.core, self.group)
        self.across = (1 - self.section, self.core, self.group)
        self.far = [(f, g) for f in (0, 1) for g in range(RING) if (f, g) != (0, 0)]

    def load_all(self, *names):
        for n, (name, at) in enumerate(self.lazy):
            if name in self.loaded or (names and name not in names):
                continue
            self.loaded.add(name)
            source, here = getattr(self.ref, name + "_"), getattr(self.ref, name)
            if at is not None:
                source = source.at[at]
            self.loads[name] = pltpu.make_async_copy(source, here, self.ref.load_sem.at[n])
            self.loads[name].start()

    def need(self, *names):
        for name in names:
            if name in self.loads:
                self.loads.pop(name).wait()

    def local(self, here, there):
        copy = pltpu.make_async_copy(here, there, self.ref.store_sem.at[len(self.stores)])
        copy.start()
        self.stores.append(copy)
        return copy

    def store(self, *names):
        for name in names:
            self.local(getattr(self.ref, name), getattr(self.ref, name + "_out"))

    def start(self, copy):
        copy.start()
        self.sent.append(copy)
        return copy

    def start_side(self, copy):
        copy.start()
        self.side.append(copy)
        return copy

    def drain(self):
        for copy in self.sent:
            copy.wait_send()
        self.sent = []

    def finish(self):
        self.need(*list(self.loads))
        self.drain()
        for copy in self.side:
            copy.wait_send()
        for copy in self.stores:
            if copy is not None:
                copy.wait()

    def stored(self, copy):
        copy.wait()
        self.stores = [None if other is copy else other for other in self.stores]

    def greet(self, devices):
        barrier = pltpu.get_barrier_semaphore()
        for device in devices:
            pl.semaphore_signal(barrier, inc=1, device_id=device, device_id_type=MESH_ID)
        pl.semaphore_wait(barrier, len(devices))

    def greet_ring(self):
        self.greet([self.right, self.left, self.sibling])

    def greet_all(self):
        self.greet([self.sibling] + [self.far_device(f, g) for f, g in self.far])

    def far_step(self, f, g):
        return lax.rem(self.section + f, 2), lax.rem(self.group + g, RING)

    def far_device(self, f, g):
        section, group = self.far_step(f, g)
        return (section, self.core, group)

    def group_from(self, g):
        return lax.rem(self.group + RING - g, RING)

    def far_from(self, f, g):
        return lax.rem(self.section + 2 - f, 2) * RING + self.group_from(g)

    def row_of(self, offset, c=0):
        return pl.multiple_of(ring_group(self.place + offset) * CAP + c * (CAP // 2), CAP // 2)

    def columns(self, width, own=True):
        half = width // 2
        core = self.core if own else 1 - self.core
        return pl.ds(pl.multiple_of(core * half, half), half)

    def gather_work_sum(
        self, work, early=(), gathered=None, summed=None, ready=None, given=None
    ):
        ref = self.ref
        whole, part, mate, total = ref.whole, ref.part, ref.mate, ref.total
        width, half_r = whole.shape[1], CAP // 2
        own_cols, other_cols = self.columns(width), self.columns(width, False)
        ways = ((0, self.right), (1, self.left))
        gather = None
        if given is None:
            gather = Gather(self, whole, ref.gather_sem, ref.pass_sem, self.start)

        mate_in = {}

        def work_on(offset):
            q = offset % RING
            if q in mate_in:
                return
            if gather is not None:
                gather.slot_passed(offset)
            work(self.row_of(offset))
            mate_in[q] = self.start(
                copy_to(
                    self.sibling,
                    part.at[pl.ds(self.row_of(offset), CAP), other_cols],
                    mate.at[q],
                    ref.mate_sem.at[0, q],
                    ref.mate_sem.at[1, q],
                )
            )

        if gather is not None:
            gather.begin()
            if 0 in early:
                work_on(0)
            for i in range(7):
                gather.step(i)
                if gathered is not None:
                    gathered(i)
                for offset in ((), (-1,), (1,), (-2,), (2,), (), ())[i]:
                    if offset in early:
                        work_on(offset)
        else:
            given()
        gather_sent, self.sent = self.sent, []
        if ready is not None:
            ready()
        work_on(4)

        seen = set()

        def mine(offset, c):
            q = offset % RING
            if q not in seen:
                mate_in[q].wait_recv()
                seen.add(q)
            return part[pl.ds(self.row_of(q, c), half_r), own_cols].astype(jnp.float32) + mate[
                q, pl.ds(c * half_r, half_r)
            ].astype(jnp.float32)

        stream_sum = ((4, 0), (3, 1), (3, 0), (2, 1), (2, 0), (1, 1), (1, 0))
        ahead = ((3, -3), (2, -2), (), (1, -1), (0,), (), ())
        moves = []
        for i, (q, c) in enumerate(stream_sum):
            if i == 5:
                for copy in gather_sent:
                    copy.wait_send()
            for way, device in ways:
                offset, chunk = (q, c) if way == 0 else (-q, 1 - c)
                value = mine(offset, chunk)
                if i >= 2:
                    moves[2 * (i - 2) + way].wait_recv()
                    value = value + ref.sum_recv[way, i - 2].astype(jnp.float32)
                ref.sum_send[way, i] = value.astype(jnp.bfloat16)
                moves.append(
                    self.start(
                        copy_to(
                            device,
                            ref.sum_send.at[way, i],
                            ref.sum_recv.at[way, i],
                            ref.sum_sem.at[0, way, i],
                            ref.sum_sem.at[1, way, i],
                        )
                    )
                )
            for offset in ahead[i]:
                work_on(offset)
            if i == 0 and gather is not None:
                gather.all_passed()
            if summed is not None:
                summed(i)
        halves = []
        for c in (1, 0):
            value = mine(0, c)
            at = (5, 6) if c == 1 else (6, 5)
            for way in (0, 1):
                moves[2 * at[way] + way].wait_recv()
                value = value + ref.sum_recv[way, at[way]].astype(jnp.float32)
            here = (pl.ds(c * half_r, half_r), own_cols)
            total[here] = value
            halves.append(
                self.start(
                    copy_to(
                        self.sibling,
                        total.at[here],
                        total.at[here],
                        ref.half_sem.at[0, c],
                        ref.half_sem.at[1, c],
                    )
                )
            )
        for copy in halves:
            copy.wait_recv()
        self.drain()


class Gather:
    stream = ((0, 0), (0, 1), (1, 0), (1, 1), (2, 0), (2, 1), (3, 0))

    def __init__(self, ring, whole, gather_sem, pass_sem, start):
        self.ring, self.whole, self.start = ring, whole, start
        self.gather_sem, self.pass_sem = gather_sem, pass_sem
        self.own_cols = ring.columns(whole.shape[1])
        self.other_cols = ring.columns(whole.shape[1], False)
        self.seen = set()

    def landing(self, way, k, c, columns):
        offset, chunk = (-k, c) if way == 0 else (k, 1 - c)
        return self.whole.at[pl.ds(self.ring.row_of(offset, chunk), CAP // 2), columns]

    def move(self, device, where, sems, way, i):
        return copy_to(device, where, where, sems.at[0, way, i], sems.at[1, way, i])

    def forward(self, i, way):
        k, c = self.stream[i]
        where = self.landing(way, k, c, self.own_cols)
        device = (self.ring.right, self.ring.left)[way]
        self.start(self.move(device, where, self.gather_sem, way, i))

    def begin(self):
        for i in (0, 1):
            for way in (0, 1):
                self.forward(i, way)

    def step(self, i):
        k, c = self.stream[i]
        for way in (0, 1):
            where = self.landing(way, k + 1, c, self.own_cols)
            device = (self.ring.right, self.ring.left)[way]
            self.move(device, where, self.gather_sem, way, i).wait_recv()
            self.start(self.move(self.ring.sibling, where, self.pass_sem, way, i))
            if i < 5:
                self.forward(i + 2, way)

    def passed(self, i, way):
        if (i, way) in self.seen:
            return
        self.seen.add((i, way))
        k, c = self.stream[i]
        where = self.landing(way, k + 1, c, self.other_cols)
        self.move(self.ring.sibling, where, self.pass_sem, way, i).wait_recv()

    def slot_passed(self, offset):
        if offset == RING // 2:
            for way in (0, 1):
                self.passed(6, way)
        elif offset != 0:
            way, k = (0, -offset) if offset < 0 else (1, offset)
            for i in (2 * k - 2, 2 * k - 1):
                self.passed(i, way)

    def all_passed(self):
        for i in range(7):
            for way in (0, 1):
                self.passed(i, way)


def by_rows(body, step=16):
    @pl.loop(0, CAP, step=step)
    def _(at):
        body(pl.ds(pl.multiple_of(at, step), step), at)


def inverse_rms(value):
    return lax.rsqrt(jnp.mean(value * value, axis=-1, keepdims=True) + eps_norm)


def norm_rows(ring, source, gain):
    own = ring.row_of(0)

    def body(here, at):
        value = source[here, :].astype(jnp.float32)
        low = (value * inverse_rms(value) * gain).astype(jnp.bfloat16)
        ring.ref.whole[pl.ds(pl.multiple_of(own + at, 16), 16), :] = low

    by_rows(body)


def own_rows(ring, matrix):
    return matrix.at[pl.ds(pl.multiple_of(ring.section * CAP, CAP), CAP)]


def back_rows(ring, base, source, gain, out, gain_grad, also=None):
    gain_grad[...] = jnp.zeros_like(gain_grad)

    def body(here, at):
        x = source[here, :].astype(jnp.float32)
        inverse = inverse_rms(x)
        scaled = x * inverse
        grad = ring.ref.total[here, :]
        moved = grad * scaled
        gain_grad[...] += moved[:8] + moved[8:]
        inner = grad * gain
        value = base[here, :].astype(jnp.float32) + inverse * (
            inner - scaled * jnp.mean(inner * scaled, axis=-1, keepdims=True)
        )
        out[here, :] = value
        if also is not None:
            also[here, :] = value.astype(jnp.bfloat16)

    by_rows(body)


def lane_low(shape, span):
    return lax.rem(lax.broadcasted_iota(jnp.int32, shape, 1), span) < span // 2


def rot_rows(value, cosines, sines):
    low = lane_low(value.shape, HEAD_DIM)
    partner = jnp.where(
        low, pltpu.roll(value, LANES - HEAD_DIM // 2, 1), pltpu.roll(value, HEAD_DIM // 2, 1)
    )
    return value * cosines + partner * sines


def heads_apart(value):
    low = lane_low(value.shape, LANES)
    return jnp.concatenate([jnp.where(low, value, 0.0), jnp.where(low, 0.0, value)], axis=0)


def heads_together(value):
    rows = value.shape[0] // 2
    return jnp.where(lane_low((rows, LANES), LANES), value[:rows], value[rows:])


def twice(kv):
    low = lane_low(kv.shape, LANES)
    other = pltpu.roll(kv, HEAD_DIM, 1)
    return (
        jnp.where(low, kv, other).astype(jnp.bfloat16),
        jnp.where(low, other, kv).astype(jnp.bfloat16),
    )


def dot_wide(left, right):
    return jnp.dot(left, right, preferred_element_type=jnp.float32)


def side_moves(ring, sources, place, sems, shard):
    def rows_of(section, group, columns=slice(None)):
        at = pl.ds(pl.multiple_of(group * shard, shard), shard)
        return place.at[section, at, columns]

    def send(g):
        copies = []
        for n, (block, columns) in enumerate(sources):
            there = rows_of(ring.section, ring.group, columns)
            if g == 0:
                copies.append(ring.local(block(ring.group), there))
            else:
                copies.append(
                    ring.start_side(
                        copy_to(
                            ring.far_device(0, g),
                            block(lax.rem(ring.group + g, RING)),
                            there,
                            sems.at[0, n, g],
                            sems.at[1, n, g],
                        )
                    )
                )
        return copies

    def pass_on(g):
        group = ring.group_from(g)
        if g > 0:
            for n, (_, columns) in enumerate(sources):
                where = rows_of(ring.section, group, columns)
                copy_to(
                    ring.sibling, where, where, sems.at[0, n, g], sems.at[1, n, g]
                ).wait_recv()
        where = rows_of(ring.section, group)
        ring.start_side(copy_to(ring.across, where, where, sems.at[0, 2, g], sems.at[1, 2, g]))

    def wait_passed(g):
        where = rows_of(1 - ring.section, ring.group_from(g))
        copy_to(ring.across, where, where, sems.at[0, 2, g], sems.at[1, 2, g]).wait_recv()

    return send, pass_on, wait_passed


def unit_blocks(source, span, units, b):
    at = b * units
    base, turn = at // LANES * LANES, at % LANES
    wide = -(-(turn + units) // LANES) * LANES
    value = source[:, base : base + wide].astype(F32)
    if turn:
        value = pltpu.roll(value, wide - turn, 1)
    value = value[:, :span]
    lanes = lax.broadcasted_iota(jnp.int32, value.shape, 1)
    return jnp.where(lanes < units, value, 0.0).astype(LOW)


def layer_kernel(moving, names, lazy, *refs):
    ring = Ring(names, lazy, refs)
    ref = ring.ref
    width = ref.whole.shape[1]
    shard = width // RING
    ring.load_all()
    if moving:
        ring.greet_all()
        mine_at = ring.section * RING + ring.group
        ref.gains[mine_at] = ref.own_gain[...]
        for n, (f, g) in enumerate(ring.far):
            ring.start_side(
                copy_to(
                    ring.far_device(f, g),
                    ref.own_gain,
                    ref.gains.at[mine_at],
                    ref.far_sem.at[0, n],
                    ref.far_sem.at[1, n],
                )
            )
        key, value = ref.key[...].astype(F32), ref.value[...].astype(F32)
        low = lane_low(key.shape, LANES)
        ref.kv_blocks[0] = jnp.where(low, key, pltpu.roll(value, HEAD_DIM, 1)).astype(LOW)
        ref.kv_blocks[1] = jnp.where(low, pltpu.roll(key, HEAD_DIM, 1), value).astype(LOW)
        q_width = ref.w_out.shape[1]

        def query_block(group):
            at = pl.multiple_of(group * q_width, q_width)
            return ref.w_query.at[0, :, pl.ds(at, q_width)]

        def kv_block(group):
            return ref.kv_blocks.at[group // (RING // 2)]

        send_attn, pass_attn, attn_passed = side_moves(
            ring,
            ((query_block, slice(0, q_width)), (kv_block, slice(q_width, 2 * q_width))),
            ref.w_attn,
            ref.attn_sem,
            shard,
        )
        send_mlp, pass_mlp, mlp_passed = side_moves(
            ring,
            ((lambda group: ref.mlp_blocks.at[group], slice(None)),),
            ref.w_mlp,
            ref.mlp_sem,
            shard,
        )
        at_home = [send_attn(g) for g in range(RING)][0]
        units = ref.own_down.shape[1]
        span = ref.w_down.shape[1]
        if span > units:
            ref.w_down[:, units:, :] = jnp.zeros((2, span - units, width), LOW)

        def across_big(own, place, n):
            where = place.at[ring.section, pl.ds(0, own.shape[1])]
            at_home.append(ring.local(own.at[0], where))
            ring.start_side(
                copy_to(
                    ring.across, own.at[0], where, ref.big_sem.at[0, n], ref.big_sem.at[1, n]
                )
            )

        def big_passed(own, place, n):
            where = place.at[1 - ring.section, pl.ds(0, own.shape[1])]
            copy_to(
                ring.across, where, where, ref.big_sem.at[0, n], ref.big_sem.at[1, n]
            ).wait_recv()

        across_big(ref.own_out, ref.w_out, 0)
        for n, (f, g) in enumerate(ring.far):
            copy_to(
                ring.sibling,
                ref.own_gain,
                ref.gains.at[ring.far_from(f, g)],
                ref.far_sem.at[0, n],
                ref.far_sem.at[1, n],
            ).wait_recv()

        def gain_of(kind):
            return jnp.concatenate(
                [ref.gains[g, kind : kind + 1, :] for g in range(RING)], axis=-1
            )

        w_attn, w_out = ref.w_attn.at[0], ref.w_out.at[0]
        w_mlp, w_down = ref.w_mlp.at[0], ref.w_down.at[0]
    else:
        ring.greet_ring()

        def gain_of(kind):
            return ref.gains[kind]

        w_attn, w_out, w_mlp, w_down = ref.w_attn, ref.w_out, ref.w_mlp, ref.w_down
        target = own_rows(ring, ref.cotangent)[...].astype(F32) * ref.live[...]
        ref.target[...] = target.astype(LOW)
        ref.low[pl.ds(ring.row_of(0), CAP), :] = target.astype(LOW)
        aside = Gather(ring, ref.low, ref.aside_sem, ref.aside_pass_sem, ring.start_side)
        aside.begin()
    x = own_rows(ring, ref.tokens) if moving else ref.x
    norm_rows(ring, x, gain_of(0))
    heads = w_out.shape[0]
    span = w_down.shape[0]

    def attend(row):
        here = pl.ds(row, CAP)
        both = dot_wide(ref.whole[here, :], w_attn[...])
        queries, kv = both[:, :heads], both[:, heads:]
        cosines, sines = ref.cosines[here, :], ref.sines[here, :]
        queries = rot_rows(queries, cosines, sines)
        kv = jnp.where(lane_low(kv.shape, LANES), rot_rows(kv, cosines, sines), kv)
        ref.queries[here, :] = queries.astype(jnp.bfloat16)
        ref.kv[here, :] = kv.astype(jnp.bfloat16)
        keys, values = twice(kv)
        apart = heads_apart(queries).astype(jnp.bfloat16)
        allowed = ref.mask[here, :] > 0.5
        allowed = jnp.concatenate([allowed, allowed], axis=0)
        scores = jnp.where(allowed, dot_trans(apart, keys) * HEAD_DIM ** (-0.5), -1e30)
        weights = jnp.exp(scores - jnp.max(scores, axis=-1, keepdims=True))
        probs = weights / jnp.sum(weights, axis=-1, keepdims=True)
        ref.probs[pl.ds(pl.multiple_of(2 * row, 2 * CAP), 2 * CAP), :] = probs
        mixed = heads_together(dot_wide(probs.astype(jnp.bfloat16), values)).astype(jnp.bfloat16)
        ref.mixed[here, :] = mixed
        ref.part[here, :] = dot_wide(mixed, w_out[...]).astype(jnp.bfloat16)

    keeping = []

    def attn_gathered(i):
        if moving:
            if i == 0:
                for copy in at_home[:2]:
                    ring.stored(copy)
                pass_attn(0)
                ring.need("w_gate", "w_up")
            pass_attn(i + 1)
            if i == 4:
                across_big(ref.own_down, ref.w_down, 1)
            for b in (i,) if i < 6 else (6, 7):
                ref.mlp_blocks[b, :, :span] = unit_blocks(ref.w_gate, span, units, b)
                ref.mlp_blocks[b, :, span:] = unit_blocks(ref.w_up, span, units, b)
            if i == 6:
                for g in range(1, RING):
                    send_mlp(g)
                at_home.extend(send_mlp(0))

    def attn_ready():
        ring.need("cosines", "sines", "mask")
        if moving:
            ring.stored(at_home[2])

            @pl.when(ring.section == 1)
            def _():
                for g in range(RING):
                    attn_passed(g)
                big_passed(ref.own_out, ref.w_out, 0)

        else:
            ring.need("w_attn", "w_out")
            aside.step(0)
            aside.step(1)

    def attn_summed(i):
        if moving:
            if i == 0:
                ring.stored(at_home[4])
            for g in (i,):
                pass_mlp(g)

    def keep(there, also=None):
        def summed(i):
            if also is not None:
                also(i)
            if i == 0:
                keeping.append(ring.local(ref.whole, there))
            if i == 4:
                ring.stored(keeping.pop())

        return summed

    ring.gather_work_sum(attend, gathered=attn_gathered, ready=attn_ready, summed=keep(ref.normed_out, attn_summed))
    ring.store("queries", "kv", "probs", "mixed")
    if not moving:
        aside.step(2)
        aside.step(3)

    def add_rows(here, at):
        ref.residual[here, :] = x[here, :].astype(jnp.float32) + ref.total[here, :]

    by_rows(add_rows)
    norm_rows(ring, ref.residual, gain_of(1))

    def feed(row):
        here = pl.ds(row, CAP)
        both = dot_wide(ref.whole[here, :], w_mlp[...])
        gate, up = both[:, :span], both[:, span:]
        ref.gate[here, :] = gate
        ref.up[here, :] = up
        hidden = (gate * jax.nn.sigmoid(gate) * up).astype(jnp.bfloat16)
        ref.hidden[here, :] = hidden
        ref.part[here, :] = dot_wide(hidden, w_down[...]).astype(jnp.bfloat16)

    def mlp_gathered(i):
        if moving:
            if i == 0:
                pass_mlp(7)

    def mlp_ready():
        if moving:
            ring.stored(at_home[3])

            @pl.when(ring.section == 1)
            def _():
                for g in range(RING):
                    mlp_passed(g)
                big_passed(ref.own_down, ref.w_down, 1)

        else:
            ring.need("w_mlp", "w_down")
            aside.step(4)

    ring.gather_work_sum(feed, gathered=mlp_gathered, ready=mlp_ready, summed=keep(ref.normed_mlp_out))
    ring.store("gate", "up", "hidden")
    if not moving:
        aside.step(5)
        aside.step(6)
        aside.all_passed()
        ring.local(ref.low, ref.low_out)

    def round_rows(here, at):
        ref.out[here, :] = (ref.residual[here, :] + ref.total[here, :]).astype(jnp.bfloat16)

    by_rows(round_rows)
    if moving:

        @pl.when(ring.section == 0)
        def _():
            for g in range(RING):
                attn_passed(g)
                mlp_passed(g)
            big_passed(ref.own_out, ref.w_out, 0)
            big_passed(ref.own_down, ref.w_down, 1)

    ring.finish()


def back_kernel(last, units, names, lazy, *refs):
    ring = Ring(names, lazy, refs)
    ref = ring.ref
    width = ref.whole.shape[1]
    shard = width // RING
    span, heads = ref.w_down.shape[0], ref.w_out.shape[0]
    ring.load_all(*FIRST)
    if last:
        ring.greet_all()
        normed_attn, x = ref.normed, own_rows(ring, ref.tokens)
    else:
        ring.greet_ring()
        normed_attn, x = ref.normed_attn, ref.x
    again = pltpu.make_async_copy(ref.normed_attn_, normed_attn, ref.again_sem.at[0])
    if last:
        ref.whole[pl.ds(ring.row_of(0), CAP), :] = ref.base[...]
        given = None
    else:
        whole_in = pltpu.make_async_copy(ref.low_in, ref.whole, ref.again_sem.at[1])
        whole_in.start()
        given = whole_in.wait

    def block(matrix, g):
        at = lax.rem(ring.group + g, RING) * shard
        return matrix.at[pl.ds(pl.multiple_of(at, shard), shard)]

    order = (1, 2, 3, 4, 5, 6, 7, 0)
    if last:

        def cross(source, place, sems):
            return copy_to(ring.across, source, place, sems.at[0], sems.at[1])

        def cross_mlp(g, source):
            return cross(block(source, g), block(ref.stage_mlp, g), ref.cross_sem.at[0, g])

        def cross_attn(g, source):
            return cross(block(source, g), block(ref.stage_attn, g), ref.cross_sem.at[1, g])

        def cross_big(n, source):
            rows = pl.ds(0, (units, heads)[n])
            place = (ref.stage_down, ref.stage_out)[n].at[rows]
            return cross(source.at[rows], place, ref.big_sem.at[n])

        def deal(g, own, fin, n):
            if g == 0:
                return pltpu.make_async_copy(
                    block(own, 0), fin.at[ring.group], ref.deal_sem.at[n, 0, 0]
                )
            return copy_to(
                ring.far_device(0, g),
                block(own, g),
                fin.at[ring.group],
                ref.deal_sem.at[n, 0, g],
                ref.deal_sem.at[n, 1, g],
            )

        def add_and_deal(g, own, n):
            crossed = (cross_mlp, cross_attn)[n](g, own)
            crossed.wait_recv()
            stage, fin = ((ref.stage_mlp, ref.fin_mlp), (ref.stage_attn, ref.fin_attn))[n]
            rows, other = block(own, g), block(stage, g)
            rows[...] = (rows[...].astype(F32) + other[...].astype(F32)).astype(LOW)
            deal(g, own, fin, n).start()

        def dealt(own, n):
            fin = (ref.fin_mlp, ref.fin_attn)[n]
            for g in range(RING):
                copy = deal(g, own, fin, n)
                if g == 0:
                    copy.wait()
                else:
                    copy.wait_send()
                    where = fin.at[ring.group_from(g)]
                    copy_to(
                        ring.sibling,
                        where,
                        where,
                        ref.deal_sem.at[n, 0, g],
                        ref.deal_sem.at[n, 1, g],
                    ).wait_recv()

        @pl.when(ring.section == 0)
        def _():
            for g in order:
                cross_mlp(g, ref.late_mlp_).start()
            for g in order:
                cross_attn(g, ref.late_attn_).start()
            cross_big(1, ref.late_out).start()
            cross_big(0, ref.late_down).start()
            cross(ref.late_rows, ref.far_rows, ref.big_sem.at[2]).start()
            cross(ref.out_1, ref.far_out, ref.big_sem.at[3]).start()

        @pl.when(ring.section == 1)
        def _():
            cross(ref.out_0, ref.far_out, ref.big_sem.at[3]).start()

    def when(section, body):
        if last:
            pl.when(ring.section == section)(body)

    def layer_0(n, *steps):
        if not steps:
            return

        def body():
            for g in steps:
                add_and_deal(g, (ref.grad_mlp, ref.grad_attn)[n], n)

        when(0, body)

    def feed_back(row):
        here = pl.ds(row, CAP)
        ring.need("w_mlp", "w_down", "gate", "up")
        grad_hidden = dot_trans(ref.whole[here, :], ref.w_down[...])
        gate, up = ref.gate[here, :], ref.up[here, :]
        sigmoid = jax.nn.sigmoid(gate)
        grad_gate = grad_hidden * up * sigmoid * (1.0 + gate * (1.0 - sigmoid))
        grad_up = grad_hidden * gate * sigmoid
        both = jnp.concatenate([grad_gate, grad_up], axis=1).astype(jnp.bfloat16)
        ref.g_mlp[here, :] = both
        ref.part[here, :] = dot_trans(both, ref.w_mlp[...]).astype(jnp.bfloat16)

    def weight_rows(g, normed, grads, place):
        at = pl.multiple_of(lax.rem(ring.group + g, RING) * shard, shard)
        piece = normed[:, pl.ds(at, shard)]
        place[pl.ds(at, shard), :] = dot_rows(piece, grads[...]).astype(jnp.bfloat16)

    def mlp_summed(i):
        if i == 0:
            ring.load_all()
            if not last:
                again.start()
        ring.need("hidden")
        if last:
            ring.need("normed")
        if last:
            weights, downs = ((), (1, 2, 3), (4, 5, 6), (7, 0), (), (), ()), (3, 4, 4, 5)
        else:
            weights, downs = ((),) * 7, (0, 1, 2, 3)
        for g in weights[i]:
            weight_rows(g, ref.normed, ref.g_mlp, ref.grad_mlp)
            when(1, lambda: cross_mlp(g, ref.grad_mlp).start())
        piece = width // 4
        for j in range(4):
            if downs[j] != i:
                continue
            at = slice(j * piece, (j + 1) * piece)
            ref.grad_down[:, at] = dot_rows(ref.hidden[...], ref.whole[:, at]).astype(LOW)
        if last:
            if i == 2:
                ring.need("late_mlp", "late_attn")
            layer_0(0, *((), (), (), (), (), (1,), (2,))[i])

    early = (0, 1, -1, 2, -2)
    ring.gather_work_sum(feed_back, early=early, summed=mlp_summed, given=given)
    if last:
        again.start()
    else:
        ring.store("grad_down")
    back_rows(ring, ref.base, ref.residual, ref.gains[1], ref.middle, ref.gain_grad_mlp)
    own = ring.row_of(0)

    def low_rows(here, at):
        low = ref.middle[here, :].astype(jnp.bfloat16)
        ref.whole[pl.ds(pl.multiple_of(own + at, 16), 16), :] = low

    by_rows(low_rows)

    def attend_back(row):
        here = pl.ds(row, CAP)
        ring.need("w_attn", "w_out", "queries", "kv", "probs", "cosines", "sines")
        grad_mixed = dot_trans(ref.whole[here, :], ref.w_out[...])
        grad_apart = heads_apart(grad_mixed).astype(jnp.bfloat16)
        keys, values = twice(ref.kv[here, :].astype(jnp.float32))
        apart = heads_apart(ref.queries[here, :].astype(jnp.float32)).astype(jnp.bfloat16)
        probs = ref.probs[pl.ds(pl.multiple_of(2 * row, 2 * CAP), 2 * CAP), :]
        grad_probs = dot_trans(grad_apart, values)
        grad_values = dot_rows(probs.astype(jnp.bfloat16), grad_apart)
        spread = jnp.sum(grad_probs * probs, axis=-1, keepdims=True)
        grad_scores = (probs * (grad_probs - spread) * HEAD_DIM ** (-0.5)).astype(jnp.bfloat16)
        grad_queries = heads_together(dot_wide(grad_scores, keys))
        grad_keys = dot_rows(grad_scores, apart)
        cosines, sines = ref.cosines[here, :], -ref.sines[here, :]
        grad_queries = rot_rows(grad_queries, cosines, sines)
        grad_keys = rot_rows(grad_keys + pltpu.roll(grad_keys, HEAD_DIM, 1), cosines, sines)
        grad_values = grad_values + pltpu.roll(grad_values, HEAD_DIM, 1)
        grad_kv = jnp.where(lane_low(grad_keys.shape, LANES), grad_keys, grad_values)
        both = jnp.concatenate([grad_queries, grad_kv], axis=1).astype(jnp.bfloat16)
        ref.g_attn[here, :] = both
        ref.part[here, :] = dot_trans(both, ref.w_attn[...]).astype(jnp.bfloat16)

    def attn_gathered(i):
        layer_0(0, *((3,), (), (), (4,), (), (), (5,))[i])
        if not last:
            ring.need("normed")
            for g in ((1, 2), (3,), (4,), (5,), (6,), (7,), (0,))[i]:
                weight_rows(g, ref.normed, ref.g_mlp, ref.grad_mlp)
            if i == 6:
                ring.store("grad_mlp")

    def attn_summed(i):
        if i == 1:
            again.wait()
        if last:
            weights, out_at = ((), (1, 2, 3, 4), (5, 6, 7, 0), (), (), (), ()), 3
        else:
            weights, out_at = ((), (), (), (), (), (1, 2, 3, 4), (5, 6, 7, 0)), 1
        for g in weights[i]:
            weight_rows(g, normed_attn, ref.g_attn, ref.grad_attn)
            when(1, lambda: cross_attn(g, ref.grad_attn).start())
        if i == out_at:
            ring.need("mixed")
            ref.grad_out[...] = dot_rows(ref.mixed[...], ref.whole[...]).astype(LOW)

            def rest():
                cross_big(1, ref.grad_out).start()
                cross_big(0, ref.grad_down).start()

            when(1, rest)
        layer_0(0, *((), (6,), (), (), (7,), (), (0,))[i])

    ring.gather_work_sum(
        attend_back,
        early=early if last else (),
        gathered=attn_gathered,
        summed=attn_summed,
    )
    back_rows(
        ring,
        ref.middle,
        x,
        ref.gains[0],
        ref.out,
        ref.gain_grad_attn,
        ref.low,
    )
    if last:
        end_exchange = last_exchange(ring)
        ring.store("grad_down", "grad_out")

        @pl.when(ring.section == 1)
        def _():
            for g in order:
                add_and_deal(g, ref.late_mlp, 0)
            for g in order:
                add_and_deal(g, ref.late_attn, 1)
            dealt(ref.late_mlp, 0)
            dealt(ref.late_attn, 1)
            places = (ref.stage_down.at[pl.ds(0, units)], ref.stage_out, ref.far_rows, ref.far_out)
            for n, place in enumerate(places):
                copy_to(
                    ring.across, place, place, ref.big_sem.at[n, 0], ref.big_sem.at[n, 1]
                ).wait_recv()
            for g in range(RING):
                cross_mlp(g, ref.grad_mlp).wait_send()
                cross_attn(g, ref.grad_attn).wait_send()
            cross_big(0, ref.grad_down).wait_send()
            cross_big(1, ref.grad_out).wait_send()
            cross(ref.out_0, ref.far_out, ref.big_sem.at[3]).wait_send()

        @pl.when(ring.section == 0)
        def _():
            for g in order:
                add_and_deal(g, ref.grad_attn, 1)
            dealt(ref.grad_mlp, 0)
            dealt(ref.grad_attn, 1)
            places = ((0, ref.stage_down.at[pl.ds(0, units)]), (1, ref.stage_out), (3, ref.far_out))
            for n, place in places:
                copy_to(
                    ring.across, place, place, ref.big_sem.at[n, 0], ref.big_sem.at[n, 1]
                ).wait_recv()
            for g in range(RING):
                cross_mlp(g, ref.late_mlp_).wait_send()
                cross_attn(g, ref.late_attn_).wait_send()
            cross_big(0, ref.late_down).wait_send()
            cross_big(1, ref.late_out).wait_send()
            cross(ref.late_rows, ref.far_rows, ref.big_sem.at[2]).wait_send()
            cross(ref.out_1, ref.far_out, ref.big_sem.at[3]).wait_send()

        end_exchange()
    else:
        ring.store("grad_attn", "grad_out")
    ring.finish()


def last_exchange(ring):
    ref = ring.ref
    width = ref.whole.shape[1]
    shard, half_r = width // RING, CAP // 2
    own_cols = ring.columns(width)
    halves = []
    for c in (0, 1):
        here = (pl.ds(c * half_r, half_r), own_cols)
        halves.append(
            ring.start(
                copy_to(
                    ring.across,
                    ref.low.at[here],
                    ref.far_low.at[here],
                    ref.half_sem.at[0, 2 + c],
                    ref.half_sem.at[1, 2 + c],
                )
            )
        )
    mine_at = ring.section * RING + ring.group
    grads = ((ref.gain_grad_attn, ref.gain_grad_mlp), (ref.gg1a, ref.gg1m))
    for layer in (0, 1):
        for g in range(RING):
            for kind in (0, 1):
                ref.gains_out[layer * RING + g, kind] = grads[layer][kind][
                    :, g * shard : (g + 1) * shard
                ]
    ref.gains_in[mine_at] = ref.gains_out[mine_at]
    for n, (f, g) in enumerate(ring.far):
        to_s, to_g = ring.far_step(f, g)
        ring.start(
            copy_to(
                ring.far_device(f, g),
                ref.gains_out.at[to_s * RING + to_g],
                ref.gains_in.at[mine_at],
                ref.far_sem.at[0, n],
                ref.far_sem.at[1, n],
            )
        )
    return lambda: last_waits(ring, halves)


def last_waits(ring, halves):
    ref = ring.ref
    width = ref.whole.shape[1]
    half_r = CAP // 2
    own_cols, other_cols = ring.columns(width), ring.columns(width, False)
    for c in (0, 1):
        halves[c].wait_recv()
        where = ref.far_low.at[pl.ds(c * half_r, half_r), own_cols]
        ring.start(
            copy_to(
                ring.sibling, where, where, ref.half_sem.at[0, 4 + c], ref.half_sem.at[1, 4 + c]
            )
        )
    for n, (f, g) in enumerate(ring.far):
        copy_to(
            ring.sibling,
            ref.gains_out.at[0],
            ref.gains_in.at[ring.far_from(f, g)],
            ref.far_sem.at[0, n],
            ref.far_sem.at[1, n],
        ).wait_recv()
    for kind in (0, 1):
        ref.gain_sum[kind : kind + 1, :] = jnp.sum(
            jnp.sum(ref.gains_in[:, kind], axis=0), axis=0, keepdims=True
        )
    for c in (0, 1):
        where = ref.far_low.at[pl.ds(c * half_r, half_r), other_cols]
        copy_to(
            ring.sibling, where, where, ref.half_sem.at[0, 4 + c], ref.half_sem.at[1, 4 + c]
        ).wait_recv()


F32, LOW = jnp.float32, jnp.bfloat16
MLP, ATTN, DOWN, OUT = "grad_mlp", "grad_attn", "grad_down", "grad_out"
MLP_IN, ATTN_IN, ROWS, OUT_0 = "mlp", "attn", "rows_0", "out_0"
WIDE = ("gate", "up", "query", "key", "value")
FIRST = ("w_mlp", "w_down", "gate", "up", "hidden")
SAVED = ("gate", "up", "hidden", "queries", "kv", "probs", "mixed")


def ring_call(
    kernel, collective_id, width, now, later, beside, outs, kept, direct, scratch, sems
):
    rows = CAP
    later = {name: a if isinstance(a, tuple) else (a, None) for name, a in later.items()}
    arrays = dict(
        whole=((RING * rows, width), LOW),
        part=((RING * rows, width), LOW),
        mate=((RING, rows, width // 2), LOW),
        sum_send=((2, 7, rows // 2, width // 2), LOW),
        sum_recv=((2, 7, rows // 2, width // 2), LOW),
        total=((rows, width), F32),
        **kept,
        **scratch,
    )
    sems = dict(
        gather_sem=(2, 2, 7),
        pass_sem=(2, 2, 7),
        mate_sem=(2, RING),
        sum_sem=(2, 2, 7),
        half_sem=(2, 6),
        load_sem=(len(later),),
        store_sem=(16,),
        **sems,
    )
    vmem, anywhere = pl.BlockSpec(memory_space=pltpu.VMEM), pl.BlockSpec(memory_space=pl.ANY)
    names = list(now) + [name + "_" for name in later] + list(beside) + list(outs)
    names += [name + "_out" for name in kept] + list(direct) + list(later)
    names += list(arrays) + list(sems)
    results = pl.pallas_call(
        functools.partial(kernel, names, [(name, at) for name, (_, at) in later.items()]),
        out_shape=tuple(
            jax.ShapeDtypeStruct(*a) for a in (*outs.values(), *kept.values(), *direct.values())
        ),
        in_specs=[vmem] * len(now) + [anywhere] * (len(later) + len(beside)),
        out_specs=tuple([vmem] * len(outs) + [anywhere] * (len(kept) + len(direct))),
        scratch_shapes=[
            pltpu.VMEM(a.shape if at is None else a.shape[1:], a.dtype) for a, at in later.values()
        ]
        + [pltpu.VMEM(*a) for a in arrays.values()]
        + [pltpu.SemaphoreType.DMA(a) for a in sems.values()],
        compiler_params=pltpu.CompilerParams(
            collective_id=collective_id, has_side_effects=True, vmem_limit_bytes=VMEM_BYTES
        ),
        cost_estimate=pl.CostEstimate(
            flops=80 * 10**9, bytes_accessed=360 * 10**6, transcendentals=0
        ),
    )(*now.values(), *[a for a, _ in later.values()], *beside.values())
    return types.SimpleNamespace(**dict(zip([*outs, *kept, *direct], results)))


def lay_out_kernel(units, names, *refs):
    ref = types.SimpleNamespace(**dict(zip(names, refs)))
    first = lax.axis_index("section") == 0
    rows, span = ref.mlp.shape[1], ref.mlp.shape[2] // 2
    for start, place in ((0, ref.gate), (span, ref.up)):
        place[...] = jnp.zeros_like(place)
        for b in range(RING):
            at = b * units
            base, turn = at // LANES * LANES, at % LANES
            wide = -(-(turn + units) // LANES) * LANES
            block = ref.mlp[b, :, start : start + span].astype(F32)
            if wide > span:
                block = jnp.concatenate([block, jnp.zeros((rows, wide - span), F32)], axis=1)
            if turn:
                block = pltpu.roll(block, turn, 1)
            place[0, :, base : base + wide] += block[:, :wide]
    q_width = ref.attn.shape[2] // 2
    for b in range(RING):
        ref.query[0, :, b * q_width : (b + 1) * q_width] = ref.attn[b, :, :q_width].astype(F32)
    sums = []
    for head in (0, 1):
        blocks = range(head * RING // 2, (head + 1) * RING // 2)
        sums.append(sum(ref.attn[b, :, q_width:].astype(F32) for b in blocks))
    low = lane_low(sums[0].shape, LANES)
    ref.key[0] = jnp.where(low, sums[0], pltpu.roll(sums[1], HEAD_DIM, 1))
    ref.value[0] = jnp.where(low, pltpu.roll(sums[0], HEAD_DIM, 1), sums[1])
    down = jnp.where(first, ref.down_0[:units, :].astype(F32), ref.down_1[:units, :].astype(F32))
    ref.down[0] = down + ref.stage_down[:units, :].astype(F32)
    out = jnp.where(first, ref.out_0[...].astype(F32), ref.out_1[...].astype(F32))
    ref.out[0] = out + ref.stage_out[...].astype(F32)
    for place, low_first, low_second, high_first, high_second in (
        (ref.rows, ref.rows_0, ref.far_rows, ref.far_rows, ref.rows_1),
        (ref.grads, ref.grads_0, ref.far_low, ref.far_grads, ref.grads_1),
    ):
        kind = place.dtype
        place[0, :CAP, :] = jnp.where(
            first, low_first[...].astype(kind), high_first[...].astype(kind)
        )
        place[0, CAP:, :] = jnp.where(
            first, low_second[...].astype(kind), high_second[...].astype(kind)
        )


def lay_out(units, mlp, attn, **by_columns):
    _, shard, mlp_width = mlp.shape
    attn_width = attn.shape[2]
    width = by_columns[ROWS].shape[1]
    heads = by_columns[OUT_0].shape[0]
    steps = RING
    step, columns = shard // steps, width // steps
    wide = [RING * units] * 2 + [RING * attn_width // 2] + [attn_width // 2] * 2
    tall = dict(down=(units, F32), out=(heads, F32), rows=(2 * CAP, LOW), grads=(2 * CAP, F32))
    names = [MLP_IN, ATTN_IN, *by_columns, *WIDE, *tall]
    results = pl.pallas_call(
        functools.partial(lay_out_kernel, units, names),
        grid=(steps,),
        in_specs=[
            pl.BlockSpec((RING, step, mlp_width), lambda i: (0, i, 0)),
            pl.BlockSpec((RING, step, attn_width), lambda i: (0, i, 0)),
        ]
        + [pl.BlockSpec((a.shape[0], columns), lambda i: (0, i)) for a in by_columns.values()],
        out_shape=[jax.ShapeDtypeStruct((1, shard, w), F32) for w in wide]
        + [jax.ShapeDtypeStruct((1, rows, width), kind) for rows, kind in tall.values()],
        out_specs=[pl.BlockSpec((1, step, w), lambda i: (0, i, 0)) for w in wide]
        + [pl.BlockSpec((1, rows, columns), lambda i: (0, 0, i)) for rows, _ in tall.values()],
        compiler_params=pltpu.CompilerParams(vmem_limit_bytes=VMEM_BYTES),
    )(mlp, attn, *by_columns.values())
    return types.SimpleNamespace(**dict(zip([*WIDE, *tall], results)))


def ring_device(
    tokens,
    cotangent,
    seq_lengths,
    seq_group,
    seq_micro,
    attn_gain,
    w_query,
    key_matrix,
    value_matrix,
    w_out,
    mlp_gain,
    w_gate,
    w_up,
    w_down,
):
    section_id = lax.axis_index("section")
    group_id = lax.axis_index("dp")
    width = tokens.shape[1]
    rows = CAP
    whole_rows = RING * rows
    shard = w_query.shape[1]
    groups = jnp.arange(RING, dtype=jnp.int32)

    kv_heads = key_matrix.shape[2] // HEAD_DIM
    units = w_down.shape[1]
    span = -(-units // LANES) * LANES
    heads = w_out.shape[1]

    labels, places = jax.vmap(
        lambda g: jax.tree.map(
            lambda a: a[0],
            slot_layout(
                seq_lengths,
                jnp.where(seq_micro == section_id, seq_group, -1),
                seq_micro * 0,
                g,
                1,
                rows,
            ),
        )
    )(groups)
    row_ids = jnp.arange(rows, dtype=jnp.int32)
    mask = (labels[:, :, None] == labels[:, None, :]) & (row_ids[None, :] <= row_ids[:, None])
    half = HEAD_DIM // 2
    frequency = rope_base ** (-2.0 * jnp.arange(half, dtype=jnp.float32) / HEAD_DIM)
    angles = places.astype(jnp.float32).reshape(whole_rows, 1) * frequency
    cosines, sines = jnp.cos(angles), jnp.sin(angles)
    tables = dict(
        cosines=jnp.concatenate([cosines] * (LANES // half), axis=1),
        sines=jnp.concatenate([-sines, sines] * (LANES // HEAD_DIM), axis=1),
    )
    mask = mask.astype(F32).reshape(whole_rows, rows)

    own_live = lax.dynamic_index_in_dim(labels, group_id, 0, keepdims=False) > 0
    own_live = own_live.astype(F32)[:, None]
    own_gains = jnp.concatenate([attn_gain, mlp_gain]).astype(F32)
    own_gains = jnp.pad(own_gains, ((0, 6), (0, 0)))

    row_f32, row_low = ((rows, width), F32), ((rows, width), LOW)
    weights = dict(
        w_attn=((2, width, 2 * heads), LOW),
        w_out=((2, heads, width), LOW),
        w_mlp=((2, width, 2 * span), LOW),
        w_down=((2, span, width), LOW),
    )
    kept = dict(
        queries=((whole_rows, heads), LOW),
        kv=((whole_rows, heads), LOW),
        probs=((2 * whole_rows, rows), F32),
        mixed=((whole_rows, heads), LOW),
        gate=((whole_rows, span), F32),
        up=((whole_rows, span), F32),
        hidden=((whole_rows, span), LOW),
    )
    direct = dict(normed_out=((whole_rows, width), LOW), normed_mlp_out=((whole_rows, width), LOW))
    outs = dict(out=row_low, residual=row_f32)
    layer_0 = ring_call(
        functools.partial(layer_kernel, True),
        1,
        width,
        dict(tokens=tokens, own_gain=own_gains, key=key_matrix[0], value=value_matrix[0]),
        dict(w_gate=(w_gate, 0), w_up=(w_up, 0), **tables, mask=mask),
        dict(w_query=w_query, own_out=w_out, own_down=w_down),
        dict(**outs, **weights, gains=((2 * RING, 8, shard), F32)),
        kept,
        direct,
        dict(
            kv_blocks=((kv_heads, shard, heads), LOW),
            mlp_blocks=((RING, shard, 2 * span), LOW),
        ),
        dict(
            far_sem=(2, 2 * RING - 1),
            attn_sem=(2, 3, RING),
            mlp_sem=(2, 3, RING),
            big_sem=(2, 2),
        ),
    )
    gains = layer_0.gains.reshape(2, RING, 8, shard)[:, :, :2].transpose(0, 2, 1, 3)
    gains = gains.reshape(2, 2, 1, width)

    def weights_of(layer):
        return {name: (getattr(layer_0, name), layer) for name in weights}

    layer_1 = ring_call(
        functools.partial(layer_kernel, False),
        2,
        width,
        dict(x=layer_0.out, gains=gains[1], cotangent=cotangent, live=own_live),
        dict(**weights_of(1), **tables, mask=mask),
        {},
        dict(**outs, target=row_low),
        kept,
        dict(**direct, low_out=((whole_rows, width), LOW)),
        dict(low=((whole_rows, width), LOW)),
        dict(aside_sem=(2, 2, 7), aside_pass_sem=(2, 2, 7)),
    )

    def back(layer, forward, base, now, later, beside, outs, kept, direct, scratch, sems):
        return ring_call(
            functools.partial(back_kernel, layer == 0, units),
            3 + layer,
            width,
            dict(base=base, residual=forward.residual, gains=gains[layer], **now),
            dict(
                **weights_of(layer),
                **tables,
                **{name: getattr(forward, name) for name in SAVED},
                normed=forward.normed_mlp_out,
                **later,
            ),
            dict(normed_attn_=forward.normed_out, **beside),
            dict(
                out=row_f32,
                gain_grad_mlp=((8, width), F32),
                gain_grad_attn=((8, width), F32),
                **outs,
            ),
            kept,
            direct,
            dict(
                g_mlp=((whole_rows, 2 * span), LOW),
                g_attn=((whole_rows, 2 * heads), LOW),
                middle=row_f32,
                **scratch,
            ),
            dict(again_sem=(2,), **sems),
        )

    pairs = dict(grad_mlp=((width, 2 * span), LOW), grad_attn=((width, 2 * heads), LOW))
    grad_rows = dict(grad_down=((span, width), LOW), grad_out=((heads, width), LOW))
    back_1 = back(
        1,
        layer_1,
        layer_1.target,
        dict(x=layer_0.out),
        {},
        dict(low_in=layer_1.low_out),
        dict(low=row_low),
        dict(**pairs, **grad_rows),
        {},
        dict(normed_attn=((whole_rows, width), LOW)),
        {},
    )
    back_0 = back(
        0,
        layer_0,
        back_1.low,
        dict(tokens=tokens, gg1a=back_1.gain_grad_attn, gg1m=back_1.gain_grad_mlp),
        dict(late_mlp=back_1.grad_mlp, late_attn=back_1.grad_attn),
        dict(
            late_down=back_1.grad_down,
            late_out=back_1.grad_out,
            late_rows=back_1.out,
            out_0=layer_0.out,
            out_1=layer_1.out,
        ),
        dict(far_low=row_low, gain_sum=((2, shard), F32)),
        grad_rows,
        dict(
            fin_mlp=((RING, shard, 2 * span), LOW),
            fin_attn=((RING, shard, 2 * heads), LOW),
            stage_down=grad_rows[DOWN],
            stage_out=grad_rows[OUT],
            far_rows=row_f32,
            far_out=row_low,
        ),
        dict(
            **pairs,
            low=row_low,
            gains_out=((2 * RING, 2, 8, shard), F32),
            gains_in=((2 * RING, 2, 8, shard), F32),
            stage_mlp=pairs[MLP],
            stage_attn=pairs[ATTN],
        ),
        dict(
            far_sem=(2, 2 * RING - 1),
            cross_sem=(2, RING, 2),
            big_sem=(4, 2),
            deal_sem=(2, 2, RING),
        ),
    )
    final = lay_out(
        units,
        back_0.fin_mlp,
        back_0.fin_attn,
        down_0=back_0.grad_down,
        down_1=back_1.grad_down,
        stage_down=back_0.stage_down,
        out_0=back_0.grad_out,
        out_1=back_1.grad_out,
        stage_out=back_0.stage_out,
        rows_0=layer_0.out,
        rows_1=layer_1.out,
        far_rows=back_0.far_out,
        grads_0=back_0.out,
        grads_1=back_1.out,
        far_low=back_0.far_low,
        far_grads=back_0.far_rows,
    )
    return (
        final.rows,
        final.grads,
        back_0.gain_sum[:1],
        final.query,
        final.key,
        final.value,
        final.out,
        back_0.gain_sum[1:],
        final.gate,
        final.up,
        final.down,
    )


def solution(mesh):
    in_specs = (
        P("dp", None),
        P("dp", None),
        P(),
        P(),
        P(),
        P("section", "dp"),
        P("section", "dp", "tensor"),
        P("section", "dp", "tensor"),
        P("section", "dp", "tensor"),
        P("section", ("tensor", "dp"), None),
        P("section", "dp"),
        P("section", "dp", "tensor"),
        P("section", "dp", "tensor"),
        P("section", ("tensor", "dp"), None),
    )
    out_specs = (
        P("section", "dp", None),
        P("section", "dp", None),
        P("section", "dp"),
        P("section", "dp", "tensor"),
        P("section", "dp", "tensor"),
        P("section", "dp", "tensor"),
        P("section", ("tensor", "dp"), None),
        P("section", "dp"),
        P("section", "dp", "tensor"),
        P("section", "dp", "tensor"),
        P("section", ("tensor", "dp"), None),
    )
    per_device = ring_device if ring_fits(mesh) else general_device
    return jax.shard_map(
        per_device, mesh=mesh, in_specs=in_specs, out_specs=out_specs, check_vma=False
    )
```

```python
import functools
import types

import jax
import jax.numpy as jnp
from jax import lax
from jax.experimental import pallas as pl
from jax.experimental.pallas import tpu as pltpu
from jax.sharding import PartitionSpec as P

HEAD_DIM = 64
CAP = 128
MICRO = 2


eps_norm = 1e-05
rope_base = 10000.0


def passed_along(shard, axis, by):
    count = lax.axis_size(axis)
    pairs = [(i, i + by) for i in range(count) if 0 <= i + by < count]
    return lax.ppermute(shard, axis, pairs)


def slot_layout(seq_lengths, seq_group, seq_micro, group_id, micro_total, slot_rows):
    row_ids = jnp.arange(slot_rows, dtype=jnp.int32)
    numbers = jnp.arange(seq_lengths.shape[0], dtype=jnp.int32) + 1
    label_list = []
    place_list = []
    for micro_id in range(micro_total):
        inside = ((seq_group == group_id) & (seq_micro == micro_id)).astype(jnp.int32)
        taken_len = seq_lengths * inside
        starts = jnp.cumsum(taken_len) - taken_len
        member = (
            (row_ids[:, None] >= starts[None, :])
            & (row_ids[:, None] < (starts + taken_len)[None, :])
        ).astype(jnp.int32)
        label_list.append(jnp.sum(member * numbers[None, :], axis=1))
        place_list.append(jnp.sum(member * (row_ids[:, None] - starts[None, :]), axis=1))
    return (jnp.stack(label_list), jnp.stack(place_list))


def apply_rotary(value_rows, token_positions, direction):
    half_size = value_rows.shape[-1] // 2
    frequency = rope_base ** (
        -2.0 * jnp.arange(half_size, dtype=jnp.float32) / value_rows.shape[-1]
    )
    angles = token_positions.astype(jnp.float32)[:, None] * frequency[None, :]
    cosines = jnp.cos(angles)[:, None, :]
    sines_part = direction * jnp.sin(angles)[:, None, :]
    first_half = value_rows[..., :half_size]
    second_half = value_rows[..., half_size:]
    return jnp.concatenate(
        [
            first_half * cosines - second_half * sines_part,
            second_half * cosines + first_half * sines_part,
        ],
        axis=-1,
    )


def rms_parts(value_rows):
    inverse = lax.rsqrt(jnp.mean(value_rows * value_rows, axis=-1, keepdims=True) + eps_norm)
    return (value_rows * inverse, inverse)


def dot_trans(left, right):
    return lax.dot_general(
        left, right, (((1,), (1,)), ((), ())), preferred_element_type=jnp.float32
    )


def dot_rows(left, right):
    return lax.dot_general(
        left, right, (((0,), (0,)), ((), ())), preferred_element_type=jnp.float32
    )


def tensor_total(partial_sum):
    return lax.psum(partial_sum, "tensor")


def input_total(partial_sum):
    return lax.psum(partial_sum.astype(jnp.bfloat16), "tensor").astype(jnp.float32)


def mask_of(labels):
    row_ids = jnp.arange(labels.shape[0], dtype=jnp.int32)
    return (labels[:, None] == labels[None, :]) & (row_ids[None, :] <= row_ids[:, None])


def forward_slot(inputs, labels, token_positions, attn_w, mlp_w):
    attn_gain, w_query, key_matrix, value_matrix, w_out = attn_w
    mlp_gain, w_gate, w_up, w_down = mlp_w
    total_row_count = inputs.shape[0]
    head_count = w_query.shape[1] // HEAD_DIM
    kv_count = key_matrix.shape[1] // HEAD_DIM
    query_group_width = head_count // kv_count
    scaled, inverse_attn = rms_parts(inputs)
    normalized_input = (scaled * attn_gain.astype(jnp.float32)).astype(jnp.bfloat16)
    query_rows = jnp.dot(normalized_input, w_query, preferred_element_type=jnp.float32)
    unrotated_keys = jnp.dot(normalized_input, key_matrix, preferred_element_type=jnp.float32)
    value_rows = (
        jnp.dot(normalized_input, value_matrix, preferred_element_type=jnp.float32)
        .astype(jnp.bfloat16)
        .reshape(total_row_count, kv_count, HEAD_DIM)
    )
    query_rows = (
        apply_rotary(
            query_rows.reshape(total_row_count, head_count, HEAD_DIM), token_positions, 1.0
        )
        .astype(jnp.bfloat16)
        .reshape(total_row_count, kv_count, query_group_width, HEAD_DIM)
    )
    rotated_keys = apply_rotary(
        unrotated_keys.reshape(total_row_count, kv_count, HEAD_DIM), token_positions, 1.0
    ).astype(jnp.bfloat16)
    scores = jnp.einsum(
        "qgjd,kgd->gjqk", query_rows, rotated_keys, preferred_element_type=jnp.float32
    ) * HEAD_DIM ** (-0.5)
    scores = jnp.where(mask_of(labels), scores, -1e30)
    top_score = jnp.max(scores, axis=-1, keepdims=True)
    exp_scores = jnp.exp(scores - top_score)
    total_mass = jnp.sum(exp_scores, axis=-1, keepdims=True)
    attn_probs = (exp_scores / total_mass).astype(jnp.bfloat16)
    log_mass = top_score + jnp.log(total_mass)
    mixed_heads = jnp.einsum(
        "gjqk,kgd->qgjd", attn_probs, value_rows, preferred_element_type=jnp.float32
    )
    mixed_heads = mixed_heads.reshape(total_row_count, head_count * HEAD_DIM).astype(jnp.bfloat16)
    residual = inputs + tensor_total(
        jnp.dot(mixed_heads, w_out, preferred_element_type=jnp.float32)
    )
    scaled_mlp, inverse_mlp = rms_parts(residual)
    normed_mlp = (scaled_mlp * mlp_gain.astype(jnp.float32)).astype(jnp.bfloat16)
    gate_proj = jnp.dot(normed_mlp, w_gate, preferred_element_type=jnp.float32)
    up_proj = jnp.dot(normed_mlp, w_up, preferred_element_type=jnp.float32)
    hidden = (jax.nn.silu(gate_proj) * up_proj).astype(jnp.bfloat16)
    result = residual + tensor_total(jnp.dot(hidden, w_down, preferred_element_type=jnp.float32))
    kept_state = (
        inputs,
        inverse_attn,
        normalized_input,
        query_rows,
        rotated_keys,
        value_rows,
        log_mass,
        mixed_heads,
        residual,
        inverse_mlp,
        normed_mlp,
        gate_proj,
        up_proj,
        hidden,
    )
    return (result, kept_state)


def backward_slot(grad_out, kept_state, labels, token_positions, attn_w, mlp_w):
    attn_gain, w_query, key_matrix, value_matrix, w_out = attn_w
    mlp_gain, w_gate, w_up, w_down = mlp_w
    (
        inputs,
        inverse_attn,
        normalized_input,
        query_rows,
        rotated_keys,
        value_rows,
        log_mass,
        mixed_heads,
        residual,
        inverse_mlp,
        normed_mlp,
        gate_proj,
        up_proj,
        hidden,
    ) = kept_state
    total_row_count = inputs.shape[0]
    head_count = w_query.shape[1] // HEAD_DIM
    kv_count = key_matrix.shape[1] // HEAD_DIM
    query_group_width = head_count // kv_count
    down_in = grad_out.astype(jnp.bfloat16)
    grad_hidden = dot_trans(down_in, w_down)
    grad_w_down = dot_rows(hidden, down_in)
    sigmoid_gate = jax.nn.sigmoid(gate_proj)
    grad_gate = (
        grad_hidden * up_proj * sigmoid_gate * (1.0 + gate_proj * (1.0 - sigmoid_gate))
    ).astype(jnp.bfloat16)
    grad_up = (grad_hidden * gate_proj * sigmoid_gate).astype(jnp.bfloat16)
    grad_w_gate = dot_rows(normed_mlp, grad_gate)
    grad_w_up = dot_rows(normed_mlp, grad_up)
    grad_normed_mlp = input_total(dot_trans(grad_gate, w_gate) + dot_trans(grad_up, w_up))
    scaled_mlp = residual * inverse_mlp
    grad_mlp_gain = jnp.sum(grad_normed_mlp * scaled_mlp, axis=0)
    inner_mlp = grad_normed_mlp * mlp_gain.astype(jnp.float32)
    grad_residual = grad_out + inverse_mlp * (
        inner_mlp - scaled_mlp * jnp.mean(inner_mlp * scaled_mlp, axis=-1, keepdims=True)
    )
    out_in = grad_residual.astype(jnp.bfloat16)
    grad_w_out = dot_rows(mixed_heads, out_in)
    grad_mixed = (
        dot_trans(out_in, w_out)
        .astype(jnp.bfloat16)
        .reshape(total_row_count, kv_count, query_group_width, HEAD_DIM)
    )
    scores = jnp.einsum(
        "qgjd,kgd->gjqk", query_rows, rotated_keys, preferred_element_type=jnp.float32
    ) * HEAD_DIM ** (-0.5)
    scores = jnp.where(mask_of(labels), scores, -1e30)
    probs_full = jnp.exp(scores - log_mass)
    attn_probs = probs_full.astype(jnp.bfloat16)
    grad_probs = jnp.einsum(
        "qgjd,kgd->gjqk", grad_mixed, value_rows, preferred_element_type=jnp.float32
    )
    grad_values = jnp.einsum(
        "gjqk,qgjd->kgd", attn_probs, grad_mixed, preferred_element_type=jnp.float32
    )
    spread_term = jnp.sum(grad_probs * probs_full, axis=-1, keepdims=True)
    grad_scores = (probs_full * (grad_probs - spread_term) * HEAD_DIM ** (-0.5)).astype(
        jnp.bfloat16
    )
    grad_queries = jnp.einsum(
        "gjqk,kgd->qgjd", grad_scores, rotated_keys, preferred_element_type=jnp.float32
    )
    grad_keys = jnp.einsum(
        "gjqk,qgjd->kgd", grad_scores, query_rows, preferred_element_type=jnp.float32
    )
    grad_queries = (
        apply_rotary(
            grad_queries.reshape(total_row_count, head_count, HEAD_DIM), token_positions, -1.0
        )
        .reshape(total_row_count, head_count * HEAD_DIM)
        .astype(jnp.bfloat16)
    )
    grad_keys = (
        apply_rotary(grad_keys, token_positions, -1.0)
        .reshape(total_row_count, kv_count * HEAD_DIM)
        .astype(jnp.bfloat16)
    )
    grad_values = grad_values.reshape(total_row_count, kv_count * HEAD_DIM).astype(jnp.bfloat16)
    grad_w_query = dot_rows(normalized_input, grad_queries)
    grad_w_key = dot_rows(normalized_input, grad_keys)
    grad_w_value = dot_rows(normalized_input, grad_values)
    grad_normed = input_total(
        dot_trans(grad_queries, w_query)
        + dot_trans(grad_keys, key_matrix)
        + dot_trans(grad_values, value_matrix)
    )
    scaled = inputs * inverse_attn
    grad_attn_gain = jnp.sum(grad_normed * scaled, axis=0)
    inner_attn = grad_normed * attn_gain.astype(jnp.float32)
    grad_inputs = grad_residual + inverse_attn * (
        inner_attn - scaled * jnp.mean(inner_attn * scaled, axis=-1, keepdims=True)
    )
    attn_grads = (grad_attn_gain, grad_w_query, grad_w_key, grad_w_value, grad_w_out)
    mlp_grads = (grad_mlp_gain, grad_w_gate, grad_w_up, grad_w_down)
    return (grad_inputs, attn_grads, mlp_grads)


def general_device(
    tokens,
    cotangent,
    seq_lengths,
    seq_group,
    seq_micro,
    attn_gain,
    w_query,
    key_matrix,
    value_matrix,
    w_out,
    mlp_gain,
    w_gate,
    w_up,
    w_down,
):
    section_count = lax.axis_size("section")
    section_id = lax.axis_index("section")
    group_id = lax.axis_index("dp")
    slot_rows = CAP
    micro_total = MICRO
    tick_count = micro_total + section_count - 1
    model_width = tokens.shape[1]
    labels, token_positions = slot_layout(
        seq_lengths, seq_group, seq_micro, group_id, micro_total, slot_rows
    )
    live_rows = (labels > 0).astype(jnp.float32)
    attn_w = (
        lax.all_gather(attn_gain[0], "dp", axis=0, tiled=True),
        lax.all_gather(w_query[0], "dp", axis=0, tiled=True),
        lax.all_gather(key_matrix[0], "dp", axis=0, tiled=True),
        lax.all_gather(value_matrix[0], "dp", axis=0, tiled=True),
        lax.all_gather(w_out[0], "dp", axis=0, tiled=True),
    )
    mlp_w = (
        lax.all_gather(mlp_gain[0], "dp", axis=0, tiled=True),
        lax.all_gather(w_gate[0], "dp", axis=0, tiled=True),
        lax.all_gather(w_up[0], "dp", axis=0, tiled=True),
        lax.all_gather(w_down[0], "dp", axis=0, tiled=True),
    )
    is_first = section_id == 0
    received = jnp.zeros((slot_rows, model_width), jnp.bfloat16)
    sent_list = []
    kept_list = []
    for tick_id in range(tick_count):
        micro_id = jnp.clip(tick_id - section_id, 0, micro_total - 1)
        fresh_slot = min(tick_id, micro_total - 1)
        fresh_rows = tokens[fresh_slot * slot_rows : (fresh_slot + 1) * slot_rows]
        section_input = jnp.where(is_first, fresh_rows, received).astype(jnp.float32)
        result, kept_state = forward_slot(
            section_input, labels[micro_id], token_positions[micro_id], attn_w, mlp_w
        )
        handed = result.astype(jnp.bfloat16)
        sent_list.append(handed)
        kept_list.append(kept_state)
        if tick_id + 1 < tick_count:
            received = passed_along(handed, "section", 1)
    sent_all = jnp.stack(sent_list)
    section_out = lax.dynamic_slice_in_dim(sent_all, section_id, micro_total, 0).reshape(
        micro_total * slot_rows, model_width
    )[None]
    kept_all = jax.tree.map(lambda *pieces: jnp.stack(pieces), *kept_list)
    attn_w = (
        lax.all_gather(attn_gain[0], "dp", axis=0, tiled=True),
        lax.all_gather(w_query[0], "dp", axis=0, tiled=True),
        lax.all_gather(key_matrix[0], "dp", axis=0, tiled=True),
        lax.all_gather(value_matrix[0], "dp", axis=0, tiled=True),
        lax.all_gather(w_out[0], "dp", axis=0, tiled=True),
    )
    mlp_w = (
        lax.all_gather(mlp_gain[0], "dp", axis=0, tiled=True),
        lax.all_gather(w_gate[0], "dp", axis=0, tiled=True),
        lax.all_gather(w_up[0], "dp", axis=0, tiled=True),
        lax.all_gather(w_down[0], "dp", axis=0, tiled=True),
    )
    is_last = section_id == section_count - 1
    back_received = jnp.zeros((slot_rows, model_width), jnp.bfloat16)
    grad_list = []
    attn_sum = None
    mlp_sum = None
    for tick_id in range(tick_count):
        micro_raw = tick_id - (section_count - 1 - section_id)
        active = ((micro_raw >= 0) & (micro_raw < micro_total)).astype(jnp.float32)
        micro_id = jnp.clip(micro_raw, 0, micro_total - 1)
        target = lax.dynamic_slice_in_dim(cotangent, micro_id * slot_rows, slot_rows, 0).astype(
            jnp.float32
        )
        grad_out = (
            jnp.where(
                is_last, target * live_rows[micro_id][:, None], back_received.astype(jnp.float32)
            )
            * active
        )
        kept_state = jax.tree.map(lambda stacked: stacked[micro_id + section_id], kept_all)
        grad_inputs, attn_grads, mlp_grads = backward_slot(
            grad_out, kept_state, labels[micro_id], token_positions[micro_id], attn_w, mlp_w
        )
        grad_list.append(grad_inputs)
        gain_a, query_g, key_g, value_g, out_g = attn_grads
        attn_grads = (
            lax.psum_scatter(
                gain_a.astype(jnp.bfloat16), "dp", scatter_dimension=0, tiled=True
            ).astype(jnp.float32),
            lax.psum_scatter(
                query_g.astype(jnp.bfloat16), "dp", scatter_dimension=0, tiled=True
            ).astype(jnp.float32),
            lax.psum_scatter(
                key_g.astype(jnp.bfloat16), "dp", scatter_dimension=0, tiled=True
            ).astype(jnp.float32),
            lax.psum_scatter(
                value_g.astype(jnp.bfloat16), "dp", scatter_dimension=0, tiled=True
            ).astype(jnp.float32),
            lax.psum_scatter(
                out_g.astype(jnp.bfloat16), "dp", scatter_dimension=0, tiled=True
            ).astype(jnp.float32),
        )
        gain_m, gate_g, up_g, down_g = mlp_grads
        mlp_grads = (
            lax.psum_scatter(
                gain_m.astype(jnp.bfloat16), "dp", scatter_dimension=0, tiled=True
            ).astype(jnp.float32),
            lax.psum_scatter(
                gate_g.astype(jnp.bfloat16), "dp", scatter_dimension=0, tiled=True
            ).astype(jnp.float32),
            lax.psum_scatter(
                up_g.astype(jnp.bfloat16), "dp", scatter_dimension=0, tiled=True
            ).astype(jnp.float32),
            lax.psum_scatter(
                down_g.astype(jnp.bfloat16), "dp", scatter_dimension=0, tiled=True
            ).astype(jnp.float32),
        )
        attn_sum = attn_grads if attn_sum is None else jax.tree.map(jnp.add, attn_sum, attn_grads)
        mlp_sum = mlp_grads if mlp_sum is None else jax.tree.map(jnp.add, mlp_sum, mlp_grads)
        if tick_id + 1 < tick_count:
            back_received = passed_along(grad_inputs.astype(jnp.bfloat16), "section", -1)
    grad_all = jnp.stack(grad_list)
    input_grad = lax.dynamic_slice_in_dim(
        grad_all, section_count - 1 - section_id, micro_total, 0
    ).reshape(micro_total * slot_rows, model_width)[None]
    return (
        section_out,
        input_grad,
        attn_sum[0][None],
        attn_sum[1][None],
        attn_sum[2][None],
        attn_sum[3][None],
        attn_sum[4][None],
        mlp_sum[0][None],
        mlp_sum[1][None],
        mlp_sum[2][None],
        mlp_sum[3][None],
    )


RING = 8
LANES = 128
MESH_ID = pl.DeviceIdType.MESH
VMEM_BYTES = 60 * 2**20


def ring_fits(mesh):
    shape = dict(mesh.shape)
    return shape["section"] == 2 and shape["tensor"] == 2 and shape["dp"] == RING and MICRO == 2


def ring_place(group_id):
    z, y = group_id // 2, group_id % 2
    return jnp.where(y == 0, z, RING - 1 - z)


def ring_group(place):
    place = lax.rem(place + 2 * RING, RING)
    return jnp.where(place < RING // 2, 2 * place, 2 * (RING - 1 - place) + 1)


def copy_to(device, src, dst, send_sem, recv_sem):
    return pltpu.make_async_remote_copy(
        src_ref=src,
        dst_ref=dst,
        send_sem=send_sem,
        recv_sem=recv_sem,
        device_id=device,
        device_id_type=MESH_ID,
    )


class Ring:
    def __init__(self, names, lazy, refs):
        self.ref = types.SimpleNamespace(**dict(zip(names, refs)))
        self.lazy = lazy
        self.loads = {}
        self.loaded = set()
        self.stores = []
        self.sent = []
        self.side = []
        self.section = lax.axis_index("section")
        self.core = lax.axis_index("tensor")
        self.group = lax.axis_index("dp")
        self.place = ring_place(self.group)
        self.right = (self.section, self.core, ring_group(self.place + 1))
        self.left = (self.section, self.core, ring_group(self.place - 1))
        self.sibling = (self.section, 1 - self.core, self.group)
        self.across = (1 - self.section, self.core, self.group)
        self.far = [(f, g) for f in (0, 1) for g in range(RING) if (f, g) != (0, 0)]

    def load_all(self, *names):
        for n, (name, at) in enumerate(self.lazy):
            if name in self.loaded or (names and name not in names):
                continue
            self.loaded.add(name)
            source, here = getattr(self.ref, name + "_"), getattr(self.ref, name)
            if at is not None:
                source = source.at[at]
            self.loads[name] = pltpu.make_async_copy(source, here, self.ref.load_sem.at[n])
            self.loads[name].start()

    def need(self, *names):
        for name in names:
            if name in self.loads:
                self.loads.pop(name).wait()

    def local(self, here, there):
        copy = pltpu.make_async_copy(here, there, self.ref.store_sem.at[len(self.stores)])
        copy.start()
        self.stores.append(copy)
        return copy

    def store(self, *names):
        for name in names:
            self.local(getattr(self.ref, name), getattr(self.ref, name + "_out"))

    def start(self, copy):
        copy.start()
        self.sent.append(copy)
        return copy

    def start_side(self, copy):
        copy.start()
        self.side.append(copy)
        return copy

    def drain(self):
        for copy in self.sent:
            copy.wait_send()
        self.sent = []

    def finish(self):
        self.need(*list(self.loads))
        self.drain()
        for copy in self.side:
            copy.wait_send()
        for copy in self.stores:
            if copy is not None:
                copy.wait()

    def stored(self, copy):
        copy.wait()
        self.stores = [None if other is copy else other for other in self.stores]

    def greet(self, devices):
        barrier = pltpu.get_barrier_semaphore()
        for device in devices:
            pl.semaphore_signal(barrier, inc=1, device_id=device, device_id_type=MESH_ID)
        pl.semaphore_wait(barrier, len(devices))

    def greet_ring(self):
        self.greet([self.right, self.left, self.sibling])

    def greet_all(self):
        self.greet([self.sibling] + [self.far_device(f, g) for f, g in self.far])

    def far_step(self, f, g):
        return lax.rem(self.section + f, 2), lax.rem(self.group + g, RING)

    def far_device(self, f, g):
        section, group = self.far_step(f, g)
        return (section, self.core, group)

    def group_from(self, g):
        return lax.rem(self.group + RING - g, RING)

    def far_from(self, f, g):
        return lax.rem(self.section + 2 - f, 2) * RING + self.group_from(g)

    def gain(self, layer, kind):
        blocks = [self.ref.gains[layer * RING + g, kind : kind + 1, :] for g in range(RING)]
        return jnp.concatenate(blocks, axis=-1)

    def row_of(self, offset, c=0):
        return pl.multiple_of(ring_group(self.place + offset) * CAP + c * (CAP // 2), CAP // 2)

    def columns(self, width, own=True):
        half = width // 2
        core = self.core if own else 1 - self.core
        return pl.ds(pl.multiple_of(core * half, half), half)

    def gather_work_sum(
        self, work, early=(), gathered=None, summed=None, ready=None, given=None, into=None
    ):
        ref = self.ref
        whole, part, mate, total = ref.whole, ref.part, ref.mate, ref.total
        sum_recv, sum_sem = into or (ref.sum_recv, ref.sum_sem)
        width, half_r = whole.shape[1], CAP // 2
        own_cols, other_cols = self.columns(width), self.columns(width, False)
        ways = ((0, self.right), (1, self.left))
        gather = None
        if given is None:
            gather = Gather(self, whole, ref.gather_sem, ref.pass_sem, self.start)

        mate_in = {}

        def work_on(offset):
            q = offset % RING
            if q in mate_in:
                return
            if gather is not None:
                gather.slot_passed(offset)
            here = pl.ds(self.row_of(offset), CAP)
            part[here, :] = work(self.row_of(offset)).astype(jnp.bfloat16)
            mate_in[q] = self.start(
                copy_to(
                    self.sibling,
                    part.at[here, other_cols],
                    mate.at[q],
                    ref.mate_sem.at[0, q],
                    ref.mate_sem.at[1, q],
                )
            )

        if gather is not None:
            gather.begin()
            if 0 in early:
                work_on(0)
            for i in range(7):
                gather.step(i)
                if gathered is not None:
                    gathered(i)
                for offset in ((), (-1,), (1,), (-2,), (2,), (), ())[i]:
                    if offset in early:
                        work_on(offset)
        else:
            given()
        gather_sent, self.sent = self.sent, []
        if ready is not None:
            ready()
        work_on(4)

        seen = set()

        def mine(offset, c):
            q = offset % RING
            if q not in seen:
                mate_in[q].wait_recv()
                seen.add(q)
            return part[pl.ds(self.row_of(q, c), half_r), own_cols].astype(jnp.float32) + mate[
                q, pl.ds(c * half_r, half_r)
            ].astype(jnp.float32)

        stream_sum = ((4, 0), (3, 1), (3, 0), (2, 1), (2, 0), (1, 1), (1, 0))
        ahead = ((3, -3), (2, -2), (), (1, -1), (0,), (), ())
        moves = []
        for i, (q, c) in enumerate(stream_sum):
            if i == 5:
                for copy in gather_sent:
                    copy.wait_send()
            for way, device in ways:
                offset, chunk = (q, c) if way == 0 else (-q, 1 - c)
                value = mine(offset, chunk)
                if i >= 2:
                    moves[2 * (i - 2) + way].wait_recv()
                    value = value + sum_recv[way, i - 2].astype(jnp.float32)
                ref.sum_send[way, i] = value.astype(jnp.bfloat16)
                moves.append(
                    self.start(
                        copy_to(
                            device,
                            ref.sum_send.at[way, i],
                            sum_recv.at[way, i],
                            sum_sem.at[0, way, i],
                            sum_sem.at[1, way, i],
                        )
                    )
                )
            for offset in ahead[i]:
                work_on(offset)
            if i == 0 and gather is not None:
                gather.all_passed()
            if summed is not None:
                summed(i)
        halves = []
        for c in (1, 0):
            value = mine(0, c)
            at = (5, 6) if c == 1 else (6, 5)
            for way in (0, 1):
                moves[2 * at[way] + way].wait_recv()
                value = value + sum_recv[way, at[way]].astype(jnp.float32)
            here = (pl.ds(c * half_r, half_r), own_cols)
            total[here] = value
            halves.append(
                self.start(
                    copy_to(
                        self.sibling,
                        total.at[here],
                        total.at[here],
                        ref.half_sem.at[0, c],
                        ref.half_sem.at[1, c],
                    )
                )
            )
        for copy in halves:
            copy.wait_recv()
        self.drain()


class Gather:
    stream = ((0, 0), (0, 1), (1, 0), (1, 1), (2, 0), (2, 1), (3, 0))

    def __init__(self, ring, whole, gather_sem, pass_sem, start):
        self.ring, self.whole, self.start = ring, whole, start
        self.gather_sem, self.pass_sem = gather_sem, pass_sem
        self.own_cols = ring.columns(whole.shape[1])
        self.other_cols = ring.columns(whole.shape[1], False)
        self.seen = set()

    def landing(self, way, k, c, columns):
        offset, chunk = (-k, c) if way == 0 else (k, 1 - c)
        return self.whole.at[pl.ds(self.ring.row_of(offset, chunk), CAP // 2), columns]

    def move(self, device, where, sems, way, i):
        return copy_to(device, where, where, sems.at[0, way, i], sems.at[1, way, i])

    def forward(self, i, way):
        k, c = self.stream[i]
        where = self.landing(way, k, c, self.own_cols)
        device = (self.ring.right, self.ring.left)[way]
        self.start(self.move(device, where, self.gather_sem, way, i))

    def begin(self):
        for i in (0, 1):
            for way in (0, 1):
                self.forward(i, way)

    def step(self, i):
        k, c = self.stream[i]
        for way in (0, 1):
            where = self.landing(way, k + 1, c, self.own_cols)
            device = (self.ring.right, self.ring.left)[way]
            self.move(device, where, self.gather_sem, way, i).wait_recv()
            self.start(self.move(self.ring.sibling, where, self.pass_sem, way, i))
            if i < 5:
                self.forward(i + 2, way)

    def passed(self, i, way):
        if (i, way) in self.seen:
            return
        self.seen.add((i, way))
        k, c = self.stream[i]
        where = self.landing(way, k + 1, c, self.other_cols)
        self.move(self.ring.sibling, where, self.pass_sem, way, i).wait_recv()

    def slot_passed(self, offset):
        if offset == RING // 2:
            for way in (0, 1):
                self.passed(6, way)
        elif offset != 0:
            way, k = (0, -offset) if offset < 0 else (1, offset)
            for i in (2 * k - 2, 2 * k - 1):
                self.passed(i, way)

    def all_passed(self):
        for i in range(7):
            for way in (0, 1):
                self.passed(i, way)


def by_rows(body, step=16):
    @pl.loop(0, CAP, step=step)
    def _(at):
        body(pl.ds(pl.multiple_of(at, step), step), at)


def inverse_rms(value):
    return lax.rsqrt(jnp.mean(value * value, axis=-1, keepdims=True) + eps_norm)


def norm_rows(ring, source, gain):
    own = ring.row_of(0)

    def body(here, at):
        value = source[here, :].astype(jnp.float32)
        low = (value * inverse_rms(value) * gain).astype(jnp.bfloat16)
        ring.ref.whole[pl.ds(pl.multiple_of(own + at, 16), 16), :] = low

    by_rows(body)


def own_rows(ring, matrix):
    return matrix.at[pl.ds(pl.multiple_of(ring.section * CAP, CAP), CAP)]


def back_rows(ring, base, source, gain, out, gain_grad, also):
    gain_grad[...] = jnp.zeros_like(gain_grad)

    def body(here, at):
        x = source[here, :].astype(jnp.float32)
        inverse = inverse_rms(x)
        scaled = x * inverse
        grad = ring.ref.total[here, :]
        moved = grad * scaled
        gain_grad[...] += moved[:8] + moved[8:]
        inner = grad * gain
        value = base[here, :].astype(jnp.float32) + inverse * (
            inner - scaled * jnp.mean(inner * scaled, axis=-1, keepdims=True)
        )
        out[here, :] = value
        also(here, at, value.astype(jnp.bfloat16))

    by_rows(body)


def lane_low(shape, span):
    return lax.rem(lax.broadcasted_iota(jnp.int32, shape, 1), span) < span // 2


def rot_rows(value, cosines, sines):
    low = lane_low(value.shape, HEAD_DIM)
    partner = jnp.where(
        low, pltpu.roll(value, LANES - HEAD_DIM // 2, 1), pltpu.roll(value, HEAD_DIM // 2, 1)
    )
    return value * cosines + partner * sines


def heads_apart(value):
    low = lane_low(value.shape, LANES)
    return jnp.concatenate([jnp.where(low, value, 0.0), jnp.where(low, 0.0, value)], axis=0)


def heads_together(value):
    rows = value.shape[0] // 2
    return jnp.where(lane_low((rows, LANES), LANES), value[:rows], value[rows:])


def twice(kv):
    low = lane_low(kv.shape, LANES)
    other = pltpu.roll(kv, HEAD_DIM, 1)
    return (
        jnp.where(low, kv, other).astype(jnp.bfloat16),
        jnp.where(low, other, kv).astype(jnp.bfloat16),
    )


def dot_wide(left, right):
    return jnp.dot(left, right, preferred_element_type=jnp.float32)


def side_moves(ring, sources, place, sems, shard):
    def rows_of(section, group, columns=slice(None)):
        at = pl.ds(pl.multiple_of(group * shard, shard), shard)
        return place.at[section, at, columns]

    def send(g):
        copies = []
        for n, (block, columns) in enumerate(sources):
            there = rows_of(ring.section, ring.group, columns)
            if g == 0:
                copies.append(ring.local(block(ring.group), there))
            else:
                copies.append(
                    ring.start_side(
                        copy_to(
                            ring.far_device(0, g),
                            block(lax.rem(ring.group + g, RING)),
                            there,
                            sems.at[0, n, g],
                            sems.at[1, n, g],
                        )
                    )
                )
        return copies

    def pass_on(g):
        group = ring.group_from(g)
        if g > 0:
            for n, (_, columns) in enumerate(sources):
                where = rows_of(ring.section, group, columns)
                copy_to(
                    ring.sibling, where, where, sems.at[0, n, g], sems.at[1, n, g]
                ).wait_recv()
        where = rows_of(ring.section, group)
        ring.start_side(copy_to(ring.across, where, where, sems.at[0, 2, g], sems.at[1, 2, g]))

    def wait_passed(g):
        where = rows_of(1 - ring.section, ring.group_from(g))
        copy_to(ring.across, where, where, sems.at[0, 2, g], sems.at[1, 2, g]).wait_recv()

    return send, pass_on, wait_passed


def unit_blocks(source, span, units, b):
    at = b * units
    base, turn = at // LANES * LANES, at % LANES
    wide = -(-(turn + units) // LANES) * LANES
    value = source[:, base : base + wide].astype(F32)
    if turn:
        value = pltpu.roll(value, wide - turn, 1)
    value = value[:, :span]
    lanes = lax.broadcasted_iota(jnp.int32, value.shape, 1)
    return jnp.where(lanes < units, value, 0.0).astype(LOW)


def first_kernel(names, lazy, *refs):
    ring = Ring(names, lazy, refs)
    layer_forward(ring, True, ring.ref.normed_out, ring.ref.normed_mlp_out)
    ring.finish()


def middle_kernel(units, names, lazy, *refs):
    ring = Ring(names, lazy, refs)
    rest = layer_forward(ring, False, ring.ref.normed_attn, ring.ref.normed)
    layer_backward(ring, False, units, rest)
    ring.finish()


def last_kernel(units, names, lazy, *refs):
    ring = Ring(names, lazy, refs)
    layer_backward(ring, True, units)
    ring.finish()


def layer_forward(ring, moving, keep_attn, keep_mlp):
    ref = ring.ref
    width = ref.whole.shape[1]
    shard = width // RING
    ring.load_all()
    if moving:
        ring.greet_all()
        mine_at = ring.section * RING + ring.group
        ref.gains[mine_at] = ref.own_gain[...]
        for n, (f, g) in enumerate(ring.far):
            ring.start_side(
                copy_to(
                    ring.far_device(f, g),
                    ref.own_gain,
                    ref.gains.at[mine_at],
                    ref.far_sem.at[0, n],
                    ref.far_sem.at[1, n],
                )
            )
        key, value = ref.key[...].astype(F32), ref.value[...].astype(F32)
        low = lane_low(key.shape, LANES)
        ref.kv_blocks[0] = jnp.where(low, key, pltpu.roll(value, HEAD_DIM, 1)).astype(LOW)
        ref.kv_blocks[1] = jnp.where(low, pltpu.roll(key, HEAD_DIM, 1), value).astype(LOW)
        q_width = ref.w_out.shape[1]

        def query_block(group):
            at = pl.multiple_of(group * q_width, q_width)
            return ref.w_query.at[0, :, pl.ds(at, q_width)]

        def kv_block(group):
            return ref.kv_blocks.at[group // (RING // 2)]

        send_attn, pass_attn, attn_passed = side_moves(
            ring,
            ((query_block, slice(0, q_width)), (kv_block, slice(q_width, 2 * q_width))),
            ref.w_attn,
            ref.attn_sem,
            shard,
        )
        send_mlp, pass_mlp, mlp_passed = side_moves(
            ring,
            ((lambda group: ref.mlp_blocks.at[group], slice(None)),),
            ref.w_mlp,
            ref.mlp_sem,
            shard,
        )
        at_home = [send_attn(g) for g in range(RING)][0]
        units = ref.own_down.shape[1]
        span = ref.w_down.shape[1]
        if span > units:
            ref.w_down[:, units:, :] = jnp.zeros((2, span - units, width), LOW)

        def across_big(own, place, n):
            where = place.at[ring.section, pl.ds(0, own.shape[1])]
            at_home.append(ring.local(own.at[0], where))
            ring.start_side(
                copy_to(
                    ring.across, own.at[0], where, ref.big_sem.at[0, n], ref.big_sem.at[1, n]
                )
            )

        def big_passed(own, place, n):
            where = place.at[1 - ring.section, pl.ds(0, own.shape[1])]
            copy_to(
                ring.across, where, where, ref.big_sem.at[0, n], ref.big_sem.at[1, n]
            ).wait_recv()

        across_big(ref.own_out, ref.w_out, 0)
        for n, (f, g) in enumerate(ring.far):
            copy_to(
                ring.sibling,
                ref.own_gain,
                ref.gains.at[ring.far_from(f, g)],
                ref.far_sem.at[0, n],
                ref.far_sem.at[1, n],
            ).wait_recv()

        w_attn, w_out = ref.w_attn.at[0], ref.w_out.at[0]
        w_mlp, w_down = ref.w_mlp.at[0], ref.w_down.at[0]
    else:
        ring.greet_ring()
        w_attn, w_out, w_mlp, w_down = ref.w_attn, ref.w_out, ref.w_mlp, ref.w_down
        target = own_rows(ring, ref.cotangent)[...].astype(F32) * ref.live[...]
        ref.target[...] = target.astype(LOW)
        ref.low[pl.ds(ring.row_of(0), CAP), :] = target.astype(LOW)
        aside = Gather(ring, ref.low, ref.aside_sem, ref.aside_pass_sem, ring.start_side)
        aside.begin()
    x = own_rows(ring, ref.tokens) if moving else ref.x
    layer = 0 if moving else 1
    norm_rows(ring, x, ring.gain(layer, 0))
    heads = w_out.shape[0]
    span = w_down.shape[0]

    def attend(row):
        here = pl.ds(row, CAP)
        both = dot_wide(ref.whole[here, :], w_attn[...])
        queries, kv = both[:, :heads], both[:, heads:]
        cosines, sines = ref.cosines[here, :], ref.sines[here, :]
        queries = rot_rows(queries, cosines, sines)
        kv = jnp.where(lane_low(kv.shape, LANES), rot_rows(kv, cosines, sines), kv)
        ref.queries[here, :] = queries.astype(jnp.bfloat16)
        ref.kv[here, :] = kv.astype(jnp.bfloat16)
        keys, values = twice(kv)
        apart = heads_apart(queries).astype(jnp.bfloat16)
        allowed = ref.mask[here, :] > 0.5
        allowed = jnp.concatenate([allowed, allowed], axis=0)
        scores = jnp.where(allowed, dot_trans(apart, keys) * HEAD_DIM ** (-0.5), -1e30)
        weights = jnp.exp(scores - jnp.max(scores, axis=-1, keepdims=True))
        probs = weights / jnp.sum(weights, axis=-1, keepdims=True)
        ref.probs[pl.ds(pl.multiple_of(2 * row, 2 * CAP), 2 * CAP), :] = probs
        mixed = heads_together(dot_wide(probs.astype(jnp.bfloat16), values)).astype(jnp.bfloat16)
        ref.mixed[here, :] = mixed
        return dot_wide(mixed, w_out[...])

    keeping = []

    def attn_gathered(i):
        if moving:
            if i == 0:
                for copy in at_home[:2]:
                    ring.stored(copy)
                pass_attn(0)
                ring.need("w_gate", "w_up")
            pass_attn(i + 1)
            if i == 4:
                across_big(ref.own_down, ref.w_down, 1)
            for b in (i,) if i < 6 else (6, 7):
                ref.mlp_blocks[b, :, :span] = unit_blocks(ref.w_gate, span, units, b)
                ref.mlp_blocks[b, :, span:] = unit_blocks(ref.w_up, span, units, b)
            if i == 6:
                for g in range(1, RING):
                    send_mlp(g)
                at_home.extend(send_mlp(0))

    def attn_ready():
        ring.need("cosines", "sines", "mask")
        if moving:
            ring.stored(at_home[2])

            @pl.when(ring.section == 1)
            def _():
                for g in range(RING):
                    attn_passed(g)
                big_passed(ref.own_out, ref.w_out, 0)

        else:
            ring.need("w_attn", "w_out")
            aside.step(0)
            aside.step(1)

    def attn_summed(i):
        if moving:
            if i == 0:
                ring.stored(at_home[4])
            for g in (i,):
                pass_mlp(g)

    def keep(there, also=None):
        def summed(i):
            if also is not None:
                also(i)
            if i == 0:
                keeping.append(ring.local(ref.whole, there))
            if i == 4:
                ring.stored(keeping.pop())

        return summed

    ring.gather_work_sum(attend, gathered=attn_gathered, ready=attn_ready, summed=keep(keep_attn, attn_summed))
    if moving:
        ring.store("queries", "kv", "probs", "mixed")
    else:
        aside.step(2)
        aside.step(3)

    own, mlp_gain = ring.row_of(0), ring.gain(layer, 1)

    def add_rows(here, at):
        value = x[here, :].astype(jnp.float32) + ref.total[here, :]
        ref.residual[here, :] = value
        low = (value * inverse_rms(value) * mlp_gain).astype(jnp.bfloat16)
        ref.whole[pl.ds(pl.multiple_of(own + at, 16), 16), :] = low

    by_rows(add_rows)

    def feed(row):
        here = pl.ds(row, CAP)
        both = dot_wide(ref.whole[here, :], w_mlp[...])
        gate, up = both[:, :span], both[:, span:]
        ref.gate[here, :] = gate
        ref.up[here, :] = up
        hidden = (gate * jax.nn.sigmoid(gate) * up).astype(jnp.bfloat16)
        ref.hidden[here, :] = hidden
        return dot_wide(hidden, w_down[...])

    def mlp_gathered(i):
        if moving:
            if i == 0:
                pass_mlp(7)

    def mlp_ready():
        if moving:
            ring.stored(at_home[3])

            @pl.when(ring.section == 1)
            def _():
                for g in range(RING):
                    mlp_passed(g)
                big_passed(ref.own_down, ref.w_down, 1)

        else:
            ring.need("w_mlp", "w_down")
            aside.step(4)

    ring.gather_work_sum(feed, gathered=mlp_gathered, ready=mlp_ready, summed=keep(keep_mlp))
    if moving:
        ring.store("gate", "up", "hidden")
    else:
        aside.step(5)
        aside.step(6)
        aside.all_passed()

    def round_rows(here, at):
        ref.out[here, :] = (ref.residual[here, :] + ref.total[here, :]).astype(jnp.bfloat16)

    if not moving:
        return lambda: by_rows(round_rows)
    by_rows(round_rows)
    if moving:

        @pl.when(ring.section == 0)
        def _():
            for g in range(RING):
                attn_passed(g)
                mlp_passed(g)
            big_passed(ref.own_out, ref.w_out, 0)
            big_passed(ref.own_down, ref.w_down, 1)


def layer_backward(ring, last, units, rest=None):
    ref = ring.ref
    width = ref.whole.shape[1]
    shard = width // RING
    span, heads = ref.w_down.shape[0], ref.w_out.shape[0]
    if last:
        ring.load_all(*FIRST)
        ring.greet_all()
        normed_attn, x, base, low_in = ref.normed, own_rows(ring, ref.tokens), ref.base, ref.whole
        again = pltpu.make_async_copy(ref.normed_attn_, normed_attn, ref.again_sem.at[0])
        ref.whole[pl.ds(ring.row_of(0), CAP), :] = ref.base[...]
        given = into = None
    else:
        normed_attn, x, base, low_in = ref.normed_attn, ref.x, ref.target, ref.low
        given, into = lambda: None, (ref.sum_recv_2, ref.sum_sem_2)

    def block(matrix, g):
        at = lax.rem(ring.group + g, RING) * shard
        return matrix.at[pl.ds(pl.multiple_of(at, shard), shard)]

    order = (1, 2, 3, 4, 5, 6, 7, 0)
    if last:

        def cross(source, place, sems):
            return copy_to(ring.across, source, place, sems.at[0], sems.at[1])

        def cross_mlp(g, source):
            return cross(block(source, g), block(ref.stage_mlp, g), ref.cross_sem.at[0, g])

        def cross_attn(g, source):
            return cross(block(source, g), block(ref.stage_attn, g), ref.cross_sem.at[1, g])

        def cross_big(n, source):
            rows = pl.ds(0, (units, heads)[n])
            place = (ref.stage_down, ref.stage_out)[n].at[rows]
            return cross(source.at[rows], place, ref.big_sem.at[n])

        def deal(g, own, fin, n):
            if g == 0:
                return pltpu.make_async_copy(
                    block(own, 0), fin.at[ring.group], ref.deal_sem.at[n, 0, 0]
                )
            return copy_to(
                ring.far_device(0, g),
                block(own, g),
                fin.at[ring.group],
                ref.deal_sem.at[n, 0, g],
                ref.deal_sem.at[n, 1, g],
            )

        def add_and_deal(g, own, n):
            crossed = (cross_mlp, cross_attn)[n](g, own)
            crossed.wait_recv()
            stage, fin = ((ref.stage_mlp, ref.fin_mlp), (ref.stage_attn, ref.fin_attn))[n]
            rows, other = block(own, g), block(stage, g)
            rows[...] = (rows[...].astype(F32) + other[...].astype(F32)).astype(LOW)
            deal(g, own, fin, n).start()

        def dealt(own, n):
            fin = (ref.fin_mlp, ref.fin_attn)[n]
            for g in range(RING):
                copy = deal(g, own, fin, n)
                if g == 0:
                    copy.wait()
                else:
                    copy.wait_send()
                    where = fin.at[ring.group_from(g)]
                    copy_to(
                        ring.sibling,
                        where,
                        where,
                        ref.deal_sem.at[n, 0, g],
                        ref.deal_sem.at[n, 1, g],
                    ).wait_recv()

        @pl.when(ring.section == 0)
        def _():
            for g in order:
                cross_mlp(g, ref.late_mlp_).start()
            for g in order:
                cross_attn(g, ref.late_attn_).start()
            cross_big(1, ref.late_out).start()
            cross_big(0, ref.late_down).start()
            cross(ref.late_rows, ref.far_rows, ref.big_sem.at[2]).start()
            cross(ref.out_1, ref.far_out, ref.big_sem.at[3]).start()

        @pl.when(ring.section == 1)
        def _():
            cross(ref.out_0, ref.far_out, ref.big_sem.at[3]).start()

    def when(section, body):
        if last:
            pl.when(ring.section == section)(body)

    def layer_0(n, *steps):
        if not steps:
            return

        def body():
            for g in steps:
                add_and_deal(g, (ref.grad_mlp, ref.grad_attn)[n], n)

        when(0, body)

    def feed_back(row):
        here = pl.ds(row, CAP)
        ring.need("w_mlp", "w_down", "gate", "up")
        grad_hidden = dot_trans(low_in[here, :], ref.w_down[...])
        gate, up = ref.gate[here, :], ref.up[here, :]
        sigmoid = jax.nn.sigmoid(gate)
        grad_gate = grad_hidden * up * sigmoid * (1.0 + gate * (1.0 - sigmoid))
        grad_up = grad_hidden * gate * sigmoid
        both = jnp.concatenate([grad_gate, grad_up], axis=1).astype(jnp.bfloat16)
        ref.g_mlp[here, :] = both
        return dot_trans(both, ref.w_mlp[...])

    def weight_rows(g, normed, grads, place):
        at = pl.multiple_of(lax.rem(ring.group + g, RING) * shard, shard)
        piece = normed[:, pl.ds(at, shard)]
        place[pl.ds(at, shard), :] = dot_rows(piece, grads[...]).astype(jnp.bfloat16)

    def mlp_summed(i):
        if i == 0:
            if last:
                ring.load_all()
            else:
                rest()
        ring.need("hidden")
        if last:
            ring.need("normed")
        if last:
            weights, downs = ((), (1, 2, 3), (4, 5, 6), (7, 0), (), (), ()), (3, 4, 4, 5)
        else:
            weights, downs = ((),) * 7, (5, 5, 6, 6)
        for g in weights[i]:
            weight_rows(g, ref.normed, ref.g_mlp, ref.grad_mlp)
            when(1, lambda: cross_mlp(g, ref.grad_mlp).start())
        piece = width // 4
        for j in range(4):
            if downs[j] != i:
                continue
            at = slice(j * piece, (j + 1) * piece)
            ref.grad_down[:, at] = dot_rows(ref.hidden[...], low_in[:, at]).astype(LOW)
        if last:
            if i == 2:
                ring.need("late_mlp", "late_attn")
            layer_0(0, *((), (), (), (), (), (1,), (2,))[i])

    early = (0, 1, -1, 2, -2)
    ring.gather_work_sum(
        feed_back, early=early, summed=mlp_summed, given=given, into=into
    )
    if last:
        again.start()
    else:
        ring.store("grad_down")
    layer = 0 if last else 1
    own = ring.row_of(0)

    def gathered_next(here, at, low):
        ref.whole[pl.ds(pl.multiple_of(own + at, 16), 16), :] = low

    gain = ring.gain(layer, 1)
    back_rows(ring, base, ref.residual, gain, ref.middle, ref.gain_grad_mlp, gathered_next)

    def attend_back(row):
        here = pl.ds(row, CAP)
        ring.need("w_attn", "w_out", "queries", "kv", "probs", "cosines", "sines")
        grad_mixed = dot_trans(ref.whole[here, :], ref.w_out[...])
        grad_apart = heads_apart(grad_mixed).astype(jnp.bfloat16)
        keys, values = twice(ref.kv[here, :].astype(jnp.float32))
        apart = heads_apart(ref.queries[here, :].astype(jnp.float32)).astype(jnp.bfloat16)
        probs = ref.probs[pl.ds(pl.multiple_of(2 * row, 2 * CAP), 2 * CAP), :]
        grad_probs = dot_trans(grad_apart, values)
        grad_values = dot_rows(probs.astype(jnp.bfloat16), grad_apart)
        spread = jnp.sum(grad_probs * probs, axis=-1, keepdims=True)
        grad_scores = (probs * (grad_probs - spread) * HEAD_DIM ** (-0.5)).astype(jnp.bfloat16)
        grad_queries = heads_together(dot_wide(grad_scores, keys))
        grad_keys = dot_rows(grad_scores, apart)
        cosines, sines = ref.cosines[here, :], -ref.sines[here, :]
        grad_queries = rot_rows(grad_queries, cosines, sines)
        grad_keys = rot_rows(grad_keys + pltpu.roll(grad_keys, HEAD_DIM, 1), cosines, sines)
        grad_values = grad_values + pltpu.roll(grad_values, HEAD_DIM, 1)
        grad_kv = jnp.where(lane_low(grad_keys.shape, LANES), grad_keys, grad_values)
        both = jnp.concatenate([grad_queries, grad_kv], axis=1).astype(jnp.bfloat16)
        ref.g_attn[here, :] = both
        return dot_trans(both, ref.w_attn[...])

    def attn_gathered(i):
        layer_0(0, *((3,), (), (), (4,), (), (), (5,))[i])
        if not last:
            ring.need("normed")
            for g in ((1, 2), (3,), (4,), (5,), (6,), (7,), (0,))[i]:
                weight_rows(g, ref.normed, ref.g_mlp, ref.grad_mlp)
            if i == 6:
                ring.store("grad_mlp")

    def attn_summed(i):
        if i == 1 and last:
            again.wait()
        if last:
            weights, out_at = ((), (1, 2, 3, 4), (5, 6, 7, 0), (), (), (), ()), 3
        else:
            weights, out_at = ((), (), (), (), (), (1, 2, 3, 4), (5, 6, 7, 0)), 1
        for g in weights[i]:
            weight_rows(g, normed_attn, ref.g_attn, ref.grad_attn)
            when(1, lambda: cross_attn(g, ref.grad_attn).start())
        if i == out_at:
            ring.need("mixed")
            ref.grad_out[...] = dot_rows(ref.mixed[...], ref.whole[...]).astype(LOW)

            def rest():
                cross_big(1, ref.grad_out).start()
                cross_big(0, ref.grad_down).start()

            when(1, rest)
        layer_0(0, *((), (6,), (), (), (7,), (), (0,))[i])

    ring.gather_work_sum(
        attend_back,
        early=early if last else (),
        gathered=attn_gathered,
        summed=attn_summed,
    )
    def handed_on(here, at, low):
        ref.low_rows[here, :] = low

    back_rows(
        ring,
        ref.middle,
        x,
        ring.gain(layer, 0),
        ref.grad_rows,
        ref.gain_grad_attn,
        handed_on,
    )
    if last:
        end_exchange = last_exchange(ring)
        ring.store("grad_down", "grad_out")

        @pl.when(ring.section == 1)
        def _():
            for g in order:
                add_and_deal(g, ref.late_mlp, 0)
            for g in order:
                add_and_deal(g, ref.late_attn, 1)

        @pl.when(ring.section == 0)
        def _():
            for g in order:
                add_and_deal(g, ref.grad_attn, 1)

        end_exchange()

        @pl.when(ring.section == 1)
        def _():
            dealt(ref.late_mlp, 0)
            dealt(ref.late_attn, 1)
            places = (ref.stage_down.at[pl.ds(0, units)], ref.stage_out, ref.far_rows, ref.far_out)
            for n, place in enumerate(places):
                copy_to(
                    ring.across, place, place, ref.big_sem.at[n, 0], ref.big_sem.at[n, 1]
                ).wait_recv()
            for g in range(RING):
                cross_mlp(g, ref.grad_mlp).wait_send()
                cross_attn(g, ref.grad_attn).wait_send()
            cross_big(0, ref.grad_down).wait_send()
            cross_big(1, ref.grad_out).wait_send()
            cross(ref.out_0, ref.far_out, ref.big_sem.at[3]).wait_send()

        @pl.when(ring.section == 0)
        def _():
            dealt(ref.grad_mlp, 0)
            dealt(ref.grad_attn, 1)
            places = ((0, ref.stage_down.at[pl.ds(0, units)]), (1, ref.stage_out), (3, ref.far_out))
            for n, place in places:
                copy_to(
                    ring.across, place, place, ref.big_sem.at[n, 0], ref.big_sem.at[n, 1]
                ).wait_recv()
            for g in range(RING):
                cross_mlp(g, ref.late_mlp_).wait_send()
                cross_attn(g, ref.late_attn_).wait_send()
            cross_big(0, ref.late_down).wait_send()
            cross_big(1, ref.late_out).wait_send()
            cross(ref.late_rows, ref.far_rows, ref.big_sem.at[2]).wait_send()
            cross(ref.out_1, ref.far_out, ref.big_sem.at[3]).wait_send()

    else:
        ring.store("grad_attn", "grad_out")


def last_exchange(ring):
    ref = ring.ref
    width = ref.whole.shape[1]
    shard, half_r = width // RING, CAP // 2
    own_cols = ring.columns(width)
    halves = []
    for c in (0, 1):
        here = (pl.ds(c * half_r, half_r), own_cols)
        halves.append(
            ring.start(
                copy_to(
                    ring.across,
                    ref.low_rows.at[here],
                    ref.far_low.at[here],
                    ref.half_sem.at[0, 2 + c],
                    ref.half_sem.at[1, 2 + c],
                )
            )
        )
    mine_at = ring.section * RING + ring.group
    grads = ((ref.gain_grad_attn, ref.gain_grad_mlp), (ref.gg1a, ref.gg1m))
    for layer in (0, 1):
        for g in range(RING):
            for kind in (0, 1):
                ref.gains_out[layer * RING + g, kind] = grads[layer][kind][
                    :, g * shard : (g + 1) * shard
                ]
    ref.gains_in[mine_at] = ref.gains_out[mine_at]
    for n, (f, g) in enumerate(ring.far):
        to_s, to_g = ring.far_step(f, g)
        ring.start(
            copy_to(
                ring.far_device(f, g),
                ref.gains_out.at[to_s * RING + to_g],
                ref.gains_in.at[mine_at],
                ref.far_sem.at[0, n],
                ref.far_sem.at[1, n],
            )
        )
    return lambda: last_waits(ring, halves)


def last_waits(ring, halves):
    ref = ring.ref
    width = ref.whole.shape[1]
    half_r = CAP // 2
    own_cols, other_cols = ring.columns(width), ring.columns(width, False)
    for c in (0, 1):
        halves[c].wait_recv()
        where = ref.far_low.at[pl.ds(c * half_r, half_r), own_cols]
        ring.start(
            copy_to(
                ring.sibling, where, where, ref.half_sem.at[0, 4 + c], ref.half_sem.at[1, 4 + c]
            )
        )
    for n, (f, g) in enumerate(ring.far):
        copy_to(
            ring.sibling,
            ref.gains_out.at[0],
            ref.gains_in.at[ring.far_from(f, g)],
            ref.far_sem.at[0, n],
            ref.far_sem.at[1, n],
        ).wait_recv()
    for kind in (0, 1):
        ref.gain_sum[kind : kind + 1, :] = jnp.sum(
            jnp.sum(ref.gains_in[:, kind], axis=0), axis=0, keepdims=True
        )
    for c in (0, 1):
        where = ref.far_low.at[pl.ds(c * half_r, half_r), other_cols]
        copy_to(
            ring.sibling, where, where, ref.half_sem.at[0, 4 + c], ref.half_sem.at[1, 4 + c]
        ).wait_recv()


F32, LOW = jnp.float32, jnp.bfloat16
MLP, ATTN, DOWN, OUT = "grad_mlp", "grad_attn", "grad_down", "grad_out"
MLP_IN, ATTN_IN, ROWS, OUT_0 = "mlp", "attn", "rows_0", "out_0"
WIDE = ("gate", "up", "query", "key", "value")
FIRST = ("w_mlp", "w_down", "gate", "up", "hidden")
SAVED = ("gate", "up", "hidden", "queries", "kv", "probs", "mixed")


def ring_call(
    kernel, collective_id, width, now, later, beside, outs, kept, direct, scratch, sems
):
    rows = CAP
    later = {name: a if isinstance(a, tuple) else (a, None) for name, a in later.items()}
    arrays = dict(
        whole=((RING * rows, width), LOW),
        part=((RING * rows, width), LOW),
        mate=((RING, rows, width // 2), LOW),
        sum_send=((2, 7, rows // 2, width // 2), LOW),
        sum_recv=((2, 7, rows // 2, width // 2), LOW),
        total=((rows, width), F32),
        **kept,
        **scratch,
    )
    sems = dict(
        gather_sem=(2, 2, 7),
        pass_sem=(2, 2, 7),
        mate_sem=(2, RING),
        sum_sem=(2, 2, 7),
        half_sem=(2, 6),
        load_sem=(len(later),),
        store_sem=(16,),
        **sems,
    )
    vmem, anywhere = pl.BlockSpec(memory_space=pltpu.VMEM), pl.BlockSpec(memory_space=pl.ANY)
    names = list(now) + [name + "_" for name in later] + list(beside) + list(outs)
    names += [name + "_out" for name in kept] + list(direct) + list(later)
    names += list(arrays) + list(sems)
    results = pl.pallas_call(
        functools.partial(kernel, names, [(name, at) for name, (_, at) in later.items()]),
        out_shape=tuple(
            jax.ShapeDtypeStruct(*a) for a in (*outs.values(), *kept.values(), *direct.values())
        ),
        in_specs=[vmem] * len(now) + [anywhere] * (len(later) + len(beside)),
        out_specs=tuple([vmem] * len(outs) + [anywhere] * (len(kept) + len(direct))),
        scratch_shapes=[
            pltpu.VMEM(a.shape if at is None else a.shape[1:], a.dtype) for a, at in later.values()
        ]
        + [pltpu.VMEM(*a) for a in arrays.values()]
        + [pltpu.SemaphoreType.DMA(a) for a in sems.values()],
        compiler_params=pltpu.CompilerParams(
            collective_id=collective_id, has_side_effects=True, vmem_limit_bytes=VMEM_BYTES
        ),
        cost_estimate=pl.CostEstimate(
            flops=80 * 10**9, bytes_accessed=360 * 10**6, transcendentals=0
        ),
    )(*now.values(), *[a for a, _ in later.values()], *beside.values())
    return types.SimpleNamespace(**dict(zip([*outs, *kept, *direct], results)))


def lay_out_kernel(units, names, *refs):
    ref = types.SimpleNamespace(**dict(zip(names, refs)))
    first = lax.axis_index("section") == 0
    rows, span = ref.mlp.shape[1], ref.mlp.shape[2] // 2
    for start, place in ((0, ref.gate), (span, ref.up)):
        place[...] = jnp.zeros_like(place)
        for b in range(RING):
            at = b * units
            base, turn = at // LANES * LANES, at % LANES
            wide = -(-(turn + units) // LANES) * LANES
            block = ref.mlp[b, :, start : start + span].astype(F32)
            if wide > span:
                block = jnp.concatenate([block, jnp.zeros((rows, wide - span), F32)], axis=1)
            if turn:
                block = pltpu.roll(block, turn, 1)
            place[0, :, base : base + wide] += block[:, :wide]
    q_width = ref.attn.shape[2] // 2
    for b in range(RING):
        ref.query[0, :, b * q_width : (b + 1) * q_width] = ref.attn[b, :, :q_width].astype(F32)
    sums = []
    for head in (0, 1):
        blocks = range(head * RING // 2, (head + 1) * RING // 2)
        sums.append(sum(ref.attn[b, :, q_width:].astype(F32) for b in blocks))
    low = lane_low(sums[0].shape, LANES)
    ref.key[0] = jnp.where(low, sums[0], pltpu.roll(sums[1], HEAD_DIM, 1))
    ref.value[0] = jnp.where(low, pltpu.roll(sums[0], HEAD_DIM, 1), sums[1])
    down = jnp.where(first, ref.down_0[:units, :].astype(F32), ref.down_1[:units, :].astype(F32))
    ref.down[0] = down + ref.stage_down[:units, :].astype(F32)
    out = jnp.where(first, ref.out_0[...].astype(F32), ref.out_1[...].astype(F32))
    ref.out[0] = out + ref.stage_out[...].astype(F32)
    for place, low_first, low_second, high_first, high_second in (
        (ref.rows, ref.rows_0, ref.far_rows, ref.far_rows, ref.rows_1),
        (ref.grads, ref.grads_0, ref.far_low, ref.far_grads, ref.grads_1),
    ):
        kind = place.dtype
        place[0, :CAP, :] = jnp.where(
            first, low_first[...].astype(kind), high_first[...].astype(kind)
        )
        place[0, CAP:, :] = jnp.where(
            first, low_second[...].astype(kind), high_second[...].astype(kind)
        )


def lay_out(units, mlp, attn, **by_columns):
    _, shard, mlp_width = mlp.shape
    attn_width = attn.shape[2]
    width = by_columns[ROWS].shape[1]
    heads = by_columns[OUT_0].shape[0]
    steps = RING // 2
    step, columns = shard // steps, width // steps
    wide = [RING * units] * 2 + [RING * attn_width // 2] + [attn_width // 2] * 2
    tall = dict(down=(units, F32), out=(heads, F32), rows=(2 * CAP, LOW), grads=(2 * CAP, F32))
    names = [MLP_IN, ATTN_IN, *by_columns, *WIDE, *tall]
    results = pl.pallas_call(
        functools.partial(lay_out_kernel, units, names),
        grid=(steps,),
        in_specs=[
            pl.BlockSpec((RING, step, mlp_width), lambda i: (0, i, 0)),
            pl.BlockSpec((RING, step, attn_width), lambda i: (0, i, 0)),
        ]
        + [pl.BlockSpec((a.shape[0], columns), lambda i: (0, i)) for a in by_columns.values()],
        out_shape=[jax.ShapeDtypeStruct((1, shard, w), F32) for w in wide]
        + [jax.ShapeDtypeStruct((1, rows, width), kind) for rows, kind in tall.values()],
        out_specs=[pl.BlockSpec((1, step, w), lambda i: (0, i, 0)) for w in wide]
        + [pl.BlockSpec((1, rows, columns), lambda i: (0, 0, i)) for rows, _ in tall.values()],
        compiler_params=pltpu.CompilerParams(vmem_limit_bytes=VMEM_BYTES),
    )(mlp, attn, *by_columns.values())
    return types.SimpleNamespace(**dict(zip([*WIDE, *tall], results)))


def ring_device(
    tokens,
    cotangent,
    seq_lengths,
    seq_group,
    seq_micro,
    attn_gain,
    w_query,
    key_matrix,
    value_matrix,
    w_out,
    mlp_gain,
    w_gate,
    w_up,
    w_down,
):
    section_id = lax.axis_index("section")
    group_id = lax.axis_index("dp")
    width = tokens.shape[1]
    rows = CAP
    whole_rows = RING * rows
    shard = w_query.shape[1]
    groups = jnp.arange(RING, dtype=jnp.int32)

    kv_heads = key_matrix.shape[2] // HEAD_DIM
    units = w_down.shape[1]
    span = -(-units // LANES) * LANES
    heads = w_out.shape[1]

    labels, places = jax.vmap(
        lambda g: jax.tree.map(
            lambda a: a[0],
            slot_layout(
                seq_lengths,
                jnp.where(seq_micro == section_id, seq_group, -1),
                seq_micro * 0,
                g,
                1,
                rows,
            ),
        )
    )(groups)
    row_ids = jnp.arange(rows, dtype=jnp.int32)
    mask = (labels[:, :, None] == labels[:, None, :]) & (row_ids[None, :] <= row_ids[:, None])
    half = HEAD_DIM // 2
    lanes = jnp.arange(LANES, dtype=jnp.int32)
    frequency = rope_base ** (-2.0 * (lanes % half).astype(F32) / HEAD_DIM)
    angles = places.astype(jnp.float32).reshape(whole_rows, 1) * frequency
    tables = dict(
        cosines=jnp.cos(angles),
        sines=jnp.sin(angles) * jnp.where(lanes % HEAD_DIM < half, -1.0, 1.0),
    )
    mask = mask.astype(F32).reshape(whole_rows, rows)

    own_live = lax.dynamic_index_in_dim(labels, group_id, 0, keepdims=False) > 0
    own_live = own_live.astype(F32)[:, None]
    own_gains = jnp.concatenate([attn_gain, mlp_gain]).astype(F32)
    own_gains = jnp.pad(own_gains, ((0, 6), (0, 0)))

    row_f32, row_low = ((rows, width), F32), ((rows, width), LOW)
    weights = dict(
        w_attn=((2, width, 2 * heads), LOW),
        w_out=((2, heads, width), LOW),
        w_mlp=((2, width, 2 * span), LOW),
        w_down=((2, span, width), LOW),
    )
    kept = dict(
        queries=((whole_rows, heads), LOW),
        kv=((whole_rows, heads), LOW),
        probs=((2 * whole_rows, rows), F32),
        mixed=((whole_rows, heads), LOW),
        gate=((whole_rows, span), F32),
        up=((whole_rows, span), F32),
        hidden=((whole_rows, span), LOW),
    )
    direct = dict(normed_out=((whole_rows, width), LOW), normed_mlp_out=((whole_rows, width), LOW))
    outs = dict(out=row_low, residual=row_f32)
    layer_0 = ring_call(
        first_kernel,
        1,
        width,
        dict(tokens=tokens, own_gain=own_gains, key=key_matrix[0], value=value_matrix[0]),
        dict(w_gate=(w_gate, 0), w_up=(w_up, 0), **tables, mask=mask),
        dict(w_query=w_query, own_out=w_out, own_down=w_down),
        dict(**outs, **weights, gains=((2 * RING, 8, shard), F32)),
        kept,
        direct,
        dict(
            kv_blocks=((kv_heads, shard, heads), LOW),
            mlp_blocks=((RING, shard, 2 * span), LOW),
        ),
        dict(
            far_sem=(2, 2 * RING - 1),
            attn_sem=(2, 3, RING),
            mlp_sem=(2, 3, RING),
            big_sem=(2, 2),
        ),
    )
    def weights_of(layer):
        return {name: (getattr(layer_0, name), layer) for name in weights}

    pairs = dict(grad_mlp=((width, 2 * span), LOW), grad_attn=((width, 2 * heads), LOW))
    grad_sums = dict(grad_down=((span, width), LOW), grad_out=((heads, width), LOW))
    back_outs = dict(
        grad_rows=row_f32, gain_grad_mlp=((8, width), F32), gain_grad_attn=((8, width), F32)
    )
    back_scratch = dict(
        g_mlp=((whole_rows, 2 * span), LOW), g_attn=((whole_rows, 2 * heads), LOW), middle=row_f32
    )
    whole = ((whole_rows, width), LOW)
    layer_1 = ring_call(
        functools.partial(middle_kernel, units),
        2,
        width,
        dict(x=layer_0.out, gains=layer_0.gains, cotangent=cotangent, live=own_live),
        dict(**weights_of(1), **tables, mask=mask),
        {},
        dict(**outs, **back_outs, low_rows=row_low),
        dict(**pairs, **grad_sums),
        {},
        dict(
            **kept,
            **back_scratch,
            target=row_low,
            low=whole,
            normed=whole,
            normed_attn=whole,
            sum_recv_2=((2, 7, rows // 2, width // 2), LOW),
        ),
        dict(aside_sem=(2, 2, 7), aside_pass_sem=(2, 2, 7), sum_sem_2=(2, 2, 7)),
    )
    back_0 = ring_call(
        functools.partial(last_kernel, units),
        3,
        width,
        dict(
            base=layer_1.low_rows,
            tokens=tokens,
            residual=layer_0.residual,
            gains=layer_0.gains,
            gg1a=layer_1.gain_grad_attn,
            gg1m=layer_1.gain_grad_mlp,
        ),
        dict(
            **weights_of(0),
            **tables,
            **{name: getattr(layer_0, name) for name in SAVED},
            normed=layer_0.normed_mlp_out,
            late_mlp=layer_1.grad_mlp,
            late_attn=layer_1.grad_attn,
        ),
        dict(
            normed_attn_=layer_0.normed_out,
            late_down=layer_1.grad_down,
            late_out=layer_1.grad_out,
            late_rows=layer_1.grad_rows,
            out_0=layer_0.out,
            out_1=layer_1.out,
        ),
        dict(**back_outs, far_low=row_low, gain_sum=((2, shard), F32)),
        grad_sums,
        dict(
            fin_mlp=((RING, shard, 2 * span), LOW),
            fin_attn=((RING, shard, 2 * heads), LOW),
            stage_down=grad_sums[DOWN],
            stage_out=grad_sums[OUT],
            far_rows=row_f32,
            far_out=row_low,
        ),
        dict(
            **back_scratch,
            **pairs,
            low_rows=row_low,
            gains_out=((2 * RING, 2, 8, shard), F32),
            gains_in=((2 * RING, 2, 8, shard), F32),
            stage_mlp=pairs[MLP],
            stage_attn=pairs[ATTN],
        ),
        dict(
            far_sem=(2, 2 * RING - 1),
            cross_sem=(2, RING, 2),
            big_sem=(4, 2),
            deal_sem=(2, 2, RING),
            again_sem=(1,),
        ),
    )
    final = lay_out(
        units,
        back_0.fin_mlp,
        back_0.fin_attn,
        down_0=back_0.grad_down,
        down_1=layer_1.grad_down,
        stage_down=back_0.stage_down,
        out_0=back_0.grad_out,
        out_1=layer_1.grad_out,
        stage_out=back_0.stage_out,
        rows_0=layer_0.out,
        rows_1=layer_1.out,
        far_rows=back_0.far_out,
        grads_0=back_0.grad_rows,
        grads_1=layer_1.grad_rows,
        far_low=back_0.far_low,
        far_grads=back_0.far_rows,
    )
    return (
        final.rows,
        final.grads,
        back_0.gain_sum[:1],
        final.query,
        final.key,
        final.value,
        final.out,
        back_0.gain_sum[1:],
        final.gate,
        final.up,
        final.down,
    )


def solution(mesh):
    in_specs = (
        P("dp", None),
        P("dp", None),
        P(),
        P(),
        P(),
        P("section", "dp"),
        P("section", "dp", "tensor"),
        P("section", "dp", "tensor"),
        P("section", "dp", "tensor"),
        P("section", ("tensor", "dp"), None),
        P("section", "dp"),
        P("section", "dp", "tensor"),
        P("section", "dp", "tensor"),
        P("section", ("tensor", "dp"), None),
    )
    out_specs = (
        P("section", "dp", None),
        P("section", "dp", None),
        P("section", "dp"),
        P("section", "dp", "tensor"),
        P("section", "dp", "tensor"),
        P("section", "dp", "tensor"),
        P("section", ("tensor", "dp"), None),
        P("section", "dp"),
        P("section", "dp", "tensor"),
        P("section", "dp", "tensor"),
        P("section", ("tensor", "dp"), None),
    )
    per_device = ring_device if ring_fits(mesh) else general_device
    return jax.shard_map(
        per_device, mesh=mesh, in_specs=in_specs, out_specs=out_specs, check_vma=False
    )
```

```python
import functools
import types

import jax
import jax.numpy as jnp
from jax import lax
from jax.experimental import pallas as pl
from jax.experimental.pallas import tpu as pltpu
from jax.sharding import PartitionSpec as P

HEAD_DIM = 64
CAP = 128
MICRO = 2


eps_norm = 1e-05
rope_base = 10000.0


def passed_along(shard, axis, by):
    count = lax.axis_size(axis)
    pairs = [(i, i + by) for i in range(count) if 0 <= i + by < count]
    return lax.ppermute(shard, axis, pairs)


def slot_layout(seq_lengths, seq_group, seq_micro, group_id, micro_total, slot_rows):
    row_ids = jnp.arange(slot_rows, dtype=jnp.int32)
    numbers = jnp.arange(seq_lengths.shape[0], dtype=jnp.int32) + 1
    label_list = []
    place_list = []
    for micro_id in range(micro_total):
        inside = ((seq_group == group_id) & (seq_micro == micro_id)).astype(jnp.int32)
        taken_len = seq_lengths * inside
        starts = jnp.cumsum(taken_len) - taken_len
        member = (
            (row_ids[:, None] >= starts[None, :])
            & (row_ids[:, None] < (starts + taken_len)[None, :])
        ).astype(jnp.int32)
        label_list.append(jnp.sum(member * numbers[None, :], axis=1))
        place_list.append(jnp.sum(member * (row_ids[:, None] - starts[None, :]), axis=1))
    return (jnp.stack(label_list), jnp.stack(place_list))


def apply_rotary(value_rows, token_positions, direction):
    half_size = value_rows.shape[-1] // 2
    frequency = rope_base ** (
        -2.0 * jnp.arange(half_size, dtype=jnp.float32) / value_rows.shape[-1]
    )
    angles = token_positions.astype(jnp.float32)[:, None] * frequency[None, :]
    cosines = jnp.cos(angles)[:, None, :]
    sines_part = direction * jnp.sin(angles)[:, None, :]
    first_half = value_rows[..., :half_size]
    second_half = value_rows[..., half_size:]
    return jnp.concatenate(
        [
            first_half * cosines - second_half * sines_part,
            second_half * cosines + first_half * sines_part,
        ],
        axis=-1,
    )


def rms_parts(value_rows):
    inverse = lax.rsqrt(jnp.mean(value_rows * value_rows, axis=-1, keepdims=True) + eps_norm)
    return (value_rows * inverse, inverse)


def dot_trans(left, right):
    return lax.dot_general(
        left, right, (((1,), (1,)), ((), ())), preferred_element_type=jnp.float32
    )


def dot_rows(left, right):
    return lax.dot_general(
        left, right, (((0,), (0,)), ((), ())), preferred_element_type=jnp.float32
    )


def tensor_total(partial_sum):
    return lax.psum(partial_sum, "tensor")


def input_total(partial_sum):
    return lax.psum(partial_sum.astype(jnp.bfloat16), "tensor").astype(jnp.float32)


def mask_of(labels):
    row_ids = jnp.arange(labels.shape[0], dtype=jnp.int32)
    return (labels[:, None] == labels[None, :]) & (row_ids[None, :] <= row_ids[:, None])


def forward_slot(inputs, labels, token_positions, attn_w, mlp_w):
    attn_gain, w_query, key_matrix, value_matrix, w_out = attn_w
    mlp_gain, w_gate, w_up, w_down = mlp_w
    total_row_count = inputs.shape[0]
    head_count = w_query.shape[1] // HEAD_DIM
    kv_count = key_matrix.shape[1] // HEAD_DIM
    query_group_width = head_count // kv_count
    scaled, inverse_attn = rms_parts(inputs)
    normalized_input = (scaled * attn_gain.astype(jnp.float32)).astype(jnp.bfloat16)
    query_rows = jnp.dot(normalized_input, w_query, preferred_element_type=jnp.float32)
    unrotated_keys = jnp.dot(normalized_input, key_matrix, preferred_element_type=jnp.float32)
    value_rows = (
        jnp.dot(normalized_input, value_matrix, preferred_element_type=jnp.float32)
        .astype(jnp.bfloat16)
        .reshape(total_row_count, kv_count, HEAD_DIM)
    )
    query_rows = (
        apply_rotary(
            query_rows.reshape(total_row_count, head_count, HEAD_DIM), token_positions, 1.0
        )
        .astype(jnp.bfloat16)
        .reshape(total_row_count, kv_count, query_group_width, HEAD_DIM)
    )
    rotated_keys = apply_rotary(
        unrotated_keys.reshape(total_row_count, kv_count, HEAD_DIM), token_positions, 1.0
    ).astype(jnp.bfloat16)
    scores = jnp.einsum(
        "qgjd,kgd->gjqk", query_rows, rotated_keys, preferred_element_type=jnp.float32
    ) * HEAD_DIM ** (-0.5)
    scores = jnp.where(mask_of(labels), scores, -1e30)
    top_score = jnp.max(scores, axis=-1, keepdims=True)
    exp_scores = jnp.exp(scores - top_score)
    total_mass = jnp.sum(exp_scores, axis=-1, keepdims=True)
    attn_probs = (exp_scores / total_mass).astype(jnp.bfloat16)
    log_mass = top_score + jnp.log(total_mass)
    mixed_heads = jnp.einsum(
        "gjqk,kgd->qgjd", attn_probs, value_rows, preferred_element_type=jnp.float32
    )
    mixed_heads = mixed_heads.reshape(total_row_count, head_count * HEAD_DIM).astype(jnp.bfloat16)
    residual = inputs + tensor_total(
        jnp.dot(mixed_heads, w_out, preferred_element_type=jnp.float32)
    )
    scaled_mlp, inverse_mlp = rms_parts(residual)
    normed_mlp = (scaled_mlp * mlp_gain.astype(jnp.float32)).astype(jnp.bfloat16)
    gate_proj = jnp.dot(normed_mlp, w_gate, preferred_element_type=jnp.float32)
    up_proj = jnp.dot(normed_mlp, w_up, preferred_element_type=jnp.float32)
    hidden = (jax.nn.silu(gate_proj) * up_proj).astype(jnp.bfloat16)
    result = residual + tensor_total(jnp.dot(hidden, w_down, preferred_element_type=jnp.float32))
    kept_state = (
        inputs,
        inverse_attn,
        normalized_input,
        query_rows,
        rotated_keys,
        value_rows,
        log_mass,
        mixed_heads,
        residual,
        inverse_mlp,
        normed_mlp,
        gate_proj,
        up_proj,
        hidden,
    )
    return (result, kept_state)


def backward_slot(grad_out, kept_state, labels, token_positions, attn_w, mlp_w):
    attn_gain, w_query, key_matrix, value_matrix, w_out = attn_w
    mlp_gain, w_gate, w_up, w_down = mlp_w
    (
        inputs,
        inverse_attn,
        normalized_input,
        query_rows,
        rotated_keys,
        value_rows,
        log_mass,
        mixed_heads,
        residual,
        inverse_mlp,
        normed_mlp,
        gate_proj,
        up_proj,
        hidden,
    ) = kept_state
    total_row_count = inputs.shape[0]
    head_count = w_query.shape[1] // HEAD_DIM
    kv_count = key_matrix.shape[1] // HEAD_DIM
    query_group_width = head_count // kv_count
    down_in = grad_out.astype(jnp.bfloat16)
    grad_hidden = dot_trans(down_in, w_down)
    grad_w_down = dot_rows(hidden, down_in)
    sigmoid_gate = jax.nn.sigmoid(gate_proj)
    grad_gate = (
        grad_hidden * up_proj * sigmoid_gate * (1.0 + gate_proj * (1.0 - sigmoid_gate))
    ).astype(jnp.bfloat16)
    grad_up = (grad_hidden * gate_proj * sigmoid_gate).astype(jnp.bfloat16)
    grad_w_gate = dot_rows(normed_mlp, grad_gate)
    grad_w_up = dot_rows(normed_mlp, grad_up)
    grad_normed_mlp = input_total(dot_trans(grad_gate, w_gate) + dot_trans(grad_up, w_up))
    scaled_mlp = residual * inverse_mlp
    grad_mlp_gain = jnp.sum(grad_normed_mlp * scaled_mlp, axis=0)
    inner_mlp = grad_normed_mlp * mlp_gain.astype(jnp.float32)
    grad_residual = grad_out + inverse_mlp * (
        inner_mlp - scaled_mlp * jnp.mean(inner_mlp * scaled_mlp, axis=-1, keepdims=True)
    )
    out_in = grad_residual.astype(jnp.bfloat16)
    grad_w_out = dot_rows(mixed_heads, out_in)
    grad_mixed = (
        dot_trans(out_in, w_out)
        .astype(jnp.bfloat16)
        .reshape(total_row_count, kv_count, query_group_width, HEAD_DIM)
    )
    scores = jnp.einsum(
        "qgjd,kgd->gjqk", query_rows, rotated_keys, preferred_element_type=jnp.float32
    ) * HEAD_DIM ** (-0.5)
    scores = jnp.where(mask_of(labels), scores, -1e30)
    probs_full = jnp.exp(scores - log_mass)
    attn_probs = probs_full.astype(jnp.bfloat16)
    grad_probs = jnp.einsum(
        "qgjd,kgd->gjqk", grad_mixed, value_rows, preferred_element_type=jnp.float32
    )
    grad_values = jnp.einsum(
        "gjqk,qgjd->kgd", attn_probs, grad_mixed, preferred_element_type=jnp.float32
    )
    spread_term = jnp.sum(grad_probs * probs_full, axis=-1, keepdims=True)
    grad_scores = (probs_full * (grad_probs - spread_term) * HEAD_DIM ** (-0.5)).astype(
        jnp.bfloat16
    )
    grad_queries = jnp.einsum(
        "gjqk,kgd->qgjd", grad_scores, rotated_keys, preferred_element_type=jnp.float32
    )
    grad_keys = jnp.einsum(
        "gjqk,qgjd->kgd", grad_scores, query_rows, preferred_element_type=jnp.float32
    )
    grad_queries = (
        apply_rotary(
            grad_queries.reshape(total_row_count, head_count, HEAD_DIM), token_positions, -1.0
        )
        .reshape(total_row_count, head_count * HEAD_DIM)
        .astype(jnp.bfloat16)
    )
    grad_keys = (
        apply_rotary(grad_keys, token_positions, -1.0)
        .reshape(total_row_count, kv_count * HEAD_DIM)
        .astype(jnp.bfloat16)
    )
    grad_values = grad_values.reshape(total_row_count, kv_count * HEAD_DIM).astype(jnp.bfloat16)
    grad_w_query = dot_rows(normalized_input, grad_queries)
    grad_w_key = dot_rows(normalized_input, grad_keys)
    grad_w_value = dot_rows(normalized_input, grad_values)
    grad_normed = input_total(
        dot_trans(grad_queries, w_query)
        + dot_trans(grad_keys, key_matrix)
        + dot_trans(grad_values, value_matrix)
    )
    scaled = inputs * inverse_attn
    grad_attn_gain = jnp.sum(grad_normed * scaled, axis=0)
    inner_attn = grad_normed * attn_gain.astype(jnp.float32)
    grad_inputs = grad_residual + inverse_attn * (
        inner_attn - scaled * jnp.mean(inner_attn * scaled, axis=-1, keepdims=True)
    )
    attn_grads = (grad_attn_gain, grad_w_query, grad_w_key, grad_w_value, grad_w_out)
    mlp_grads = (grad_mlp_gain, grad_w_gate, grad_w_up, grad_w_down)
    return (grad_inputs, attn_grads, mlp_grads)


def general_device(
    tokens,
    cotangent,
    seq_lengths,
    seq_group,
    seq_micro,
    attn_gain,
    w_query,
    key_matrix,
    value_matrix,
    w_out,
    mlp_gain,
    w_gate,
    w_up,
    w_down,
):
    section_count = lax.axis_size("section")
    section_id = lax.axis_index("section")
    group_id = lax.axis_index("dp")
    slot_rows = CAP
    micro_total = MICRO
    tick_count = micro_total + section_count - 1
    model_width = tokens.shape[1]
    labels, token_positions = slot_layout(
        seq_lengths, seq_group, seq_micro, group_id, micro_total, slot_rows
    )
    live_rows = (labels > 0).astype(jnp.float32)
    attn_w = (
        lax.all_gather(attn_gain[0], "dp", axis=0, tiled=True),
        lax.all_gather(w_query[0], "dp", axis=0, tiled=True),
        lax.all_gather(key_matrix[0], "dp", axis=0, tiled=True),
        lax.all_gather(value_matrix[0], "dp", axis=0, tiled=True),
        lax.all_gather(w_out[0], "dp", axis=0, tiled=True),
    )
    mlp_w = (
        lax.all_gather(mlp_gain[0], "dp", axis=0, tiled=True),
        lax.all_gather(w_gate[0], "dp", axis=0, tiled=True),
        lax.all_gather(w_up[0], "dp", axis=0, tiled=True),
        lax.all_gather(w_down[0], "dp", axis=0, tiled=True),
    )
    is_first = section_id == 0
    received = jnp.zeros((slot_rows, model_width), jnp.bfloat16)
    sent_list = []
    kept_list = []
    for tick_id in range(tick_count):
        micro_id = jnp.clip(tick_id - section_id, 0, micro_total - 1)
        fresh_slot = min(tick_id, micro_total - 1)
        fresh_rows = tokens[fresh_slot * slot_rows : (fresh_slot + 1) * slot_rows]
        section_input = jnp.where(is_first, fresh_rows, received).astype(jnp.float32)
        result, kept_state = forward_slot(
            section_input, labels[micro_id], token_positions[micro_id], attn_w, mlp_w
        )
        handed = result.astype(jnp.bfloat16)
        sent_list.append(handed)
        kept_list.append(kept_state)
        if tick_id + 1 < tick_count:
            received = passed_along(handed, "section", 1)
    sent_all = jnp.stack(sent_list)
    section_out = lax.dynamic_slice_in_dim(sent_all, section_id, micro_total, 0).reshape(
        micro_total * slot_rows, model_width
    )[None]
    kept_all = jax.tree.map(lambda *pieces: jnp.stack(pieces), *kept_list)
    attn_w = (
        lax.all_gather(attn_gain[0], "dp", axis=0, tiled=True),
        lax.all_gather(w_query[0], "dp", axis=0, tiled=True),
        lax.all_gather(key_matrix[0], "dp", axis=0, tiled=True),
        lax.all_gather(value_matrix[0], "dp", axis=0, tiled=True),
        lax.all_gather(w_out[0], "dp", axis=0, tiled=True),
    )
    mlp_w = (
        lax.all_gather(mlp_gain[0], "dp", axis=0, tiled=True),
        lax.all_gather(w_gate[0], "dp", axis=0, tiled=True),
        lax.all_gather(w_up[0], "dp", axis=0, tiled=True),
        lax.all_gather(w_down[0], "dp", axis=0, tiled=True),
    )
    is_last = section_id == section_count - 1
    back_received = jnp.zeros((slot_rows, model_width), jnp.bfloat16)
    grad_list = []
    attn_sum = None
    mlp_sum = None
    for tick_id in range(tick_count):
        micro_raw = tick_id - (section_count - 1 - section_id)
        active = ((micro_raw >= 0) & (micro_raw < micro_total)).astype(jnp.float32)
        micro_id = jnp.clip(micro_raw, 0, micro_total - 1)
        target = lax.dynamic_slice_in_dim(cotangent, micro_id * slot_rows, slot_rows, 0).astype(
            jnp.float32
        )
        grad_out = (
            jnp.where(
                is_last, target * live_rows[micro_id][:, None], back_received.astype(jnp.float32)
            )
            * active
        )
        kept_state = jax.tree.map(lambda stacked: stacked[micro_id + section_id], kept_all)
        grad_inputs, attn_grads, mlp_grads = backward_slot(
            grad_out, kept_state, labels[micro_id], token_positions[micro_id], attn_w, mlp_w
        )
        grad_list.append(grad_inputs)
        gain_a, query_g, key_g, value_g, out_g = attn_grads
        attn_grads = (
            lax.psum_scatter(
                gain_a.astype(jnp.bfloat16), "dp", scatter_dimension=0, tiled=True
            ).astype(jnp.float32),
            lax.psum_scatter(
                query_g.astype(jnp.bfloat16), "dp", scatter_dimension=0, tiled=True
            ).astype(jnp.float32),
            lax.psum_scatter(
                key_g.astype(jnp.bfloat16), "dp", scatter_dimension=0, tiled=True
            ).astype(jnp.float32),
            lax.psum_scatter(
                value_g.astype(jnp.bfloat16), "dp", scatter_dimension=0, tiled=True
            ).astype(jnp.float32),
            lax.psum_scatter(
                out_g.astype(jnp.bfloat16), "dp", scatter_dimension=0, tiled=True
            ).astype(jnp.float32),
        )
        gain_m, gate_g, up_g, down_g = mlp_grads
        mlp_grads = (
            lax.psum_scatter(
                gain_m.astype(jnp.bfloat16), "dp", scatter_dimension=0, tiled=True
            ).astype(jnp.float32),
            lax.psum_scatter(
                gate_g.astype(jnp.bfloat16), "dp", scatter_dimension=0, tiled=True
            ).astype(jnp.float32),
            lax.psum_scatter(
                up_g.astype(jnp.bfloat16), "dp", scatter_dimension=0, tiled=True
            ).astype(jnp.float32),
            lax.psum_scatter(
                down_g.astype(jnp.bfloat16), "dp", scatter_dimension=0, tiled=True
            ).astype(jnp.float32),
        )
        attn_sum = attn_grads if attn_sum is None else jax.tree.map(jnp.add, attn_sum, attn_grads)
        mlp_sum = mlp_grads if mlp_sum is None else jax.tree.map(jnp.add, mlp_sum, mlp_grads)
        if tick_id + 1 < tick_count:
            back_received = passed_along(grad_inputs.astype(jnp.bfloat16), "section", -1)
    grad_all = jnp.stack(grad_list)
    input_grad = lax.dynamic_slice_in_dim(
        grad_all, section_count - 1 - section_id, micro_total, 0
    ).reshape(micro_total * slot_rows, model_width)[None]
    return (
        section_out,
        input_grad,
        attn_sum[0][None],
        attn_sum[1][None],
        attn_sum[2][None],
        attn_sum[3][None],
        attn_sum[4][None],
        mlp_sum[0][None],
        mlp_sum[1][None],
        mlp_sum[2][None],
        mlp_sum[3][None],
    )


RING = 8
LANES = 128
MESH_ID = pl.DeviceIdType.MESH
VMEM_BYTES = 60 * 2**20


def ring_fits(mesh):
    shape = dict(mesh.shape)
    return shape["section"] == 2 and shape["tensor"] == 2 and shape["dp"] == RING and MICRO == 2


def ring_place(group_id):
    z, y = group_id // 2, group_id % 2
    return jnp.where(y == 0, z, RING - 1 - z)


def ring_group(place):
    place = lax.rem(place + 2 * RING, RING)
    return jnp.where(place < RING // 2, 2 * place, 2 * (RING - 1 - place) + 1)


def copy_to(device, src, dst, send_sem, recv_sem):
    return pltpu.make_async_remote_copy(
        src_ref=src,
        dst_ref=dst,
        send_sem=send_sem,
        recv_sem=recv_sem,
        device_id=device,
        device_id_type=MESH_ID,
    )


class Ring:
    def __init__(self, names, lazy, refs):
        self.ref = types.SimpleNamespace(**dict(zip(names, refs)))
        self.lazy = lazy
        self.loads = {}
        self.loaded = set()
        self.stores = []
        self.sent = []
        self.side = []
        self.section = lax.axis_index("section")
        self.core = lax.axis_index("tensor")
        self.group = lax.axis_index("dp")
        self.place = ring_place(self.group)
        self.right = (self.section, self.core, ring_group(self.place + 1))
        self.left = (self.section, self.core, ring_group(self.place - 1))
        self.sibling = (self.section, 1 - self.core, self.group)
        self.across = (1 - self.section, self.core, self.group)
        self.far = [(f, g) for f in (0, 1) for g in range(RING) if (f, g) != (0, 0)]

    def load_all(self, *names):
        for n, (name, at) in enumerate(self.lazy):
            if name in self.loaded or (names and name not in names):
                continue
            self.loaded.add(name)
            source, here = getattr(self.ref, name + "_"), getattr(self.ref, name)
            if at is not None:
                source = source.at[at]
            self.loads[name] = pltpu.make_async_copy(source, here, self.ref.load_sem.at[n])
            self.loads[name].start()

    def need(self, *names):
        for name in names:
            if name in self.loads:
                self.loads.pop(name).wait()

    def local(self, here, there):
        copy = pltpu.make_async_copy(here, there, self.ref.store_sem.at[len(self.stores)])
        copy.start()
        self.stores.append(copy)
        return copy

    def store(self, *names):
        for name in names:
            self.local(getattr(self.ref, name), getattr(self.ref, name + "_out"))

    def start(self, copy):
        copy.start()
        self.sent.append(copy)
        return copy

    def start_side(self, copy):
        copy.start()
        self.side.append(copy)
        return copy

    def drain(self):
        for copy in self.sent:
            copy.wait_send()
        self.sent = []

    def finish(self):
        self.need(*list(self.loads))
        self.drain()
        for copy in self.side:
            copy.wait_send()
        for copy in self.stores:
            if copy is not None:
                copy.wait()

    def stored(self, copy):
        copy.wait()
        self.stores = [None if other is copy else other for other in self.stores]

    def greet(self, devices):
        barrier = pltpu.get_barrier_semaphore()
        for device in devices:
            pl.semaphore_signal(barrier, inc=1, device_id=device, device_id_type=MESH_ID)
        pl.semaphore_wait(barrier, len(devices))

    def greet_ring(self):
        self.greet([self.right, self.left, self.sibling])

    def greet_all(self):
        self.greet([self.sibling] + [self.far_device(f, g) for f, g in self.far])

    def far_step(self, f, g):
        return lax.rem(self.section + f, 2), lax.rem(self.group + g, RING)

    def far_device(self, f, g):
        section, group = self.far_step(f, g)
        return (section, self.core, group)

    def group_from(self, g):
        return lax.rem(self.group + RING - g, RING)

    def far_from(self, f, g):
        return lax.rem(self.section + 2 - f, 2) * RING + self.group_from(g)

    def gain(self, layer, kind):
        blocks = [self.ref.gains[layer * RING + g, kind : kind + 1, :] for g in range(RING)]
        return jnp.concatenate(blocks, axis=-1)

    def row_of(self, offset, c=0):
        return pl.multiple_of(ring_group(self.place + offset) * CAP + c * (CAP // 2), CAP // 2)

    def columns(self, width, own=True):
        half = width // 2
        core = self.core if own else 1 - self.core
        return pl.ds(pl.multiple_of(core * half, half), half)

    def gather_work_sum(
        self, work, early=(), gathered=None, summed=None, ready=None, given=None, into=None
    ):
        ref = self.ref
        whole, part, mate, total = ref.whole, ref.part, ref.mate, ref.total
        sum_recv, sum_sem = into or (ref.sum_recv, ref.sum_sem)
        width, half_r = whole.shape[1], CAP // 2
        own_cols, other_cols = self.columns(width), self.columns(width, False)
        ways = ((0, self.right), (1, self.left))
        gather = None
        if given is None:
            gather = Gather(self, whole, ref.gather_sem, ref.pass_sem, self.start)

        mate_in = {}

        def work_on(offset):
            q = offset % RING
            if q in mate_in:
                return
            if gather is not None:
                gather.slot_passed(offset)
            here = pl.ds(self.row_of(offset), CAP)
            part[here, :] = work(self.row_of(offset)).astype(jnp.bfloat16)
            mate_in[q] = self.start(
                copy_to(
                    self.sibling,
                    part.at[here, other_cols],
                    mate.at[q],
                    ref.mate_sem.at[0, q],
                    ref.mate_sem.at[1, q],
                )
            )

        if gather is not None:
            gather.begin()
            if 0 in early:
                work_on(0)
            for i in range(7):
                gather.step(i)
                if gathered is not None:
                    gathered(i)
                for offset in ((), (-1,), (1,), (-2,), (2,), (), ())[i]:
                    if offset in early:
                        work_on(offset)
        else:
            given()
        gather_sent, self.sent = self.sent, []
        if ready is not None:
            ready()
        work_on(4)

        seen = set()

        def mine(offset, c):
            q = offset % RING
            if q not in seen:
                mate_in[q].wait_recv()
                seen.add(q)
            return part[pl.ds(self.row_of(q, c), half_r), own_cols].astype(jnp.float32) + mate[
                q, pl.ds(c * half_r, half_r)
            ].astype(jnp.float32)

        stream_sum = ((4, 0), (3, 1), (3, 0), (2, 1), (2, 0), (1, 1), (1, 0))
        ahead = ((3, -3), (2, -2), (), (1, -1), (0,), (), ())
        moves = []
        for i, (q, c) in enumerate(stream_sum):
            if i == 5:
                for copy in gather_sent:
                    copy.wait_send()
            for way, device in ways:
                offset, chunk = (q, c) if way == 0 else (-q, 1 - c)
                value = mine(offset, chunk)
                if i >= 2:
                    moves[2 * (i - 2) + way].wait_recv()
                    value = value + sum_recv[way, i - 2].astype(jnp.float32)
                ref.sum_send[way, i] = value.astype(jnp.bfloat16)
                moves.append(
                    self.start(
                        copy_to(
                            device,
                            ref.sum_send.at[way, i],
                            sum_recv.at[way, i],
                            sum_sem.at[0, way, i],
                            sum_sem.at[1, way, i],
                        )
                    )
                )
            for offset in ahead[i]:
                work_on(offset)
            if i == 0 and gather is not None:
                gather.all_passed()
            if summed is not None:
                summed(i)
        halves = []
        for c in (1, 0):
            value = mine(0, c)
            at = (5, 6) if c == 1 else (6, 5)
            for way in (0, 1):
                moves[2 * at[way] + way].wait_recv()
                value = value + sum_recv[way, at[way]].astype(jnp.float32)
            here = (pl.ds(c * half_r, half_r), own_cols)
            total[here] = value
            halves.append(
                self.start(
                    copy_to(
                        self.sibling,
                        total.at[here],
                        total.at[here],
                        ref.half_sem.at[0, c],
                        ref.half_sem.at[1, c],
                    )
                )
            )
        for copy in halves:
            copy.wait_recv()
        self.drain()


class Gather:
    stream = ((0, 0), (0, 1), (1, 0), (1, 1), (2, 0), (2, 1), (3, 0))

    def __init__(self, ring, whole, gather_sem, pass_sem, start):
        self.ring, self.whole, self.start = ring, whole, start
        self.gather_sem, self.pass_sem = gather_sem, pass_sem
        self.own_cols = ring.columns(whole.shape[1])
        self.other_cols = ring.columns(whole.shape[1], False)
        self.seen = set()

    def landing(self, way, k, c, columns):
        offset, chunk = (-k, c) if way == 0 else (k, 1 - c)
        return self.whole.at[pl.ds(self.ring.row_of(offset, chunk), CAP // 2), columns]

    def move(self, device, where, sems, way, i):
        return copy_to(device, where, where, sems.at[0, way, i], sems.at[1, way, i])

    def forward(self, i, way):
        k, c = self.stream[i]
        where = self.landing(way, k, c, self.own_cols)
        device = (self.ring.right, self.ring.left)[way]
        self.start(self.move(device, where, self.gather_sem, way, i))

    def begin(self):
        for i in (0, 1):
            for way in (0, 1):
                self.forward(i, way)

    def step(self, i):
        k, c = self.stream[i]
        for way in (0, 1):
            where = self.landing(way, k + 1, c, self.own_cols)
            device = (self.ring.right, self.ring.left)[way]
            self.move(device, where, self.gather_sem, way, i).wait_recv()
            self.start(self.move(self.ring.sibling, where, self.pass_sem, way, i))
            if i < 5:
                self.forward(i + 2, way)

    def passed(self, i, way):
        if (i, way) in self.seen:
            return
        self.seen.add((i, way))
        k, c = self.stream[i]
        where = self.landing(way, k + 1, c, self.other_cols)
        self.move(self.ring.sibling, where, self.pass_sem, way, i).wait_recv()

    def slot_passed(self, offset):
        if offset == RING // 2:
            for way in (0, 1):
                self.passed(6, way)
        elif offset != 0:
            way, k = (0, -offset) if offset < 0 else (1, offset)
            for i in (2 * k - 2, 2 * k - 1):
                self.passed(i, way)

    def all_passed(self):
        for i in range(7):
            for way in (0, 1):
                self.passed(i, way)


def by_rows(body, step=16):
    @pl.loop(0, CAP, step=step)
    def _(at):
        body(pl.ds(pl.multiple_of(at, step), step), at)


def inverse_rms(value):
    return lax.rsqrt(jnp.mean(value * value, axis=-1, keepdims=True) + eps_norm)


def norm_rows(ring, source, gain):
    own = ring.row_of(0)

    def body(here, at):
        value = source[here, :].astype(jnp.float32)
        low = (value * inverse_rms(value) * gain).astype(jnp.bfloat16)
        ring.ref.whole[pl.ds(pl.multiple_of(own + at, 16), 16), :] = low

    by_rows(body)


def own_rows(ring, matrix):
    return matrix.at[pl.ds(pl.multiple_of(ring.section * CAP, CAP), CAP)]


def back_rows(ring, base, source, gain, out, gain_grad, also):
    gain_grad[...] = jnp.zeros_like(gain_grad)

    def body(here, at):
        x = source[here, :].astype(jnp.float32)
        inverse = inverse_rms(x)
        scaled = x * inverse
        grad = ring.ref.total[here, :]
        moved = grad * scaled
        gain_grad[...] += moved[:8] + moved[8:]
        inner = grad * gain
        value = base[here, :].astype(jnp.float32) + inverse * (
            inner - scaled * jnp.mean(inner * scaled, axis=-1, keepdims=True)
        )
        out[here, :] = value
        also(here, at, value.astype(jnp.bfloat16))

    by_rows(body)


def lane_low(shape, span):
    return lax.rem(lax.broadcasted_iota(jnp.int32, shape, 1), span) < span // 2


def rot_rows(value, cosines, sines):
    low = lane_low(value.shape, HEAD_DIM)
    partner = jnp.where(
        low, pltpu.roll(value, LANES - HEAD_DIM // 2, 1), pltpu.roll(value, HEAD_DIM // 2, 1)
    )
    return value * cosines + partner * sines


def heads_apart(value):
    low = lane_low(value.shape, LANES)
    return jnp.concatenate([jnp.where(low, value, 0.0), jnp.where(low, 0.0, value)], axis=0)


def heads_together(value):
    rows = value.shape[0] // 2
    return jnp.where(lane_low((rows, LANES), LANES), value[:rows], value[rows:])


def twice(kv):
    low = lane_low(kv.shape, LANES)
    other = pltpu.roll(kv, HEAD_DIM, 1)
    return (
        jnp.where(low, kv, other).astype(jnp.bfloat16),
        jnp.where(low, other, kv).astype(jnp.bfloat16),
    )


def dot_wide(left, right):
    return jnp.dot(left, right, preferred_element_type=jnp.float32)


def side_moves(ring, sources, place, sems, shard):
    def rows_of(section, group, columns=slice(None)):
        at = pl.ds(pl.multiple_of(group * shard, shard), shard)
        return place.at[section, at, columns]

    def send(g):
        copies = []
        for n, (block, columns) in enumerate(sources):
            there = rows_of(ring.section, ring.group, columns)
            if g == 0:
                copies.append(ring.local(block(ring.group), there))
            else:
                copies.append(
                    ring.start_side(
                        copy_to(
                            ring.far_device(0, g),
                            block(lax.rem(ring.group + g, RING)),
                            there,
                            sems.at[0, n, g],
                            sems.at[1, n, g],
                        )
                    )
                )
        return copies

    def pass_on(g):
        group = ring.group_from(g)
        if g > 0:
            for n, (_, columns) in enumerate(sources):
                where = rows_of(ring.section, group, columns)
                copy_to(
                    ring.sibling, where, where, sems.at[0, n, g], sems.at[1, n, g]
                ).wait_recv()
        where = rows_of(ring.section, group)
        ring.start_side(copy_to(ring.across, where, where, sems.at[0, 2, g], sems.at[1, 2, g]))

    def wait_passed(g):
        where = rows_of(1 - ring.section, ring.group_from(g))
        copy_to(ring.across, where, where, sems.at[0, 2, g], sems.at[1, 2, g]).wait_recv()

    return send, pass_on, wait_passed


def unit_blocks(source, span, units, b):
    at = b * units
    base, turn = at // LANES * LANES, at % LANES
    wide = -(-(turn + units) // LANES) * LANES
    value = source[:, base : base + wide].astype(F32)
    if turn:
        value = pltpu.roll(value, wide - turn, 1)
    value = value[:, :span]
    lanes = lax.broadcasted_iota(jnp.int32, value.shape, 1)
    return jnp.where(lanes < units, value, 0.0).astype(LOW)


def first_kernel(names, lazy, *refs):
    ring = Ring(names, lazy, refs)
    layer_forward(ring, True, ring.ref.normed_out, ring.ref.normed_mlp_out)
    ring.finish()


def middle_kernel(units, names, lazy, *refs):
    ring = Ring(names, lazy, refs)
    rest = layer_forward(ring, False, ring.ref.normed_attn, ring.ref.normed)
    layer_backward(ring, False, units, rest)
    ring.finish()


def last_kernel(units, names, lazy, *refs):
    ring = Ring(names, lazy, refs)
    layer_backward(ring, True, units)
    ring.finish()


def layer_forward(ring, moving, keep_attn, keep_mlp):
    ref = ring.ref
    width = ref.whole.shape[1]
    shard = width // RING
    ring.load_all()
    if moving:
        ring.greet_all()
        mine_at = ring.section * RING + ring.group
        ref.gains[mine_at] = ref.own_gain[...]
        for n, (f, g) in enumerate(ring.far):
            ring.start_side(
                copy_to(
                    ring.far_device(f, g),
                    ref.own_gain,
                    ref.gains.at[mine_at],
                    ref.far_sem.at[0, n],
                    ref.far_sem.at[1, n],
                )
            )
        key, value = ref.key[...].astype(F32), ref.value[...].astype(F32)
        low = lane_low(key.shape, LANES)
        ref.kv_blocks[0] = jnp.where(low, key, pltpu.roll(value, HEAD_DIM, 1)).astype(LOW)
        ref.kv_blocks[1] = jnp.where(low, pltpu.roll(key, HEAD_DIM, 1), value).astype(LOW)
        q_width = ref.w_out.shape[1]

        def query_block(group):
            at = pl.multiple_of(group * q_width, q_width)
            return ref.w_query.at[0, :, pl.ds(at, q_width)]

        def kv_block(group):
            return ref.kv_blocks.at[group // (RING // 2)]

        send_attn, pass_attn, attn_passed = side_moves(
            ring,
            ((query_block, slice(0, q_width)), (kv_block, slice(q_width, 2 * q_width))),
            ref.w_attn,
            ref.attn_sem,
            shard,
        )
        send_mlp, pass_mlp, mlp_passed = side_moves(
            ring,
            ((lambda group: ref.mlp_blocks.at[group], slice(None)),),
            ref.w_mlp,
            ref.mlp_sem,
            shard,
        )
        at_home = [send_attn(g) for g in range(RING)][0]
        units = ref.own_down.shape[1]
        span = ref.w_down.shape[1]
        if span > units:
            ref.w_down[:, units:, :] = jnp.zeros((2, span - units, width), LOW)

        def across_big(own, place, n):
            where = place.at[ring.section, pl.ds(0, own.shape[1])]
            at_home.append(ring.local(own.at[0], where))
            ring.start_side(
                copy_to(
                    ring.across, own.at[0], where, ref.big_sem.at[0, n], ref.big_sem.at[1, n]
                )
            )

        def big_passed(own, place, n):
            where = place.at[1 - ring.section, pl.ds(0, own.shape[1])]
            copy_to(
                ring.across, where, where, ref.big_sem.at[0, n], ref.big_sem.at[1, n]
            ).wait_recv()

        across_big(ref.own_out, ref.w_out, 0)
        for n, (f, g) in enumerate(ring.far):
            copy_to(
                ring.sibling,
                ref.own_gain,
                ref.gains.at[ring.far_from(f, g)],
                ref.far_sem.at[0, n],
                ref.far_sem.at[1, n],
            ).wait_recv()

        w_attn, w_out = ref.w_attn.at[0], ref.w_out.at[0]
        w_mlp, w_down = ref.w_mlp.at[0], ref.w_down.at[0]
    else:
        ring.greet_ring()
        w_attn, w_out, w_mlp, w_down = ref.w_attn, ref.w_out, ref.w_mlp, ref.w_down
        target = own_rows(ring, ref.cotangent)[...].astype(F32) * ref.live[...]
        ref.target[...] = target.astype(LOW)
        ref.low[pl.ds(ring.row_of(0), CAP), :] = target.astype(LOW)
        aside = Gather(ring, ref.low, ref.aside_sem, ref.aside_pass_sem, ring.start_side)
        aside.begin()
    x = own_rows(ring, ref.tokens) if moving else ref.x
    layer = 0 if moving else 1
    norm_rows(ring, x, ring.gain(layer, 0))
    heads = w_out.shape[0]
    span = w_down.shape[0]

    def attend(row):
        here = pl.ds(row, CAP)
        both = dot_wide(ref.whole[here, :], w_attn[...])
        queries, kv = both[:, :heads], both[:, heads:]
        cosines, sines = ref.cosines[here, :], ref.sines[here, :]
        queries = rot_rows(queries, cosines, sines)
        kv = jnp.where(lane_low(kv.shape, LANES), rot_rows(kv, cosines, sines), kv)
        ref.queries[here, :] = queries.astype(jnp.bfloat16)
        ref.kv[here, :] = kv.astype(jnp.bfloat16)
        keys, values = twice(kv)
        apart = heads_apart(queries).astype(jnp.bfloat16)
        allowed = ref.mask[here, :] > 0.5
        allowed = jnp.concatenate([allowed, allowed], axis=0)
        scores = jnp.where(allowed, dot_trans(apart, keys) * HEAD_DIM ** (-0.5), -1e30)
        weights = jnp.exp(scores - jnp.max(scores, axis=-1, keepdims=True))
        probs = weights / jnp.sum(weights, axis=-1, keepdims=True)
        ref.probs[pl.ds(pl.multiple_of(2 * row, 2 * CAP), 2 * CAP), :] = probs
        mixed = heads_together(dot_wide(probs.astype(jnp.bfloat16), values)).astype(jnp.bfloat16)
        ref.mixed[here, :] = mixed
        return dot_wide(mixed, w_out[...])

    keeping = []

    def attn_gathered(i):
        if moving:
            if i == 0:
                for copy in at_home[:2]:
                    ring.stored(copy)
                pass_attn(0)
                ring.need("w_gate", "w_up")
            pass_attn(i + 1)
            if i == 2:
                across_big(ref.own_down, ref.w_down, 1)
            for b in (i,) if i < 6 else (6, 7):
                ref.mlp_blocks[b, :, :span] = unit_blocks(ref.w_gate, span, units, b)
                ref.mlp_blocks[b, :, span:] = unit_blocks(ref.w_up, span, units, b)
            if i == 6:
                for g in range(1, RING):
                    send_mlp(g)
                at_home.extend(send_mlp(0))
                ring.stored(at_home[4])
                pass_mlp(0)

    def attn_ready():
        ring.need("cosines", "sines", "mask")
        if moving:
            ring.stored(at_home[2])

            @pl.when(ring.section == 1)
            def _():
                for g in range(RING):
                    attn_passed(g)
                big_passed(ref.own_out, ref.w_out, 0)

        else:
            ring.need("w_attn", "w_out")
            aside.step(0)
            aside.step(1)

    def attn_summed(i):
        if moving:
            pass_mlp(i + 1)

    def keep(there, also=None):
        def summed(i):
            if also is not None:
                also(i)
            if i == 0:
                keeping.append(ring.local(ref.whole, there))
            if i == 4:
                ring.stored(keeping.pop())

        return summed

    ring.gather_work_sum(attend, gathered=attn_gathered, ready=attn_ready, summed=keep(keep_attn, attn_summed))
    if moving:
        ring.store("queries", "kv", "probs", "mixed")
    else:
        aside.step(2)
        aside.step(3)

    own, mlp_gain = ring.row_of(0), ring.gain(layer, 1)

    def add_rows(here, at):
        value = x[here, :].astype(jnp.float32) + ref.total[here, :]
        ref.residual[here, :] = value
        low = (value * inverse_rms(value) * mlp_gain).astype(jnp.bfloat16)
        ref.whole[pl.ds(pl.multiple_of(own + at, 16), 16), :] = low

    by_rows(add_rows)

    def feed(row):
        here = pl.ds(row, CAP)
        both = dot_wide(ref.whole[here, :], w_mlp[...])
        gate, up = both[:, :span], both[:, span:]
        ref.gate[here, :] = gate
        ref.up[here, :] = up
        hidden = (gate * jax.nn.sigmoid(gate) * up).astype(jnp.bfloat16)
        ref.hidden[here, :] = hidden
        return dot_wide(hidden, w_down[...])

    def mlp_ready():
        if moving:
            ring.stored(at_home[3])

            @pl.when(ring.section == 1)
            def _():
                for g in range(RING):
                    mlp_passed(g)
                big_passed(ref.own_down, ref.w_down, 1)

        else:
            ring.need("w_mlp", "w_down")
            aside.step(4)

    ring.gather_work_sum(feed, ready=mlp_ready, summed=keep(keep_mlp))
    if moving:
        ring.store("gate", "up", "hidden")
    else:
        aside.step(5)
        aside.step(6)
        aside.all_passed()

    def round_rows(here, at):
        ref.out[here, :] = (ref.residual[here, :] + ref.total[here, :]).astype(jnp.bfloat16)

    if not moving:
        return lambda: by_rows(round_rows)
    by_rows(round_rows)
    if moving:

        @pl.when(ring.section == 0)
        def _():
            for g in range(RING):
                attn_passed(g)
                mlp_passed(g)
            big_passed(ref.own_out, ref.w_out, 0)
            big_passed(ref.own_down, ref.w_down, 1)


def layer_backward(ring, last, units, rest=None):
    ref = ring.ref
    width = ref.whole.shape[1]
    shard = width // RING
    span, heads = ref.w_down.shape[0], ref.w_out.shape[0]
    if last:
        ring.load_all(*FIRST)
        ring.greet_all()
        normed_attn, x, base, low_in = ref.normed, own_rows(ring, ref.tokens), ref.base, ref.whole
        again = pltpu.make_async_copy(ref.normed_attn_, normed_attn, ref.again_sem.at[0])
        ref.whole[pl.ds(ring.row_of(0), CAP), :] = ref.base[...]
        given = into = None
    else:
        normed_attn, x, base, low_in = ref.normed_attn, ref.x, ref.target, ref.low
        given, into = lambda: None, (ref.sum_recv_2, ref.sum_sem_2)

    def block(matrix, g):
        at = lax.rem(ring.group + g, RING) * shard
        return matrix.at[pl.ds(pl.multiple_of(at, shard), shard)]

    order = (1, 2, 3, 4, 5, 6, 7, 0)
    if last:

        def cross(source, place, sems):
            return copy_to(ring.across, source, place, sems.at[0], sems.at[1])

        def cross_mlp(g, source):
            return cross(block(source, g), block(ref.stage_mlp, g), ref.cross_sem.at[0, g])

        def cross_attn(g, source):
            return cross(block(source, g), block(ref.stage_attn, g), ref.cross_sem.at[1, g])

        def cross_big(n, source):
            rows = pl.ds(0, (units, heads)[n])
            place = (ref.stage_down, ref.stage_out)[n].at[rows]
            return cross(source.at[rows], place, ref.big_sem.at[n])

        def deal(g, own, fin, n):
            if g == 0:
                return pltpu.make_async_copy(
                    block(own, 0), fin.at[ring.group], ref.deal_sem.at[n, 0, 0]
                )
            return copy_to(
                ring.far_device(0, g),
                block(own, g),
                fin.at[ring.group],
                ref.deal_sem.at[n, 0, g],
                ref.deal_sem.at[n, 1, g],
            )

        def add_and_deal(g, own, n):
            crossed = (cross_mlp, cross_attn)[n](g, own)
            crossed.wait_recv()
            stage, fin = ((ref.stage_mlp, ref.fin_mlp), (ref.stage_attn, ref.fin_attn))[n]
            rows, other = block(own, g), block(stage, g)
            rows[...] = (rows[...].astype(F32) + other[...].astype(F32)).astype(LOW)
            deal(g, own, fin, n).start()

        def dealt(own, n):
            fin = (ref.fin_mlp, ref.fin_attn)[n]
            for g in range(RING):
                copy = deal(g, own, fin, n)
                if g == 0:
                    copy.wait()
                else:
                    copy.wait_send()
                    where = fin.at[ring.group_from(g)]
                    copy_to(
                        ring.sibling,
                        where,
                        where,
                        ref.deal_sem.at[n, 0, g],
                        ref.deal_sem.at[n, 1, g],
                    ).wait_recv()

        @pl.when(ring.section == 0)
        def _():
            for g in order:
                cross_mlp(g, ref.late_mlp_).start()
            for g in order:
                cross_attn(g, ref.late_attn_).start()
            cross_big(1, ref.late_out).start()
            cross_big(0, ref.late_down).start()
            cross(ref.late_rows, ref.far_rows, ref.big_sem.at[2]).start()
            cross(ref.out_1, ref.far_out, ref.big_sem.at[3]).start()

        @pl.when(ring.section == 1)
        def _():
            cross(ref.out_0, ref.far_out, ref.big_sem.at[3]).start()

    def when(section, body):
        if last:
            pl.when(ring.section == section)(body)

    def layer_0(n, *steps):
        if not steps:
            return

        def body():
            for g in steps:
                add_and_deal(g, (ref.grad_mlp, ref.grad_attn)[n], n)

        when(0, body)

    def feed_back(row):
        here = pl.ds(row, CAP)
        ring.need("w_mlp", "w_down", "gate", "up")
        grad_hidden = dot_trans(low_in[here, :], ref.w_down[...])
        gate, up = ref.gate[here, :], ref.up[here, :]
        sigmoid = jax.nn.sigmoid(gate)
        grad_gate = grad_hidden * up * sigmoid * (1.0 + gate * (1.0 - sigmoid))
        grad_up = grad_hidden * gate * sigmoid
        both = jnp.concatenate([grad_gate, grad_up], axis=1).astype(jnp.bfloat16)
        ref.g_mlp[here, :] = both
        return dot_trans(both, ref.w_mlp[...])

    def weight_rows(g, normed, grads, place):
        at = pl.multiple_of(lax.rem(ring.group + g, RING) * shard, shard)
        piece = normed[:, pl.ds(at, shard)]
        place[pl.ds(at, shard), :] = dot_rows(piece, grads[...]).astype(jnp.bfloat16)

    def mlp_summed(i):
        if i == 0:
            if last:
                ring.load_all()
            else:
                rest()
        ring.need("hidden")
        if last:
            ring.need("normed")
        if last:
            weights, downs = ((), (1, 2, 3), (4, 5, 6), (7, 0), (), (), ()), (3, 4, 4, 5)
        else:
            weights, downs = ((),) * 7, (5, 5, 6, 6)
        for g in weights[i]:
            weight_rows(g, ref.normed, ref.g_mlp, ref.grad_mlp)
            when(1, lambda: cross_mlp(g, ref.grad_mlp).start())
        piece = width // 4
        for j in range(4):
            if downs[j] != i:
                continue
            at = slice(j * piece, (j + 1) * piece)
            ref.grad_down[:, at] = dot_rows(ref.hidden[...], low_in[:, at]).astype(LOW)
        if last:
            if i == 2:
                ring.need("late_mlp", "late_attn")
            layer_0(0, *((), (), (), (), (), (1,), (2,))[i])

    early = (0, 1, -1, 2, -2)
    ring.gather_work_sum(
        feed_back, early=early, summed=mlp_summed, given=given, into=into
    )
    if last:
        again.start()
    else:
        ring.store("grad_down")
    layer = 0 if last else 1
    own = ring.row_of(0)

    def gathered_next(here, at, low):
        ref.whole[pl.ds(pl.multiple_of(own + at, 16), 16), :] = low

    gain = ring.gain(layer, 1)
    back_rows(ring, base, ref.residual, gain, ref.middle, ref.gain_grad_mlp, gathered_next)

    def attend_back(row):
        here = pl.ds(row, CAP)
        ring.need("w_attn", "w_out", "queries", "kv", "probs", "cosines", "sines")
        grad_mixed = dot_trans(ref.whole[here, :], ref.w_out[...])
        grad_apart = heads_apart(grad_mixed).astype(jnp.bfloat16)
        keys, values = twice(ref.kv[here, :].astype(jnp.float32))
        apart = heads_apart(ref.queries[here, :].astype(jnp.float32)).astype(jnp.bfloat16)
        probs = ref.probs[pl.ds(pl.multiple_of(2 * row, 2 * CAP), 2 * CAP), :]
        grad_probs = dot_trans(grad_apart, values)
        grad_values = dot_rows(probs.astype(jnp.bfloat16), grad_apart)
        spread = jnp.sum(grad_probs * probs, axis=-1, keepdims=True)
        grad_scores = (probs * (grad_probs - spread) * HEAD_DIM ** (-0.5)).astype(jnp.bfloat16)
        grad_queries = heads_together(dot_wide(grad_scores, keys))
        grad_keys = dot_rows(grad_scores, apart)
        cosines, sines = ref.cosines[here, :], -ref.sines[here, :]
        grad_queries = rot_rows(grad_queries, cosines, sines)
        grad_keys = rot_rows(grad_keys + pltpu.roll(grad_keys, HEAD_DIM, 1), cosines, sines)
        grad_values = grad_values + pltpu.roll(grad_values, HEAD_DIM, 1)
        grad_kv = jnp.where(lane_low(grad_keys.shape, LANES), grad_keys, grad_values)
        both = jnp.concatenate([grad_queries, grad_kv], axis=1).astype(jnp.bfloat16)
        ref.g_attn[here, :] = both
        return dot_trans(both, ref.w_attn[...])

    def attn_gathered(i):
        layer_0(0, *((3,), (), (), (4,), (), (), (5,))[i])
        if not last:
            ring.need("normed")
            for g in ((1, 2), (3,), (4,), (5,), (6,), (7,), (0,))[i]:
                weight_rows(g, ref.normed, ref.g_mlp, ref.grad_mlp)
            if i == 6:
                ring.store("grad_mlp")

    def attn_summed(i):
        if i == 1 and last:
            again.wait()
        if last:
            weights, out_at = ((), (1, 2, 3, 4), (5, 6, 7, 0), (), (), (), ()), 3
        else:
            weights, out_at = ((), (), (), (), (), (1, 2, 3, 4), (5, 6, 7, 0)), 1
        for g in weights[i]:
            weight_rows(g, normed_attn, ref.g_attn, ref.grad_attn)
            when(1, lambda: cross_attn(g, ref.grad_attn).start())
        if i == out_at:
            ring.need("mixed")
            ref.grad_out[...] = dot_rows(ref.mixed[...], ref.whole[...]).astype(LOW)

            def rest():
                cross_big(1, ref.grad_out).start()
                cross_big(0, ref.grad_down).start()

            when(1, rest)
        layer_0(0, *((), (6,), (), (), (7,), (), (0,))[i])

    ring.gather_work_sum(
        attend_back,
        early=early if last else (),
        gathered=attn_gathered,
        summed=attn_summed,
    )
    def handed_on(here, at, low):
        ref.low_rows[here, :] = low

    back_rows(
        ring,
        ref.middle,
        x,
        ring.gain(layer, 0),
        ref.grad_rows,
        ref.gain_grad_attn,
        handed_on,
    )
    if last:
        end_exchange = last_exchange(ring)
        ring.store("grad_down", "grad_out")

        @pl.when(ring.section == 1)
        def _():
            for g in order:
                add_and_deal(g, ref.late_mlp, 0)
            for g in order:
                add_and_deal(g, ref.late_attn, 1)

        @pl.when(ring.section == 0)
        def _():
            for g in order:
                add_and_deal(g, ref.grad_attn, 1)

        end_exchange()

        @pl.when(ring.section == 1)
        def _():
            dealt(ref.late_mlp, 0)
            dealt(ref.late_attn, 1)
            places = (ref.stage_down.at[pl.ds(0, units)], ref.stage_out, ref.far_rows, ref.far_out)
            for n, place in enumerate(places):
                copy_to(
                    ring.across, place, place, ref.big_sem.at[n, 0], ref.big_sem.at[n, 1]
                ).wait_recv()
            for g in range(RING):
                cross_mlp(g, ref.grad_mlp).wait_send()
                cross_attn(g, ref.grad_attn).wait_send()
            cross_big(0, ref.grad_down).wait_send()
            cross_big(1, ref.grad_out).wait_send()
            cross(ref.out_0, ref.far_out, ref.big_sem.at[3]).wait_send()

        @pl.when(ring.section == 0)
        def _():
            dealt(ref.grad_mlp, 0)
            dealt(ref.grad_attn, 1)
            places = ((0, ref.stage_down.at[pl.ds(0, units)]), (1, ref.stage_out), (3, ref.far_out))
            for n, place in places:
                copy_to(
                    ring.across, place, place, ref.big_sem.at[n, 0], ref.big_sem.at[n, 1]
                ).wait_recv()
            for g in range(RING):
                cross_mlp(g, ref.late_mlp_).wait_send()
                cross_attn(g, ref.late_attn_).wait_send()
            cross_big(0, ref.late_down).wait_send()
            cross_big(1, ref.late_out).wait_send()
            cross(ref.late_rows, ref.far_rows, ref.big_sem.at[2]).wait_send()
            cross(ref.out_1, ref.far_out, ref.big_sem.at[3]).wait_send()

    else:
        ring.store("grad_attn", "grad_out")


def last_exchange(ring):
    ref = ring.ref
    width = ref.whole.shape[1]
    shard, half_r = width // RING, CAP // 2
    own_cols = ring.columns(width)
    halves = []
    for c in (0, 1):
        here = (pl.ds(c * half_r, half_r), own_cols)
        halves.append(
            ring.start(
                copy_to(
                    ring.across,
                    ref.low_rows.at[here],
                    ref.far_low.at[here],
                    ref.half_sem.at[0, 2 + c],
                    ref.half_sem.at[1, 2 + c],
                )
            )
        )
    mine_at = ring.section * RING + ring.group
    grads = ((ref.gain_grad_attn, ref.gain_grad_mlp), (ref.gg1a, ref.gg1m))
    for layer in (0, 1):
        for g in range(RING):
            for kind in (0, 1):
                ref.gains_out[layer * RING + g, kind] = grads[layer][kind][
                    :, g * shard : (g + 1) * shard
                ]
    ref.gains_in[mine_at] = ref.gains_out[mine_at]
    for n, (f, g) in enumerate(ring.far):
        to_s, to_g = ring.far_step(f, g)
        ring.start(
            copy_to(
                ring.far_device(f, g),
                ref.gains_out.at[to_s * RING + to_g],
                ref.gains_in.at[mine_at],
                ref.far_sem.at[0, n],
                ref.far_sem.at[1, n],
            )
        )
    return lambda: last_waits(ring, halves)


def last_waits(ring, halves):
    ref = ring.ref
    width = ref.whole.shape[1]
    half_r = CAP // 2
    own_cols, other_cols = ring.columns(width), ring.columns(width, False)
    for c in (0, 1):
        halves[c].wait_recv()
        where = ref.far_low.at[pl.ds(c * half_r, half_r), own_cols]
        ring.start(
            copy_to(
                ring.sibling, where, where, ref.half_sem.at[0, 4 + c], ref.half_sem.at[1, 4 + c]
            )
        )
    for n, (f, g) in enumerate(ring.far):
        copy_to(
            ring.sibling,
            ref.gains_out.at[0],
            ref.gains_in.at[ring.far_from(f, g)],
            ref.far_sem.at[0, n],
            ref.far_sem.at[1, n],
        ).wait_recv()
    for kind in (0, 1):
        ref.gain_sum[kind : kind + 1, :] = jnp.sum(
            jnp.sum(ref.gains_in[:, kind], axis=0), axis=0, keepdims=True
        )
    for c in (0, 1):
        where = ref.far_low.at[pl.ds(c * half_r, half_r), other_cols]
        copy_to(
            ring.sibling, where, where, ref.half_sem.at[0, 4 + c], ref.half_sem.at[1, 4 + c]
        ).wait_recv()


F32, LOW = jnp.float32, jnp.bfloat16
MLP, ATTN, DOWN, OUT = "grad_mlp", "grad_attn", "grad_down", "grad_out"
MLP_IN, ATTN_IN, ROWS, OUT_0 = "mlp", "attn", "rows_0", "out_0"
WIDE = ("gate", "up", "query", "key", "value")
FIRST = ("w_mlp", "w_down", "gate", "up", "hidden")
SAVED = ("gate", "up", "hidden", "queries", "kv", "probs", "mixed")


def ring_call(
    kernel, collective_id, width, now, later, beside, outs, kept, direct, scratch, sems
):
    rows = CAP
    later = {name: a if isinstance(a, tuple) else (a, None) for name, a in later.items()}
    arrays = dict(
        whole=((RING * rows, width), LOW),
        part=((RING * rows, width), LOW),
        mate=((RING, rows, width // 2), LOW),
        sum_send=((2, 7, rows // 2, width // 2), LOW),
        sum_recv=((2, 7, rows // 2, width // 2), LOW),
        total=((rows, width), F32),
        **kept,
        **scratch,
    )
    sems = dict(
        gather_sem=(2, 2, 7),
        pass_sem=(2, 2, 7),
        mate_sem=(2, RING),
        sum_sem=(2, 2, 7),
        half_sem=(2, 6),
        load_sem=(len(later),),
        store_sem=(16,),
        **sems,
    )
    vmem, anywhere = pl.BlockSpec(memory_space=pltpu.VMEM), pl.BlockSpec(memory_space=pl.ANY)
    names = list(now) + [name + "_" for name in later] + list(beside) + list(outs)
    names += [name + "_out" for name in kept] + list(direct) + list(later)
    names += list(arrays) + list(sems)
    results = pl.pallas_call(
        functools.partial(kernel, names, [(name, at) for name, (_, at) in later.items()]),
        out_shape=tuple(
            jax.ShapeDtypeStruct(*a) for a in (*outs.values(), *kept.values(), *direct.values())
        ),
        in_specs=[vmem] * len(now) + [anywhere] * (len(later) + len(beside)),
        out_specs=tuple([vmem] * len(outs) + [anywhere] * (len(kept) + len(direct))),
        scratch_shapes=[
            pltpu.VMEM(a.shape if at is None else a.shape[1:], a.dtype) for a, at in later.values()
        ]
        + [pltpu.VMEM(*a) for a in arrays.values()]
        + [pltpu.SemaphoreType.DMA(a) for a in sems.values()],
        compiler_params=pltpu.CompilerParams(
            collective_id=collective_id, has_side_effects=True, vmem_limit_bytes=VMEM_BYTES
        ),
        cost_estimate=pl.CostEstimate(
            flops=80 * 10**9, bytes_accessed=360 * 10**6, transcendentals=0
        ),
    )(*now.values(), *[a for a, _ in later.values()], *beside.values())
    return types.SimpleNamespace(**dict(zip([*outs, *kept, *direct], results)))


def lay_out_kernel(units, names, *refs):
    ref = types.SimpleNamespace(**dict(zip(names, refs)))
    first = lax.axis_index("section") == 0
    rows, span = ref.mlp.shape[1], ref.mlp.shape[2] // 2
    for start, place in ((0, ref.gate), (span, ref.up)):
        place[...] = jnp.zeros_like(place)
        for b in range(RING):
            at = b * units
            base, turn = at // LANES * LANES, at % LANES
            wide = -(-(turn + units) // LANES) * LANES
            block = ref.mlp[b, :, start : start + span].astype(F32)
            if wide > span:
                block = jnp.concatenate([block, jnp.zeros((rows, wide - span), F32)], axis=1)
            if turn:
                block = pltpu.roll(block, turn, 1)
            place[0, :, base : base + wide] += block[:, :wide]
    q_width = ref.attn.shape[2] // 2
    for b in range(RING):
        ref.query[0, :, b * q_width : (b + 1) * q_width] = ref.attn[b, :, :q_width].astype(F32)
    sums = []
    for head in (0, 1):
        blocks = range(head * RING // 2, (head + 1) * RING // 2)
        sums.append(sum(ref.attn[b, :, q_width:].astype(F32) for b in blocks))
    low = lane_low(sums[0].shape, LANES)
    ref.key[0] = jnp.where(low, sums[0], pltpu.roll(sums[1], HEAD_DIM, 1))
    ref.value[0] = jnp.where(low, pltpu.roll(sums[0], HEAD_DIM, 1), sums[1])
    down = jnp.where(first, ref.down_0[:units, :].astype(F32), ref.down_1[:units, :].astype(F32))
    ref.down[0] = down + ref.stage_down[:units, :].astype(F32)
    out = jnp.where(first, ref.out_0[...].astype(F32), ref.out_1[...].astype(F32))
    ref.out[0] = out + ref.stage_out[...].astype(F32)
    for place, low_first, low_second, high_first, high_second in (
        (ref.rows, ref.rows_0, ref.far_rows, ref.far_rows, ref.rows_1),
        (ref.grads, ref.grads_0, ref.far_low, ref.far_grads, ref.grads_1),
    ):
        kind = place.dtype
        place[0, :CAP, :] = jnp.where(
            first, low_first[...].astype(kind), high_first[...].astype(kind)
        )
        place[0, CAP:, :] = jnp.where(
            first, low_second[...].astype(kind), high_second[...].astype(kind)
        )


def lay_out(units, mlp, attn, **by_columns):
    _, shard, mlp_width = mlp.shape
    attn_width = attn.shape[2]
    width = by_columns[ROWS].shape[1]
    heads = by_columns[OUT_0].shape[0]
    steps = RING // 2
    step, columns = shard // steps, width // steps
    wide = [RING * units] * 2 + [RING * attn_width // 2] + [attn_width // 2] * 2
    tall = dict(down=(units, F32), out=(heads, F32), rows=(2 * CAP, LOW), grads=(2 * CAP, F32))
    names = [MLP_IN, ATTN_IN, *by_columns, *WIDE, *tall]
    results = pl.pallas_call(
        functools.partial(lay_out_kernel, units, names),
        grid=(steps,),
        in_specs=[
            pl.BlockSpec((RING, step, mlp_width), lambda i: (0, i, 0)),
            pl.BlockSpec((RING, step, attn_width), lambda i: (0, i, 0)),
        ]
        + [pl.BlockSpec((a.shape[0], columns), lambda i: (0, i)) for a in by_columns.values()],
        out_shape=[jax.ShapeDtypeStruct((1, shard, w), F32) for w in wide]
        + [jax.ShapeDtypeStruct((1, rows, width), kind) for rows, kind in tall.values()],
        out_specs=[pl.BlockSpec((1, step, w), lambda i: (0, i, 0)) for w in wide]
        + [pl.BlockSpec((1, rows, columns), lambda i: (0, 0, i)) for rows, _ in tall.values()],
        compiler_params=pltpu.CompilerParams(vmem_limit_bytes=VMEM_BYTES),
    )(mlp, attn, *by_columns.values())
    return types.SimpleNamespace(**dict(zip([*WIDE, *tall], results)))


def ring_device(
    tokens,
    cotangent,
    seq_lengths,
    seq_group,
    seq_micro,
    attn_gain,
    w_query,
    key_matrix,
    value_matrix,
    w_out,
    mlp_gain,
    w_gate,
    w_up,
    w_down,
):
    section_id = lax.axis_index("section")
    group_id = lax.axis_index("dp")
    width = tokens.shape[1]
    rows = CAP
    whole_rows = RING * rows
    shard = w_query.shape[1]
    groups = jnp.arange(RING, dtype=jnp.int32)

    kv_heads = key_matrix.shape[2] // HEAD_DIM
    units = w_down.shape[1]
    span = -(-units // LANES) * LANES
    heads = w_out.shape[1]

    labels, places = jax.vmap(
        lambda g: jax.tree.map(
            lambda a: a[0],
            slot_layout(
                seq_lengths,
                jnp.where(seq_micro == section_id, seq_group, -1),
                seq_micro * 0,
                g,
                1,
                rows,
            ),
        )
    )(groups)
    row_ids = jnp.arange(rows, dtype=jnp.int32)
    mask = (labels[:, :, None] == labels[:, None, :]) & (row_ids[None, :] <= row_ids[:, None])
    half = HEAD_DIM // 2
    lanes = jnp.arange(LANES, dtype=jnp.int32)
    frequency = rope_base ** (-2.0 * (lanes % half).astype(F32) / HEAD_DIM)
    angles = places.astype(jnp.float32).reshape(whole_rows, 1) * frequency
    tables = dict(
        cosines=jnp.cos(angles),
        sines=jnp.sin(angles) * jnp.where(lanes % HEAD_DIM < half, -1.0, 1.0),
    )
    mask = mask.astype(F32).reshape(whole_rows, rows)

    own_live = lax.dynamic_index_in_dim(labels, group_id, 0, keepdims=False) > 0
    own_live = own_live.astype(F32)[:, None]
    own_gains = jnp.concatenate([attn_gain, mlp_gain]).astype(F32)
    own_gains = jnp.pad(own_gains, ((0, 6), (0, 0)))

    row_f32, row_low = ((rows, width), F32), ((rows, width), LOW)
    weights = dict(
        w_attn=((2, width, 2 * heads), LOW),
        w_out=((2, heads, width), LOW),
        w_mlp=((2, width, 2 * span), LOW),
        w_down=((2, span, width), LOW),
    )
    kept = dict(
        queries=((whole_rows, heads), LOW),
        kv=((whole_rows, heads), LOW),
        probs=((2 * whole_rows, rows), F32),
        mixed=((whole_rows, heads), LOW),
        gate=((whole_rows, span), F32),
        up=((whole_rows, span), F32),
        hidden=((whole_rows, span), LOW),
    )
    direct = dict(normed_out=((whole_rows, width), LOW), normed_mlp_out=((whole_rows, width), LOW))
    outs = dict(out=row_low, residual=row_f32)
    layer_0 = ring_call(
        first_kernel,
        1,
        width,
        dict(tokens=tokens, own_gain=own_gains, key=key_matrix[0], value=value_matrix[0]),
        dict(w_gate=(w_gate, 0), w_up=(w_up, 0), **tables, mask=mask),
        dict(w_query=w_query, own_out=w_out, own_down=w_down),
        dict(**outs, **weights, gains=((2 * RING, 8, shard), F32)),
        kept,
        direct,
        dict(
            kv_blocks=((kv_heads, shard, heads), LOW),
            mlp_blocks=((RING, shard, 2 * span), LOW),
        ),
        dict(
            far_sem=(2, 2 * RING - 1),
            attn_sem=(2, 3, RING),
            mlp_sem=(2, 3, RING),
            big_sem=(2, 2),
        ),
    )
    def weights_of(layer):
        return {name: (getattr(layer_0, name), layer) for name in weights}

    pairs = dict(grad_mlp=((width, 2 * span), LOW), grad_attn=((width, 2 * heads), LOW))
    grad_sums = dict(grad_down=((span, width), LOW), grad_out=((heads, width), LOW))
    back_outs = dict(
        grad_rows=row_f32, gain_grad_mlp=((8, width), F32), gain_grad_attn=((8, width), F32)
    )
    back_scratch = dict(
        g_mlp=((whole_rows, 2 * span), LOW), g_attn=((whole_rows, 2 * heads), LOW), middle=row_f32
    )
    whole = ((whole_rows, width), LOW)
    layer_1 = ring_call(
        functools.partial(middle_kernel, units),
        2,
        width,
        dict(x=layer_0.out, gains=layer_0.gains, cotangent=cotangent, live=own_live),
        dict(**weights_of(1), **tables, mask=mask),
        {},
        dict(**outs, **back_outs, low_rows=row_low),
        dict(**pairs, **grad_sums),
        {},
        dict(
            **kept,
            **back_scratch,
            target=row_low,
            low=whole,
            normed=whole,
            normed_attn=whole,
            sum_recv_2=((2, 7, rows // 2, width // 2), LOW),
        ),
        dict(aside_sem=(2, 2, 7), aside_pass_sem=(2, 2, 7), sum_sem_2=(2, 2, 7)),
    )
    back_0 = ring_call(
        functools.partial(last_kernel, units),
        3,
        width,
        dict(
            base=layer_1.low_rows,
            tokens=tokens,
            residual=layer_0.residual,
            gains=layer_0.gains,
            gg1a=layer_1.gain_grad_attn,
            gg1m=layer_1.gain_grad_mlp,
        ),
        dict(
            **weights_of(0),
            **tables,
            **{name: getattr(layer_0, name) for name in SAVED},
            normed=layer_0.normed_mlp_out,
            late_mlp=layer_1.grad_mlp,
            late_attn=layer_1.grad_attn,
        ),
        dict(
            normed_attn_=layer_0.normed_out,
            late_down=layer_1.grad_down,
            late_out=layer_1.grad_out,
            late_rows=layer_1.grad_rows,
            out_0=layer_0.out,
            out_1=layer_1.out,
        ),
        dict(**back_outs, far_low=row_low, gain_sum=((2, shard), F32)),
        grad_sums,
        dict(
            fin_mlp=((RING, shard, 2 * span), LOW),
            fin_attn=((RING, shard, 2 * heads), LOW),
            stage_down=grad_sums[DOWN],
            stage_out=grad_sums[OUT],
            far_rows=row_f32,
            far_out=row_low,
        ),
        dict(
            **back_scratch,
            **pairs,
            low_rows=row_low,
            gains_out=((2 * RING, 2, 8, shard), F32),
            gains_in=((2 * RING, 2, 8, shard), F32),
            stage_mlp=pairs[MLP],
            stage_attn=pairs[ATTN],
        ),
        dict(
            far_sem=(2, 2 * RING - 1),
            cross_sem=(2, RING, 2),
            big_sem=(4, 2),
            deal_sem=(2, 2, RING),
            again_sem=(1,),
        ),
    )
    final = lay_out(
        units,
        back_0.fin_mlp,
        back_0.fin_attn,
        down_0=back_0.grad_down,
        down_1=layer_1.grad_down,
        stage_down=back_0.stage_down,
        out_0=back_0.grad_out,
        out_1=layer_1.grad_out,
        stage_out=back_0.stage_out,
        rows_0=layer_0.out,
        rows_1=layer_1.out,
        far_rows=back_0.far_out,
        grads_0=back_0.grad_rows,
        grads_1=layer_1.grad_rows,
        far_low=back_0.far_low,
        far_grads=back_0.far_rows,
    )
    return (
        final.rows,
        final.grads,
        back_0.gain_sum[:1],
        final.query,
        final.key,
        final.value,
        final.out,
        back_0.gain_sum[1:],
        final.gate,
        final.up,
        final.down,
    )


def solution(mesh):
    in_specs = (
        P("dp", None),
        P("dp", None),
        P(),
        P(),
        P(),
        P("section", "dp"),
        P("section", "dp", "tensor"),
        P("section", "dp", "tensor"),
        P("section", "dp", "tensor"),
        P("section", ("tensor", "dp"), None),
        P("section", "dp"),
        P("section", "dp", "tensor"),
        P("section", "dp", "tensor"),
        P("section", ("tensor", "dp"), None),
    )
    out_specs = (
        P("section", "dp", None),
        P("section", "dp", None),
        P("section", "dp"),
        P("section", "dp", "tensor"),
        P("section", "dp", "tensor"),
        P("section", "dp", "tensor"),
        P("section", ("tensor", "dp"), None),
        P("section", "dp"),
        P("section", "dp", "tensor"),
        P("section", "dp", "tensor"),
        P("section", ("tensor", "dp"), None),
    )
    per_device = ring_device if ring_fits(mesh) else general_device
    return jax.shard_map(
        per_device, mesh=mesh, in_specs=in_specs, out_specs=out_specs, check_vma=False
    )
```

```python
import functools
import types

import jax
import jax.numpy as jnp
from jax import lax
from jax.experimental import pallas as pl
from jax.experimental.pallas import tpu as pltpu
from jax.sharding import PartitionSpec as P

HEAD_DIM = 64
CAP = 128
MICRO = 2


eps_norm = 1e-05
rope_base = 10000.0


def passed_along(shard, axis, by):
    count = lax.axis_size(axis)
    pairs = [(i, i + by) for i in range(count) if 0 <= i + by < count]
    return lax.ppermute(shard, axis, pairs)


def slot_layout(seq_lengths, seq_group, seq_micro, group_id, micro_total, slot_rows):
    row_ids = jnp.arange(slot_rows, dtype=jnp.int32)
    numbers = jnp.arange(seq_lengths.shape[0], dtype=jnp.int32) + 1
    label_list = []
    place_list = []
    for micro_id in range(micro_total):
        inside = ((seq_group == group_id) & (seq_micro == micro_id)).astype(jnp.int32)
        taken_len = seq_lengths * inside
        starts = jnp.cumsum(taken_len) - taken_len
        member = (
            (row_ids[:, None] >= starts[None, :])
            & (row_ids[:, None] < (starts + taken_len)[None, :])
        ).astype(jnp.int32)
        label_list.append(jnp.sum(member * numbers[None, :], axis=1))
        place_list.append(jnp.sum(member * (row_ids[:, None] - starts[None, :]), axis=1))
    return (jnp.stack(label_list), jnp.stack(place_list))


def apply_rotary(value_rows, token_positions, direction):
    half_size = value_rows.shape[-1] // 2
    frequency = rope_base ** (
        -2.0 * jnp.arange(half_size, dtype=jnp.float32) / value_rows.shape[-1]
    )
    angles = token_positions.astype(jnp.float32)[:, None] * frequency[None, :]
    cosines = jnp.cos(angles)[:, None, :]
    sines_part = direction * jnp.sin(angles)[:, None, :]
    first_half = value_rows[..., :half_size]
    second_half = value_rows[..., half_size:]
    return jnp.concatenate(
        [
            first_half * cosines - second_half * sines_part,
            second_half * cosines + first_half * sines_part,
        ],
        axis=-1,
    )


def rms_parts(value_rows):
    inverse = lax.rsqrt(jnp.mean(value_rows * value_rows, axis=-1, keepdims=True) + eps_norm)
    return (value_rows * inverse, inverse)


def dot_trans(left, right):
    return lax.dot_general(
        left, right, (((1,), (1,)), ((), ())), preferred_element_type=jnp.float32
    )


def dot_rows(left, right):
    return lax.dot_general(
        left, right, (((0,), (0,)), ((), ())), preferred_element_type=jnp.float32
    )


def tensor_total(partial_sum):
    return lax.psum(partial_sum, "tensor")


def input_total(partial_sum):
    return lax.psum(partial_sum.astype(jnp.bfloat16), "tensor").astype(jnp.float32)


def mask_of(labels):
    row_ids = jnp.arange(labels.shape[0], dtype=jnp.int32)
    return (labels[:, None] == labels[None, :]) & (row_ids[None, :] <= row_ids[:, None])


def forward_slot(inputs, labels, token_positions, attn_w, mlp_w):
    attn_gain, w_query, key_matrix, value_matrix, w_out = attn_w
    mlp_gain, w_gate, w_up, w_down = mlp_w
    total_row_count = inputs.shape[0]
    head_count = w_query.shape[1] // HEAD_DIM
    kv_count = key_matrix.shape[1] // HEAD_DIM
    query_group_width = head_count // kv_count
    scaled, inverse_attn = rms_parts(inputs)
    normalized_input = (scaled * attn_gain.astype(jnp.float32)).astype(jnp.bfloat16)
    query_rows = jnp.dot(normalized_input, w_query, preferred_element_type=jnp.float32)
    unrotated_keys = jnp.dot(normalized_input, key_matrix, preferred_element_type=jnp.float32)
    value_rows = (
        jnp.dot(normalized_input, value_matrix, preferred_element_type=jnp.float32)
        .astype(jnp.bfloat16)
        .reshape(total_row_count, kv_count, HEAD_DIM)
    )
    query_rows = (
        apply_rotary(
            query_rows.reshape(total_row_count, head_count, HEAD_DIM), token_positions, 1.0
        )
        .astype(jnp.bfloat16)
        .reshape(total_row_count, kv_count, query_group_width, HEAD_DIM)
    )
    rotated_keys = apply_rotary(
        unrotated_keys.reshape(total_row_count, kv_count, HEAD_DIM), token_positions, 1.0
    ).astype(jnp.bfloat16)
    scores = jnp.einsum(
        "qgjd,kgd->gjqk", query_rows, rotated_keys, preferred_element_type=jnp.float32
    ) * HEAD_DIM ** (-0.5)
    scores = jnp.where(mask_of(labels), scores, -1e30)
    top_score = jnp.max(scores, axis=-1, keepdims=True)
    exp_scores = jnp.exp(scores - top_score)
    total_mass = jnp.sum(exp_scores, axis=-1, keepdims=True)
    attn_probs = (exp_scores / total_mass).astype(jnp.bfloat16)
    log_mass = top_score + jnp.log(total_mass)
    mixed_heads = jnp.einsum(
        "gjqk,kgd->qgjd", attn_probs, value_rows, preferred_element_type=jnp.float32
    )
    mixed_heads = mixed_heads.reshape(total_row_count, head_count * HEAD_DIM).astype(jnp.bfloat16)
    residual = inputs + tensor_total(
        jnp.dot(mixed_heads, w_out, preferred_element_type=jnp.float32)
    )
    scaled_mlp, inverse_mlp = rms_parts(residual)
    normed_mlp = (scaled_mlp * mlp_gain.astype(jnp.float32)).astype(jnp.bfloat16)
    gate_proj = jnp.dot(normed_mlp, w_gate, preferred_element_type=jnp.float32)
    up_proj = jnp.dot(normed_mlp, w_up, preferred_element_type=jnp.float32)
    hidden = (jax.nn.silu(gate_proj) * up_proj).astype(jnp.bfloat16)
    result = residual + tensor_total(jnp.dot(hidden, w_down, preferred_element_type=jnp.float32))
    kept_state = (
        inputs,
        inverse_attn,
        normalized_input,
        query_rows,
        rotated_keys,
        value_rows,
        log_mass,
        mixed_heads,
        residual,
        inverse_mlp,
        normed_mlp,
        gate_proj,
        up_proj,
        hidden,
    )
    return (result, kept_state)


def backward_slot(grad_out, kept_state, labels, token_positions, attn_w, mlp_w):
    attn_gain, w_query, key_matrix, value_matrix, w_out = attn_w
    mlp_gain, w_gate, w_up, w_down = mlp_w
    (
        inputs,
        inverse_attn,
        normalized_input,
        query_rows,
        rotated_keys,
        value_rows,
        log_mass,
        mixed_heads,
        residual,
        inverse_mlp,
        normed_mlp,
        gate_proj,
        up_proj,
        hidden,
    ) = kept_state
    total_row_count = inputs.shape[0]
    head_count = w_query.shape[1] // HEAD_DIM
    kv_count = key_matrix.shape[1] // HEAD_DIM
    query_group_width = head_count // kv_count
    down_in = grad_out.astype(jnp.bfloat16)
    grad_hidden = dot_trans(down_in, w_down)
    grad_w_down = dot_rows(hidden, down_in)
    sigmoid_gate = jax.nn.sigmoid(gate_proj)
    grad_gate = (
        grad_hidden * up_proj * sigmoid_gate * (1.0 + gate_proj * (1.0 - sigmoid_gate))
    ).astype(jnp.bfloat16)
    grad_up = (grad_hidden * gate_proj * sigmoid_gate).astype(jnp.bfloat16)
    grad_w_gate = dot_rows(normed_mlp, grad_gate)
    grad_w_up = dot_rows(normed_mlp, grad_up)
    grad_normed_mlp = input_total(dot_trans(grad_gate, w_gate) + dot_trans(grad_up, w_up))
    scaled_mlp = residual * inverse_mlp
    grad_mlp_gain = jnp.sum(grad_normed_mlp * scaled_mlp, axis=0)
    inner_mlp = grad_normed_mlp * mlp_gain.astype(jnp.float32)
    grad_residual = grad_out + inverse_mlp * (
        inner_mlp - scaled_mlp * jnp.mean(inner_mlp * scaled_mlp, axis=-1, keepdims=True)
    )
    out_in = grad_residual.astype(jnp.bfloat16)
    grad_w_out = dot_rows(mixed_heads, out_in)
    grad_mixed = (
        dot_trans(out_in, w_out)
        .astype(jnp.bfloat16)
        .reshape(total_row_count, kv_count, query_group_width, HEAD_DIM)
    )
    scores = jnp.einsum(
        "qgjd,kgd->gjqk", query_rows, rotated_keys, preferred_element_type=jnp.float32
    ) * HEAD_DIM ** (-0.5)
    scores = jnp.where(mask_of(labels), scores, -1e30)
    probs_full = jnp.exp(scores - log_mass)
    attn_probs = probs_full.astype(jnp.bfloat16)
    grad_probs = jnp.einsum(
        "qgjd,kgd->gjqk", grad_mixed, value_rows, preferred_element_type=jnp.float32
    )
    grad_values = jnp.einsum(
        "gjqk,qgjd->kgd", attn_probs, grad_mixed, preferred_element_type=jnp.float32
    )
    spread_term = jnp.sum(grad_probs * probs_full, axis=-1, keepdims=True)
    grad_scores = (probs_full * (grad_probs - spread_term) * HEAD_DIM ** (-0.5)).astype(
        jnp.bfloat16
    )
    grad_queries = jnp.einsum(
        "gjqk,kgd->qgjd", grad_scores, rotated_keys, preferred_element_type=jnp.float32
    )
    grad_keys = jnp.einsum(
        "gjqk,qgjd->kgd", grad_scores, query_rows, preferred_element_type=jnp.float32
    )
    grad_queries = (
        apply_rotary(
            grad_queries.reshape(total_row_count, head_count, HEAD_DIM), token_positions, -1.0
        )
        .reshape(total_row_count, head_count * HEAD_DIM)
        .astype(jnp.bfloat16)
    )
    grad_keys = (
        apply_rotary(grad_keys, token_positions, -1.0)
        .reshape(total_row_count, kv_count * HEAD_DIM)
        .astype(jnp.bfloat16)
    )
    grad_values = grad_values.reshape(total_row_count, kv_count * HEAD_DIM).astype(jnp.bfloat16)
    grad_w_query = dot_rows(normalized_input, grad_queries)
    grad_w_key = dot_rows(normalized_input, grad_keys)
    grad_w_value = dot_rows(normalized_input, grad_values)
    grad_normed = input_total(
        dot_trans(grad_queries, w_query)
        + dot_trans(grad_keys, key_matrix)
        + dot_trans(grad_values, value_matrix)
    )
    scaled = inputs * inverse_attn
    grad_attn_gain = jnp.sum(grad_normed * scaled, axis=0)
    inner_attn = grad_normed * attn_gain.astype(jnp.float32)
    grad_inputs = grad_residual + inverse_attn * (
        inner_attn - scaled * jnp.mean(inner_attn * scaled, axis=-1, keepdims=True)
    )
    attn_grads = (grad_attn_gain, grad_w_query, grad_w_key, grad_w_value, grad_w_out)
    mlp_grads = (grad_mlp_gain, grad_w_gate, grad_w_up, grad_w_down)
    return (grad_inputs, attn_grads, mlp_grads)


def general_device(
    tokens,
    cotangent,
    seq_lengths,
    seq_group,
    seq_micro,
    attn_gain,
    w_query,
    key_matrix,
    value_matrix,
    w_out,
    mlp_gain,
    w_gate,
    w_up,
    w_down,
):
    section_count = lax.axis_size("section")
    section_id = lax.axis_index("section")
    group_id = lax.axis_index("dp")
    slot_rows = CAP
    micro_total = MICRO
    tick_count = micro_total + section_count - 1
    model_width = tokens.shape[1]
    labels, token_positions = slot_layout(
        seq_lengths, seq_group, seq_micro, group_id, micro_total, slot_rows
    )
    live_rows = (labels > 0).astype(jnp.float32)
    attn_w = (
        lax.all_gather(attn_gain[0], "dp", axis=0, tiled=True),
        lax.all_gather(w_query[0], "dp", axis=0, tiled=True),
        lax.all_gather(key_matrix[0], "dp", axis=0, tiled=True),
        lax.all_gather(value_matrix[0], "dp", axis=0, tiled=True),
        lax.all_gather(w_out[0], "dp", axis=0, tiled=True),
    )
    mlp_w = (
        lax.all_gather(mlp_gain[0], "dp", axis=0, tiled=True),
        lax.all_gather(w_gate[0], "dp", axis=0, tiled=True),
        lax.all_gather(w_up[0], "dp", axis=0, tiled=True),
        lax.all_gather(w_down[0], "dp", axis=0, tiled=True),
    )
    is_first = section_id == 0
    received = jnp.zeros((slot_rows, model_width), jnp.bfloat16)
    sent_list = []
    kept_list = []
    for tick_id in range(tick_count):
        micro_id = jnp.clip(tick_id - section_id, 0, micro_total - 1)
        fresh_slot = min(tick_id, micro_total - 1)
        fresh_rows = tokens[fresh_slot * slot_rows : (fresh_slot + 1) * slot_rows]
        section_input = jnp.where(is_first, fresh_rows, received).astype(jnp.float32)
        result, kept_state = forward_slot(
            section_input, labels[micro_id], token_positions[micro_id], attn_w, mlp_w
        )
        handed = result.astype(jnp.bfloat16)
        sent_list.append(handed)
        kept_list.append(kept_state)
        if tick_id + 1 < tick_count:
            received = passed_along(handed, "section", 1)
    sent_all = jnp.stack(sent_list)
    section_out = lax.dynamic_slice_in_dim(sent_all, section_id, micro_total, 0).reshape(
        micro_total * slot_rows, model_width
    )[None]
    kept_all = jax.tree.map(lambda *pieces: jnp.stack(pieces), *kept_list)
    attn_w = (
        lax.all_gather(attn_gain[0], "dp", axis=0, tiled=True),
        lax.all_gather(w_query[0], "dp", axis=0, tiled=True),
        lax.all_gather(key_matrix[0], "dp", axis=0, tiled=True),
        lax.all_gather(value_matrix[0], "dp", axis=0, tiled=True),
        lax.all_gather(w_out[0], "dp", axis=0, tiled=True),
    )
    mlp_w = (
        lax.all_gather(mlp_gain[0], "dp", axis=0, tiled=True),
        lax.all_gather(w_gate[0], "dp", axis=0, tiled=True),
        lax.all_gather(w_up[0], "dp", axis=0, tiled=True),
        lax.all_gather(w_down[0], "dp", axis=0, tiled=True),
    )
    is_last = section_id == section_count - 1
    back_received = jnp.zeros((slot_rows, model_width), jnp.bfloat16)
    grad_list = []
    attn_sum = None
    mlp_sum = None
    for tick_id in range(tick_count):
        micro_raw = tick_id - (section_count - 1 - section_id)
        active = ((micro_raw >= 0) & (micro_raw < micro_total)).astype(jnp.float32)
        micro_id = jnp.clip(micro_raw, 0, micro_total - 1)
        target = lax.dynamic_slice_in_dim(cotangent, micro_id * slot_rows, slot_rows, 0).astype(
            jnp.float32
        )
        grad_out = (
            jnp.where(
                is_last, target * live_rows[micro_id][:, None], back_received.astype(jnp.float32)
            )
            * active
        )
        kept_state = jax.tree.map(lambda stacked: stacked[micro_id + section_id], kept_all)
        grad_inputs, attn_grads, mlp_grads = backward_slot(
            grad_out, kept_state, labels[micro_id], token_positions[micro_id], attn_w, mlp_w
        )
        grad_list.append(grad_inputs)
        gain_a, query_g, key_g, value_g, out_g = attn_grads
        attn_grads = (
            lax.psum_scatter(
                gain_a.astype(jnp.bfloat16), "dp", scatter_dimension=0, tiled=True
            ).astype(jnp.float32),
            lax.psum_scatter(
                query_g.astype(jnp.bfloat16), "dp", scatter_dimension=0, tiled=True
            ).astype(jnp.float32),
            lax.psum_scatter(
                key_g.astype(jnp.bfloat16), "dp", scatter_dimension=0, tiled=True
            ).astype(jnp.float32),
            lax.psum_scatter(
                value_g.astype(jnp.bfloat16), "dp", scatter_dimension=0, tiled=True
            ).astype(jnp.float32),
            lax.psum_scatter(
                out_g.astype(jnp.bfloat16), "dp", scatter_dimension=0, tiled=True
            ).astype(jnp.float32),
        )
        gain_m, gate_g, up_g, down_g = mlp_grads
        mlp_grads = (
            lax.psum_scatter(
                gain_m.astype(jnp.bfloat16), "dp", scatter_dimension=0, tiled=True
            ).astype(jnp.float32),
            lax.psum_scatter(
                gate_g.astype(jnp.bfloat16), "dp", scatter_dimension=0, tiled=True
            ).astype(jnp.float32),
            lax.psum_scatter(
                up_g.astype(jnp.bfloat16), "dp", scatter_dimension=0, tiled=True
            ).astype(jnp.float32),
            lax.psum_scatter(
                down_g.astype(jnp.bfloat16), "dp", scatter_dimension=0, tiled=True
            ).astype(jnp.float32),
        )
        attn_sum = attn_grads if attn_sum is None else jax.tree.map(jnp.add, attn_sum, attn_grads)
        mlp_sum = mlp_grads if mlp_sum is None else jax.tree.map(jnp.add, mlp_sum, mlp_grads)
        if tick_id + 1 < tick_count:
            back_received = passed_along(grad_inputs.astype(jnp.bfloat16), "section", -1)
    grad_all = jnp.stack(grad_list)
    input_grad = lax.dynamic_slice_in_dim(
        grad_all, section_count - 1 - section_id, micro_total, 0
    ).reshape(micro_total * slot_rows, model_width)[None]
    return (
        section_out,
        input_grad,
        attn_sum[0][None],
        attn_sum[1][None],
        attn_sum[2][None],
        attn_sum[3][None],
        attn_sum[4][None],
        mlp_sum[0][None],
        mlp_sum[1][None],
        mlp_sum[2][None],
        mlp_sum[3][None],
    )


RING = 8
LANES = 128
MESH_ID = pl.DeviceIdType.MESH
VMEM_BYTES = 60 * 2**20


def ring_fits(mesh):
    shape = dict(mesh.shape)
    return shape["section"] == 2 and shape["tensor"] == 2 and shape["dp"] == RING and MICRO == 2


def ring_place(group_id):
    z, y = group_id // 2, group_id % 2
    return jnp.where(y == 0, z, RING - 1 - z)


def ring_group(place):
    place = lax.rem(place + 2 * RING, RING)
    return jnp.where(place < RING // 2, 2 * place, 2 * (RING - 1 - place) + 1)


def copy_to(device, src, dst, send_sem, recv_sem):
    return pltpu.make_async_remote_copy(
        src_ref=src,
        dst_ref=dst,
        send_sem=send_sem,
        recv_sem=recv_sem,
        device_id=device,
        device_id_type=MESH_ID,
    )


class Ring:
    def __init__(self, names, lazy, refs):
        self.ref = types.SimpleNamespace(**dict(zip(names, refs)))
        self.lazy = lazy
        self.loads = {}
        self.loaded = set()
        self.stores = []
        self.sent = []
        self.side = []
        self.section = lax.axis_index("section")
        self.core = lax.axis_index("tensor")
        self.group = lax.axis_index("dp")
        self.place = ring_place(self.group)
        self.right = (self.section, self.core, ring_group(self.place + 1))
        self.left = (self.section, self.core, ring_group(self.place - 1))
        self.sibling = (self.section, 1 - self.core, self.group)
        self.across = (1 - self.section, self.core, self.group)
        self.far = [(f, g) for f in (0, 1) for g in range(RING) if (f, g) != (0, 0)]

    def load_all(self, *names):
        for n, (name, at) in enumerate(self.lazy):
            if name in self.loaded or (names and name not in names):
                continue
            self.loaded.add(name)
            source, here = getattr(self.ref, name + "_"), getattr(self.ref, name)
            if at is not None:
                source = source.at[at]
            self.loads[name] = pltpu.make_async_copy(source, here, self.ref.load_sem.at[n])
            self.loads[name].start()

    def need(self, *names):
        for name in names:
            if name in self.loads:
                self.loads.pop(name).wait()

    def local(self, here, there):
        copy = pltpu.make_async_copy(here, there, self.ref.store_sem.at[len(self.stores)])
        copy.start()
        self.stores.append(copy)
        return copy

    def store(self, *names):
        for name in names:
            self.local(getattr(self.ref, name), getattr(self.ref, name + "_out"))

    def start(self, copy):
        copy.start()
        self.sent.append(copy)
        return copy

    def start_side(self, copy):
        copy.start()
        self.side.append(copy)
        return copy

    def drain(self):
        for copy in self.sent:
            copy.wait_send()
        self.sent = []

    def finish(self):
        self.need(*list(self.loads))
        self.drain()
        for copy in self.side:
            copy.wait_send()
        for copy in self.stores:
            if copy is not None:
                copy.wait()

    def stored(self, copy):
        copy.wait()
        self.stores = [None if other is copy else other for other in self.stores]

    def greet(self, devices):
        barrier = pltpu.get_barrier_semaphore()
        for device in devices:
            pl.semaphore_signal(barrier, inc=1, device_id=device, device_id_type=MESH_ID)
        pl.semaphore_wait(barrier, len(devices))

    def greet_ring(self):
        self.greet([self.right, self.left, self.sibling])

    def greet_all(self):
        self.greet([self.sibling] + [self.far_device(f, g) for f, g in self.far])

    def far_step(self, f, g):
        return lax.rem(self.section + f, 2), lax.rem(self.group + g, RING)

    def far_device(self, f, g):
        section, group = self.far_step(f, g)
        return (section, self.core, group)

    def group_from(self, g):
        return lax.rem(self.group + RING - g, RING)

    def far_from(self, f, g):
        return lax.rem(self.section + 2 - f, 2) * RING + self.group_from(g)

    def gain(self, layer, kind):
        blocks = [self.ref.gains[layer * RING + g, kind : kind + 1, :] for g in range(RING)]
        return jnp.concatenate(blocks, axis=-1)

    def row_of(self, offset, c=0):
        return pl.multiple_of(ring_group(self.place + offset) * CAP + c * (CAP // 2), CAP // 2)

    def columns(self, width, own=True):
        half = width // 2
        core = self.core if own else 1 - self.core
        return pl.ds(pl.multiple_of(core * half, half), half)

    def gather_work_sum(
        self, work, early=(), gathered=None, summed=None, ready=None, given=None, into=None
    ):
        ref = self.ref
        whole, part, mate, total = ref.whole, ref.part, ref.mate, ref.total
        sum_recv, sum_sem = into or (ref.sum_recv, ref.sum_sem)
        width, half_r = whole.shape[1], CAP // 2
        own_cols, other_cols = self.columns(width), self.columns(width, False)
        ways = ((0, self.right), (1, self.left))
        gather = None
        if given is None:
            gather = Gather(self, whole, ref.gather_sem, ref.pass_sem, self.start)

        mate_in = {}

        def work_on(offset):
            q = offset % RING
            if q in mate_in:
                return
            if gather is not None:
                gather.slot_passed(offset)
            here = pl.ds(self.row_of(offset), CAP)
            part[here, :] = work(self.row_of(offset)).astype(jnp.bfloat16)
            mate_in[q] = self.start(
                copy_to(
                    self.sibling,
                    part.at[here, other_cols],
                    mate.at[q],
                    ref.mate_sem.at[0, q],
                    ref.mate_sem.at[1, q],
                )
            )

        if gather is not None:
            gather.begin()
            if 0 in early:
                work_on(0)
            for i in range(7):
                gather.step(i)
                if gathered is not None:
                    gathered(i)
                for offset in ((), (-1,), (1,), (-2,), (2,), (), ())[i]:
                    if offset in early:
                        work_on(offset)
        else:
            given()
        gather_sent, self.sent = self.sent, []
        if ready is not None:
            ready()
        work_on(4)

        seen = set()

        def mine(offset, c):
            q = offset % RING
            if q not in seen:
                mate_in[q].wait_recv()
                seen.add(q)
            return part[pl.ds(self.row_of(q, c), half_r), own_cols].astype(jnp.float32) + mate[
                q, pl.ds(c * half_r, half_r)
            ].astype(jnp.float32)

        stream_sum = ((4, 0), (3, 1), (3, 0), (2, 1), (2, 0), (1, 1), (1, 0))
        ahead = ((3, -3), (2, -2), (), (1, -1), (0,), (), ())
        moves = []
        for i, (q, c) in enumerate(stream_sum):
            if i == 5:
                for copy in gather_sent:
                    copy.wait_send()
            for way, device in ways:
                offset, chunk = (q, c) if way == 0 else (-q, 1 - c)
                value = mine(offset, chunk)
                if i >= 2:
                    moves[2 * (i - 2) + way].wait_recv()
                    value = value + sum_recv[way, i - 2].astype(jnp.float32)
                ref.sum_send[way, i] = value.astype(jnp.bfloat16)
                moves.append(
                    self.start(
                        copy_to(
                            device,
                            ref.sum_send.at[way, i],
                            sum_recv.at[way, i],
                            sum_sem.at[0, way, i],
                            sum_sem.at[1, way, i],
                        )
                    )
                )
            for offset in ahead[i]:
                work_on(offset)
            if i == 0 and gather is not None:
                gather.all_passed()
            if summed is not None:
                summed(i)
        halves = []
        for c in (1, 0):
            value = mine(0, c)
            at = (5, 6) if c == 1 else (6, 5)
            for way in (0, 1):
                moves[2 * at[way] + way].wait_recv()
                value = value + sum_recv[way, at[way]].astype(jnp.float32)
            here = (pl.ds(c * half_r, half_r), own_cols)
            total[here] = value
            halves.append(
                self.start(
                    copy_to(
                        self.sibling,
                        total.at[here],
                        total.at[here],
                        ref.half_sem.at[0, c],
                        ref.half_sem.at[1, c],
                    )
                )
            )
        for copy in halves:
            copy.wait_recv()
        self.drain()


class Gather:
    stream = ((0, 0), (0, 1), (1, 0), (1, 1), (2, 0), (2, 1), (3, 0))

    def __init__(self, ring, whole, gather_sem, pass_sem, start):
        self.ring, self.whole, self.start = ring, whole, start
        self.gather_sem, self.pass_sem = gather_sem, pass_sem
        self.own_cols = ring.columns(whole.shape[1])
        self.other_cols = ring.columns(whole.shape[1], False)
        self.seen = set()

    def landing(self, way, k, c, columns):
        offset, chunk = (-k, c) if way == 0 else (k, 1 - c)
        return self.whole.at[pl.ds(self.ring.row_of(offset, chunk), CAP // 2), columns]

    def move(self, device, where, sems, way, i):
        return copy_to(device, where, where, sems.at[0, way, i], sems.at[1, way, i])

    def forward(self, i, way):
        k, c = self.stream[i]
        where = self.landing(way, k, c, self.own_cols)
        device = (self.ring.right, self.ring.left)[way]
        self.start(self.move(device, where, self.gather_sem, way, i))

    def begin(self):
        for i in (0, 1):
            for way in (0, 1):
                self.forward(i, way)

    def step(self, i):
        k, c = self.stream[i]
        for way in (0, 1):
            where = self.landing(way, k + 1, c, self.own_cols)
            device = (self.ring.right, self.ring.left)[way]
            self.move(device, where, self.gather_sem, way, i).wait_recv()
            self.start(self.move(self.ring.sibling, where, self.pass_sem, way, i))
            if i < 5:
                self.forward(i + 2, way)

    def passed(self, i, way):
        if (i, way) in self.seen:
            return
        self.seen.add((i, way))
        k, c = self.stream[i]
        where = self.landing(way, k + 1, c, self.other_cols)
        self.move(self.ring.sibling, where, self.pass_sem, way, i).wait_recv()

    def slot_passed(self, offset):
        if offset == RING // 2:
            for way in (0, 1):
                self.passed(6, way)
        elif offset != 0:
            way, k = (0, -offset) if offset < 0 else (1, offset)
            for i in (2 * k - 2, 2 * k - 1):
                self.passed(i, way)

    def all_passed(self):
        for i in range(7):
            for way in (0, 1):
                self.passed(i, way)


def by_rows(body, step=16):
    @pl.loop(0, CAP, step=step)
    def _(at):
        body(pl.ds(pl.multiple_of(at, step), step), at)


def inverse_rms(value):
    return lax.rsqrt(jnp.mean(value * value, axis=-1, keepdims=True) + eps_norm)


def norm_rows(ring, source, gain):
    own = ring.row_of(0)

    def body(here, at):
        value = source[here, :].astype(jnp.float32)
        low = (value * inverse_rms(value) * gain).astype(jnp.bfloat16)
        ring.ref.whole[pl.ds(pl.multiple_of(own + at, 16), 16), :] = low

    by_rows(body)


def own_rows(ring, matrix):
    return matrix.at[pl.ds(pl.multiple_of(ring.section * CAP, CAP), CAP)]


def back_rows(ring, base, source, gain, out, gain_grad, also):
    gain_grad[...] = jnp.zeros_like(gain_grad)

    def body(here, at):
        x = source[here, :].astype(jnp.float32)
        inverse = inverse_rms(x)
        scaled = x * inverse
        grad = ring.ref.total[here, :]
        moved = grad * scaled
        gain_grad[...] += moved[:8] + moved[8:]
        inner = grad * gain
        value = base[here, :].astype(jnp.float32) + inverse * (
            inner - scaled * jnp.mean(inner * scaled, axis=-1, keepdims=True)
        )
        out[here, :] = value
        also(here, at, value.astype(jnp.bfloat16))

    by_rows(body)


def lane_low(shape, span):
    return lax.rem(lax.broadcasted_iota(jnp.int32, shape, 1), span) < span // 2


def rot_rows(value, cosines, sines):
    low = lane_low(value.shape, HEAD_DIM)
    partner = jnp.where(
        low, pltpu.roll(value, LANES - HEAD_DIM // 2, 1), pltpu.roll(value, HEAD_DIM // 2, 1)
    )
    return value * cosines + partner * sines


def heads_apart(value):
    low = lane_low(value.shape, LANES)
    return jnp.concatenate([jnp.where(low, value, 0.0), jnp.where(low, 0.0, value)], axis=0)


def heads_together(value):
    rows = value.shape[0] // 2
    return jnp.where(lane_low((rows, LANES), LANES), value[:rows], value[rows:])


def twice(kv):
    low = lane_low(kv.shape, LANES)
    other = pltpu.roll(kv, HEAD_DIM, 1)
    return (
        jnp.where(low, kv, other).astype(jnp.bfloat16),
        jnp.where(low, other, kv).astype(jnp.bfloat16),
    )


def dot_wide(left, right):
    return jnp.dot(left, right, preferred_element_type=jnp.float32)


def side_moves(ring, sources, place, sems, shard):
    def rows_of(section, group, columns=slice(None)):
        at = pl.ds(pl.multiple_of(group * shard, shard), shard)
        return place.at[section, at, columns]

    def send(g):
        copies = []
        for n, (block, columns) in enumerate(sources):
            there = rows_of(ring.section, ring.group, columns)
            if g == 0:
                copies.append(ring.local(block(ring.group), there))
            else:
                copies.append(
                    ring.start_side(
                        copy_to(
                            ring.far_device(0, g),
                            block(lax.rem(ring.group + g, RING)),
                            there,
                            sems.at[0, n, g],
                            sems.at[1, n, g],
                        )
                    )
                )
        return copies

    def pass_on(g):
        group = ring.group_from(g)
        if g > 0:
            for n, (_, columns) in enumerate(sources):
                where = rows_of(ring.section, group, columns)
                copy_to(
                    ring.sibling, where, where, sems.at[0, n, g], sems.at[1, n, g]
                ).wait_recv()
        where = rows_of(ring.section, group)
        ring.start_side(copy_to(ring.across, where, where, sems.at[0, 2, g], sems.at[1, 2, g]))

    def wait_passed(g):
        where = rows_of(1 - ring.section, ring.group_from(g))
        copy_to(ring.across, where, where, sems.at[0, 2, g], sems.at[1, 2, g]).wait_recv()

    return send, pass_on, wait_passed


def unit_blocks(source, span, units, b):
    at = b * units
    base, turn = at // LANES * LANES, at % LANES
    wide = -(-(turn + units) // LANES) * LANES
    value = source[:, base : base + wide].astype(F32)
    if turn:
        value = pltpu.roll(value, wide - turn, 1)
    value = value[:, :span]
    lanes = lax.broadcasted_iota(jnp.int32, value.shape, 1)
    return jnp.where(lanes < units, value, 0.0).astype(LOW)


def first_kernel(names, lazy, *refs):
    ring = Ring(names, lazy, refs)
    layer_forward(ring, True, ring.ref.normed_out, ring.ref.normed_mlp_out)
    ring.finish()


def middle_kernel(units, names, lazy, *refs):
    ring = Ring(names, lazy, refs)
    rest = layer_forward(ring, False, ring.ref.normed_attn, ring.ref.normed)
    layer_backward(ring, False, units, rest)
    ring.finish()


def last_kernel(units, names, lazy, *refs):
    ring = Ring(names, lazy, refs)
    layer_backward(ring, True, units)
    ring.finish()


def layer_forward(ring, moving, keep_attn, keep_mlp):
    ref = ring.ref
    width = ref.whole.shape[1]
    shard = width // RING
    ring.load_all()
    if moving:
        ring.greet_all()
        mine_at = ring.section * RING + ring.group
        ref.gains[mine_at] = ref.own_gain[...]
        for n, (f, g) in enumerate(ring.far):
            ring.start_side(
                copy_to(
                    ring.far_device(f, g),
                    ref.own_gain,
                    ref.gains.at[mine_at],
                    ref.far_sem.at[0, n],
                    ref.far_sem.at[1, n],
                )
            )
        key, value = ref.key[...].astype(F32), ref.value[...].astype(F32)
        low = lane_low(key.shape, LANES)
        ref.kv_blocks[0] = jnp.where(low, key, pltpu.roll(value, HEAD_DIM, 1)).astype(LOW)
        ref.kv_blocks[1] = jnp.where(low, pltpu.roll(key, HEAD_DIM, 1), value).astype(LOW)
        q_width = ref.w_out.shape[1]

        def query_block(group):
            at = pl.multiple_of(group * q_width, q_width)
            return ref.w_query.at[0, :, pl.ds(at, q_width)]

        def kv_block(group):
            return ref.kv_blocks.at[group // (RING // 2)]

        send_attn, pass_attn, attn_passed = side_moves(
            ring,
            ((query_block, slice(0, q_width)), (kv_block, slice(q_width, 2 * q_width))),
            ref.w_attn,
            ref.attn_sem,
            shard,
        )
        send_mlp, pass_mlp, mlp_passed = side_moves(
            ring,
            ((lambda group: ref.mlp_blocks.at[group], slice(None)),),
            ref.w_mlp,
            ref.mlp_sem,
            shard,
        )
        at_home = [send_attn(g) for g in range(RING)][0]
        units = ref.own_down.shape[1]
        span = ref.w_down.shape[1]
        if span > units:
            ref.w_down[:, units:, :] = jnp.zeros((2, span - units, width), LOW)

        def across_big(own, place, n):
            where = place.at[ring.section, pl.ds(0, own.shape[1])]
            at_home.append(ring.local(own.at[0], where))
            ring.start_side(
                copy_to(
                    ring.across, own.at[0], where, ref.big_sem.at[0, n], ref.big_sem.at[1, n]
                )
            )

        def big_passed(own, place, n):
            where = place.at[1 - ring.section, pl.ds(0, own.shape[1])]
            copy_to(
                ring.across, where, where, ref.big_sem.at[0, n], ref.big_sem.at[1, n]
            ).wait_recv()

        across_big(ref.own_out, ref.w_out, 0)
        for n, (f, g) in enumerate(ring.far):
            copy_to(
                ring.sibling,
                ref.own_gain,
                ref.gains.at[ring.far_from(f, g)],
                ref.far_sem.at[0, n],
                ref.far_sem.at[1, n],
            ).wait_recv()

        w_attn, w_out = ref.w_attn.at[0], ref.w_out.at[0]
        w_mlp, w_down = ref.w_mlp.at[0], ref.w_down.at[0]
    else:
        ring.greet_ring()
        w_attn, w_out, w_mlp, w_down = ref.w_attn, ref.w_out, ref.w_mlp, ref.w_down
        target = own_rows(ring, ref.cotangent)[...].astype(F32) * ref.live[...]
        ref.target[...] = target.astype(LOW)
        ref.low[pl.ds(ring.row_of(0), CAP), :] = target.astype(LOW)
        aside = Gather(ring, ref.low, ref.aside_sem, ref.aside_pass_sem, ring.start_side)
        aside.begin()
    x = own_rows(ring, ref.tokens) if moving else ref.x
    layer = 0 if moving else 1
    norm_rows(ring, x, ring.gain(layer, 0))
    heads = w_out.shape[0]
    span = w_down.shape[0]

    def attend(row):
        here = pl.ds(row, CAP)
        both = dot_wide(ref.whole[here, :], w_attn[...])
        queries, kv = both[:, :heads], both[:, heads:]
        cosines, sines = ref.cosines[here, :], ref.sines[here, :]
        queries = rot_rows(queries, cosines, sines)
        kv = jnp.where(lane_low(kv.shape, LANES), rot_rows(kv, cosines, sines), kv)
        ref.queries[here, :] = queries.astype(jnp.bfloat16)
        ref.kv[here, :] = kv.astype(jnp.bfloat16)
        keys, values = twice(kv)
        apart = heads_apart(queries).astype(jnp.bfloat16)
        allowed = ref.mask[here, :] > 0.5
        allowed = jnp.concatenate([allowed, allowed], axis=0)
        scores = jnp.where(allowed, dot_trans(apart, keys) * HEAD_DIM ** (-0.5), -1e30)
        weights = jnp.exp(scores - jnp.max(scores, axis=-1, keepdims=True))
        probs = weights / jnp.sum(weights, axis=-1, keepdims=True)
        ref.probs[pl.ds(pl.multiple_of(2 * row, 2 * CAP), 2 * CAP), :] = probs
        mixed = heads_together(dot_wide(probs.astype(jnp.bfloat16), values)).astype(jnp.bfloat16)
        ref.mixed[here, :] = mixed
        return dot_wide(mixed, w_out[...])

    keeping = []

    def attn_gathered(i):
        if moving:
            if i == 0:
                for copy in at_home[:2]:
                    ring.stored(copy)
                pass_attn(0)
                ring.need("w_gate", "w_up")
            pass_attn(i + 1)
            if i == 2:
                across_big(ref.own_down, ref.w_down, 1)
            for b in ((0, 1), (2, 3), (4,), (5,), (6,), (7,), ())[i]:
                ref.mlp_blocks[b, :, :span] = unit_blocks(ref.w_gate, span, units, b)
                ref.mlp_blocks[b, :, span:] = unit_blocks(ref.w_up, span, units, b)
            if i == 5:
                for g in range(1, RING):
                    send_mlp(g)
                at_home.extend(send_mlp(0))
                ring.stored(at_home[4])
                pass_mlp(0)

    def attn_ready():
        ring.need("cosines", "sines", "mask")
        if moving:
            ring.stored(at_home[2])

            @pl.when(ring.section == 1)
            def _():
                for g in range(RING):
                    attn_passed(g)
                big_passed(ref.own_out, ref.w_out, 0)

        else:
            ring.need("w_attn", "w_out")
            aside.step(0)
            aside.step(1)

    def attn_summed(i):
        if moving:
            pass_mlp(i + 1)

    def keep(there, also=None):
        def summed(i):
            if also is not None:
                also(i)
            if i == 0:
                keeping.append(ring.local(ref.whole, there))
            if i == 4:
                ring.stored(keeping.pop())

        return summed

    ring.gather_work_sum(attend, gathered=attn_gathered, ready=attn_ready, summed=keep(keep_attn, attn_summed))
    if moving:
        ring.store("queries", "kv", "probs", "mixed")
    else:
        aside.step(2)
        aside.step(3)

    own, mlp_gain = ring.row_of(0), ring.gain(layer, 1)

    def add_rows(here, at):
        value = x[here, :].astype(jnp.float32) + ref.total[here, :]
        ref.residual[here, :] = value
        low = (value * inverse_rms(value) * mlp_gain).astype(jnp.bfloat16)
        ref.whole[pl.ds(pl.multiple_of(own + at, 16), 16), :] = low

    by_rows(add_rows)

    def feed(row):
        here = pl.ds(row, CAP)
        both = dot_wide(ref.whole[here, :], w_mlp[...])
        gate, up = both[:, :span], both[:, span:]
        ref.gate[here, :] = gate
        ref.up[here, :] = up
        hidden = (gate * jax.nn.sigmoid(gate) * up).astype(jnp.bfloat16)
        ref.hidden[here, :] = hidden
        return dot_wide(hidden, w_down[...])

    def mlp_ready():
        if moving:
            ring.stored(at_home[3])

            @pl.when(ring.section == 1)
            def _():
                for g in range(RING):
                    mlp_passed(g)
                big_passed(ref.own_down, ref.w_down, 1)

        else:
            ring.need("w_mlp", "w_down")
            aside.step(4)

    ring.gather_work_sum(feed, ready=mlp_ready, summed=keep(keep_mlp))
    if moving:
        ring.store("gate", "up", "hidden")
    else:
        aside.step(5)
        aside.step(6)
        aside.all_passed()

    def round_rows(here, at):
        ref.out[here, :] = (ref.residual[here, :] + ref.total[here, :]).astype(jnp.bfloat16)

    if not moving:
        return lambda: by_rows(round_rows)
    by_rows(round_rows)
    if moving:

        @pl.when(ring.section == 0)
        def _():
            for g in range(RING):
                attn_passed(g)
                mlp_passed(g)
            big_passed(ref.own_out, ref.w_out, 0)
            big_passed(ref.own_down, ref.w_down, 1)


def layer_backward(ring, last, units, rest=None):
    ref = ring.ref
    width = ref.whole.shape[1]
    shard = width // RING
    span, heads = ref.w_down.shape[0], ref.w_out.shape[0]
    if last:
        ring.load_all(*FIRST)
        ring.greet_all()
        normed_attn, x, base, low_in = ref.normed, own_rows(ring, ref.tokens), ref.base, ref.whole
        again = pltpu.make_async_copy(ref.normed_attn_, normed_attn, ref.again_sem.at[0])
        ref.whole[pl.ds(ring.row_of(0), CAP), :] = ref.base[...]
        given = into = None
    else:
        normed_attn, x, base, low_in = ref.normed_attn, ref.x, ref.target, ref.low
        given, into = lambda: None, (ref.sum_recv_2, ref.sum_sem_2)

    def block(matrix, g):
        at = lax.rem(ring.group + g, RING) * shard
        return matrix.at[pl.ds(pl.multiple_of(at, shard), shard)]

    order = (1, 2, 3, 4, 5, 6, 7, 0)
    if last:

        def cross(source, place, sems):
            return copy_to(ring.across, source, place, sems.at[0], sems.at[1])

        def cross_mlp(g, source):
            return cross(block(source, g), block(ref.stage_mlp, g), ref.cross_sem.at[0, g])

        def cross_attn(g, source):
            return cross(block(source, g), block(ref.stage_attn, g), ref.cross_sem.at[1, g])

        def cross_big(n, source):
            rows = pl.ds(0, (units, heads)[n])
            place = (ref.stage_down, ref.stage_out)[n].at[rows]
            return cross(source.at[rows], place, ref.big_sem.at[n])

        def deal(g, own, fin, n):
            if g == 0:
                return pltpu.make_async_copy(
                    block(own, 0), fin.at[ring.group], ref.deal_sem.at[n, 0, 0]
                )
            return copy_to(
                ring.far_device(0, g),
                block(own, g),
                fin.at[ring.group],
                ref.deal_sem.at[n, 0, g],
                ref.deal_sem.at[n, 1, g],
            )

        def add_and_deal(g, own, n):
            crossed = (cross_mlp, cross_attn)[n](g, own)
            crossed.wait_recv()
            stage, fin = ((ref.stage_mlp, ref.fin_mlp), (ref.stage_attn, ref.fin_attn))[n]
            rows, other = block(own, g), block(stage, g)
            rows[...] = (rows[...].astype(F32) + other[...].astype(F32)).astype(LOW)
            deal(g, own, fin, n).start()

        def dealt(own, n):
            fin = (ref.fin_mlp, ref.fin_attn)[n]
            for g in range(RING):
                copy = deal(g, own, fin, n)
                if g == 0:
                    copy.wait()
                else:
                    copy.wait_send()
                    where = fin.at[ring.group_from(g)]
                    copy_to(
                        ring.sibling,
                        where,
                        where,
                        ref.deal_sem.at[n, 0, g],
                        ref.deal_sem.at[n, 1, g],
                    ).wait_recv()

        @pl.when(ring.section == 0)
        def _():
            for g in order:
                cross_mlp(g, ref.late_mlp_).start()
            for g in order:
                cross_attn(g, ref.late_attn_).start()
            cross_big(1, ref.late_out).start()
            cross_big(0, ref.late_down).start()
            cross(ref.late_rows, ref.far_rows, ref.big_sem.at[2]).start()
            cross(ref.out_1, ref.far_out, ref.big_sem.at[3]).start()

        @pl.when(ring.section == 1)
        def _():
            cross(ref.out_0, ref.far_out, ref.big_sem.at[3]).start()

    def when(section, body):
        if last:
            pl.when(ring.section == section)(body)

    def layer_0(n, *steps):
        if not steps:
            return

        def body():
            for g in steps:
                add_and_deal(g, (ref.grad_mlp, ref.grad_attn)[n], n)

        when(0, body)

    def feed_back(row):
        here = pl.ds(row, CAP)
        ring.need("w_mlp", "w_down", "gate", "up")
        grad_hidden = dot_trans(low_in[here, :], ref.w_down[...])
        gate, up = ref.gate[here, :], ref.up[here, :]
        sigmoid = jax.nn.sigmoid(gate)
        grad_gate = grad_hidden * up * sigmoid * (1.0 + gate * (1.0 - sigmoid))
        grad_up = grad_hidden * gate * sigmoid
        both = jnp.concatenate([grad_gate, grad_up], axis=1).astype(jnp.bfloat16)
        ref.g_mlp[here, :] = both
        return dot_trans(both, ref.w_mlp[...])

    def weight_rows(g, normed, grads, place):
        at = pl.multiple_of(lax.rem(ring.group + g, RING) * shard, shard)
        piece = normed[:, pl.ds(at, shard)]
        place[pl.ds(at, shard), :] = dot_rows(piece, grads[...]).astype(jnp.bfloat16)

    def mlp_summed(i):
        if i == 0:
            if last:
                ring.load_all()
            else:
                rest()
        ring.need("hidden")
        if last:
            ring.need("normed")
        if last:
            weights, downs = ((), (1, 2, 3), (4, 5, 6), (7, 0), (), (), ()), (3, 4, 4, 5)
        else:
            weights, downs = ((),) * 7, (5, 5, 6, 6)
        for g in weights[i]:
            weight_rows(g, ref.normed, ref.g_mlp, ref.grad_mlp)
            when(1, lambda: cross_mlp(g, ref.grad_mlp).start())
        piece = width // 4
        for j in range(4):
            if downs[j] != i:
                continue
            at = slice(j * piece, (j + 1) * piece)
            ref.grad_down[:, at] = dot_rows(ref.hidden[...], low_in[:, at]).astype(LOW)
        if last:
            if i == 2:
                ring.need("late_mlp", "late_attn")
            layer_0(0, *((), (), (), (), (), (1,), (2,))[i])

    early = (0, 1, -1, 2, -2)
    ring.gather_work_sum(
        feed_back, early=early, summed=mlp_summed, given=given, into=into
    )
    if last:
        again.start()
    else:
        ring.store("grad_down")
    layer = 0 if last else 1
    own = ring.row_of(0)

    def gathered_next(here, at, low):
        ref.whole[pl.ds(pl.multiple_of(own + at, 16), 16), :] = low

    gain = ring.gain(layer, 1)
    back_rows(ring, base, ref.residual, gain, ref.middle, ref.gain_grad_mlp, gathered_next)

    def attend_back(row):
        here = pl.ds(row, CAP)
        ring.need("w_attn", "w_out", "queries", "kv", "probs", "cosines", "sines")
        grad_mixed = dot_trans(ref.whole[here, :], ref.w_out[...])
        grad_apart = heads_apart(grad_mixed).astype(jnp.bfloat16)
        keys, values = twice(ref.kv[here, :].astype(jnp.float32))
        apart = heads_apart(ref.queries[here, :].astype(jnp.float32)).astype(jnp.bfloat16)
        probs = ref.probs[pl.ds(pl.multiple_of(2 * row, 2 * CAP), 2 * CAP), :]
        grad_probs = dot_trans(grad_apart, values)
        grad_values = dot_rows(probs.astype(jnp.bfloat16), grad_apart)
        spread = jnp.sum(grad_probs * probs, axis=-1, keepdims=True)
        grad_scores = (probs * (grad_probs - spread) * HEAD_DIM ** (-0.5)).astype(jnp.bfloat16)
        grad_queries = heads_together(dot_wide(grad_scores, keys))
        grad_keys = dot_rows(grad_scores, apart)
        cosines, sines = ref.cosines[here, :], -ref.sines[here, :]
        grad_queries = rot_rows(grad_queries, cosines, sines)
        grad_keys = rot_rows(grad_keys + pltpu.roll(grad_keys, HEAD_DIM, 1), cosines, sines)
        grad_values = grad_values + pltpu.roll(grad_values, HEAD_DIM, 1)
        grad_kv = jnp.where(lane_low(grad_keys.shape, LANES), grad_keys, grad_values)
        both = jnp.concatenate([grad_queries, grad_kv], axis=1).astype(jnp.bfloat16)
        ref.g_attn[here, :] = both
        return dot_trans(both, ref.w_attn[...])

    def attn_gathered(i):
        layer_0(0, *((3,), (), (), (4,), (), (), (5,))[i])
        if not last:
            ring.need("normed")
            for g in ((1, 2), (3,), (4,), (5,), (6,), (7,), (0,))[i]:
                weight_rows(g, ref.normed, ref.g_mlp, ref.grad_mlp)
            if i == 6:
                ring.store("grad_mlp")

    def attn_summed(i):
        if i == 1 and last:
            again.wait()
        if last:
            weights, out_at = ((), (1, 2, 3, 4), (5, 6, 7, 0), (), (), (), ()), 3
        else:
            weights, out_at = ((), (), (), (), (), (1, 2, 3, 4), (5, 6, 7, 0)), 1
        for g in weights[i]:
            weight_rows(g, normed_attn, ref.g_attn, ref.grad_attn)
            when(1, lambda: cross_attn(g, ref.grad_attn).start())
        if i == out_at:
            ring.need("mixed")
            ref.grad_out[...] = dot_rows(ref.mixed[...], ref.whole[...]).astype(LOW)

            def rest():
                cross_big(1, ref.grad_out).start()
                cross_big(0, ref.grad_down).start()

            when(1, rest)
        layer_0(0, *((), (6,), (), (), (7,), (), (0,))[i])

    ring.gather_work_sum(
        attend_back,
        early=early if last else (),
        gathered=attn_gathered,
        summed=attn_summed,
    )
    def handed_on(here, at, low):
        ref.low_rows[here, :] = low

    back_rows(
        ring,
        ref.middle,
        x,
        ring.gain(layer, 0),
        ref.grad_rows,
        ref.gain_grad_attn,
        handed_on,
    )
    if last:
        end_exchange = last_exchange(ring)
        ring.store("grad_down", "grad_out")

        @pl.when(ring.section == 1)
        def _():
            for g in order:
                add_and_deal(g, ref.late_mlp, 0)
            for g in order:
                add_and_deal(g, ref.late_attn, 1)

        @pl.when(ring.section == 0)
        def _():
            for g in order:
                add_and_deal(g, ref.grad_attn, 1)

        end_exchange()

        @pl.when(ring.section == 1)
        def _():
            dealt(ref.late_mlp, 0)
            dealt(ref.late_attn, 1)
            places = (ref.stage_down.at[pl.ds(0, units)], ref.stage_out, ref.far_rows, ref.far_out)
            for n, place in enumerate(places):
                copy_to(
                    ring.across, place, place, ref.big_sem.at[n, 0], ref.big_sem.at[n, 1]
                ).wait_recv()
            for g in range(RING):
                cross_mlp(g, ref.grad_mlp).wait_send()
                cross_attn(g, ref.grad_attn).wait_send()
            cross_big(0, ref.grad_down).wait_send()
            cross_big(1, ref.grad_out).wait_send()
            cross(ref.out_0, ref.far_out, ref.big_sem.at[3]).wait_send()

        @pl.when(ring.section == 0)
        def _():
            dealt(ref.grad_mlp, 0)
            dealt(ref.grad_attn, 1)
            places = ((0, ref.stage_down.at[pl.ds(0, units)]), (1, ref.stage_out), (3, ref.far_out))
            for n, place in places:
                copy_to(
                    ring.across, place, place, ref.big_sem.at[n, 0], ref.big_sem.at[n, 1]
                ).wait_recv()
            for g in range(RING):
                cross_mlp(g, ref.late_mlp_).wait_send()
                cross_attn(g, ref.late_attn_).wait_send()
            cross_big(0, ref.late_down).wait_send()
            cross_big(1, ref.late_out).wait_send()
            cross(ref.late_rows, ref.far_rows, ref.big_sem.at[2]).wait_send()
            cross(ref.out_1, ref.far_out, ref.big_sem.at[3]).wait_send()

    else:
        ring.store("grad_attn", "grad_out")


def last_exchange(ring):
    ref = ring.ref
    width = ref.whole.shape[1]
    shard, half_r = width // RING, CAP // 2
    own_cols = ring.columns(width)
    halves = []
    for c in (0, 1):
        here = (pl.ds(c * half_r, half_r), own_cols)
        halves.append(
            ring.start(
                copy_to(
                    ring.across,
                    ref.low_rows.at[here],
                    ref.far_low.at[here],
                    ref.half_sem.at[0, 2 + c],
                    ref.half_sem.at[1, 2 + c],
                )
            )
        )
    mine_at = ring.section * RING + ring.group
    grads = ((ref.gain_grad_attn, ref.gain_grad_mlp), (ref.gg1a, ref.gg1m))
    for layer in (0, 1):
        for g in range(RING):
            for kind in (0, 1):
                ref.gains_out[layer * RING + g, kind] = grads[layer][kind][
                    :, g * shard : (g + 1) * shard
                ]
    ref.gains_in[mine_at] = ref.gains_out[mine_at]
    for n, (f, g) in enumerate(ring.far):
        to_s, to_g = ring.far_step(f, g)
        ring.start(
            copy_to(
                ring.far_device(f, g),
                ref.gains_out.at[to_s * RING + to_g],
                ref.gains_in.at[mine_at],
                ref.far_sem.at[0, n],
                ref.far_sem.at[1, n],
            )
        )
    return lambda: last_waits(ring, halves)


def last_waits(ring, halves):
    ref = ring.ref
    width = ref.whole.shape[1]
    half_r = CAP // 2
    own_cols, other_cols = ring.columns(width), ring.columns(width, False)
    for c in (0, 1):
        halves[c].wait_recv()
        where = ref.far_low.at[pl.ds(c * half_r, half_r), own_cols]
        ring.start(
            copy_to(
                ring.sibling, where, where, ref.half_sem.at[0, 4 + c], ref.half_sem.at[1, 4 + c]
            )
        )
    for n, (f, g) in enumerate(ring.far):
        copy_to(
            ring.sibling,
            ref.gains_out.at[0],
            ref.gains_in.at[ring.far_from(f, g)],
            ref.far_sem.at[0, n],
            ref.far_sem.at[1, n],
        ).wait_recv()
    for kind in (0, 1):
        ref.gain_sum[kind : kind + 1, :] = jnp.sum(
            jnp.sum(ref.gains_in[:, kind], axis=0), axis=0, keepdims=True
        )
    for c in (0, 1):
        where = ref.far_low.at[pl.ds(c * half_r, half_r), other_cols]
        copy_to(
            ring.sibling, where, where, ref.half_sem.at[0, 4 + c], ref.half_sem.at[1, 4 + c]
        ).wait_recv()


F32, LOW = jnp.float32, jnp.bfloat16
MLP, ATTN, DOWN, OUT = "grad_mlp", "grad_attn", "grad_down", "grad_out"
MLP_IN, ATTN_IN, ROWS, OUT_0 = "mlp", "attn", "rows_0", "out_0"
WIDE = ("gate", "up", "query", "key", "value")
FIRST = ("w_mlp", "w_down", "gate", "up", "hidden")
SAVED = ("gate", "up", "hidden", "queries", "kv", "probs", "mixed")


def ring_call(
    kernel, collective_id, width, now, later, beside, outs, kept, direct, scratch, sems
):
    rows = CAP
    later = {name: a if isinstance(a, tuple) else (a, None) for name, a in later.items()}
    arrays = dict(
        whole=((RING * rows, width), LOW),
        part=((RING * rows, width), LOW),
        mate=((RING, rows, width // 2), LOW),
        sum_send=((2, 7, rows // 2, width // 2), LOW),
        sum_recv=((2, 7, rows // 2, width // 2), LOW),
        total=((rows, width), F32),
        **kept,
        **scratch,
    )
    sems = dict(
        gather_sem=(2, 2, 7),
        pass_sem=(2, 2, 7),
        mate_sem=(2, RING),
        sum_sem=(2, 2, 7),
        half_sem=(2, 6),
        load_sem=(len(later),),
        store_sem=(16,),
        **sems,
    )
    vmem, anywhere = pl.BlockSpec(memory_space=pltpu.VMEM), pl.BlockSpec(memory_space=pl.ANY)
    names = list(now) + [name + "_" for name in later] + list(beside) + list(outs)
    names += [name + "_out" for name in kept] + list(direct) + list(later)
    names += list(arrays) + list(sems)
    results = pl.pallas_call(
        functools.partial(kernel, names, [(name, at) for name, (_, at) in later.items()]),
        out_shape=tuple(
            jax.ShapeDtypeStruct(*a) for a in (*outs.values(), *kept.values(), *direct.values())
        ),
        in_specs=[vmem] * len(now) + [anywhere] * (len(later) + len(beside)),
        out_specs=tuple([vmem] * len(outs) + [anywhere] * (len(kept) + len(direct))),
        scratch_shapes=[
            pltpu.VMEM(a.shape if at is None else a.shape[1:], a.dtype) for a, at in later.values()
        ]
        + [pltpu.VMEM(*a) for a in arrays.values()]
        + [pltpu.SemaphoreType.DMA(a) for a in sems.values()],
        compiler_params=pltpu.CompilerParams(
            collective_id=collective_id, has_side_effects=True, vmem_limit_bytes=VMEM_BYTES
        ),
        cost_estimate=pl.CostEstimate(
            flops=80 * 10**9, bytes_accessed=360 * 10**6, transcendentals=0
        ),
    )(*now.values(), *[a for a, _ in later.values()], *beside.values())
    return types.SimpleNamespace(**dict(zip([*outs, *kept, *direct], results)))


def lay_out_kernel(units, names, *refs):
    ref = types.SimpleNamespace(**dict(zip(names, refs)))
    first = lax.axis_index("section") == 0
    rows, span = ref.mlp.shape[1], ref.mlp.shape[2] // 2
    for start, place in ((0, ref.gate), (span, ref.up)):
        place[...] = jnp.zeros_like(place)
        for b in range(RING):
            at = b * units
            base, turn = at // LANES * LANES, at % LANES
            wide = -(-(turn + units) // LANES) * LANES
            block = ref.mlp[b, :, start : start + span].astype(F32)
            if wide > span:
                block = jnp.concatenate([block, jnp.zeros((rows, wide - span), F32)], axis=1)
            if turn:
                block = pltpu.roll(block, turn, 1)
            place[0, :, base : base + wide] += block[:, :wide]
    q_width = ref.attn.shape[2] // 2
    for b in range(RING):
        ref.query[0, :, b * q_width : (b + 1) * q_width] = ref.attn[b, :, :q_width].astype(F32)
    sums = []
    for head in (0, 1):
        blocks = range(head * RING // 2, (head + 1) * RING // 2)
        sums.append(sum(ref.attn[b, :, q_width:].astype(F32) for b in blocks))
    low = lane_low(sums[0].shape, LANES)
    ref.key[0] = jnp.where(low, sums[0], pltpu.roll(sums[1], HEAD_DIM, 1))
    ref.value[0] = jnp.where(low, pltpu.roll(sums[0], HEAD_DIM, 1), sums[1])
    down = jnp.where(first, ref.down_0[:units, :].astype(F32), ref.down_1[:units, :].astype(F32))
    ref.down[0] = down + ref.stage_down[:units, :].astype(F32)
    out = jnp.where(first, ref.out_0[...].astype(F32), ref.out_1[...].astype(F32))
    ref.out[0] = out + ref.stage_out[...].astype(F32)
    for place, low_first, low_second, high_first, high_second in (
        (ref.rows, ref.rows_0, ref.far_rows, ref.far_rows, ref.rows_1),
        (ref.grads, ref.grads_0, ref.far_low, ref.far_grads, ref.grads_1),
    ):
        kind = place.dtype
        place[0, :CAP, :] = jnp.where(
            first, low_first[...].astype(kind), high_first[...].astype(kind)
        )
        place[0, CAP:, :] = jnp.where(
            first, low_second[...].astype(kind), high_second[...].astype(kind)
        )


def lay_out(units, mlp, attn, **by_columns):
    _, shard, mlp_width = mlp.shape
    attn_width = attn.shape[2]
    width = by_columns[ROWS].shape[1]
    heads = by_columns[OUT_0].shape[0]
    steps = RING // 2
    step, columns = shard // steps, width // steps
    wide = [RING * units] * 2 + [RING * attn_width // 2] + [attn_width // 2] * 2
    tall = dict(down=(units, F32), out=(heads, F32), rows=(2 * CAP, LOW), grads=(2 * CAP, F32))
    names = [MLP_IN, ATTN_IN, *by_columns, *WIDE, *tall]
    results = pl.pallas_call(
        functools.partial(lay_out_kernel, units, names),
        grid=(steps,),
        in_specs=[
            pl.BlockSpec((RING, step, mlp_width), lambda i: (0, i, 0)),
            pl.BlockSpec((RING, step, attn_width), lambda i: (0, i, 0)),
        ]
        + [pl.BlockSpec((a.shape[0], columns), lambda i: (0, i)) for a in by_columns.values()],
        out_shape=[jax.ShapeDtypeStruct((1, shard, w), F32) for w in wide]
        + [jax.ShapeDtypeStruct((1, rows, width), kind) for rows, kind in tall.values()],
        out_specs=[pl.BlockSpec((1, step, w), lambda i: (0, i, 0)) for w in wide]
        + [pl.BlockSpec((1, rows, columns), lambda i: (0, 0, i)) for rows, _ in tall.values()],
        compiler_params=pltpu.CompilerParams(vmem_limit_bytes=VMEM_BYTES),
    )(mlp, attn, *by_columns.values())
    return types.SimpleNamespace(**dict(zip([*WIDE, *tall], results)))


def ring_device(
    tokens,
    cotangent,
    seq_lengths,
    seq_group,
    seq_micro,
    attn_gain,
    w_query,
    key_matrix,
    value_matrix,
    w_out,
    mlp_gain,
    w_gate,
    w_up,
    w_down,
):
    section_id = lax.axis_index("section")
    group_id = lax.axis_index("dp")
    width = tokens.shape[1]
    rows = CAP
    whole_rows = RING * rows
    shard = w_query.shape[1]
    groups = jnp.arange(RING, dtype=jnp.int32)

    kv_heads = key_matrix.shape[2] // HEAD_DIM
    units = w_down.shape[1]
    span = -(-units // LANES) * LANES
    heads = w_out.shape[1]

    labels, places = jax.vmap(
        lambda g: jax.tree.map(
            lambda a: a[0],
            slot_layout(
                seq_lengths,
                jnp.where(seq_micro == section_id, seq_group, -1),
                seq_micro * 0,
                g,
                1,
                rows,
            ),
        )
    )(groups)
    row_ids = jnp.arange(rows, dtype=jnp.int32)
    mask = (labels[:, :, None] == labels[:, None, :]) & (row_ids[None, :] <= row_ids[:, None])
    half = HEAD_DIM // 2
    lanes = jnp.arange(LANES, dtype=jnp.int32)
    frequency = rope_base ** (-2.0 * (lanes % half).astype(F32) / HEAD_DIM)
    angles = places.astype(jnp.float32).reshape(whole_rows, 1) * frequency
    tables = dict(
        cosines=jnp.cos(angles),
        sines=jnp.sin(angles) * jnp.where(lanes % HEAD_DIM < half, -1.0, 1.0),
    )
    mask = mask.astype(F32).reshape(whole_rows, rows)

    own_live = lax.dynamic_index_in_dim(labels, group_id, 0, keepdims=False) > 0
    own_live = own_live.astype(F32)[:, None]
    own_gains = jnp.concatenate([attn_gain, mlp_gain]).astype(F32)
    own_gains = jnp.pad(own_gains, ((0, 6), (0, 0)))

    row_f32, row_low = ((rows, width), F32), ((rows, width), LOW)
    weights = dict(
        w_attn=((2, width, 2 * heads), LOW),
        w_out=((2, heads, width), LOW),
        w_mlp=((2, width, 2 * span), LOW),
        w_down=((2, span, width), LOW),
    )
    kept = dict(
        queries=((whole_rows, heads), LOW),
        kv=((whole_rows, heads), LOW),
        probs=((2 * whole_rows, rows), F32),
        mixed=((whole_rows, heads), LOW),
        gate=((whole_rows, span), F32),
        up=((whole_rows, span), F32),
        hidden=((whole_rows, span), LOW),
    )
    direct = dict(normed_out=((whole_rows, width), LOW), normed_mlp_out=((whole_rows, width), LOW))
    outs = dict(out=row_low, residual=row_f32)
    layer_0 = ring_call(
        first_kernel,
        1,
        width,
        dict(tokens=tokens, own_gain=own_gains, key=key_matrix[0], value=value_matrix[0]),
        dict(w_gate=(w_gate, 0), w_up=(w_up, 0), **tables, mask=mask),
        dict(w_query=w_query, own_out=w_out, own_down=w_down),
        dict(**outs, **weights, gains=((2 * RING, 8, shard), F32)),
        kept,
        direct,
        dict(
            kv_blocks=((kv_heads, shard, heads), LOW),
            mlp_blocks=((RING, shard, 2 * span), LOW),
        ),
        dict(
            far_sem=(2, 2 * RING - 1),
            attn_sem=(2, 3, RING),
            mlp_sem=(2, 3, RING),
            big_sem=(2, 2),
        ),
    )
    def weights_of(layer):
        return {name: (getattr(layer_0, name), layer) for name in weights}

    pairs = dict(grad_mlp=((width, 2 * span), LOW), grad_attn=((width, 2 * heads), LOW))
    grad_sums = dict(grad_down=((span, width), LOW), grad_out=((heads, width), LOW))
    back_outs = dict(
        grad_rows=row_f32, gain_grad_mlp=((8, width), F32), gain_grad_attn=((8, width), F32)
    )
    back_scratch = dict(
        g_mlp=((whole_rows, 2 * span), LOW), g_attn=((whole_rows, 2 * heads), LOW), middle=row_f32
    )
    whole = ((whole_rows, width), LOW)
    layer_1 = ring_call(
        functools.partial(middle_kernel, units),
        2,
        width,
        dict(x=layer_0.out, gains=layer_0.gains, cotangent=cotangent, live=own_live),
        dict(**weights_of(1), **tables, mask=mask),
        {},
        dict(**outs, **back_outs, low_rows=row_low),
        dict(**pairs, **grad_sums),
        {},
        dict(
            **kept,
            **back_scratch,
            target=row_low,
            low=whole,
            normed=whole,
            normed_attn=whole,
            sum_recv_2=((2, 7, rows // 2, width // 2), LOW),
        ),
        dict(aside_sem=(2, 2, 7), aside_pass_sem=(2, 2, 7), sum_sem_2=(2, 2, 7)),
    )
    back_0 = ring_call(
        functools.partial(last_kernel, units),
        3,
        width,
        dict(
            base=layer_1.low_rows,
            tokens=tokens,
            residual=layer_0.residual,
            gains=layer_0.gains,
            gg1a=layer_1.gain_grad_attn,
            gg1m=layer_1.gain_grad_mlp,
        ),
        dict(
            **weights_of(0),
            **tables,
            **{name: getattr(layer_0, name) for name in SAVED},
            normed=layer_0.normed_mlp_out,
            late_mlp=layer_1.grad_mlp,
            late_attn=layer_1.grad_attn,
        ),
        dict(
            normed_attn_=layer_0.normed_out,
            late_down=layer_1.grad_down,
            late_out=layer_1.grad_out,
            late_rows=layer_1.grad_rows,
            out_0=layer_0.out,
            out_1=layer_1.out,
        ),
        dict(**back_outs, far_low=row_low, gain_sum=((2, shard), F32)),
        grad_sums,
        dict(
            fin_mlp=((RING, shard, 2 * span), LOW),
            fin_attn=((RING, shard, 2 * heads), LOW),
            stage_down=grad_sums[DOWN],
            stage_out=grad_sums[OUT],
            far_rows=row_f32,
            far_out=row_low,
        ),
        dict(
            **back_scratch,
            **pairs,
            low_rows=row_low,
            gains_out=((2 * RING, 2, 8, shard), F32),
            gains_in=((2 * RING, 2, 8, shard), F32),
            stage_mlp=pairs[MLP],
            stage_attn=pairs[ATTN],
        ),
        dict(
            far_sem=(2, 2 * RING - 1),
            cross_sem=(2, RING, 2),
            big_sem=(4, 2),
            deal_sem=(2, 2, RING),
            again_sem=(1,),
        ),
    )
    final = lay_out(
        units,
        back_0.fin_mlp,
        back_0.fin_attn,
        down_0=back_0.grad_down,
        down_1=layer_1.grad_down,
        stage_down=back_0.stage_down,
        out_0=back_0.grad_out,
        out_1=layer_1.grad_out,
        stage_out=back_0.stage_out,
        rows_0=layer_0.out,
        rows_1=layer_1.out,
        far_rows=back_0.far_out,
        grads_0=back_0.grad_rows,
        grads_1=layer_1.grad_rows,
        far_low=back_0.far_low,
        far_grads=back_0.far_rows,
    )
    return (
        final.rows,
        final.grads,
        back_0.gain_sum[:1],
        final.query,
        final.key,
        final.value,
        final.out,
        back_0.gain_sum[1:],
        final.gate,
        final.up,
        final.down,
    )


def solution(mesh):
    in_specs = (
        P("dp", None),
        P("dp", None),
        P(),
        P(),
        P(),
        P("section", "dp"),
        P("section", "dp", "tensor"),
        P("section", "dp", "tensor"),
        P("section", "dp", "tensor"),
        P("section", ("tensor", "dp"), None),
        P("section", "dp"),
        P("section", "dp", "tensor"),
        P("section", "dp", "tensor"),
        P("section", ("tensor", "dp"), None),
    )
    out_specs = (
        P("section", "dp", None),
        P("section", "dp", None),
        P("section", "dp"),
        P("section", "dp", "tensor"),
        P("section", "dp", "tensor"),
        P("section", "dp", "tensor"),
        P("section", ("tensor", "dp"), None),
        P("section", "dp"),
        P("section", "dp", "tensor"),
        P("section", "dp", "tensor"),
        P("section", ("tensor", "dp"), None),
    )
    per_device = ring_device if ring_fits(mesh) else general_device
    return jax.shard_map(
        per_device, mesh=mesh, in_specs=in_specs, out_specs=out_specs, check_vma=False
    )
```
